32 devices in a mesh: group: 8 (over y, x, core), mp: 4 (over z).
Axes of the slice: x: 2, y: 2, z: 4, core: 2. Of those that a mesh axis runs over, the one named last changes fastest.
Arguments:
- hidden: bfloat16 [4096, 1792], P('group')
- norm_gain: float32 [1792], replicated, may hold values from 0.1 to 1.9
- qkv_weight: bfloat16 [1792, 2304], P(None, 'mp'), may hold values from -0.125 to 0.125
- out_weight: bfloat16 [1792, 1792], P('mp'), may hold values from -0.125 to 0.125
- adapter_down: bfloat16 [1792, 512], P(None, 'mp'), may hold values from -0.125 to 0.125
- adapter_up: bfloat16 [512, 1792], P('mp'), may hold values from -1.5 to 1.5
- vocab_rows: bfloat16 [512, 1792], P(('group', 'mp')), may hold values from -0.125 to 0.125
- segments: int32 [4096], P('group'), may hold values from 0 to 31, never falling along the last dimension, each value on 1 to 512 neighbouring positions
- request_adapter: int32 [32], replicated, may hold values from 0 to 31
- adapter_slot: int32 [32], replicated, may hold values from 0 to 31, each once
- page_table: int32 [128], replicated, may hold values from 0 to 127, as said below
Outputs:
- layer_update: bfloat16 [4096, 1792], P('group', 'mp')
- state_norms: float32 [16, 4096], P('mp', 'group')
- max_logits: float32 [4096], P(('group', 'mp'))
The draws below stay inside these ranges and needn't reach their ends.
Inputs may be any that keep to these rules, and one draw needn't show every extreme that they name: A permutation of all pages. Logical page k of group g (entry g * 16 + k) lies in group page_table[g * 16 + k] // 16, and every group holds exactly two of the logical pages of every group. `segments`: every request's tokens stand together and in order; no request has more than 512 tokens. `adapter_slot`: A permutation.
All inputs are finite; a program needn't handle non-finite values.
Results may differ from the reference program's by a relative error of at most 0.013.
Values may be sent and summed in bfloat16 or wider, within the bound.
No kernel may reach another device: no remote copies, remote signals or barrier semaphores. Data moves between devices by JAX's collectives and lax.ppermute only.
A program may use at most 64 MiB of HBM per device.

```python
import math
import jax
import jax.numpy as jnp
import numpy as np
from jax import lax

D = 1792
HEADS = 16
FEAT = 16
HD = 112
PHI = 273
RANK = 16
ADAPT_DEV = 8
ADAPTERS = 32
ROWS = 512
REQS = 32
TOKENS = 4096
PAGES_DEV = 16
PAGE = 32
ALL_PAGES = 128
VOCAB = 512
N_MP = 4


def draw_hidden(key, part):
    key_rows, key_cols, key_base = jax.random.split(key, 3)
    row_scale = jnp.exp(jax.random.uniform(key_rows, (TOKENS, 1), jnp.float32, -1.15, 1.15))
    col_scale = jnp.exp(jax.random.uniform(key_cols, (1, D), jnp.float32, -1.15, 1.15))
    pattern = jnp.clip(jax.random.normal(key_base, (TOKENS, D), jnp.float32), -5.0, 5.0)
    return (pattern * row_scale * col_scale).astype(jnp.bfloat16)


def draw_page_table(key, part):
    groups = ALL_PAGES // PAGES_DEV
    key_source, key_slot = jax.random.split(key)
    pattern = jnp.arange(PAGES_DEV, dtype=jnp.int32) % groups
    holders = jax.vmap(lambda sub: jax.random.permutation(sub, pattern))(jax.random.split(key_source, groups))
    sources = holders.reshape(-1)
    onehot = (sources[:, None] == jnp.arange(groups, dtype=jnp.int32)[None, :]).astype(jnp.int32)
    before = jnp.cumsum(onehot, axis=0) - onehot
    ranking = jnp.sum(before * onehot, axis=1)
    shuffles = jax.vmap(lambda sub: jax.random.permutation(sub, PAGES_DEV))(jax.random.split(key_slot, groups))
    slot_ids = shuffles[sources, ranking]
    return (sources * PAGES_DEV + slot_ids).astype(jnp.int32)


def plant(values, rng, least, high):
    longest = values.shape.index(max(values.shape))
    spots = []
    for shift in (0, 1):
        where = [jax.random.randint(jax.random.fold_in(rng, axis), (), 0, length) for axis, length in enumerate(values.shape)]
        where[longest] = (where[longest] + shift) % values.shape[longest]
        spots.append(tuple(where))
    return values.at[spots[0]].set(least).at[spots[1]].set(high)


def block_scale(stream_key, dims, pieces, smallest, high):
    def one(dim, parts):
        steps = jax.random.uniform(jax.random.fold_in(jax.random.fold_in(stream_key, 6), dim), (parts,), jnp.float32, smallest / len(pieces), high / len(pieces))
        return jnp.repeat(jnp.exp(steps), dims[dim] // parts).reshape((-1,) + (1,) * (len(dims) - dim - 1))

    factor_of = one(*pieces[0])
    for cut in pieces[1:]:
        factor_of = factor_of * one(*cut)
    return factor_of


def cumulative_ranks(number_of, skew):
    weights = [(1 << 20) // math.isqrt(standing ** skew) + 1 for standing in range(1, number_of + 1)]
    width = 1 + sum(weights) // (1 << 30)
    return np.cumsum(np.array([max(1, weight // width) for weight in weights]))


def skewed_ids(own_key, extent, amount, slope):
    table = cumulative_ranks(amount, slope)
    lot = jax.random.randint(jax.random.fold_in(own_key, 1), extent, 0, int(table[amount - 1]))
    rank = jnp.searchsorted(jnp.asarray(table, jnp.int32), lot, side="right")
    return jax.random.permutation(jax.random.fold_in(own_key, 2), amount)[rank].astype(jnp.int32)


def profile(count, total, reach, skew):
    weights = [(1 << 20) // math.isqrt(grade ** skew) + 1 for grade in range(2, count + 1)]
    rest, holding = total - reach - (count - 1), [1] * (count - 1)
    while rest > 0:
        free = [i for i in range(count - 1) if holding[i] < reach]
        mass, left = sum([weights[i] for i in free]), rest
        for i in free:
            addition = min(reach - holding[i], max(1, left * weights[i] // mass), rest)
            holding[i] = holding[i] + addition
            rest = rest - addition
    return np.array([reach] + holding)


def ragged_sizes(rng, amount, total, bound, skew):
    if amount == 2:
        one = jax.random.randint(rng, (), max(1, total - bound), min(bound, total - 1) + 1)
        return jnp.stack([one, total - one])
    sizes = jnp.asarray(profile(amount, total, bound, skew), jnp.int32)
    twos = (amount - 1) // 2
    giver, receiver = sizes[1:1 + 2 * twos:2], sizes[2:2 + 2 * twos:2]
    room = jnp.minimum(giver - 1, bound - receiver)
    shifted = jax.random.randint(jax.random.fold_in(rng, 1), (twos,), 0, 1 << 20) % (room + 1)
    sizes = sizes.at[1:1 + 2 * twos:2].set(giver - shifted).at[2:2 + 2 * twos:2].set(receiver + shifted)
    return sizes[jax.random.permutation(jax.random.fold_in(rng, 2), amount)]


def gaussian(stream_key, shape, scale, bound, cuts=(), held_as=jnp.bfloat16):
    level = block_scale(stream_key, shape, cuts, -0.22, 0.18) if cuts else 1.0
    drawn = jax.random.normal(stream_key, shape, jnp.float32) * scale * level
    return jnp.minimum(jnp.maximum(drawn, -bound), bound).astype(held_as)


def setup_inputs(seed: int = 0) -> dict:
    seeds = jax.random.split(jax.random.key(seed), 12)
    hidden = draw_hidden(jax.random.fold_in(seeds[11], 71), 0)
    norm_gain = jnp.clip(1.0 + 0.18 * jax.random.normal(seeds[1], (D,), jnp.float32), 0.1, 1.9)
    qkv_weight = gaussian(seeds[2], (D, HEADS * (2 * FEAT + HD)), D ** -0.5, 0.125, ((1, 4),))
    out_weight = gaussian(seeds[3], (D, D), D ** -0.5, 0.125, ((0, 4),))
    adapter_down = gaussian(seeds[4], (D, ADAPTERS * RANK), D ** -0.5, 0.125, ((1, 4),))
    adapter_up = gaussian(seeds[5], (ADAPTERS * RANK, D), RANK ** -0.5, 1.5, ((0, 4),))
    vocab_rows = gaussian(seeds[6], (VOCAB, D), D ** -0.5, 0.125, ((0, 32),))
    segments = jnp.searchsorted(jnp.cumsum(ragged_sizes(seeds[7], REQS, TOKENS, ROWS, 2)), jnp.arange(TOKENS), side="right").astype(jnp.int32)
    request_adapter = plant(skewed_ids(seeds[8], (REQS,), ADAPTERS, 2), jax.random.fold_in(seeds[8], 3), 0, ADAPTERS - 1).astype(jnp.int32)
    adapter_slot = jax.random.permutation(seeds[9], ADAPTERS).astype(jnp.int32)
    page_table = draw_page_table(jax.random.fold_in(seeds[11], 71), 0)
    return dict(hidden=hidden, norm_gain=norm_gain, qkv_weight=qkv_weight, out_weight=out_weight, adapter_down=adapter_down, adapter_up=adapter_up, vocab_rows=vocab_rows, segments=segments, request_adapter=request_adapter, adapter_slot=adapter_slot, page_table=page_table)


EPSILON = 1e-05
PRECISE = lax.Precision.HIGHEST

def rms_normed(values, norm_gain):
    wide = values.astype(jnp.float32)
    meansq = lax.optimization_barrier(jnp.mean(wide * wide, axis=-1, keepdims=True))
    return (wide * lax.rsqrt(meansq + EPSILON) * norm_gain.astype(jnp.float32)).astype(jnp.bfloat16)

def features(vectors, feat_width):
    linear_part = vectors / feat_width ** 0.25
    outer_part = (vectors[..., :, None] * vectors[..., None, :]).reshape(vectors.shape[:-1] + (feat_width * feat_width,))
    outer_part = outer_part / (2.0 * feat_width) ** 0.5
    ones_part = jnp.ones(vectors.shape[:-1] + (1,), jnp.float32)
    return jnp.concatenate([ones_part, linear_part, outer_part], axis=-1)

def block_step(state_carry, block_inputs, feat_width):
    states, totals, owner_seg = state_carry
    phi_query, phi_key, query_rows, key_rows, value_rows, seg_ids = block_inputs
    scaling = feat_width ** (-0.5)
    block_len = seg_ids.shape[0]
    position = jnp.arange(block_len, dtype=jnp.int32)
    allowed = ((position[:, None] >= position[None, :]) & (seg_ids[:, None] == seg_ids[None, :])).astype(jnp.float32)
    carried = (seg_ids == owner_seg).astype(jnp.float32)[None, :]
    scores = jnp.einsum('hcf,hdf->hcd', query_rows, key_rows, precision=PRECISE) * scaling
    weights = (1.0 + scores + 0.5 * scores * scores) * allowed[None]
    numerator = jnp.einsum('hcd,hde->hce', weights, value_rows, precision=PRECISE)
    numerator = numerator + carried[..., None] * jnp.einsum('hcp,hpe->hce', phi_query, states, precision=PRECISE)
    denominator = lax.optimization_barrier(jnp.sum(weights, axis=-1)) + carried * jnp.einsum('hcp,hp->hc', phi_query, totals, precision=PRECISE)
    mixed_out = numerator / denominator[..., None]
    key_scores = jnp.einsum('hcf,hdf->hcd', key_rows, key_rows, precision=PRECISE) * scaling
    value_gram = jnp.einsum('hce,hde->hcd', value_rows, value_rows, precision=PRECISE)
    key_gram = (1.0 + key_scores + 0.5 * key_scores * key_scores) * value_gram
    masked_gram = jnp.einsum('cd,hde->hce', allowed, key_gram, precision=PRECISE)
    local_squares = lax.optimization_barrier(jnp.sum(masked_gram * allowed[None], axis=-1))
    along = lax.optimization_barrier(jnp.sum(jnp.einsum('hcp,hpe->hce', phi_key, states, precision=PRECISE) * value_rows, axis=-1))
    cross_squares = jnp.einsum('cd,hd->hc', allowed, along, precision=PRECISE)
    state_squares = lax.optimization_barrier(jnp.sum(states * states, axis=(1, 2)))
    squares = carried * (state_squares[:, None] + 2.0 * cross_squares) + local_squares
    counted = carried * totals[:, :1] + lax.optimization_barrier(jnp.sum(allowed, axis=-1))[None, :]
    state_norm = jnp.sqrt(squares / (counted * (feat_width * value_rows.shape[-1])))
    last_seg = seg_ids[-1]
    member = (seg_ids == last_seg).astype(jnp.float32)
    continues = (owner_seg == last_seg).astype(jnp.float32)
    new_states = continues * states + jnp.einsum('hcp,hce->hpe', phi_key * member[None, :, None], value_rows, precision=PRECISE)
    new_totals = continues * totals + jnp.einsum('hcp,c->hp', phi_key, member, precision=PRECISE)
    return ((new_states, new_totals, last_seg), (mixed_out, state_norm))

def reference(hidden, norm_gain, qkv_weight, out_weight, adapter_down, adapter_up, vocab_rows, segments, request_adapter, adapter_slot, page_table):
    ordered = hidden.reshape(ALL_PAGES, PAGE, D)[page_table].reshape(TOKENS, D)
    normed = rms_normed(ordered, norm_gain)
    projected = jnp.dot(normed, qkv_weight, preferred_element_type=jnp.float32).astype(jnp.bfloat16)
    block_len = min(256, ROWS)
    blocks = TOKENS // block_len
    grouped = projected.reshape(blocks, block_len, HEADS, 2 * FEAT + HD)
    seg_blocks = segments.reshape(blocks, block_len)

    def scan_step(state_carry, block_inputs):
        part_rows, seg_ids = block_inputs
        split_heads = jnp.transpose(part_rows.astype(jnp.float32), (1, 0, 2))
        query_rows = split_heads[..., :FEAT]
        key_rows = split_heads[..., FEAT:2 * FEAT]
        value_rows = split_heads[..., 2 * FEAT:]
        return block_step(state_carry, (features(query_rows, FEAT), features(key_rows, FEAT), query_rows, key_rows, value_rows, seg_ids), FEAT)
    initial = (jnp.zeros((HEADS, PHI, HD), jnp.float32), jnp.zeros((HEADS, PHI), jnp.float32), jnp.int32(-1))
    _, (mixed_out, state_norm) = lax.scan(scan_step, initial, (grouped, seg_blocks))
    attended = jnp.transpose(mixed_out, (0, 2, 1, 3)).reshape(TOKENS, HEADS * HD).astype(jnp.bfloat16)
    state_norms = jnp.transpose(state_norm, (1, 0, 2)).reshape(HEADS, TOKENS)
    adapter_of = request_adapter[segments]
    slot_ids = adapter_slot[adapter_of]
    slot_cols = ADAPT_DEV * RANK
    column_slot = jnp.arange(slot_cols, dtype=jnp.int32) // RANK
    head_cols = D // N_MP
    update = jnp.zeros((TOKENS, D), jnp.float32)
    for block_index in range(N_MP):
        lowered = jnp.dot(normed, adapter_down[:, block_index * slot_cols:(block_index + 1) * slot_cols], preferred_element_type=jnp.float32)
        matches = slot_ids[:, None] - block_index * ADAPT_DEV == column_slot[None, :]
        low_rank = jnp.where(matches, lowered, 0.0).astype(jnp.bfloat16)
        partial_value = jnp.dot(attended[:, block_index * head_cols:(block_index + 1) * head_cols], out_weight[block_index * head_cols:(block_index + 1) * head_cols, :], preferred_element_type=jnp.float32)
        partial_value = partial_value + jnp.dot(low_rank, adapter_up[block_index * slot_cols:(block_index + 1) * slot_cols, :], preferred_element_type=jnp.float32)
        rounded = lax.optimization_barrier(partial_value.astype(jnp.bfloat16))
        update = update + rounded.astype(jnp.float32)
    layer_update = update.astype(jnp.bfloat16)
    final_rows = (ordered.astype(jnp.float32) + layer_update.astype(jnp.float32)).astype(jnp.bfloat16)
    score_block = min(1024, TOKENS)

    def row_best(row_block):
        return lax.optimization_barrier(jnp.max(jnp.dot(row_block, vocab_rows.T, preferred_element_type=jnp.float32), axis=1))
    max_logits = lax.map(row_best, final_rows.reshape(TOKENS // score_block, score_block, D)).reshape(TOKENS)
    return (layer_update, state_norms, max_logits)
```

```python
import functools

import jax
import jax.numpy as jnp
import numpy as np
from jax import lax
from jax.experimental import pallas as pl
from jax.experimental.pallas import tpu as pltpu
from jax.sharding import PartitionSpec as P

FEAT = 16
HD = 112
RANK = 16
EPSILON = 1e-05
HEAD = 2 * FEAT + HD
PHI = 1 + FEAT + FEAT * (FEAT + 1) // 2
PHI_PAD = 160
LANES = 128
ONE, TAG, REST = HD, HD + 1, HD + 2
VMEM_LIMIT = 48 * 1024 * 1024

BF = jnp.bfloat16
F32 = jnp.float32
SMEM = pl.BlockSpec(memory_space=pltpu.SMEM)
VMEM = pl.BlockSpec(memory_space=pltpu.VMEM)


def feature_tables():
    left = np.zeros((FEAT, PHI_PAD), np.float32)
    right = np.zeros((FEAT, PHI_PAD), np.float32)
    rows = np.zeros((8, PHI_PAD), np.float32)
    rows[0, 0] = rows[1, 0] = rows[2, 0] = 1.0
    at = 1
    for i in range(FEAT):
        left[i, at] = 1.0
        rows[1, at] = 1.0
        rows[2, at] = FEAT**-0.25
        at += 1
    for i in range(FEAT):
        for j in range(i, FEAT):
            left[i, at] = 1.0
            right[j, at] = 1.0
            rows[2, at] = (1.0 if i == j else 2.0**0.5) / (2.0 * FEAT) ** 0.5
            at += 1
    return left.astype(jnp.bfloat16), right.astype(jnp.bfloat16), rows


def dot(a, b, dims=((1,), (0,))):
    return lax.dot_general(a, b, (dims, ((), ())), preferred_element_type=F32)


def kernel_call(body, out_shape, in_specs, scratch, flops, nbytes):
    outs = jax.tree.map(lambda _: VMEM, out_shape)
    return pl.pallas_call(
        body,
        out_shape=out_shape,
        in_specs=in_specs,
        out_specs=outs,
        scratch_shapes=scratch,
        compiler_params=pltpu.CompilerParams(vmem_limit_bytes=VMEM_LIMIT),
        cost_estimate=pl.CostEstimate(flops=flops, bytes_accessed=nbytes, transcendentals=0),
    )


def pick_pages(table, own, picked, groups, per_group, per_peer):
    def one_group(g, carry):
        spot = g * per_peer
        for k in range(per_group):
            local = table[g * per_group + k] - own * per_group
            picked[spot] = local
            spot = spot + jnp.where((local >= 0) & (local < per_group), 1, 0)
        return carry

    lax.fori_loop(0, groups, one_group, 0)


def place_pages(table, own, seen, source, target, groups, per_group, per_peer, page_len):
    for g in range(groups):
        seen[g] = 0
    for k in range(per_group):
        holder = lax.div(table[own * per_group + k], per_group)
        slot = holder * per_peer + seen[holder]
        seen[holder] = seen[holder] + 1
        start = pl.multiple_of(slot * page_len, page_len)
        target[k * page_len : (k + 1) * page_len, :] = source[pl.ds(start, page_len), :]


def send_pages(source, picked, out_ref, groups, per_peer, page_len):
    for g in range(groups):
        pages = []
        for b in range(per_peer):
            start = pl.multiple_of(picked[g * per_peer + b] * page_len, page_len)
            pages.append(source[pl.ds(start, page_len), :])
        rows = per_peer * page_len
        out_ref[g * rows : (g + 1) * rows, :] = jnp.concatenate(pages, axis=0).astype(BF)


def project_kernel(dims, table, own, hidden, gain, wq, wd, out, normed, wide, picked):
    groups, per_group, per_peer, page_len = dims
    rows = hidden.shape[0]
    low = wd.shape[1]
    pick_pages(table, own[0], picked, groups, per_group, per_peer)
    step = 32
    scale = gain[...]

    def norm_rows(i, carry):
        at = pl.ds(pl.multiple_of(i * step, step), step)
        x = hidden[at, :].astype(F32)
        meansq = jnp.mean(x * x, axis=-1, keepdims=True)
        normed[at, :] = (x * lax.rsqrt(meansq + EPSILON) * scale).astype(BF)
        return carry

    lax.fori_loop(0, rows // step, norm_rows, 0, unroll=2)
    wide[:, :low] = dot(normed[...], wd[...])
    wide[:, low:] = dot(normed[...], wq[...])
    send_pages(wide, picked, out, groups, per_peer, page_len)


def residual_kernel(dims, table, own, hidden, vocab, out, wide, picked):
    groups, per_group, per_peer, page_len = dims
    pick_pages(table, own[0], picked, groups, per_group, per_peer)
    wide[...] = dot(hidden[...], vocab[...], ((1,), (1,)))
    send_pages(wide, picked, out, groups, per_peer, page_len)


def phi_of(vectors, left, right, rows):
    first = dot(vectors, left[...]) + rows[0:1, :]
    second = dot(vectors, right[...]) + rows[1:2, :]
    return first * second * rows[2:3, :]


def head_parts(ordered, low, h):
    at = low + h * HEAD
    return (
        ordered[:, at : at + FEAT],
        ordered[:, at + FEAT : at + 2 * FEAT],
        ordered[:, at + 2 * FEAT : at + HEAD],
    )


def with_ones(values):
    lane = lax.broadcasted_iota(jnp.int32, (values.shape[0], LANES - HD), 1)
    return jnp.concatenate([values, jnp.where(lane == 0, 1.0, 0.0).astype(values.dtype)], axis=1)


def order_kernel(
    dims, low, heads, table, own, arrived, segcol, left, right, rows, out, state, wide, placed, seen
):
    groups, per_group, per_peer, page_len = dims
    wide[...] = arrived[...].astype(F32)
    place_pages(table, own[0], seen, wide, placed, groups, per_group, per_peer, page_len)
    out[...] = placed[...].astype(BF)
    ordered = out[...]
    count = segcol.shape[0]
    last = segcol[count - 1 : count, :]
    member = jnp.where(segcol[...] == last, 1.0, 0.0)
    total = jnp.sum(member, axis=0, keepdims=True)
    rest = total - total.astype(BF).astype(F32)
    tag = last.astype(F32) + 1.0
    row = lax.broadcasted_iota(jnp.int32, (PHI_PAD, LANES), 0)
    lane = lax.broadcasted_iota(jnp.int32, (PHI_PAD, LANES), 1)
    for h in range(heads):
        _, key, value = head_parts(ordered, low, h)
        phi = (phi_of(key, left, right, rows) * member).astype(BF)
        summed = dot(phi, with_ones(value), ((0,), (0,)))
        summed = jnp.where((row == 0) & (lane == TAG), tag, summed)
        summed = jnp.where((row == 0) & (lane == REST), rest, summed)
        state[h] = summed.astype(BF)


def local_kernel(low, heads, ordered_ref, segcol, segrow, nd, squares, mask, mask_t):
    count = segcol.shape[0]
    block = 256 if count % 256 == 0 else count
    behind = lax.broadcasted_iota(jnp.int32, (count, count), 0)
    ahead = lax.broadcasted_iota(jnp.int32, (count, count), 1)
    same = segcol[...] == segrow[...]
    mask[...] = jnp.where(same & (behind >= ahead), 1.0, 0.0)
    mask_t[...] = jnp.where(same & (behind <= ahead), jnp.where(behind == ahead, 1.0, 2.0), 0.0)
    ordered = ordered_ref[...]
    squares[...] = jnp.zeros(squares.shape, F32)
    for h in range(heads):
        query, key, value = head_parts(ordered, low, h)
        extended = with_ones(value)
        scaled_query = query * BF(0.25)
        scaled_key = key * BF(0.25)
        for start in range(0, count, block):
            end = start + block
            s = dot(scaled_query[start:end], key[:end], ((1,), (1,)))
            w = (1.0 + s * (1.0 + 0.5 * s)) * mask[start:end, :end]
            nd[h, start:end, :] = dot(w.astype(BF), extended[:end])
            kk = dot(scaled_key[:end], key[start:end], ((1,), (1,)))
            vv = dot(value[:end], value[start:end], ((1,), (1,)))
            gram = (1.0 + kk * (1.0 + 0.5 * kk)) * vv * mask_t[:end, start:end]
            squares[h : h + 1, start:end] = jnp.sum(gram, axis=0, keepdims=True)
    squares[heads : heads + 1, :] = jnp.sum(jnp.minimum(mask_t[...], 1.0), axis=0, keepdims=True)


def split3(x):
    a = x.astype(BF)
    rest = x - a.astype(F32)
    b = rest.astype(BF)
    return a, b, (rest - b.astype(F32)).astype(BF)


def finish_kernel(
    low, heads, shards, ordered_ref, nd, squares, state, segcol, segrow, slotcol, left, right, rows,
    w_out, w_up, m_all, out, norms, attended
):
    count = segcol.shape[0]
    width = w_out.shape[1] // shards
    ordered = ordered_ref[...]
    corner = state[0, 0:1, :].astype(F32)
    tag = corner[:, TAG : TAG + 1]
    held = corner[:, ONE : ONE + 1] + corner[:, REST : REST + 1]
    carried_col = jnp.where(segcol[...].astype(F32) + 1.0 == tag, 1.0, 0.0)
    carried_row = jnp.where(segrow[...].astype(F32) + 1.0 == tag, 1.0, 0.0)
    behind = lax.broadcasted_iota(jnp.int32, (count, count), 0)
    ahead = lax.broadcasted_iota(jnp.int32, (count, count), 1)
    upto = jnp.where((segcol[...] == segrow[...]) & (behind <= ahead), 1.0, 0.0).astype(BF)
    counted = carried_row * held + squares[heads : heads + 1, :]
    ones = jnp.ones((16, LANES), BF)
    value_lane = lax.broadcasted_iota(jnp.int32, (1, LANES), 1) < HD
    mixed = []
    increments = []
    before = []
    for h in range(heads):
        query, key, value = head_parts(ordered, low, h)
        held_state = state[h]
        cross = dot(phi_of(query, left, right, rows).astype(BF), held_state)
        both = nd[h] + carried_col * cross
        mixed.append((both[:, :HD] / both[:, ONE : ONE + 1]).astype(BF))
        against = dot(phi_of(key, left, right, rows).astype(BF), held_state)[:, :HD] * value.astype(F32)
        coarse = against.astype(BF)
        fine = (against - coarse.astype(F32)).astype(BF)
        along = dot(ones[:, :HD], coarse, ((1,), (1,))) + dot(ones[:, :HD], fine, ((1,), (1,)))
        increments.append(squares[h : h + 1, :] + 2.0 * carried_row * along[0:1, :])
        wide_state = jnp.where(value_lane, held_state.astype(F32), 0.0)
        per_lane = jnp.sum(wide_state * wide_state, axis=0, keepdims=True)
        before.append(jnp.sum(per_lane, axis=1, keepdims=True))
    pad = jnp.zeros((8 - heads % 8, count), F32) if heads % 8 else None
    stacked = jnp.concatenate(increments + ([pad] if pad is not None else []), axis=0)
    summed = sum(dot(part, upto) for part in split3(stacked))
    for h in range(heads):
        total = carried_row * before[h] + summed[h : h + 1, :]
        norms[h : h + 1, :] = jnp.sqrt(total / (counted * float(FEAT * HD)))
    attended[...] = jnp.concatenate(mixed, axis=1)
    column_slot = lax.div(lax.broadcasted_iota(jnp.int32, (1, low), 1), RANK)
    low_rank = jnp.where(slotcol[...] == column_slot, ordered[:, :low].astype(F32), 0.0).astype(BF)
    inner = attended.shape[1]
    portion = m_all.shape[0] // shards
    groups = portion // 16
    for j in range(shards):
        cols = slice(j * width, (j + 1) * width)
        part = dot(attended[...], w_out[:, cols]) + dot(low_rank, w_up[:, cols])
        vocab = jnp.concatenate(
            [m_all[(g * shards + j) * 16 : (g * shards + j + 1) * 16, :] for g in range(groups)], axis=0
        )
        logits = dot(attended[...], vocab[:, :inner], ((1,), (1,))) + dot(low_rank, vocab[:, inner:], ((1,), (1,)))
        out[j] = jnp.concatenate([part, logits], axis=1).astype(BF)


def last_kernel(dims, table, own, summed, arrived, update, best, wide, placed, seen):
    groups, per_group, per_peer, page_len = dims
    width = update.shape[1]
    update[...] = summed[:, :width]
    wide[...] = arrived[...].astype(F32)
    place_pages(table, own[0], seen, wide, placed, groups, per_group, per_peer, page_len)
    logits = placed[...] + summed[:, width:].astype(F32)
    best[...] = jnp.max(jnp.transpose(logits), axis=0, keepdims=True)


def on_device(
    hidden,
    norm_gain,
    qkv_weight,
    out_weight,
    adapter_down,
    adapter_up,
    vocab_rows,
    segments,
    request_adapter,
    adapter_slot,
    page_table,
):
    groups = lax.axis_size("group")
    shards = lax.axis_size("mp")
    own_shard = lax.axis_index("mp")
    own = lax.axis_index("group").astype(jnp.int32).reshape(1)
    count, model_width = hidden.shape
    per_group = page_table.shape[0] // groups
    per_peer = per_group // groups
    page_len = count // per_group
    dims = (groups, per_group, per_peer, page_len)
    qkv_cols = qkv_weight.shape[1]
    heads = qkv_cols // HEAD
    low = adapter_down.shape[1]
    inner = heads * HD
    sent = low + qkv_cols
    width = model_width // shards
    vocab_here = groups * vocab_rows.shape[0]
    shape = jax.ShapeDtypeStruct
    page_scalars = pltpu.SMEM((groups * per_peer + 1,), jnp.int32)

    own_vocab = lax.all_gather(vocab_rows, "group", axis=0, tiled=True)
    some_vocab = lax.all_gather(vocab_rows, "mp", axis=0, tiled=True)
    m_some = jnp.concatenate(
        [
            dot(some_vocab, out_weight, ((1,), (1,))).astype(BF),
            dot(some_vocab, adapter_up, ((1,), (1,))).astype(BF),
        ],
        axis=1,
    )
    m_all = lax.all_gather(m_some, "group", axis=0, tiled=True)

    segcol = segments.reshape(count, 1)
    segrow = segments.reshape(1, count)
    request_ids = jnp.arange(request_adapter.shape[0], dtype=jnp.int32)
    adapter_ids = jnp.arange(adapter_slot.shape[0], dtype=jnp.int32)
    request_slot = jnp.sum(
        jnp.where(request_adapter[:, None] == adapter_ids[None, :], adapter_slot[None, :], 0), axis=1
    )
    slots = jnp.sum(
        jnp.where(segcol == request_ids[None, :], request_slot[None, :], 0), axis=1, keepdims=True
    )
    slotcol = slots - own_shard * (low // RANK)

    left, right, rows = [jnp.asarray(t) for t in feature_tables()]

    outgoing = kernel_call(
        functools.partial(project_kernel, dims),
        shape((count, sent), BF),
        [SMEM, SMEM, VMEM, VMEM, VMEM, VMEM],
        [pltpu.VMEM((count, model_width), BF), pltpu.VMEM((count, sent), F32), page_scalars],
        2 * count * model_width * sent,
        2 * (count * model_width + model_width * sent),
    )(page_table, own, hidden, norm_gain.reshape(1, -1), qkv_weight, adapter_down)
    arrived = lax.all_to_all(
        outgoing.reshape(groups, per_peer * page_len, sent), "group", split_axis=0, concat_axis=0, tiled=True
    ).reshape(count, sent)

    ordered, state = kernel_call(
        functools.partial(order_kernel, dims, low, heads),
        (shape((count, sent), BF), shape((heads, PHI_PAD, LANES), BF)),
        [SMEM, SMEM] + [VMEM] * 5,
        [
            pltpu.VMEM((count, sent), F32),
            pltpu.VMEM((count, sent), F32),
            pltpu.SMEM((groups,), jnp.int32),
        ],
        heads * 2 * count * PHI_PAD * (LANES + 2 * FEAT),
        6 * count * sent,
    )(page_table, own, arrived, segcol, left, right, rows)
    state = lax.ppermute(state, "group", [(i, i + 1) for i in range(groups - 1)])

    nd, squares = kernel_call(
        functools.partial(local_kernel, low, heads),
        (shape((heads, count, LANES), F32), shape((8 * (heads // 8 + 1), count), F32)),
        [VMEM] * 3,
        [pltpu.VMEM((count, count), F32), pltpu.VMEM((count, count), F32)],
        heads * 2 * count * count * 512,
        2 * count * sent + 4 * heads * count * LANES,
    )(ordered, segcol, segrow)

    partial_sums, state_norms = kernel_call(
        functools.partial(finish_kernel, low, heads, shards),
        (shape((shards, count, width + vocab_here), BF), shape((heads, count), F32)),
        [VMEM] * 13,
        [pltpu.VMEM((count, inner), BF)],
        2 * count * (inner + low) * (model_width + shards * vocab_here),
        4 * count * (model_width + shards * vocab_here),
    )(ordered, nd, squares, state, segcol, segrow, slotcol, left, right, rows, out_weight, adapter_up, m_all)

    later_hidden, partial_sums = lax.optimization_barrier((hidden, partial_sums))
    summed = lax.psum_scatter(partial_sums, "mp", scatter_dimension=0, tiled=False)

    residual = kernel_call(
        functools.partial(residual_kernel, dims),
        shape((count, vocab_here), BF),
        [SMEM, SMEM, VMEM, VMEM],
        [pltpu.VMEM((count, vocab_here), F32), page_scalars],
        2 * count * model_width * vocab_here,
        2 * count * model_width,
    )(page_table, own, later_hidden, own_vocab)
    residual = lax.all_to_all(
        residual.reshape(groups, per_peer * page_len, vocab_here), "group", split_axis=0, concat_axis=0, tiled=True
    ).reshape(count, vocab_here)

    update, best = kernel_call(
        functools.partial(last_kernel, dims),
        (shape((count, width), BF), shape((1, count), F32)),
        [SMEM, SMEM, VMEM, VMEM],
        [
            pltpu.VMEM((count, vocab_here), F32),
            pltpu.VMEM((count, vocab_here), F32),
            pltpu.SMEM((groups,), jnp.int32),
        ],
        4 * count * vocab_here,
        4 * count * (width + vocab_here),
    )(page_table, own, summed, residual)
    best = lax.all_to_all(best.reshape(shards, count // shards), "mp", split_axis=0, concat_axis=0, tiled=True)
    return update, state_norms, jnp.max(best, axis=0)


def solution(mesh):
    placed = (
        P("group", None),
        P(),
        P(None, "mp"),
        P("mp", None),
        P(None, "mp"),
        P("mp", None),
        P(("group", "mp"), None),
        P("group"),
        P(),
        P(),
        P(),
    )
    return jax.shard_map(
        on_device,
        mesh=mesh,
        in_specs=placed,
        out_specs=(P("group", "mp"), P("mp", "group"), P(("group", "mp"))),
        check_vma=False,
    )
```

```python
import functools

import jax
import jax.numpy as jnp
import numpy as np
from jax import lax
from jax.experimental import pallas as pl
from jax.experimental.pallas import tpu as pltpu
from jax.sharding import PartitionSpec as P

FEAT = 16
HD = 112
RANK = 16
EPSILON = 1e-05
HEAD = 2 * FEAT + HD
PHI = 1 + FEAT + FEAT * (FEAT + 1) // 2
PHI_PAD = 160
LANES = 128
ONE, TAG, REST = HD, HD + 1, HD + 2
VMEM_LIMIT = 48 * 1024 * 1024

BF = jnp.bfloat16
F32 = jnp.float32
SMEM = pl.BlockSpec(memory_space=pltpu.SMEM)
VMEM = pl.BlockSpec(memory_space=pltpu.VMEM)


def feature_tables():
    left = np.zeros((PHI_PAD, FEAT), np.float32)
    right = np.zeros((PHI_PAD, FEAT), np.float32)
    cols = np.zeros((PHI_PAD, 8), np.float32)
    cols[0, :3] = 1.0
    at = 1
    for i in range(FEAT):
        left[at, i] = 1.0
        cols[at, 1] = 1.0
        cols[at, 2] = FEAT**-0.25
        at += 1
    for i in range(FEAT):
        for j in range(i, FEAT):
            left[at, i] = 1.0
            right[at, j] = 1.0
            cols[at, 2] = (1.0 if i == j else 2.0**0.5) / (2.0 * FEAT) ** 0.5
            at += 1
    return left.astype(jnp.bfloat16), right.astype(jnp.bfloat16), cols


def dot(a, b, dims=((1,), (0,))):
    return lax.dot_general(a, b, (dims, ((), ())), preferred_element_type=F32)


def kernel_call(body, out_shape, in_specs, scratch, flops, nbytes):
    outs = jax.tree.map(lambda _: VMEM, out_shape)
    return pl.pallas_call(
        body,
        out_shape=out_shape,
        in_specs=in_specs,
        out_specs=outs,
        scratch_shapes=scratch,
        compiler_params=pltpu.CompilerParams(vmem_limit_bytes=VMEM_LIMIT),
        cost_estimate=pl.CostEstimate(flops=flops, bytes_accessed=nbytes, transcendentals=0),
    )


def pick_pages(table, own, picked, groups, per_group, per_peer):
    def one_group(g, carry):
        spot = g * per_peer
        for k in range(per_group):
            local = table[g * per_group + k] - own * per_group
            picked[spot] = local
            spot = spot + jnp.where((local >= 0) & (local < per_group), 1, 0)
        return carry

    lax.fori_loop(0, groups, one_group, 0)


def place_pages(table, own, seen, source, target, groups, per_group, per_peer, page_len):
    for g in range(groups):
        seen[g] = 0
    for k in range(per_group):
        holder = lax.div(table[own * per_group + k], per_group)
        slot = holder * per_peer + seen[holder]
        seen[holder] = seen[holder] + 1
        start = pl.multiple_of(slot * page_len, page_len)
        target[k * page_len : (k + 1) * page_len, :] = source[pl.ds(start, page_len), :]


def send_pages(source, picked, out_ref, groups, per_peer, page_len):
    for g in range(groups):
        pages = []
        for b in range(per_peer):
            start = pl.multiple_of(picked[g * per_peer + b] * page_len, page_len)
            pages.append(source[pl.ds(start, page_len), :])
        rows = per_peer * page_len
        out_ref[g * rows : (g + 1) * rows, :] = jnp.concatenate(pages, axis=0).astype(BF)


def project_kernel(dims, table, own, hidden, gain, wq, wd, out, normed, wide, picked):
    groups, per_group, per_peer, page_len = dims
    rows = hidden.shape[0]
    low = wd.shape[1]
    pick_pages(table, own[0], picked, groups, per_group, per_peer)
    step = 32
    scale = gain[...]

    def norm_rows(i, carry):
        at = pl.ds(pl.multiple_of(i * step, step), step)
        x = hidden[at, :].astype(F32)
        meansq = jnp.mean(x * x, axis=-1, keepdims=True)
        normed[at, :] = (x * lax.rsqrt(meansq + EPSILON) * scale).astype(BF)
        return carry

    lax.fori_loop(0, rows // step, norm_rows, 0, unroll=2)
    wide[:, :low] = dot(normed[...], wd[...])
    wide[:, low:] = dot(normed[...], wq[...], ((1,), (1,)))
    send_pages(wide, picked, out, groups, per_peer, page_len)


def residual_kernel(dims, table, own, hidden, vocab, out, wide, picked):
    groups, per_group, per_peer, page_len = dims
    pick_pages(table, own[0], picked, groups, per_group, per_peer)
    wide[...] = dot(hidden[...], vocab[...], ((1,), (1,)))
    send_pages(wide, picked, out, groups, per_peer, page_len)


def phi_of(vectors, left, right, cols):
    first = dot(left[...], vectors) + cols[:, 0:1]
    second = dot(right[...], vectors) + cols[:, 1:2]
    return first * second * cols[:, 2:3]


def with_ones(values):
    lane = lax.broadcasted_iota(jnp.int32, (values.shape[0], LANES - HD), 1)
    return jnp.concatenate([values, jnp.where(lane == 0, 1.0, 0.0).astype(values.dtype)], axis=1)


def with_ones_t(values):
    row = lax.broadcasted_iota(jnp.int32, (LANES - HD, values.shape[1]), 0)
    return jnp.concatenate([values, jnp.where(row == 0, 1.0, 0.0).astype(values.dtype)], axis=0)


def order_kernel(
    dims, low, heads, table, own, arrived, segrow, left, right, cols, out, out_t, state, wide, placed, seen
):
    groups, per_group, per_peer, page_len = dims
    sent = arrived.shape[1]
    wide[...] = arrived[...].astype(F32)
    place_pages(table, own[0], seen, wide, placed, groups, per_group, per_peer, page_len)
    out[...] = placed[...].astype(BF)
    for start in range(0, sent, LANES):
        end = min(start + LANES, sent)
        out_t[start:end, :] = jnp.transpose(placed[:, start:end]).astype(BF)
    count = segrow.shape[1]
    last = segrow[:, count - 1 : count]
    member = jnp.where(segrow[...] == last, 1.0, 0.0)
    total = jnp.sum(member, axis=1, keepdims=True)
    rest = total - total.astype(BF).astype(F32)
    tag = last.astype(F32) + 1.0
    row = lax.broadcasted_iota(jnp.int32, (PHI_PAD, LANES), 0)
    lane = lax.broadcasted_iota(jnp.int32, (PHI_PAD, LANES), 1)
    for h in range(heads):
        at = low + h * HEAD
        phi = (phi_of(out_t[at + FEAT : at + 2 * FEAT, :], left, right, cols) * member).astype(BF)
        summed = dot(phi, with_ones(out[:, at + 2 * FEAT : at + HEAD]))
        summed = jnp.where((row == 0) & (lane == TAG), tag, summed)
        summed = jnp.where((row == 0) & (lane == REST), rest, summed)
        state[h] = summed.astype(BF)


def local_kernel(low, heads, ordered, ordered_t, segcol, segrow, nd, squares, upto, mask):
    count = segcol.shape[0]
    block = 256 if count % 256 == 0 else count
    behind = lax.broadcasted_iota(jnp.int32, (count, count), 0)
    ahead = lax.broadcasted_iota(jnp.int32, (count, count), 1)
    mask[...] = jnp.where((segcol[...] == segrow[...]) & (behind <= ahead), 1.0, 0.0)
    upto[...] = mask[...].astype(BF)
    squares[...] = jnp.zeros(squares.shape, F32)
    for h in range(heads):
        at = low + h * HEAD
        key = ordered[:, at + FEAT : at + 2 * FEAT] * BF(0.25)
        value = ordered[:, at + 2 * FEAT : at + HEAD]
        query_t = ordered_t[at : at + FEAT, :]
        key_t = ordered_t[at + FEAT : at + 2 * FEAT, :]
        value_t = ordered_t[at + 2 * FEAT : at + HEAD, :]
        extended_t = with_ones_t(value_t)
        wide_key = key_t.astype(F32)
        wide_value = value_t.astype(F32)
        self_score = 0.25 * jnp.sum(wide_key * wide_key, axis=0, keepdims=True)
        self_value = jnp.sum(wide_value * wide_value, axis=0, keepdims=True)
        diagonal = (1.0 + self_score * (1.0 + 0.5 * self_score)) * self_value
        for start in range(0, count, block):
            end = start + block
            s = dot(key[:end], query_t[:, start:end])
            w = (1.0 + s * (1.0 + 0.5 * s)) * mask[:end, start:end]
            nd[h, :, start:end] = dot(extended_t[:, :end], w.astype(BF))
            kk = dot(key[:end], key_t[:, start:end])
            vv = dot(value[:end], value_t[:, start:end])
            gram = (1.0 + kk * (1.0 + 0.5 * kk)) * vv * mask[:end, start:end]
            below = jnp.sum(gram, axis=0, keepdims=True)
            squares[h : h + 1, start:end] = 2.0 * below - diagonal[:, start:end]
    squares[heads : heads + 1, :] = jnp.sum(mask[...], axis=0, keepdims=True)


def split3(x):
    a = x.astype(BF)
    rest = x - a.astype(F32)
    b = rest.astype(BF)
    return a, b, (rest - b.astype(F32)).astype(BF)


def finish_kernel(
    low, heads, shards, ordered_t, nd, squares, upto, state, segrow, slotrow, left, right, cols,
    w_t, m_all, out, norms, inputs, vocab
):
    count = segrow.shape[1]
    width = w_t.shape[0] // shards
    vocab_here = vocab.shape[0] // shards
    block = count // shards
    corner = state[0, 0:1, :].astype(F32)
    tag = corner[:, TAG : TAG + 1]
    held = corner[:, ONE : ONE + 1] + corner[:, REST : REST + 1]
    carried = jnp.where(segrow[...].astype(F32) + 1.0 == tag, 1.0, 0.0)
    counted = carried * held + squares[heads : heads + 1, :]
    value_lane = lax.broadcasted_iota(jnp.int32, (1, LANES), 1) < HD
    increments = []
    before = []
    for h in range(heads):
        at = low + h * HEAD
        query_t = ordered_t[at : at + FEAT, :]
        key_t = ordered_t[at + FEAT : at + 2 * FEAT, :]
        value_t = ordered_t[at + 2 * FEAT : at + HEAD, :].astype(F32)
        held_state = state[h]
        cross = dot(held_state, phi_of(query_t, left, right, cols).astype(BF), ((0,), (0,)))
        both = nd[h] + carried * cross
        inputs[h * HD : (h + 1) * HD, :] = (both[:HD, :] / both[ONE : ONE + 1, :]).astype(BF)
        against = dot(held_state, phi_of(key_t, left, right, cols).astype(BF), ((0,), (0,)))[:HD, :]
        along = jnp.sum(against * value_t, axis=0, keepdims=True)
        increments.append(squares[h : h + 1, :] + 2.0 * carried * along)
        wide_state = jnp.where(value_lane, held_state.astype(F32), 0.0)
        per_lane = jnp.sum(wide_state * wide_state, axis=0, keepdims=True)
        before.append(jnp.sum(per_lane, axis=1, keepdims=True))
    if heads % 8:
        increments.append(jnp.zeros((8 - heads % 8, count), F32))
    stacked = jnp.concatenate(increments, axis=0)
    summed = sum(dot(part, upto[...]) for part in split3(stacked))
    for h in range(heads):
        total = carried * before[h] + summed[h : h + 1, :]
        norms[h : h + 1, :] = jnp.sqrt(total / (counted * float(FEAT * HD)))
    row_slot = lax.div(lax.broadcasted_iota(jnp.int32, (low, 1), 0), RANK)
    lowered = jnp.where(slotrow[...] == row_slot, ordered_t[:low, :].astype(F32), 0.0)
    inputs[heads * HD :, :] = lowered.astype(BF)
    groups = vocab_here // 16
    for i in range(shards):
        for g in range(groups):
            at = (g * shards + i) * 16
            vocab[(i * groups + g) * 16 : (i * groups + g + 1) * 16, :] = m_all[at : at + 16, :]
    for j in range(shards):
        rows = slice(j * width, (j + 1) * width)
        out[j, :width, :] = dot(w_t[rows, :], inputs[...]).astype(BF)
    for i in range(shards):
        rows = slice(i * vocab_here, (i + 1) * vocab_here)
        logits = dot(vocab[rows, :], inputs[...]).astype(BF)
        for j in range(shards):
            out[j, width:, i * block : (i + 1) * block] = logits[:, j * block : (j + 1) * block]


def turn_kernel(dims, shards, table, own, arrived, out, wide, placed, seen):
    groups, per_group, per_peer, page_len = dims
    wide[...] = arrived[...].astype(F32)
    place_pages(table, own[0], seen, wide, placed, groups, per_group, per_peer, page_len)
    turned = jnp.transpose(placed[...]).astype(BF)
    block = turned.shape[1] // shards
    for j in range(shards):
        out[j] = turned[:, j * block : (j + 1) * block]


def last_kernel(shards, *refs):
    *pieces, residual, update, best = refs
    width = update.shape[0]
    third = len(pieces) // 3
    wholes = []
    for part in range(third):
        a, b, c = [pieces[k * third + part][...].astype(F32) for k in range(3)]
        wholes.append(a + b + c)
    whole = jnp.concatenate(wholes, axis=0)
    update[...] = whole[:width].astype(BF)
    block = best.shape[1]
    top = None
    for i in range(shards):
        logits = whole[width:, i * block : (i + 1) * block] + residual[i].astype(F32)
        highest = jnp.max(logits, axis=0, keepdims=True)
        top = highest if top is None else jnp.maximum(top, highest)
    best[...] = top


def exchanged(values, axis):
    size = lax.axis_size(axis)
    spread = jnp.broadcast_to(values[None], (size,) + values.shape)
    return lax.all_to_all(spread, axis, split_axis=0, concat_axis=0, tiled=True)


def line_sums(shards_of, axis):
    size = lax.axis_size(axis)
    here = lax.axis_index(axis)

    def shard(at):
        return lax.dynamic_index_in_dim(shards_of, jnp.clip(at, 0, size - 1), 0, keepdims=False)

    up = down = None
    for step in range(1, size):
        to_up = shard(size - step + here)
        to_down = shard(here - (size - step))
        if step > 1:
            to_up = (to_up.astype(F32) + up.astype(F32)).astype(BF)
            to_down = (to_down.astype(F32) + down.astype(F32)).astype(BF)
        up = lax.ppermute(to_up, axis, [(i, i + 1) for i in range(step)])
        down = lax.ppermute(to_down, axis, [(i, i - 1) for i in range(size - 1, size - 1 - step, -1)])
    return shard(here), up, down


def on_device(
    hidden,
    norm_gain,
    qkv_weight,
    out_weight,
    adapter_down,
    adapter_up,
    vocab_rows,
    segments,
    request_adapter,
    adapter_slot,
    page_table,
):
    groups = lax.axis_size("group")
    shards = lax.axis_size("mp")
    own_shard = lax.axis_index("mp")
    own = lax.axis_index("group").astype(jnp.int32).reshape(1)
    count, model_width = hidden.shape
    per_group = page_table.shape[0] // groups
    per_peer = per_group // groups
    page_len = count // per_group
    dims = (groups, per_group, per_peer, page_len)
    qkv_cols = qkv_weight.shape[1]
    heads = qkv_cols // HEAD
    low = adapter_down.shape[1]
    inner = heads * HD
    sent = low + qkv_cols
    width = model_width // shards
    vocab_here = groups * vocab_rows.shape[0]
    shape = jax.ShapeDtypeStruct
    page_scalars = pltpu.SMEM((groups * per_peer + 1,), jnp.int32)

    left, right, cols = [jnp.asarray(t) for t in feature_tables()]
    segcol = segments.reshape(count, 1)
    segrow = segments.reshape(1, count)
    request_ids = jnp.arange(request_adapter.shape[0], dtype=jnp.int32)
    adapter_ids = jnp.arange(adapter_slot.shape[0], dtype=jnp.int32)
    request_slot = jnp.sum(
        jnp.where(request_adapter[:, None] == adapter_ids[None, :], adapter_slot[None, :], 0), axis=1
    )
    slots = jnp.sum(jnp.where(segrow == request_ids[:, None], request_slot[:, None], 0), axis=0, keepdims=True)
    slotrow = slots - own_shard * (low // RANK)

    outgoing = kernel_call(
        functools.partial(project_kernel, dims),
        shape((count, sent), BF),
        [SMEM, SMEM, VMEM, VMEM, VMEM, VMEM],
        [pltpu.VMEM((count, model_width), BF), pltpu.VMEM((count, sent), F32), page_scalars],
        2 * count * model_width * sent,
        2 * (count * model_width + model_width * sent),
    )(page_table, own, hidden, norm_gain.reshape(1, -1), qkv_weight.T, adapter_down)
    arrived = lax.all_to_all(
        outgoing.reshape(groups, per_peer * page_len, sent), "group", split_axis=0, concat_axis=0, tiled=True
    ).reshape(count, sent)

    vocab_after, _ = lax.optimization_barrier((vocab_rows, outgoing))
    some_vocab = exchanged(vocab_after, "mp").reshape(-1, model_width)
    m_some = jnp.concatenate(
        [
            dot(some_vocab, out_weight, ((1,), (1,))).astype(BF),
            dot(some_vocab, adapter_up, ((1,), (1,))).astype(BF),
        ],
        axis=1,
    )
    m_all = exchanged(m_some, "group").reshape(-1, inner + low)
    w_t = jnp.concatenate([out_weight.T, adapter_up.T], axis=1)

    ordered, ordered_t, state = kernel_call(
        functools.partial(order_kernel, dims, low, heads),
        (shape((count, sent), BF), shape((sent, count), BF), shape((heads, PHI_PAD, LANES), BF)),
        [SMEM, SMEM] + [VMEM] * 5,
        [
            pltpu.VMEM((count, sent), F32),
            pltpu.VMEM((count, sent), F32),
            pltpu.SMEM((groups,), jnp.int32),
        ],
        heads * 2 * count * PHI_PAD * (LANES + 2 * FEAT),
        6 * count * sent,
    )(page_table, own, arrived, segrow, left, right, cols)
    state = lax.ppermute(state, "group", [(i, i + 1) for i in range(groups - 1)])

    nd, squares, upto = kernel_call(
        functools.partial(local_kernel, low, heads),
        (
            shape((heads, LANES, count), F32),
            shape((8 * (heads // 8 + 1), count), F32),
            shape((count, count), BF),
        ),
        [VMEM] * 4,
        [pltpu.VMEM((count, count), F32)],
        heads * 2 * count * count * 512,
        4 * count * sent + 4 * heads * count * LANES,
    )(ordered, ordered_t, segcol, segrow)

    partial_sums, state_norms = kernel_call(
        functools.partial(finish_kernel, low, heads, shards),
        (shape((shards, width + vocab_here, count), BF), shape((heads, count), F32)),
        [VMEM] * 12,
        [pltpu.VMEM((inner + low, count), BF), pltpu.VMEM((shards * vocab_here, inner + low), BF)],
        2 * count * (inner + low) * (model_width + shards * vocab_here),
        4 * count * (model_width + shards * vocab_here),
    )(ordered_t, nd, squares, upto, state, segrow, slotrow, left, right, cols, w_t, m_all)

    parts = 2
    rows = (width + vocab_here) // parts
    pieces = [line_sums(partial_sums[:, k * rows : (k + 1) * rows], "mp") for k in range(parts)]

    later_hidden, later_vocab, _ = lax.optimization_barrier((hidden, vocab_rows, nd))
    own_vocab = exchanged(later_vocab, "group").reshape(vocab_here, model_width)
    residual = kernel_call(
        functools.partial(residual_kernel, dims),
        shape((count, vocab_here), BF),
        [SMEM, SMEM, VMEM, VMEM],
        [pltpu.VMEM((count, vocab_here), F32), page_scalars],
        2 * count * model_width * vocab_here,
        2 * count * model_width,
    )(page_table, own, later_hidden, own_vocab)
    residual = lax.all_to_all(
        residual.reshape(groups, per_peer * page_len, vocab_here), "group", split_axis=0, concat_axis=0, tiled=True
    ).reshape(count, vocab_here)
    residual = kernel_call(
        functools.partial(turn_kernel, dims, shards),
        shape((shards, vocab_here, count // shards), BF),
        [SMEM, SMEM, VMEM],
        [
            pltpu.VMEM((count, vocab_here), F32),
            pltpu.VMEM((count, vocab_here), F32),
            pltpu.SMEM((groups,), jnp.int32),
        ],
        count * vocab_here,
        4 * count * vocab_here,
    )(page_table, own, residual)
    residual = lax.all_to_all(residual, "mp", split_axis=0, concat_axis=0, tiled=True)

    update, best = kernel_call(
        functools.partial(last_kernel, shards),
        (shape((width, count), BF), shape((1, count // shards), F32)),
        [VMEM] * (3 * parts + 1),
        [],
        4 * count * vocab_here,
        8 * count * (width + vocab_here),
    )(*[piece[k] for k in range(3) for piece in pieces], residual)
    return update.T, state_norms, best.reshape(-1)


def solution(mesh):
    placed = (
        P("group", None),
        P(),
        P(None, "mp"),
        P("mp", None),
        P(None, "mp"),
        P("mp", None),
        P(("group", "mp"), None),
        P("group"),
        P(),
        P(),
        P(),
    )
    return jax.shard_map(
        on_device,
        mesh=mesh,
        in_specs=placed,
        out_specs=(P("group", "mp"), P("mp", "group"), P(("group", "mp"))),
        check_vma=False,
    )
```

```python
import functools

import jax
import jax.numpy as jnp
import numpy as np
from jax import lax
from jax.experimental import pallas as pl
from jax.experimental.pallas import tpu as pltpu
from jax.sharding import PartitionSpec as P

FEAT = 16
HD = 112
RANK = 16
EPSILON = 1e-05
HEAD = 2 * FEAT + HD
PHI = 1 + FEAT + FEAT * (FEAT + 1) // 2
PHI_PAD = 160
LANES = 128
ONE, TAG, REST = HD, HD + 1, HD + 2
VMEM_LIMIT = 32 * 1024 * 1024

BF = jnp.bfloat16
F32 = jnp.float32
SMEM = pl.BlockSpec(memory_space=pltpu.SMEM)
VMEM = pl.BlockSpec(memory_space=pltpu.VMEM)
ANY = pl.BlockSpec(memory_space=pl.ANY)


def feature_tables():
    left = np.zeros((PHI_PAD, FEAT), np.float32)
    right = np.zeros((PHI_PAD, FEAT), np.float32)
    cols = np.zeros((PHI_PAD, 8), np.float32)
    cols[0, :3] = 1.0
    at = 1
    for i in range(FEAT):
        left[at, i] = 1.0
        cols[at, 1] = 1.0
        cols[at, 2] = FEAT**-0.25
        at += 1
    for i in range(FEAT):
        for j in range(i, FEAT):
            left[at, i] = 1.0
            right[at, j] = 1.0
            cols[at, 2] = (1.0 if i == j else 2.0**0.5) / (2.0 * FEAT) ** 0.5
            at += 1
    return left.astype(jnp.bfloat16), right.astype(jnp.bfloat16), cols


def dot(a, b, dims=((1,), (0,))):
    return lax.dot_general(a, b, (dims, ((), ())), preferred_element_type=F32)


def kernel_call(body, out_shape, in_specs, out_specs, scratch, flops, nbytes):
    return pl.pallas_call(
        body,
        out_shape=out_shape,
        in_specs=in_specs,
        out_specs=out_specs,
        scratch_shapes=scratch,
        compiler_params=pltpu.CompilerParams(vmem_limit_bytes=VMEM_LIMIT),
        cost_estimate=pl.CostEstimate(flops=flops, bytes_accessed=nbytes, transcendentals=0),
    )


def start(source, target, sem):
    copy = pltpu.make_async_copy(source, target, sem)
    copy.start()
    return copy


def packing(columns, rows):
    rest = columns % LANES
    share = LANES // rest if rest and LANES % rest == 0 else 1
    if rows % (16 * share):
        share = 1
    return columns // LANES, rest, share


def pick_pages(table, own, picked, groups, per_group, per_peer):
    def one_group(g, carry):
        spot = g * per_peer
        for k in range(per_group):
            local = table[g * per_group + k] - own * per_group
            picked[spot] = local
            spot = spot + jnp.where((local >= 0) & (local < per_group), 1, 0)
        return carry

    lax.fori_loop(0, groups, one_group, 0)


def place_pages(table, own, seen, source, target, groups, per_group, per_peer, page_len):
    for g in range(groups):
        seen[g] = 0
    for k in range(per_group):
        holder = lax.div(table[own * per_group + k], per_group)
        slot = holder * per_peer + seen[holder]
        seen[holder] = seen[holder] + 1
        start = pl.multiple_of(slot * page_len, page_len)
        target[k * page_len : (k + 1) * page_len, :] = source[pl.ds(start, page_len), :]


def picked_rows(source, picked, g, per_peer, page_len):
    pages = []
    for b in range(per_peer):
        at = pl.multiple_of(picked[g * per_peer + b] * page_len, page_len)
        pages.append(source[pl.ds(at, page_len), :])
    return jnp.concatenate(pages, axis=0)


def project_kernel(
    dims, table, own, hidden_in, gain, wq_in, wd_in, out_in, hidden, wq, wd, normed, wide, out, picked, sems
):
    groups, per_group, per_peer, page_len = dims
    rows = hidden.shape[0]
    low = wd.shape[1]
    pieces = 4
    part = rows // pieces
    strip = wq.shape[0] // 2
    loads = [
        start(hidden_in.at[pl.ds(k * part, part)], hidden.at[pl.ds(k * part, part)], sems.at[k]) for k in range(pieces)
    ]
    weights = [start(wd_in, wd, sems.at[pieces])]
    for k in range(2):
        half = pl.ds(k * strip, strip)
        weights.append(start(wq_in.at[half], wq.at[half], sems.at[pieces + 1 + k]))
    pick_pages(table, own[0], picked, groups, per_group, per_peer)
    step = 32
    scale = gain[...]

    def norm_rows(i, carry):
        at = pl.ds(pl.multiple_of(i * step, step), step)
        x = hidden[at, :].astype(F32)
        meansq = jnp.mean(x * x, axis=-1, keepdims=True)
        normed[at, :] = (x * lax.rsqrt(meansq + EPSILON) * scale).astype(BF)
        return carry

    for k in range(pieces):
        loads[k].wait()
        lax.fori_loop(k * part // step, (k + 1) * part // step, norm_rows, 0, unroll=2)
    for load in weights:
        load.wait()
    wide[:, :low] = dot(normed[...], wd[...])
    wide[:, low:] = dot(normed[...], wq[...], ((1,), (1,)))
    tall = per_peer * page_len
    tiles, rest, share = packing(wide.shape[1], tall)
    sends = []
    for g in range(groups):
        block = picked_rows(wide, picked, g, per_peer, page_len)
        for t in range(tiles):
            out[g, t * tall : (t + 1) * tall, :] = block[:, t * LANES : (t + 1) * LANES].astype(BF)
        if rest:
            short = tall // share
            last = [block[q * short : (q + 1) * short, tiles * LANES :] for q in range(share)]
            if share * rest < LANES:
                last.append(jnp.zeros((short, LANES - share * rest), F32))
            out[g, tiles * tall :, :] = jnp.concatenate(last, axis=1).astype(BF)
        sends.append(start(out.at[g], out_in.at[g], sems.at[pieces + 3 + g]))
    for send in sends:
        send.wait()


def residual_kernel(dims, shards, table, own, hidden, out, wide, picked):
    groups, per_group, per_peer, page_len = dims
    pick_pages(table, own[0], picked, groups, per_group, per_peer)
    width = wide.shape[1]
    for j in range(shards):

        @pl.when(own[1] == j)
        def _():
            wide[...] = hidden[:, j * width : (j + 1) * width].astype(F32)

    tall = per_peer * page_len
    for g in range(groups):
        out[g * tall : (g + 1) * tall, :] = picked_rows(wide, picked, g, per_peer, page_len).astype(BF)


def phi_of(vectors, left, right, cols):
    first = dot(left[...], vectors) + cols[:, 0:1]
    second = dot(right[...], vectors) + cols[:, 1:2]
    return first * second * cols[:, 2:3]


def with_ones(values):
    lane = lax.broadcasted_iota(jnp.int32, (values.shape[0], LANES - HD), 1)
    return jnp.concatenate([values, jnp.where(lane == 0, 1.0, 0.0).astype(values.dtype)], axis=1)


def with_ones_t(values):
    row = lax.broadcasted_iota(jnp.int32, (LANES - HD, values.shape[1]), 0)
    return jnp.concatenate([values, jnp.where(row == 0, 1.0, 0.0).astype(values.dtype)], axis=0)


def order_kernel(
    dims, low, heads, table, own, arrived_in, segrow, left, right, cols, out_in, out_t_in, state,
    arrived, wide, placed, out, out_t, seen, sems
):
    groups, per_group, per_peer, page_len = dims
    sent = placed.shape[1]
    tall = per_peer * page_len
    tiles, rest, share = packing(sent, tall)
    loads = [start(arrived_in.at[g], arrived.at[g], sems.at[g]) for g in range(groups)]
    for g in range(groups):
        loads[g].wait()
        rows = slice(g * tall, (g + 1) * tall)
        for t in range(tiles):
            wide[rows, t * LANES : (t + 1) * LANES] = arrived[g, t * tall : (t + 1) * tall, :].astype(F32)
        if rest:
            short = tall // share
            last = arrived[g, tiles * tall :, :].astype(F32)
            for q in range(share):
                at = g * tall + q * short
                wide[at : at + short, tiles * LANES :] = last[:, q * rest : (q + 1) * rest]
    place_pages(table, own[0], seen, wide, placed, groups, per_group, per_peer, page_len)
    out[...] = placed[...].astype(BF)
    first = start(out, out_in, sems.at[0])
    for at in range(0, sent, LANES):
        end = min(at + LANES, sent)
        out_t[at:end, :] = jnp.transpose(placed[:, at:end]).astype(BF)
    second = start(out_t, out_t_in, sems.at[1])
    count = segrow.shape[1]
    last = segrow[:, count - 1 : count]
    member = jnp.where(segrow[...] == last, 1.0, 0.0)
    total = jnp.sum(member, axis=1, keepdims=True)
    fine = total - total.astype(BF).astype(F32)
    tag = last.astype(F32) + 1.0
    row = lax.broadcasted_iota(jnp.int32, (PHI_PAD, LANES), 0)
    lane = lax.broadcasted_iota(jnp.int32, (PHI_PAD, LANES), 1)
    for h in range(heads):
        at = low + h * HEAD
        phi = (phi_of(out_t[at + FEAT : at + 2 * FEAT, :], left, right, cols) * member).astype(BF)
        summed = dot(phi, with_ones(out[:, at + 2 * FEAT : at + HEAD]))
        summed = jnp.where((row == 0) & (lane == TAG), tag, summed)
        summed = jnp.where((row == 0) & (lane == REST), fine, summed)
        state[h] = summed.astype(BF)
    first.wait()
    second.wait()


def same_upto(segrow):
    count = segrow.shape[1]
    ids = segrow[...].astype(F32)
    column = jnp.transpose(jnp.broadcast_to(ids, (8, count)))[:, 0:1]
    behind = lax.broadcasted_iota(jnp.int32, (count, count), 0)
    ahead = lax.broadcasted_iota(jnp.int32, (count, count), 1)
    return jnp.where((column == ids) & (behind <= ahead), 1.0, 0.0)


def local_kernel(low, heads, ordered_in, ordered_t_in, segrow, nd, squares, ordered, ordered_t, mask, sems):
    count = segrow.shape[1]
    block = 256 if count % 256 == 0 else count
    first = start(ordered_in, ordered, sems.at[0])
    second = start(ordered_t_in, ordered_t, sems.at[1])
    mask[...] = same_upto(segrow)
    squares[...] = jnp.zeros(squares.shape, F32)
    squares[heads : heads + 1, :] = jnp.sum(mask[...], axis=0, keepdims=True)
    first.wait()
    second.wait()
    for h in range(heads):
        at = low + h * HEAD
        key = ordered[:, at + FEAT : at + 2 * FEAT] * BF(0.25)
        value = ordered[:, at + 2 * FEAT : at + HEAD]
        query_t = ordered_t[at : at + FEAT, :]
        key_t = ordered_t[at + FEAT : at + 2 * FEAT, :]
        value_t = ordered_t[at + 2 * FEAT : at + HEAD, :]
        extended_t = with_ones_t(value_t)
        wide_key = key_t.astype(F32)
        wide_value = value_t.astype(F32)
        self_score = 0.25 * jnp.sum(wide_key * wide_key, axis=0, keepdims=True)
        self_value = jnp.sum(wide_value * wide_value, axis=0, keepdims=True)
        diagonal = (1.0 + self_score * (1.0 + 0.5 * self_score)) * self_value
        for begin in range(0, count, block):
            end = begin + block
            s = dot(key[:end], query_t[:, begin:end])
            w = (1.0 + s * (1.0 + 0.5 * s)) * mask[:end, begin:end]
            nd[h, :, begin:end] = dot(extended_t[:, :end], w.astype(BF))
            kk = dot(key[:end], key_t[:, begin:end])
            vv = dot(value[:end], value_t[:, begin:end])
            gram = (1.0 + kk * (1.0 + 0.5 * kk)) * vv * mask[:end, begin:end]
            below = jnp.sum(gram, axis=0, keepdims=True)
            squares[h : h + 1, begin:end] = 2.0 * below - diagonal[:, begin:end]


def split3(x):
    a = x.astype(BF)
    rest = x - a.astype(F32)
    b = rest.astype(BF)
    return jnp.concatenate([a, b, (rest - b.astype(F32)).astype(BF)], axis=0)


def finish_kernel(
    low, heads, shards, own, ordered_t_in, nd, squares, state, segrow, slotrow, left, right, cols, w_t_in, *refs
):
    offsets = 2 * shards - 1
    outs = refs[:offsets]
    norms, inputs, ordered_t, w_t, held_out, sems = refs[offsets:]
    count = segrow.shape[1]
    width = w_t.shape[0] // shards
    fetch = start(ordered_t_in, ordered_t, sems.at[offsets])
    weights = start(w_t_in, w_t, sems.at[offsets + 1])
    upto = same_upto(segrow).astype(BF)
    corner = state[0, 0:1, :].astype(F32)
    tag = corner[:, TAG : TAG + 1]
    held = corner[:, ONE : ONE + 1] + corner[:, REST : REST + 1]
    carried = jnp.where(segrow[...].astype(F32) + 1.0 == tag, 1.0, 0.0)
    row_slot = lax.div(lax.broadcasted_iota(jnp.int32, (low, 1), 0), RANK)
    fetch.wait()
    lowered = jnp.where(slotrow[...] == row_slot, ordered_t[:low, :].astype(F32), 0.0)
    inputs[heads * HD :, :] = lowered.astype(BF)
    for h in range(heads):
        at = low + h * HEAD
        cross = dot(state[h], phi_of(ordered_t[at : at + FEAT, :], left, right, cols).astype(BF), ((0,), (0,)))
        both = nd[h] + carried * cross
        inputs[h * HD : (h + 1) * HD, :] = (both[:HD, :] / both[ONE : ONE + 1, :]).astype(BF)
    weights.wait()
    order = sorted(range(offsets), key=lambda k: -abs(k - (shards - 1)))
    for k in order:
        j = own[1] + (k - (shards - 1))

        @pl.when((j >= 0) & (j < shards))
        def _(j=j, k=k):
            rows = pl.ds(pl.multiple_of(j * width, width), width)
            held_out[j] = dot(w_t[rows, :], inputs[...]).astype(BF)
            start(held_out.at[j], outs[k], sems.at[k])

    value_lane = lax.broadcasted_iota(jnp.int32, (1, LANES), 1) < HD
    counted = carried * held + squares[heads : heads + 1, :]
    increments = []
    before = []
    for h in range(heads):
        at = low + h * HEAD
        held_state = state[h]
        key_t = ordered_t[at + FEAT : at + 2 * FEAT, :]
        value_t = ordered_t[at + 2 * FEAT : at + HEAD, :].astype(F32)
        against = dot(held_state, phi_of(key_t, left, right, cols).astype(BF), ((0,), (0,)))[:HD, :]
        along = jnp.sum(against * value_t, axis=0, keepdims=True)
        increments.append(squares[h : h + 1, :] + 2.0 * carried * along)
        wide_state = jnp.where(value_lane, held_state.astype(F32), 0.0)
        per_lane = jnp.sum(wide_state * wide_state, axis=0, keepdims=True)
        before.append(jnp.sum(per_lane, axis=1, keepdims=True))
    if heads % 8:
        increments.append(jnp.zeros((8 - heads % 8, count), F32))
    stacked = split3(jnp.concatenate(increments, axis=0))
    thrice = dot(stacked, upto)
    rows = thrice.shape[0] // 3
    summed = thrice[:rows] + thrice[rows : 2 * rows] + thrice[2 * rows :]
    for h in range(heads):
        total = carried * before[h] + summed[h : h + 1, :]
        norms[h : h + 1, :] = jnp.sqrt(total / (counted * float(FEAT * HD)))
    for k in order:
        j = own[1] + (k - (shards - 1))

        @pl.when((j >= 0) & (j < shards))
        def _(j=j, k=k):
            pltpu.make_async_copy(held_out.at[j], outs[k], sems.at[k]).wait()


def logits_kernel(dims, shards, table, own, arrived, inputs, vocab, out, wide, placed, seen):
    groups, per_group, per_peer, page_len = dims
    wide[...] = arrived[...].astype(F32)
    place_pages(table, own[0], seen, wide, placed, groups, per_group, per_peer, page_len)
    inner = inputs.shape[0]
    residual_t = jnp.transpose(placed[...]).astype(BF)
    block = inputs.shape[1] // shards
    logits = dot(vocab[:, :inner], inputs[...]) + dot(vocab[:, inner:], residual_t)
    for j in range(shards):
        out[j] = logits[:, j * block : (j + 1) * block].astype(BF)


def best_kernel(shards, pieces, best):
    whole = pieces[0].astype(F32)
    for i in range(1, shards):
        whole = whole + pieces[i].astype(F32)
    best[...] = jnp.max(whole, axis=0, keepdims=True)


def exchanged(values, axis):
    size = lax.axis_size(axis)
    spread = jnp.broadcast_to(values[None], (size,) + values.shape)
    return lax.all_to_all(spread, axis, split_axis=0, concat_axis=0, tiled=True)


def line_sums(shards_at, axis):
    size = lax.axis_size(axis)
    up = down = None
    for step in range(1, size):
        to_up = shards_at[2 * size - 1 - step]
        to_down = shards_at[step - 1]
        if step > 1:
            to_up = (to_up.astype(F32) + up.astype(F32)).astype(BF)
            to_down = (to_down.astype(F32) + down.astype(F32)).astype(BF)
        up = lax.ppermute(to_up, axis, [(i, i + 1) for i in range(step)])
        down = lax.ppermute(to_down, axis, [(i, i - 1) for i in range(size - 1, size - 1 - step, -1)])
    total = shards_at[size - 1].astype(F32) + up.astype(F32) + down.astype(F32)
    return total.astype(BF)


def on_device(
    hidden,
    norm_gain,
    qkv_weight,
    out_weight,
    adapter_down,
    adapter_up,
    vocab_rows,
    segments,
    request_adapter,
    adapter_slot,
    page_table,
):
    groups = lax.axis_size("group")
    shards = lax.axis_size("mp")
    own_shard = lax.axis_index("mp")
    own = lax.axis_index("group").astype(jnp.int32).reshape(1)
    count, model_width = hidden.shape
    per_group = page_table.shape[0] // groups
    per_peer = per_group // groups
    page_len = count // per_group
    dims = (groups, per_group, per_peer, page_len)
    qkv_cols = qkv_weight.shape[1]
    heads = qkv_cols // HEAD
    low = adapter_down.shape[1]
    inner = heads * HD
    sent = low + qkv_cols
    width = model_width // shards
    vocab_here = groups * vocab_rows.shape[0]
    shape = jax.ShapeDtypeStruct
    page_scalars = pltpu.SMEM((groups * per_peer + 1,), jnp.int32)

    tall = per_peer * page_len
    tiles, rest, share = packing(sent, tall)
    packed = tiles * tall + (tall // share if rest else 0)
    dma = pltpu.SemaphoreType.DMA
    place = jnp.concatenate([own, own_shard.astype(jnp.int32).reshape(1)])

    left, right, cols = [jnp.asarray(t) for t in feature_tables()]
    segrow = segments.reshape(1, count)
    request_ids = jnp.arange(request_adapter.shape[0], dtype=jnp.int32)
    adapter_ids = jnp.arange(adapter_slot.shape[0], dtype=jnp.int32)
    request_slot = jnp.sum(
        jnp.where(request_adapter[:, None] == adapter_ids[None, :], adapter_slot[None, :], 0), axis=1
    )
    slots = jnp.sum(jnp.where(segrow == request_ids[:, None], request_slot[:, None], 0), axis=0, keepdims=True)
    slotrow = slots - own_shard * (low // RANK)

    outgoing = kernel_call(
        functools.partial(project_kernel, dims),
        shape((groups, packed, LANES), BF),
        [SMEM, SMEM, ANY, VMEM, ANY, ANY],
        ANY,
        [
            pltpu.VMEM((count, model_width), BF),
            pltpu.VMEM((qkv_cols, model_width), BF),
            pltpu.VMEM((model_width, low), BF),
            pltpu.VMEM((count, model_width), BF),
            pltpu.VMEM((count, sent), F32),
            pltpu.VMEM((groups, packed, LANES), BF),
            page_scalars,
            dma((7 + groups,)),
        ],
        2 * count * model_width * sent,
        2 * (count * model_width + model_width * sent),
    )(page_table, place, hidden, norm_gain.reshape(1, -1), qkv_weight.T, adapter_down)
    arrived = lax.all_to_all(outgoing, "group", split_axis=0, concat_axis=0, tiled=True)

    after_out, after_up, _ = lax.optimization_barrier((out_weight, adapter_up, outgoing))
    w_t = jnp.concatenate([after_out.T, after_up.T], axis=1)
    after_vocab, w_t = lax.optimization_barrier((vocab_rows, w_t))
    some_vocab = exchanged(after_vocab, "mp").reshape(-1, model_width)

    ordered, ordered_t, state = kernel_call(
        functools.partial(order_kernel, dims, low, heads),
        (shape((count, sent), BF), shape((sent, count), BF), shape((heads, PHI_PAD, LANES), BF)),
        [SMEM, SMEM, ANY] + [VMEM] * 4,
        (ANY, ANY, VMEM),
        [
            pltpu.VMEM((groups, packed, LANES), BF),
            pltpu.VMEM((count, sent), F32),
            pltpu.VMEM((count, sent), F32),
            pltpu.VMEM((count, sent), BF),
            pltpu.VMEM((sent, count), BF),
            pltpu.SMEM((groups,), jnp.int32),
            dma((max(groups, 2),)),
        ],
        heads * 2 * count * PHI_PAD * (LANES + 2 * FEAT),
        6 * count * sent,
    )(page_table, place, arrived, segrow, left, right, cols)
    state = lax.ppermute(state, "group", [(i, i + 1) for i in range(groups - 1)])

    nd, squares = kernel_call(
        functools.partial(local_kernel, low, heads),
        (shape((heads, LANES, count), F32), shape((8 * (heads // 8 + 1), count), F32)),
        [ANY, ANY, VMEM],
        (VMEM, VMEM),
        [
            pltpu.VMEM((count, sent), BF),
            pltpu.VMEM((sent, count), BF),
            pltpu.VMEM((count, count), F32),
            dma((2,)),
        ],
        heads * 2 * count * count * 512,
        4 * count * sent + 4 * heads * count * LANES,
    )(ordered, ordered_t, segrow)

    offsets = 2 * shards - 1
    *shards_at, state_norms, inputs = kernel_call(
        functools.partial(finish_kernel, low, heads, shards),
        [shape((width, count), BF)] * offsets + [shape((heads, count), F32), shape((inner + low, count), BF)],
        [SMEM, ANY] + [VMEM] * 8 + [ANY],
        [ANY] * offsets + [VMEM, VMEM],
        [
            pltpu.VMEM((sent, count), BF),
            pltpu.VMEM((model_width, inner + low), BF),
            pltpu.VMEM((shards, width, count), BF),
            dma((offsets + 2,)),
        ],
        2 * count * (inner + low) * model_width,
        4 * count * model_width,
    )(place, ordered_t, nd, squares, state, segrow, slotrow, left, right, cols, w_t)
    update = line_sums(shards_at, "mp")

    later_vocab, later_out, later_up, later_hidden, inputs = lax.optimization_barrier(
        (some_vocab, out_weight, adapter_up, hidden, inputs)
    )
    m_some = jnp.concatenate(
        [
            dot(later_vocab, later_out, ((1,), (1,))).astype(BF),
            dot(later_vocab, later_up, ((1,), (1,))).astype(BF),
            lax.dynamic_slice_in_dim(later_vocab, own_shard * width, width, 1),
        ],
        axis=1,
    )
    m_all = exchanged(m_some, "group").reshape(-1, inner + low + width)
    residual = kernel_call(
        functools.partial(residual_kernel, dims, shards),
        shape((count, width), BF),
        [SMEM, SMEM, VMEM],
        VMEM,
        [pltpu.VMEM((count, width), F32), page_scalars],
        count * width,
        2 * count * model_width,
    )(page_table, place, later_hidden)
    residual = lax.all_to_all(
        residual.reshape(groups, tall, width), "group", split_axis=0, concat_axis=0, tiled=True
    ).reshape(count, width)
    logits = kernel_call(
        functools.partial(logits_kernel, dims, shards),
        shape((shards, m_all.shape[0], count // shards), BF),
        [SMEM, SMEM, VMEM, VMEM, VMEM],
        VMEM,
        [
            pltpu.VMEM((count, width), F32),
            pltpu.VMEM((count, width), F32),
            pltpu.SMEM((groups,), jnp.int32),
        ],
        2 * count * m_all.shape[0] * m_all.shape[1],
        4 * count * m_all.shape[0],
    )(page_table, place, residual, inputs, m_all)
    logits = lax.all_to_all(logits, "mp", split_axis=0, concat_axis=0, tiled=True)
    best = kernel_call(
        functools.partial(best_kernel, shards),
        shape((1, count // shards), F32),
        [VMEM],
        VMEM,
        [],
        count * m_all.shape[0],
        2 * count * m_all.shape[0],
    )(logits)
    return update.T, state_norms, best.reshape(-1)


def solution(mesh):
    placed = (
        P("group", None),
        P(),
        P(None, "mp"),
        P("mp", None),
        P(None, "mp"),
        P("mp", None),
        P(("group", "mp"), None),
        P("group"),
        P(),
        P(),
        P(),
    )
    return jax.shard_map(
        on_device,
        mesh=mesh,
        in_specs=placed,
        out_specs=(P("group", "mp"), P("mp", "group"), P(("group", "mp"))),
        check_vma=False,
    )
```

```python
import functools

import jax
import jax.numpy as jnp
import numpy as np
from jax import lax
from jax.experimental import pallas as pl
from jax.experimental.pallas import tpu as pltpu
from jax.sharding import PartitionSpec as P

FEAT = 16
HD = 112
RANK = 16
EPSILON = 1e-05
HEAD = 2 * FEAT + HD
PHI = 1 + FEAT + FEAT * (FEAT + 1) // 2
PHI_PAD = 160
LANES = 128
ONE, TAG, REST = HD, HD + 1, HD + 2
VMEM_LIMIT = 60 * 1024 * 1024

BF = jnp.bfloat16
F32 = jnp.float32
SMEM = pl.BlockSpec(memory_space=pltpu.SMEM)
VMEM = pl.BlockSpec(memory_space=pltpu.VMEM)
ANY = pl.BlockSpec(memory_space=pl.ANY)


def feature_tables():
    left = np.zeros((PHI_PAD, FEAT), np.float32)
    right = np.zeros((PHI_PAD, FEAT), np.float32)
    cols = np.zeros((PHI_PAD, 8), np.float32)
    cols[0, :3] = 1.0
    at = 1
    for i in range(FEAT):
        left[at, i] = 1.0
        cols[at, 1] = 1.0
        cols[at, 2] = FEAT**-0.25
        at += 1
    for i in range(FEAT):
        for j in range(i, FEAT):
            left[at, i] = 1.0
            right[at, j] = 1.0
            cols[at, 2] = (1.0 if i == j else 2.0**0.5) / (2.0 * FEAT) ** 0.5
            at += 1
    return left.astype(jnp.bfloat16), right.astype(jnp.bfloat16), cols


def dot(a, b, dims=((1,), (0,))):
    return lax.dot_general(a, b, (dims, ((), ())), preferred_element_type=F32)


def kernel_call(body, out_shape, in_specs, out_specs, scratch, flops, nbytes):
    return pl.pallas_call(
        body,
        out_shape=out_shape,
        in_specs=in_specs,
        out_specs=out_specs,
        scratch_shapes=scratch,
        compiler_params=pltpu.CompilerParams(vmem_limit_bytes=VMEM_LIMIT),
        cost_estimate=pl.CostEstimate(flops=flops, bytes_accessed=nbytes, transcendentals=0),
    )


def start(source, target, sem):
    copy = pltpu.make_async_copy(source, target, sem)
    copy.start()
    return copy


def staged_call(body, out_shape, scalars, operands, scratch, flops, nbytes):
    buffers = [pltpu.VMEM(x.shape, x.dtype) for x in list(operands) + list(out_shape)]
    ins, outs = len(operands), len(out_shape)

    def run(*refs):
        values, refs = refs[: len(scalars)], refs[len(scalars) :]
        far, refs = refs[: ins + outs], refs[ins + outs :]
        near, extra, sems = refs[: ins + outs], refs[ins + outs : -1], refs[-1]
        loads = [start(far[k], near[k], sems.at[k]) for k in range(ins)]
        for load in loads:
            load.wait()
        body(*values, *near, *extra)
        sends = [start(near[k], far[k], sems.at[k]) for k in range(ins, ins + outs)]
        for send in sends:
            send.wait()

    return kernel_call(
        run,
        list(out_shape),
        [SMEM] * len(scalars) + [ANY] * ins,
        [ANY] * outs,
        buffers + list(scratch) + [pltpu.SemaphoreType.DMA((ins + outs,))],
        flops,
        nbytes,
    )(*scalars, *operands)


def packing(columns, rows):
    rest = columns % LANES
    share = LANES // rest if rest and LANES % rest == 0 else 1
    if rows % (16 * share):
        share = 1
    return columns // LANES, rest, share


def pick_pages(table, own, picked, groups, per_group, per_peer):
    def one_group(g, carry):
        spot = g * per_peer
        for k in range(per_group):
            local = table[g * per_group + k] - own * per_group
            picked[spot] = local
            spot = spot + jnp.where((local >= 0) & (local < per_group), 1, 0)
        return carry

    lax.fori_loop(0, groups, one_group, 0)


def place_pages(table, own, seen, source, target, groups, per_group, per_peer, page_len):
    for g in range(groups):
        seen[g] = 0
    for k in range(per_group):
        holder = lax.div(table[own * per_group + k], per_group)
        slot = holder * per_peer + seen[holder]
        seen[holder] = seen[holder] + 1
        start = pl.multiple_of(slot * page_len, page_len)
        target[k * page_len : (k + 1) * page_len, :] = source[pl.ds(start, page_len), :]


def picked_rows(source, picked, g, per_peer, page_len):
    pages = []
    for b in range(per_peer):
        at = pl.multiple_of(picked[g * per_peer + b] * page_len, page_len)
        pages.append(source[pl.ds(at, page_len), :])
    return jnp.concatenate(pages, axis=0)


def project_kernel(
    dims, table, own, hidden_in, gain, wq_in, wd_in, out_in, hidden, wq, wd, normed, wide, out, picked, sems
):
    groups, per_group, per_peer, page_len = dims
    rows = hidden.shape[0]
    low = wd.shape[1]
    pieces = 4
    part = rows // pieces
    strip = wq.shape[0] // 2
    loads = [
        start(hidden_in.at[pl.ds(k * part, part)], hidden.at[pl.ds(k * part, part)], sems.at[k]) for k in range(pieces)
    ]
    weights = [start(wd_in, wd, sems.at[pieces])]
    for k in range(2):
        half = pl.ds(k * strip, strip)
        weights.append(start(wq_in.at[half], wq.at[half], sems.at[pieces + 1 + k]))
    pick_pages(table, own[0], picked, groups, per_group, per_peer)
    step = 32
    scale = gain[...]

    def norm_rows(i, carry):
        at = pl.ds(pl.multiple_of(i * step, step), step)
        x = hidden[at, :].astype(F32)
        meansq = jnp.mean(x * x, axis=-1, keepdims=True)
        normed[at, :] = (x * lax.rsqrt(meansq + EPSILON) * scale).astype(BF)
        return carry

    for k in range(pieces):
        loads[k].wait()
        lax.fori_loop(k * part // step, (k + 1) * part // step, norm_rows, 0, unroll=2)
    for load in weights:
        load.wait()
    wide[:, :low] = dot(normed[...], wd[...])
    wide[:, low:] = dot(normed[...], wq[...], ((1,), (1,)))
    tall = per_peer * page_len
    tiles, rest, share = packing(wide.shape[1], tall)
    sends = []
    for g in range(groups):
        block = picked_rows(wide, picked, g, per_peer, page_len)
        for t in range(tiles):
            out[g, t * tall : (t + 1) * tall, :] = block[:, t * LANES : (t + 1) * LANES].astype(BF)
        if rest:
            short = tall // share
            last = [block[q * short : (q + 1) * short, tiles * LANES :] for q in range(share)]
            if share * rest < LANES:
                last.append(jnp.zeros((short, LANES - share * rest), F32))
            out[g, tiles * tall :, :] = jnp.concatenate(last, axis=1).astype(BF)
        sends.append(start(out.at[g], out_in.at[g], sems.at[pieces + 3 + g]))
    for send in sends:
        send.wait()


def residual_kernel(dims, shards, table, own, hidden, out, wide, picked):
    groups, per_group, per_peer, page_len = dims
    pick_pages(table, own[0], picked, groups, per_group, per_peer)
    width = wide.shape[1]
    for j in range(shards):

        @pl.when(own[1] == j)
        def _():
            wide[...] = hidden[:, j * width : (j + 1) * width].astype(F32)

    tall = per_peer * page_len
    for g in range(groups):
        out[g * tall : (g + 1) * tall, :] = picked_rows(wide, picked, g, per_peer, page_len).astype(BF)


def phi_of(vectors, left, right, cols):
    first = dot(left[...], vectors) + cols[:, 0:1]
    second = dot(right[...], vectors) + cols[:, 1:2]
    return first * second * cols[:, 2:3]


def with_ones(values):
    lane = lax.broadcasted_iota(jnp.int32, (values.shape[0], LANES - HD), 1)
    return jnp.concatenate([values, jnp.where(lane == 0, 1.0, 0.0).astype(values.dtype)], axis=1)


def with_ones_t(values):
    row = lax.broadcasted_iota(jnp.int32, (LANES - HD, values.shape[1]), 0)
    return jnp.concatenate([values, jnp.where(row == 0, 1.0, 0.0).astype(values.dtype)], axis=0)


def order_kernel(
    dims, low, heads, table, own, arrived_in, segrow, left, right, cols, out_in, out_t_in, state,
    arrived, wide, placed, out, out_t, seen, sems
):
    groups, per_group, per_peer, page_len = dims
    sent = placed.shape[1]
    tall = per_peer * page_len
    tiles, rest, share = packing(sent, tall)
    loads = [start(arrived_in.at[g], arrived.at[g], sems.at[g]) for g in range(groups)]
    for g in range(groups):
        loads[g].wait()
        rows = slice(g * tall, (g + 1) * tall)
        for t in range(tiles):
            wide[rows, t * LANES : (t + 1) * LANES] = arrived[g, t * tall : (t + 1) * tall, :].astype(F32)
        if rest:
            short = tall // share
            last = arrived[g, tiles * tall :, :].astype(F32)
            for q in range(share):
                at = g * tall + q * short
                wide[at : at + short, tiles * LANES :] = last[:, q * rest : (q + 1) * rest]
    place_pages(table, own[0], seen, wide, placed, groups, per_group, per_peer, page_len)
    out[...] = placed[...].astype(BF)
    first = start(out, out_in, sems.at[0])
    for at in range(0, sent, LANES):
        end = min(at + LANES, sent)
        out_t[at:end, :] = jnp.transpose(placed[:, at:end]).astype(BF)
    second = start(out_t, out_t_in, sems.at[1])
    count = segrow.shape[1]
    last = segrow[:, count - 1 : count]
    member = jnp.where(segrow[...] == last, 1.0, 0.0)
    total = jnp.sum(member, axis=1, keepdims=True)
    fine = total - total.astype(BF).astype(F32)
    tag = last.astype(F32) + 1.0
    row = lax.broadcasted_iota(jnp.int32, (PHI_PAD, LANES), 0)
    lane = lax.broadcasted_iota(jnp.int32, (PHI_PAD, LANES), 1)
    for h in range(heads):
        at = low + h * HEAD
        phi = (phi_of(out_t[at + FEAT : at + 2 * FEAT, :], left, right, cols) * member).astype(BF)
        summed = dot(phi, with_ones(out[:, at + 2 * FEAT : at + HEAD]))
        summed = jnp.where((row == 0) & (lane == TAG), tag, summed)
        summed = jnp.where((row == 0) & (lane == REST), fine, summed)
        state[h] = summed.astype(BF)
    first.wait()
    second.wait()


def same_upto(segrow):
    count = segrow.shape[1]
    ids = segrow[...].astype(F32)
    column = jnp.transpose(jnp.broadcast_to(ids, (8, count)))[:, 0:1]
    behind = lax.broadcasted_iota(jnp.int32, (count, count), 0)
    ahead = lax.broadcasted_iota(jnp.int32, (count, count), 1)
    return jnp.where((column == ids) & (behind <= ahead), 1.0, 0.0)


def local_kernel(low, heads, ordered_in, ordered_t_in, segrow, nd_in, squares, ordered, ordered_t, nd, mask, sems):
    count = segrow.shape[1]
    block = 256 if count % 256 == 0 else count
    first = start(ordered_in, ordered, sems.at[0])
    second = start(ordered_t_in, ordered_t, sems.at[1])
    mask[...] = same_upto(segrow)
    squares[...] = jnp.zeros(squares.shape, F32)
    squares[heads : heads + 1, :] = jnp.sum(mask[...], axis=0, keepdims=True)
    first.wait()
    second.wait()
    sends = []
    for h in range(heads):
        at = low + h * HEAD
        key = ordered[:, at + FEAT : at + 2 * FEAT] * BF(0.25)
        value = ordered[:, at + 2 * FEAT : at + HEAD]
        query_t = ordered_t[at : at + FEAT, :]
        key_t = ordered_t[at + FEAT : at + 2 * FEAT, :]
        value_t = ordered_t[at + 2 * FEAT : at + HEAD, :]
        extended_t = with_ones_t(value_t)
        wide_key = key_t.astype(F32)
        wide_value = value_t.astype(F32)
        self_score = 0.25 * jnp.sum(wide_key * wide_key, axis=0, keepdims=True)
        self_value = jnp.sum(wide_value * wide_value, axis=0, keepdims=True)
        diagonal = (1.0 + self_score * (1.0 + 0.5 * self_score)) * self_value
        for begin in range(0, count, block):
            end = begin + block
            s = dot(key[:end], query_t[:, begin:end])
            w = (1.0 + s * (1.0 + 0.5 * s)) * mask[:end, begin:end]
            nd[h, :, begin:end] = dot(extended_t[:, :end], w.astype(BF))
            kk = dot(key[:end], key_t[:, begin:end])
            vv = dot(value[:end], value_t[:, begin:end])
            gram = (1.0 + kk * (1.0 + 0.5 * kk)) * vv * mask[:end, begin:end]
            below = jnp.sum(gram, axis=0, keepdims=True)
            squares[h : h + 1, begin:end] = 2.0 * below - diagonal[:, begin:end]
        sends.append(start(nd.at[h], nd_in.at[h], sems.at[2 + h]))
    for send in sends:
        send.wait()


def split3(x):
    a = x.astype(BF)
    rest = x - a.astype(F32)
    b = rest.astype(BF)
    return jnp.concatenate([a, b, (rest - b.astype(F32)).astype(BF)], axis=0)


def state_corner(state):
    corner = state[0, 0:1, :].astype(F32)
    return corner[:, TAG : TAG + 1], corner[:, ONE : ONE + 1] + corner[:, REST : REST + 1]


def finish_kernel(
    low, heads, shards, own, ordered_t_in, nd_in, state_in, segrow, slotrow, left, right, cols, w_t_in, *refs
):
    offsets = 2 * shards - 1
    outs = refs[: offsets - 1]
    outs = [outs[-1], *outs]
    inputs_in, ordered_t, nd, state, w_t, inputs, held_out, sems = refs[offsets - 1 :]
    width = w_t.shape[0] // shards
    fetches = [start(ordered_t_in, ordered_t, sems.at[offsets])]
    fetches.append(start(nd_in, nd, sems.at[offsets + 1]))
    fetches.append(start(state_in, state, sems.at[offsets + 2]))
    weights = start(w_t_in, w_t, sems.at[offsets + 3])
    for fetch in fetches:
        fetch.wait()
    tag, _ = state_corner(state)
    carried = jnp.where(segrow[...].astype(F32) + 1.0 == tag, 1.0, 0.0)
    row_slot = lax.div(lax.broadcasted_iota(jnp.int32, (low, 1), 0), RANK)
    lowered = jnp.where(slotrow[...] == row_slot, ordered_t[:low, :].astype(F32), 0.0)
    inputs[heads * HD :, :] = lowered.astype(BF)
    for h in range(heads):
        at = low + h * HEAD
        cross = dot(state[h], phi_of(ordered_t[at : at + FEAT, :], left, right, cols).astype(BF), ((0,), (0,)))
        both = nd[h] + carried * cross
        inputs[h * HD : (h + 1) * HD, :] = (both[:HD, :] / both[ONE : ONE + 1, :]).astype(BF)
    kept = start(inputs, inputs_in, sems.at[offsets + 4])
    weights.wait()
    order = sorted(range(offsets), key=lambda k: -abs(k - (shards - 1)))
    for k in order:
        j = own[1] + (k - (shards - 1))

        @pl.when((j >= 0) & (j < shards))
        def _(j=j, k=k):
            rows = pl.ds(pl.multiple_of(j * width, width), width)
            held_out[j] = dot(w_t[rows, :], inputs[...]).astype(BF)
            start(held_out.at[j], outs[k], sems.at[k])

    kept.wait()
    for k in order:
        j = own[1] + (k - (shards - 1))

        @pl.when((j >= 0) & (j < shards))
        def _(j=j, k=k):
            pltpu.make_async_copy(held_out.at[j], outs[k], sems.at[k]).wait()


def norms_kernel(low, heads, ordered_t, squares, state, segrow, left, right, cols, norms):
    count = segrow.shape[1]
    upto = same_upto(segrow).astype(BF)
    tag, held = state_corner(state)
    carried = jnp.where(segrow[...].astype(F32) + 1.0 == tag, 1.0, 0.0)
    value_lane = lax.broadcasted_iota(jnp.int32, (1, LANES), 1) < HD
    counted = carried * held + squares[heads : heads + 1, :]
    increments = []
    before = []
    for h in range(heads):
        at = low + h * HEAD
        held_state = state[h]
        key_t = ordered_t[at + FEAT : at + 2 * FEAT, :]
        value_t = ordered_t[at + 2 * FEAT : at + HEAD, :].astype(F32)
        against = dot(held_state, phi_of(key_t, left, right, cols).astype(BF), ((0,), (0,)))[:HD, :]
        along = jnp.sum(against * value_t, axis=0, keepdims=True)
        increments.append(squares[h : h + 1, :] + 2.0 * carried * along)
        wide_state = jnp.where(value_lane, held_state.astype(F32), 0.0)
        per_lane = jnp.sum(wide_state * wide_state, axis=0, keepdims=True)
        before.append(jnp.sum(per_lane, axis=1, keepdims=True))
    if heads % 8:
        increments.append(jnp.zeros((8 - heads % 8, count), F32))
    stacked = split3(jnp.concatenate(increments, axis=0))
    thrice = dot(stacked, upto)
    rows = thrice.shape[0] // 3
    summed = thrice[:rows] + thrice[rows : 2 * rows] + thrice[2 * rows :]
    for h in range(heads):
        total = carried * before[h] + summed[h : h + 1, :]
        norms[h : h + 1, :] = jnp.sqrt(total / (counted * float(FEAT * HD)))


def logits_kernel(dims, shards, table, own, arrived, inputs, vocab, out, wide, placed, seen):
    groups, per_group, per_peer, page_len = dims
    wide[...] = arrived[...].astype(F32)
    place_pages(table, own[0], seen, wide, placed, groups, per_group, per_peer, page_len)
    inner = inputs.shape[0]
    residual_t = jnp.transpose(placed[...]).astype(BF)
    block = inputs.shape[1] // shards
    logits = dot(vocab[:, :inner], inputs[...]) + dot(vocab[:, inner:], residual_t)
    for j in range(shards):
        out[j] = logits[:, j * block : (j + 1) * block].astype(BF)


def best_kernel(shards, pieces, best):
    whole = pieces[0].astype(F32)
    for i in range(1, shards):
        whole = whole + pieces[i].astype(F32)
    best[...] = jnp.max(whole, axis=0, keepdims=True)


def exchanged(values, axis):
    size = lax.axis_size(axis)
    spread = jnp.broadcast_to(values[None], (size,) + values.shape)
    return lax.all_to_all(spread, axis, split_axis=0, concat_axis=0, tiled=True)


def line_sums(shards_at, axis):
    size = lax.axis_size(axis)

    def at(offset):
        return shards_at[size - 2 + offset if offset > 1 - size else -1]

    def joined(*terms):
        return sum(term.astype(F32) for term in terms).astype(BF)

    def up(values, by, first, last):
        return lax.ppermute(values, axis, [(i, i + by) for i in range(first, last)])

    def down(values, by, first, last):
        return lax.ppermute(values, axis, [(i, i - by) for i in range(first, last)])

    if size == 4:
        relayed_up = up(at(2), 1, 0, size - 2)
        relayed_down = down(at(-2), 1, 2, size)
        far = lax.ppermute(at(3), axis, [(0, 3), (3, 0)])
        near_up = up(joined(at(1), relayed_up), 1, 0, size - 1)
        near_down = down(joined(at(-1), relayed_down), 1, 1, size)
        return joined(at(0), far, near_up, near_down)
    going_up = going_down = None
    for step in range(1, size):
        to_up = at(size - step)
        to_down = at(step - size)
        if step > 1:
            to_up = joined(to_up, going_up)
            to_down = joined(to_down, going_down)
        going_up = up(to_up, 1, 0, step)
        going_down = down(to_down, 1, size - step, size)
    return joined(at(0), going_up, going_down)


def on_device(
    hidden,
    norm_gain,
    qkv_weight,
    out_weight,
    adapter_down,
    adapter_up,
    vocab_rows,
    segments,
    request_adapter,
    adapter_slot,
    page_table,
):
    groups = lax.axis_size("group")
    shards = lax.axis_size("mp")
    own_shard = lax.axis_index("mp")
    own = lax.axis_index("group").astype(jnp.int32).reshape(1)
    count, model_width = hidden.shape
    per_group = page_table.shape[0] // groups
    per_peer = per_group // groups
    page_len = count // per_group
    dims = (groups, per_group, per_peer, page_len)
    qkv_cols = qkv_weight.shape[1]
    heads = qkv_cols // HEAD
    low = adapter_down.shape[1]
    inner = heads * HD
    sent = low + qkv_cols
    width = model_width // shards
    vocab_here = groups * vocab_rows.shape[0]
    shape = jax.ShapeDtypeStruct
    page_scalars = pltpu.SMEM((groups * per_peer + 1,), jnp.int32)

    tall = per_peer * page_len
    tiles, rest, share = packing(sent, tall)
    packed = tiles * tall + (tall // share if rest else 0)
    dma = pltpu.SemaphoreType.DMA
    place = jnp.concatenate([own, own_shard.astype(jnp.int32).reshape(1)])

    left, right, cols = [jnp.asarray(t) for t in feature_tables()]
    segrow = segments.reshape(1, count)
    request_ids = jnp.arange(request_adapter.shape[0], dtype=jnp.int32)
    adapter_ids = jnp.arange(adapter_slot.shape[0], dtype=jnp.int32)
    request_slot = jnp.sum(
        jnp.where(request_adapter[:, None] == adapter_ids[None, :], adapter_slot[None, :], 0), axis=1
    )
    slots = jnp.sum(jnp.where(segrow == request_ids[:, None], request_slot[:, None], 0), axis=0, keepdims=True)
    slotrow = slots - own_shard * (low // RANK)

    outgoing = kernel_call(
        functools.partial(project_kernel, dims),
        shape((groups, packed, LANES), BF),
        [SMEM, SMEM, ANY, VMEM, ANY, ANY],
        ANY,
        [
            pltpu.VMEM((count, model_width), BF),
            pltpu.VMEM((qkv_cols, model_width), BF),
            pltpu.VMEM((model_width, low), BF),
            pltpu.VMEM((count, model_width), BF),
            pltpu.VMEM((count, sent), F32),
            pltpu.VMEM((groups, packed, LANES), BF),
            page_scalars,
            dma((7 + groups,)),
        ],
        2 * count * model_width * sent,
        2 * (count * model_width + model_width * sent),
    )(page_table, place, hidden, norm_gain.reshape(1, -1), qkv_weight.T, adapter_down)
    arrived = lax.all_to_all(outgoing, "group", split_axis=0, concat_axis=0, tiled=True)

    after_out, after_up, _ = lax.optimization_barrier((out_weight, adapter_up, outgoing))
    w_t = jnp.concatenate([after_out.T, after_up.T], axis=1)

    ordered, ordered_t, state = kernel_call(
        functools.partial(order_kernel, dims, low, heads),
        (shape((count, sent), BF), shape((sent, count), BF), shape((heads, PHI_PAD, LANES), BF)),
        [SMEM, SMEM, ANY] + [VMEM] * 4,
        (ANY, ANY, VMEM),
        [
            pltpu.VMEM((groups, packed, LANES), BF),
            pltpu.VMEM((count, sent), F32),
            pltpu.VMEM((count, sent), F32),
            pltpu.VMEM((count, sent), BF),
            pltpu.VMEM((sent, count), BF),
            pltpu.SMEM((groups,), jnp.int32),
            dma((max(groups, 2),)),
        ],
        heads * 2 * count * PHI_PAD * (LANES + 2 * FEAT),
        6 * count * sent,
    )(page_table, place, arrived, segrow, left, right, cols)
    state = lax.ppermute(state, "group", [(i, i + 1) for i in range(groups - 1)])

    nd, squares = kernel_call(
        functools.partial(local_kernel, low, heads),
        (shape((heads, LANES, count), F32), shape((8 * (heads // 8 + 1), count), F32)),
        [ANY, ANY, VMEM],
        (ANY, VMEM),
        [
            pltpu.VMEM((count, sent), BF),
            pltpu.VMEM((sent, count), BF),
            pltpu.VMEM((heads, LANES, count), F32),
            pltpu.VMEM((count, count), F32),
            dma((2 + heads,)),
        ],
        heads * 2 * count * count * 512,
        4 * count * sent + 4 * heads * count * LANES,
    )(ordered, ordered_t, segrow)

    offsets = 2 * shards - 2
    *shards_at, inputs = kernel_call(
        functools.partial(finish_kernel, low, heads, shards),
        [shape((width, count), BF)] * offsets + [shape((inner + low, count), BF)],
        [SMEM, ANY, ANY, ANY] + [VMEM] * 5 + [ANY],
        [ANY] * (offsets + 1),
        [
            pltpu.VMEM((sent, count), BF),
            pltpu.VMEM((heads, LANES, count), F32),
            pltpu.VMEM((heads, PHI_PAD, LANES), BF),
            pltpu.VMEM((model_width, inner + low), BF),
            pltpu.VMEM((inner + low, count), BF),
            pltpu.VMEM((shards, width, count), BF),
            dma((offsets + 6,)),
        ],
        2 * count * (inner + low) * model_width,
        4 * count * model_width,
    )(place, ordered_t, nd, state, segrow, slotrow, left, right, cols, w_t)
    update = line_sums(shards_at, "mp")

    later_vocab, later_out, later_up, later_hidden, later_state, inputs = lax.optimization_barrier(
        (vocab_rows, out_weight, adapter_up, hidden, state, inputs)
    )
    [state_norms] = staged_call(
        functools.partial(norms_kernel, low, heads),
        [shape((heads, count), F32)],
        [],
        [ordered_t, squares, later_state, segrow, left, right, cols],
        [],
        heads * 2 * count * count * 16,
        2 * sent * count,
    )
    some_vocab = exchanged(later_vocab, "mp").reshape(-1, model_width)
    m_some = jnp.concatenate(
        [
            dot(some_vocab, later_out, ((1,), (1,))).astype(BF),
            dot(some_vocab, later_up, ((1,), (1,))).astype(BF),
            lax.dynamic_slice_in_dim(some_vocab, own_shard * width, width, 1),
        ],
        axis=1,
    )
    m_all = exchanged(m_some, "group").reshape(-1, inner + low + width)
    [residual] = staged_call(
        functools.partial(residual_kernel, dims, shards),
        [shape((count, width), BF)],
        [page_table, place],
        [later_hidden],
        [pltpu.VMEM((count, width), F32), page_scalars],
        count * width,
        2 * count * model_width,
    )
    residual = lax.all_to_all(
        residual.reshape(groups, tall, width), "group", split_axis=0, concat_axis=0, tiled=True
    ).reshape(count, width)
    [logits] = staged_call(
        functools.partial(logits_kernel, dims, shards),
        [shape((shards, m_all.shape[0], count // shards), BF)],
        [page_table, place],
        [residual, inputs, m_all],
        [
            pltpu.VMEM((count, width), F32),
            pltpu.VMEM((count, width), F32),
            pltpu.SMEM((groups,), jnp.int32),
        ],
        2 * count * m_all.shape[0] * m_all.shape[1],
        4 * count * m_all.shape[0],
    )
    logits = lax.all_to_all(logits, "mp", split_axis=0, concat_axis=0, tiled=True)
    [best] = staged_call(
        functools.partial(best_kernel, shards),
        [shape((1, count // shards), F32)],
        [],
        [logits],
        [],
        count * m_all.shape[0],
        2 * count * m_all.shape[0],
    )
    return update.T, state_norms, best.reshape(-1)


def solution(mesh):
    placed = (
        P("group", None),
        P(),
        P(None, "mp"),
        P("mp", None),
        P(None, "mp"),
        P("mp", None),
        P(("group", "mp"), None),
        P("group"),
        P(),
        P(),
        P(),
    )
    return jax.shard_map(
        on_device,
        mesh=mesh,
        in_specs=placed,
        out_specs=(P("group", "mp"), P("mp", "group"), P(("group", "mp"))),
        check_vma=False,
    )
```

```python
import functools

import jax
import jax.numpy as jnp
import numpy as np
from jax import lax
from jax.experimental import pallas as pl
from jax.experimental.pallas import tpu as pltpu
from jax.sharding import PartitionSpec as P

FEAT = 16
HD = 112
RANK = 16
EPSILON = 1e-05
HEAD = 2 * FEAT + HD
PHI = 1 + FEAT + FEAT * (FEAT + 1) // 2
PHI_PAD = 160
LANES = 128
ONE, TAG, REST = HD, HD + 1, HD + 2
VMEM_LIMIT = 60 * 1024 * 1024

BF = jnp.bfloat16
F32 = jnp.float32
SMEM = pl.BlockSpec(memory_space=pltpu.SMEM)
VMEM = pl.BlockSpec(memory_space=pltpu.VMEM)
ANY = pl.BlockSpec(memory_space=pl.ANY)


def feature_tables():
    left = np.zeros((PHI_PAD, FEAT), np.float32)
    right = np.zeros((PHI_PAD, FEAT), np.float32)
    cols = np.zeros((PHI_PAD, 8), np.float32)
    cols[0, :3] = 1.0
    at = 1
    for i in range(FEAT):
        left[at, i] = 1.0
        cols[at, 1] = 1.0
        cols[at, 2] = FEAT**-0.25
        at += 1
    for i in range(FEAT):
        for j in range(i, FEAT):
            left[at, i] = 1.0
            right[at, j] = 1.0
            cols[at, 2] = (1.0 if i == j else 2.0**0.5) / (2.0 * FEAT) ** 0.5
            at += 1
    return left.astype(jnp.bfloat16), right.astype(jnp.bfloat16), cols


def dot(a, b, dims=((1,), (0,))):
    return lax.dot_general(a, b, (dims, ((), ())), preferred_element_type=F32)


def kernel_call(body, out_shape, in_specs, out_specs, scratch, flops, nbytes):
    return pl.pallas_call(
        body,
        out_shape=out_shape,
        in_specs=in_specs,
        out_specs=out_specs,
        scratch_shapes=scratch,
        compiler_params=pltpu.CompilerParams(vmem_limit_bytes=VMEM_LIMIT),
        cost_estimate=pl.CostEstimate(flops=flops, bytes_accessed=nbytes, transcendentals=0),
    )


def start(source, target, sem):
    copy = pltpu.make_async_copy(source, target, sem)
    copy.start()
    return copy


def staged_call(body, out_shape, scalars, operands, scratch, flops, nbytes):
    buffers = [pltpu.VMEM(x.shape, x.dtype) for x in list(operands) + list(out_shape)]
    ins, outs = len(operands), len(out_shape)

    def run(*refs):
        values, refs = refs[: len(scalars)], refs[len(scalars) :]
        far, refs = refs[: ins + outs], refs[ins + outs :]
        near, extra, sems = refs[: ins + outs], refs[ins + outs : -1], refs[-1]
        loads = [start(far[k], near[k], sems.at[k]) for k in range(ins)]
        for load in loads:
            load.wait()
        body(*values, *near, *extra)
        sends = [start(near[k], far[k], sems.at[k]) for k in range(ins, ins + outs)]
        for send in sends:
            send.wait()

    return kernel_call(
        run,
        list(out_shape),
        [SMEM] * len(scalars) + [ANY] * ins,
        [ANY] * outs,
        buffers + list(scratch) + [pltpu.SemaphoreType.DMA((ins + outs,))],
        flops,
        nbytes,
    )(*scalars, *operands)


def staged_call(body, out_shape, scalars, operands, scratch, flops, nbytes):
    buffers = [pltpu.VMEM(x.shape, x.dtype) for x in list(operands) + list(out_shape)]
    ins, outs = len(operands), len(out_shape)

    def run(*refs):
        values, refs = refs[: len(scalars)], refs[len(scalars) :]
        far, refs = refs[: ins + outs], refs[ins + outs :]
        near, extra, sems = refs[: ins + outs], refs[ins + outs : -1], refs[-1]
        loads = [start(far[k], near[k], sems.at[k]) for k in range(ins)]
        for load in loads:
            load.wait()
        body(*values, *near, *extra)
        sends = [start(near[k], far[k], sems.at[k]) for k in range(ins, ins + outs)]
        for send in sends:
            send.wait()

    return kernel_call(
        run,
        list(out_shape),
        [SMEM] * len(scalars) + [ANY] * ins,
        [ANY] * outs,
        buffers + list(scratch) + [pltpu.SemaphoreType.DMA((ins + outs,))],
        flops,
        nbytes,
    )(*scalars, *operands)


def packing(columns, rows):
    rest = columns % LANES
    share = LANES // rest if rest and LANES % rest == 0 else 1
    if rows % (16 * share):
        share = 1
    return columns // LANES, rest, share


def pick_pages(table, own, picked, groups, per_group, per_peer):
    def one_group(g, carry):
        spot = g * per_peer
        for k in range(per_group):
            local = table[g * per_group + k] - own * per_group
            picked[spot] = local
            spot = spot + jnp.where((local >= 0) & (local < per_group), 1, 0)
        return carry

    lax.fori_loop(0, groups, one_group, 0)


def place_pages(table, own, seen, source, target, groups, per_group, per_peer, page_len):
    for g in range(groups):
        seen[g] = 0
    for k in range(per_group):
        holder = lax.div(table[own * per_group + k], per_group)
        slot = holder * per_peer + seen[holder]
        seen[holder] = seen[holder] + 1
        start = pl.multiple_of(slot * page_len, page_len)
        target[k * page_len : (k + 1) * page_len, :] = source[pl.ds(start, page_len), :]


def picked_rows(source, picked, g, per_peer, page_len):
    pages = []
    for b in range(per_peer):
        at = pl.multiple_of(picked[g * per_peer + b] * page_len, page_len)
        pages.append(source[pl.ds(at, page_len), :])
    return jnp.concatenate(pages, axis=0)


def project_kernel(
    dims, shards, table, hidden_in, gain, wq_in, wd_in, out_in, hidden, wq, wd, normed, wide, out, picked, sems
):
    groups, per_group, per_peer, page_len = dims
    rows, model_width = hidden.shape
    low = wd.shape[1]
    plain = low + wq.shape[0]
    width = model_width // shards
    pieces = 4
    part = rows // pieces
    strip = wq.shape[0] // 2
    loads = [
        start(hidden_in.at[pl.ds(k * part, part)], hidden.at[pl.ds(k * part, part)], sems.at[k]) for k in range(pieces)
    ]
    weights = [start(wd_in, wd, sems.at[pieces])]
    for k in range(2):
        half = pl.ds(k * strip, strip)
        weights.append(start(wq_in.at[half], wq.at[half], sems.at[pieces + 1 + k]))
    pick_pages(table, lax.axis_index("group"), picked, groups, per_group, per_peer)
    step = 32
    scale = gain[...].reshape(1, model_width)

    def norm_rows(i, carry):
        at = pl.ds(pl.multiple_of(i * step, step), step)
        x = hidden[at, :].astype(F32)
        meansq = jnp.mean(x * x, axis=-1, keepdims=True)
        normed[at, :] = (x * lax.rsqrt(meansq + EPSILON) * scale).astype(BF)
        return carry

    for k in range(pieces):
        loads[k].wait()
        lax.fori_loop(k * part // step, (k + 1) * part // step, norm_rows, 0, unroll=2)
    own_shard = lax.axis_index("mp")
    for j in range(shards):

        @pl.when(own_shard == j)
        def _(j=j):
            wide[:, plain:] = hidden[:, j * width : (j + 1) * width].astype(F32)

    for load in weights:
        load.wait()
    wide[:, :low] = dot(normed[...], wd[...])
    wide[:, low:plain] = dot(normed[...], wq[...], ((1,), (1,)))
    tall = per_peer * page_len
    tiles = wide.shape[1] // LANES
    sends = []
    for g in range(groups):
        block = picked_rows(wide, picked, g, per_peer, page_len)
        for t in range(tiles):
            out[g, t * tall : (t + 1) * tall, :] = block[:, t * LANES : (t + 1) * LANES].astype(BF)
        sends.append(start(out.at[g], out_in.at[g], sems.at[pieces + 3 + g]))
    for send in sends:
        send.wait()


def phi_of(vectors, left, right, cols):
    first = dot(left[...], vectors) + cols[:, 0:1]
    second = dot(right[...], vectors) + cols[:, 1:2]
    return first * second * cols[:, 2:3]


def with_ones(values):
    lane = lax.broadcasted_iota(jnp.int32, (values.shape[0], LANES - HD), 1)
    return jnp.concatenate([values, jnp.where(lane == 0, 1.0, 0.0).astype(values.dtype)], axis=1)


def with_ones_t(values):
    row = lax.broadcasted_iota(jnp.int32, (LANES - HD, values.shape[1]), 0)
    return jnp.concatenate([values, jnp.where(row == 0, 1.0, 0.0).astype(values.dtype)], axis=0)


def same_upto(segrow):
    count = segrow.shape[1]
    ids = segrow[...].astype(F32)
    column = jnp.transpose(jnp.broadcast_to(ids, (8, count)))[:, 0:1]
    behind = lax.broadcasted_iota(jnp.int32, (count, count), 0)
    ahead = lax.broadcasted_iota(jnp.int32, (count, count), 1)
    return jnp.where((column == ids) & (behind <= ahead), 1.0, 0.0)


def group_kernel(
    dims, low, heads, table, arrived_in, segrow, left, right, cols, ordered_t_in, state, nd_in, squares,
    arrived, wide, placed, ordered, ordered_t, nd, mask, seen, sems
):
    groups, per_group, per_peer, page_len = dims
    tall = per_peer * page_len
    count, sent = placed.shape
    qkv = ordered.shape[1]
    loads = [start(arrived_in.at[g], arrived.at[g], sems.at[g]) for g in range(groups)]
    mask[...] = same_upto(segrow)
    squares[...] = jnp.zeros(squares.shape, F32)
    squares[heads : heads + 1, :] = jnp.sum(mask[...], axis=0, keepdims=True)
    for g in range(groups):
        loads[g].wait()
        rows = slice(g * tall, (g + 1) * tall)
        for t in range(sent // LANES):
            wide[rows, t * LANES : (t + 1) * LANES] = arrived[g, t * tall : (t + 1) * tall, :].astype(F32)
    place_pages(table, lax.axis_index("group"), seen, wide, placed, groups, per_group, per_peer, page_len)
    ordered[...] = placed[:, low : low + qkv].astype(BF)
    for at in range(0, sent, LANES):
        ordered_t[at : at + LANES, :] = jnp.transpose(placed[:, at : at + LANES]).astype(BF)
    sends = [start(ordered_t, ordered_t_in, sems.at[0])]

    last = segrow[:, count - 1 : count]
    member = jnp.where(segrow[...] == last, 1.0, 0.0)
    total = jnp.sum(member, axis=1, keepdims=True)
    fine = total - total.astype(BF).astype(F32)
    tag = last.astype(F32) + 1.0
    row = lax.broadcasted_iota(jnp.int32, (PHI_PAD, LANES), 0)
    lane = lax.broadcasted_iota(jnp.int32, (PHI_PAD, LANES), 1)
    block = 256 if count % 256 == 0 else count
    for h in range(heads):
        at = h * HEAD
        key = ordered[:, at + FEAT : at + 2 * FEAT] * BF(0.25)
        value = ordered[:, at + 2 * FEAT : at + HEAD]
        at = low + h * HEAD
        query_t = ordered_t[at : at + FEAT, :]
        key_t = ordered_t[at + FEAT : at + 2 * FEAT, :]
        value_t = ordered_t[at + 2 * FEAT : at + HEAD, :]

        phi = (phi_of(key_t, left, right, cols) * member).astype(BF)
        summed = dot(phi, with_ones(value))
        summed = jnp.where((row == 0) & (lane == TAG), tag, summed)
        summed = jnp.where((row == 0) & (lane == REST), fine, summed)
        state[h] = summed.astype(BF)

        extended_t = with_ones_t(value_t)
        wide_key = key_t.astype(F32)
        wide_value = value_t.astype(F32)
        self_score = 0.25 * jnp.sum(wide_key * wide_key, axis=0, keepdims=True)
        self_value = jnp.sum(wide_value * wide_value, axis=0, keepdims=True)
        diagonal = (1.0 + self_score * (1.0 + 0.5 * self_score)) * self_value
        for begin in range(0, count, block):
            end = begin + block
            s = dot(key[:end], query_t[:, begin:end])
            w = (1.0 + s * (1.0 + 0.5 * s)) * mask[:end, begin:end]
            nd[h, :, begin:end] = dot(extended_t[:, :end], w.astype(BF))
            kk = dot(key[:end], key_t[:, begin:end])
            vv = dot(value[:end], value_t[:, begin:end])
            gram = (1.0 + kk * (1.0 + 0.5 * kk)) * vv * mask[:end, begin:end]
            below = jnp.sum(gram, axis=0, keepdims=True)
            squares[h : h + 1, begin:end] = 2.0 * below - diagonal[:, begin:end]
        sends.append(start(nd.at[h], nd_in.at[h], sems.at[1 + h]))
    for send in sends:
        send.wait()


def split3(x):
    a = x.astype(BF)
    rest = x - a.astype(F32)
    b = rest.astype(BF)
    return jnp.concatenate([a, b, (rest - b.astype(F32)).astype(BF)], axis=0)


def state_corner(state):
    corner = state[0, 0:1, :].astype(F32)
    return corner[:, TAG : TAG + 1], corner[:, ONE : ONE + 1] + corner[:, REST : REST + 1]


def finish_kernel(
    low, heads, shards, ordered_t_in, nd_in, state_in, segrow, slotrow, left, right, cols, w_t_in, up_t_in, m_in, *refs
):
    offsets = 2 * shards - 1
    outs = refs[: offsets - 1]
    outs = [outs[-1], *outs]
    logits_in, queries, nd, state, w_t, up_t, vocab, inputs, held_out, logits, sems = refs[offsets - 1 :]
    width = w_t.shape[0] // shards
    inner = heads * HD
    plain = low + heads * HEAD
    sem = iter(range(offsets, offsets + heads + 8))
    fetches = [start(state_in, state, sems.at[next(sem)])]
    for h in range(heads):
        rows = pl.ds(low + h * HEAD, FEAT)
        fetches.append(start(ordered_t_in.at[rows], queries.at[h], sems.at[next(sem)]))
    fetches.append(start(nd_in, nd, sems.at[next(sem)]))
    fetches.append(start(ordered_t_in.at[pl.ds(0, low)], inputs.at[pl.ds(inner, low)], sems.at[next(sem)]))
    weights = [start(w_t_in, w_t, sems.at[next(sem)]), start(up_t_in, up_t, sems.at[next(sem)])]
    scores = [start(m_in, vocab, sems.at[next(sem)])]
    rows = pl.ds(plain, width)
    scores.append(start(ordered_t_in.at[rows], inputs.at[pl.ds(inner + low, width)], sems.at[next(sem)]))
    for fetch in fetches:
        fetch.wait()
    tag, _ = state_corner(state)
    carried = jnp.where(segrow[...].astype(F32) + 1.0 == tag, 1.0, 0.0)
    row_slot = lax.div(lax.broadcasted_iota(jnp.int32, (low, 1), 0), RANK)
    lowered = jnp.where(slotrow[...] == row_slot, inputs[inner : inner + low, :].astype(F32), 0.0)
    inputs[inner : inner + low, :] = lowered.astype(BF)
    for h in range(heads):
        cross = dot(state[h], phi_of(queries[h], left, right, cols).astype(BF), ((0,), (0,)))
        both = nd[h] + carried * cross
        inputs[h * HD : (h + 1) * HD, :] = (both[:HD, :] / both[ONE : ONE + 1, :]).astype(BF)
    for load in weights:
        load.wait()
    own_shard = lax.axis_index("mp")
    order = sorted(range(offsets), key=lambda k: -abs(k - (shards - 1)))
    for k in order:
        j = own_shard + (k - (shards - 1))

        @pl.when((j >= 0) & (j < shards))
        def _(j=j, k=k):
            rows = pl.ds(pl.multiple_of(j * width, width), width)
            part = dot(w_t[rows, :], inputs[:inner, :]) + dot(up_t[rows, :], inputs[inner : inner + low, :])
            held_out[j] = part.astype(BF)
            start(held_out.at[j], outs[k], sems.at[k])

    for load in scores:
        load.wait()
    block = inputs.shape[1] // shards
    scored = dot(vocab[...], inputs[...])
    for j in range(shards):
        logits[j] = scored[:, j * block : (j + 1) * block].astype(BF)
    kept = start(logits, logits_in, sems.at[next(sem)])
    for k in order:
        j = own_shard + (k - (shards - 1))

        @pl.when((j >= 0) & (j < shards))
        def _(j=j, k=k):
            pltpu.make_async_copy(held_out.at[j], outs[k], sems.at[k]).wait()

    kept.wait()


def norms_kernel(low, heads, ordered_t, squares, state, segrow, left, right, cols, norms):
    count = segrow.shape[1]
    upto = same_upto(segrow).astype(BF)
    tag, held = state_corner(state)
    carried = jnp.where(segrow[...].astype(F32) + 1.0 == tag, 1.0, 0.0)
    value_lane = lax.broadcasted_iota(jnp.int32, (1, LANES), 1) < HD
    counted = carried * held + squares[heads : heads + 1, :]
    increments = []
    before = []
    for h in range(heads):
        at = low + h * HEAD
        held_state = state[h]
        key_t = ordered_t[at + FEAT : at + 2 * FEAT, :]
        value_t = ordered_t[at + 2 * FEAT : at + HEAD, :].astype(F32)
        against = dot(held_state, phi_of(key_t, left, right, cols).astype(BF), ((0,), (0,)))[:HD, :]
        along = jnp.sum(against * value_t, axis=0, keepdims=True)
        increments.append(squares[h : h + 1, :] + 2.0 * carried * along)
        wide_state = jnp.where(value_lane, held_state.astype(F32), 0.0)
        per_lane = jnp.sum(wide_state * wide_state, axis=0, keepdims=True)
        before.append(jnp.sum(per_lane, axis=1, keepdims=True))
    if heads % 8:
        increments.append(jnp.zeros((8 - heads % 8, count), F32))
    stacked = split3(jnp.concatenate(increments, axis=0))
    thrice = dot(stacked, upto)
    rows = thrice.shape[0] // 3
    summed = thrice[:rows] + thrice[rows : 2 * rows] + thrice[2 * rows :]
    for h in range(heads):
        total = carried * before[h] + summed[h : h + 1, :]
        norms[h : h + 1, :] = jnp.sqrt(total / (counted * float(FEAT * HD)))


def best_kernel(shards, pieces, best):
    whole = pieces[0].astype(F32)
    for i in range(1, shards):
        whole = whole + pieces[i].astype(F32)
    best[...] = jnp.max(whole, axis=0, keepdims=True)


def spread(values, axis):
    return jnp.broadcast_to(values[None], (lax.axis_size(axis),) + values.shape)


def exchange(blocks, axis):
    return lax.all_to_all(blocks, axis, split_axis=0, concat_axis=0, tiled=True)


def line_sums(shards_at, axis, beside):
    size = lax.axis_size(axis)

    def at(offset):
        return shards_at[size - 2 + offset if offset > 1 - size else -1]

    def joined(*terms):
        return sum(term.astype(F32) for term in terms).astype(BF)

    def up(values, by, first, last):
        return lax.ppermute(values, axis, [(i, i + by) for i in range(first, last)])

    def down(values, by, first, last):
        return lax.ppermute(values, axis, [(i, i - by) for i in range(first, last)])

    if size == 4:
        relayed_up = up(at(2), 1, 0, size - 2)
        relayed_down = down(at(-2), 1, 2, size)
        far = lax.ppermute(at(3), axis, [(0, 3), (3, 0)])
        relayed_up, relayed_down, beside = lax.optimization_barrier((relayed_up, relayed_down, beside))
        near_up = up(joined(at(1), relayed_up), 1, 0, size - 1)
        near_down = down(joined(at(-1), relayed_down), 1, 1, size)
        return joined(at(0), far, near_up, near_down), beside
    going_up = going_down = None
    for step in range(1, size):
        to_up = at(size - step)
        to_down = at(step - size)
        if step > 1:
            to_up = joined(to_up, going_up)
            to_down = joined(to_down, going_down)
        going_up = up(to_up, 1, 0, step)
        going_down = down(to_down, 1, size - step, size)
    return joined(at(0), going_up, going_down), beside


def on_device(
    hidden,
    norm_gain,
    qkv_weight,
    out_weight,
    adapter_down,
    adapter_up,
    vocab_rows,
    segments,
    request_adapter,
    adapter_slot,
    page_table,
):
    groups = lax.axis_size("group")
    shards = lax.axis_size("mp")
    own_shard = lax.axis_index("mp")
    count, model_width = hidden.shape
    per_group = page_table.shape[0] // groups
    per_peer = per_group // groups
    page_len = count // per_group
    dims = (groups, per_group, per_peer, page_len)
    qkv_cols = qkv_weight.shape[1]
    heads = qkv_cols // HEAD
    low = adapter_down.shape[1]
    inner = heads * HD
    width = model_width // shards
    sent = low + qkv_cols + width
    packed = sent // LANES * per_peer * page_len
    scored = groups * shards * vocab_rows.shape[0]
    shape = jax.ShapeDtypeStruct
    dma = pltpu.SemaphoreType.DMA

    left, right, cols = [jnp.asarray(t) for t in feature_tables()]
    segrow = segments.reshape(1, count)
    request_ids = jnp.arange(request_adapter.shape[0], dtype=jnp.int32)
    adapter_ids = jnp.arange(adapter_slot.shape[0], dtype=jnp.int32)

    outgoing = kernel_call(
        functools.partial(project_kernel, dims, shards),
        shape((groups, packed, LANES), BF),
        [SMEM, ANY, VMEM, ANY, ANY],
        ANY,
        [
            pltpu.VMEM((count, model_width), BF),
            pltpu.VMEM((qkv_cols, model_width), BF),
            pltpu.VMEM((model_width, low), BF),
            pltpu.VMEM((count, model_width), BF),
            pltpu.VMEM((count, sent), F32),
            pltpu.VMEM((groups, packed, LANES), BF),
            pltpu.SMEM((groups * per_peer + 1,), jnp.int32),
            dma((7 + groups,)),
        ],
        2 * count * model_width * sent,
        2 * (count * model_width + model_width * sent),
    )(page_table, hidden, norm_gain, qkv_weight.T, adapter_down)
    arrived = exchange(outgoing, "group")

    after_out, after_up, _ = lax.optimization_barrier((out_weight, adapter_up, outgoing))
    w_t, up_t = after_out.T, after_up.T
    after_vocab, after_adapter, w_t, up_t = lax.optimization_barrier((vocab_rows, request_adapter, w_t, up_t))
    some_vocab = exchange(spread(after_vocab, "mp"), "mp").reshape(-1, model_width)
    request_slot = jnp.sum(jnp.where(after_adapter[:, None] == adapter_ids[None, :], adapter_slot[None, :], 0), axis=1)
    slots = jnp.sum(jnp.where(segrow == request_ids[:, None], request_slot[:, None], 0), axis=0, keepdims=True)
    slotrow = slots - own_shard * (low // RANK)
    m_some = jnp.concatenate(
        [
            dot(some_vocab, out_weight, ((1,), (1,))).astype(BF),
            dot(some_vocab, adapter_up, ((1,), (1,))).astype(BF),
            lax.dynamic_slice_in_dim(some_vocab, own_shard * width, width, 1),
        ],
        axis=1,
    )
    m_some = spread(m_some, "group")
    arrived, m_some, slotrow = lax.optimization_barrier((arrived, m_some, slotrow))
    m_all = exchange(m_some, "group").reshape(scored, inner + low + width)

    ordered_t, state, nd, squares = kernel_call(
        functools.partial(group_kernel, dims, low, heads),
        (
            shape((sent, count), BF),
            shape((heads, PHI_PAD, LANES), BF),
            shape((heads, LANES, count), F32),
            shape((8 * (heads // 8 + 1), count), F32),
        ),
        [SMEM, ANY] + [VMEM] * 4,
        (ANY, VMEM, ANY, VMEM),
        [
            pltpu.VMEM((groups, packed, LANES), BF),
            pltpu.VMEM((count, sent), F32),
            pltpu.VMEM((count, sent), F32),
            pltpu.VMEM((count, qkv_cols), BF),
            pltpu.VMEM((sent, count), BF),
            pltpu.VMEM((heads, LANES, count), F32),
            pltpu.VMEM((count, count), F32),
            pltpu.SMEM((groups,), jnp.int32),
            dma((max(groups, 1 + heads),)),
        ],
        heads * 2 * count * count * 512,
        6 * count * sent,
    )(page_table, arrived, segrow, left, right, cols)
    state = lax.ppermute(state, "group", [(i, i + 1) for i in range(groups - 1)])

    *shards_at, logits = kernel_call(
        functools.partial(finish_kernel, low, heads, shards),
        [shape((width, count), BF)] * (2 * shards - 2) + [shape((shards, scored, count // shards), BF)],
        [ANY] * 3 + [VMEM] * 5 + [ANY] * 3,
        [ANY] * (2 * shards - 1),
        [
            pltpu.VMEM((heads, FEAT, count), BF),
            pltpu.VMEM((heads, LANES, count), F32),
            pltpu.VMEM((heads, PHI_PAD, LANES), BF),
            pltpu.VMEM((model_width, inner), BF),
            pltpu.VMEM((model_width, low), BF),
            pltpu.VMEM((scored, inner + low + width), BF),
            pltpu.VMEM((inner + low + width, count), BF),
            pltpu.VMEM((shards, width, count), BF),
            pltpu.VMEM((shards, scored, count // shards), BF),
            dma((2 * shards - 1 + heads + 8,)),
        ],
        2 * count * (inner + low) * (model_width + scored),
        4 * count * model_width,
    )(ordered_t, nd, state, segrow, slotrow, left, right, cols, w_t, up_t, m_all)
    update, logits = line_sums(shards_at, "mp", logits)
    logits = exchange(logits, "mp")

    [state_norms] = staged_call(
        functools.partial(norms_kernel, low, heads),
        [shape((heads, count), F32)],
        [],
        [ordered_t, squares, state, segrow, left, right, cols],
        [],
        heads * 2 * count * count * 16,
        2 * sent * count,
    )
    [best] = staged_call(
        functools.partial(best_kernel, shards),
        [shape((1, count // shards), F32)],
        [],
        [logits],
        [],
        count * scored,
        2 * count * scored,
    )
    return update.T, state_norms, best.reshape(-1)


def solution(mesh):
    placed = (
        P("group", None),
        P(),
        P(None, "mp"),
        P("mp", None),
        P(None, "mp"),
        P("mp", None),
        P(("group", "mp"), None),
        P("group"),
        P(),
        P(),
        P(),
    )
    return jax.shard_map(
        on_device,
        mesh=mesh,
        in_specs=placed,
        out_specs=(P("group", "mp"), P("mp", "group"), P(("group", "mp"))),
        check_vma=False,
    )
```

```python
import functools

import jax
import jax.numpy as jnp
import numpy as np
from jax import lax
from jax.experimental import pallas as pl
from jax.experimental.pallas import tpu as pltpu
from jax.sharding import PartitionSpec as P

FEAT = 16
HD = 112
RANK = 16
EPSILON = 1e-05
HEAD = 2 * FEAT + HD
PHI = 1 + FEAT + FEAT * (FEAT + 1) // 2
PHI_PAD = 160
LANES = 128
ONE, TAG, REST = HD, HD + 1, HD + 2
NEAR = (0, 1, -1)
VMEM_LIMIT = 60 * 1024 * 1024

BF = jnp.bfloat16
F32 = jnp.float32
SMEM = pl.BlockSpec(memory_space=pltpu.SMEM)
VMEM = pl.BlockSpec(memory_space=pltpu.VMEM)
ANY = pl.BlockSpec(memory_space=pl.ANY)


def feature_tables():
    left = np.zeros((PHI_PAD, FEAT), np.float32)
    right = np.zeros((PHI_PAD, FEAT), np.float32)
    cols = np.zeros((PHI_PAD, 8), np.float32)
    cols[0, :3] = 1.0
    at = 1
    for i in range(FEAT):
        left[at, i] = 1.0
        cols[at, 1] = 1.0
        cols[at, 2] = FEAT**-0.25
        at += 1
    for i in range(FEAT):
        for j in range(i, FEAT):
            left[at, i] = 1.0
            right[at, j] = 1.0
            cols[at, 2] = (1.0 if i == j else 2.0**0.5) / (2.0 * FEAT) ** 0.5
            at += 1
    return left.astype(jnp.bfloat16), right.astype(jnp.bfloat16), cols


def dot(a, b, dims=((1,), (0,))):
    return lax.dot_general(a, b, (dims, ((), ())), preferred_element_type=F32)


def kernel_call(body, out_shape, in_specs, out_specs, scratch, flops, nbytes):
    return pl.pallas_call(
        body,
        out_shape=out_shape,
        in_specs=in_specs,
        out_specs=out_specs,
        scratch_shapes=scratch,
        compiler_params=pltpu.CompilerParams(vmem_limit_bytes=VMEM_LIMIT),
        cost_estimate=pl.CostEstimate(flops=flops, bytes_accessed=nbytes, transcendentals=0),
    )


def start(source, target, sem):
    copy = pltpu.make_async_copy(source, target, sem)
    copy.start()
    return copy


def packing(rows, columns):
    tiles, rest = divmod(columns, LANES)
    share = LANES // rest if rest and LANES % rest == 0 else 1
    if rows % (16 * share):
        share = 1
    return tiles, rest, share, tiles * rows + (rows // share if rest else 0)


def pack(block, target, base):
    rows = block.shape[0]
    tiles, rest, share, _ = packing(*block.shape)
    for t in range(tiles):
        target[base + t * rows : base + (t + 1) * rows, :] = block[:, t * LANES : (t + 1) * LANES].astype(BF)
    if rest:
        short = rows // share
        last = [block[q * short : (q + 1) * short, tiles * LANES :] for q in range(share)]
        if share * rest < LANES:
            last.append(jnp.zeros((short, LANES - share * rest), block.dtype))
        at = base + tiles * rows
        target[at : at + short, :] = jnp.concatenate(last, axis=1).astype(BF)


def unpack(source, base, target, row, rows, columns):
    tiles, rest, share, _ = packing(rows, columns)
    for t in range(tiles):
        piece = source[base + t * rows : base + (t + 1) * rows, :]
        target[row : row + rows, t * LANES : (t + 1) * LANES] = piece.astype(target.dtype)
    if rest:
        short = rows // share
        at = base + tiles * rows
        last = source[at : at + short, :].astype(F32)
        for q in range(share):
            piece = last[:, q * rest : (q + 1) * rest].astype(target.dtype)
            target[row + q * short : row + (q + 1) * short, tiles * LANES : columns] = piece


def staged_call(body, out_shape, scalars, operands, scratch, flops, nbytes):
    buffers = [pltpu.VMEM(x.shape, x.dtype) for x in list(operands) + list(out_shape)]
    ins, outs = len(operands), len(out_shape)

    def run(*refs):
        values, refs = refs[: len(scalars)], refs[len(scalars) :]
        far, refs = refs[: ins + outs], refs[ins + outs :]
        near, extra, sems = refs[: ins + outs], refs[ins + outs : -1], refs[-1]
        loads = [start(far[k], near[k], sems.at[k]) for k in range(ins)]
        for load in loads:
            load.wait()
        body(*values, *near, *extra)
        sends = [start(near[k], far[k], sems.at[k]) for k in range(ins, ins + outs)]
        for send in sends:
            send.wait()

    return kernel_call(
        run,
        list(out_shape),
        [SMEM] * len(scalars) + [ANY] * ins,
        [ANY] * outs,
        buffers + list(scratch) + [pltpu.SemaphoreType.DMA((ins + outs,))],
        flops,
        nbytes,
    )(*scalars, *operands)


def pick_pages(table, own, picked, groups, per_group, per_peer):
    def one_group(g, carry):
        spot = g * per_peer
        for k in range(per_group):
            local = table[g * per_group + k] - own * per_group
            picked[spot] = local
            spot = spot + jnp.where((local >= 0) & (local < per_group), 1, 0)
        return carry

    lax.fori_loop(0, groups, one_group, 0)


def place_pages(table, own, seen, source, target, groups, per_group, per_peer, page_len):
    for g in range(groups):
        seen[g] = 0
    for k in range(per_group):
        holder = lax.div(table[own * per_group + k], per_group)
        slot = holder * per_peer + seen[holder]
        seen[holder] = seen[holder] + 1
        start = pl.multiple_of(slot * page_len, page_len)
        target[k * page_len : (k + 1) * page_len, :] = source[pl.ds(start, page_len), :]


def picked_rows(source, picked, g, per_peer, page_len):
    pages = []
    for b in range(per_peer):
        at = pl.multiple_of(picked[g * per_peer + b] * page_len, page_len)
        pages.append(source[pl.ds(at, page_len), :])
    return jnp.concatenate(pages, axis=0)


def project_kernel(
    dims, table, hidden_in, gain, wq_in, wd_in, out_in, hidden, wq, wd, normed, wide, out, picked, sems
):
    groups, per_group, per_peer, page_len = dims
    rows, model_width = hidden.shape
    low = wd.shape[1]
    pieces = 4
    part = rows // pieces
    strip = wq.shape[0] // 2
    loads = [
        start(hidden_in.at[pl.ds(k * part, part)], hidden.at[pl.ds(k * part, part)], sems.at[k]) for k in range(pieces)
    ]
    weights = [start(wd_in, wd, sems.at[pieces])]
    for k in range(2):
        half = pl.ds(k * strip, strip)
        weights.append(start(wq_in.at[half], wq.at[half], sems.at[pieces + 1 + k]))
    pick_pages(table, lax.axis_index("group"), picked, groups, per_group, per_peer)
    step = 32
    scale = gain[...].reshape(1, model_width)

    def norm_rows(i, carry):
        at = pl.ds(pl.multiple_of(i * step, step), step)
        x = hidden[at, :].astype(F32)
        meansq = jnp.mean(x * x, axis=-1, keepdims=True)
        normed[at, :] = (x * lax.rsqrt(meansq + EPSILON) * scale).astype(BF)
        return carry

    for k in range(pieces):
        loads[k].wait()
        lax.fori_loop(k * part // step, (k + 1) * part // step, norm_rows, 0, unroll=2)
    for load in weights:
        load.wait()
    wide[:, :low] = dot(normed[...], wd[...])
    wide[:, low:] = dot(normed[...], wq[...], ((1,), (1,)))
    sends = []
    for g in range(groups):
        pack(picked_rows(wide, picked, g, per_peer, page_len), out.at[g], 0)
        sends.append(start(out.at[g], out_in.at[g], sems.at[pieces + 3 + g]))
    for send in sends:
        send.wait()


def side_kernel(dims, shards, table, hidden, vocab, w_out, w_up, out, wide, products, picked):
    groups, per_group, per_peer, page_len = dims
    rows, model_width = hidden.shape
    width = model_width // shards
    inner, low = w_out.shape[0], w_up.shape[0]
    held = vocab.shape[0] // shards
    pick_pages(table, lax.axis_index("group"), picked, groups, per_group, per_peer)
    own_shard = lax.axis_index("mp")
    products[:, :inner] = dot(vocab[...], w_out[...], ((1,), (1,)))
    products[:, inner : inner + low] = dot(vocab[...], w_up[...], ((1,), (1,)))
    for j in range(shards):

        @pl.when(own_shard == j)
        def _(j=j):
            cols = slice(j * width, (j + 1) * width)
            wide[...] = hidden[:, cols].astype(F32)
            products[:, inner + low :] = vocab[:, cols].astype(F32)

    ordered = []
    for j in range(shards):
        at = lax.rem(j - own_shard + 2 * shards - 1, shards) * held
        ordered.append(products[pl.ds(pl.multiple_of(at, held), held), :])
    block = jnp.concatenate(ordered, axis=0)
    _, _, _, base = packing(*block.shape)
    for g in range(groups):
        pack(block, out.at[g], 0)
        pack(picked_rows(wide, picked, g, per_peer, page_len), out.at[g], base)


def phi_of(vectors, left, right, cols):
    first = dot(left[...], vectors) + cols[:, 0:1]
    second = dot(right[...], vectors) + cols[:, 1:2]
    return first * second * cols[:, 2:3]


def with_ones(values):
    lane = lax.broadcasted_iota(jnp.int32, (values.shape[0], LANES - HD), 1)
    return jnp.concatenate([values, jnp.where(lane == 0, 1.0, 0.0).astype(values.dtype)], axis=1)


def with_ones_t(values):
    row = lax.broadcasted_iota(jnp.int32, (LANES - HD, values.shape[1]), 0)
    return jnp.concatenate([values, jnp.where(row == 0, 1.0, 0.0).astype(values.dtype)], axis=0)


def same_upto(segrow):
    count = segrow.shape[1]
    ids = segrow[...].astype(F32)
    column = jnp.transpose(jnp.broadcast_to(ids, (8, count)))[:, 0:1]
    behind = lax.broadcasted_iota(jnp.int32, (count, count), 0)
    ahead = lax.broadcasted_iota(jnp.int32, (count, count), 1)
    return jnp.where((column == ids) & (behind <= ahead), 1.0, 0.0)


def group_kernel(
    dims, low, heads, table, arrived_in, segrow, left, right, cols, ordered_t_in, state, nd_in, squares,
    arrived, wide, placed, ordered, ordered_t, nd, mask, seen, sems
):
    groups, per_group, per_peer, page_len = dims
    tall = per_peer * page_len
    count, sent = placed.shape
    qkv = ordered.shape[1]
    loads = [start(arrived_in.at[g], arrived.at[g], sems.at[g]) for g in range(groups)]
    mask[...] = same_upto(segrow)
    squares[...] = jnp.zeros(squares.shape, F32)
    squares[heads : heads + 1, :] = jnp.sum(mask[...], axis=0, keepdims=True)
    for g in range(groups):
        loads[g].wait()
        unpack(arrived.at[g], 0, wide, g * tall, tall, sent)
    place_pages(table, lax.axis_index("group"), seen, wide, placed, groups, per_group, per_peer, page_len)
    ordered[...] = placed[:, low : low + qkv].astype(BF)
    for at in range(0, sent, LANES):
        end = min(at + LANES, sent)
        ordered_t[at:end, :] = jnp.transpose(placed[:, at:end]).astype(BF)
    sends = [start(ordered_t, ordered_t_in, sems.at[0])]

    last = segrow[:, count - 1 : count]
    member = jnp.where(segrow[...] == last, 1.0, 0.0)
    total = jnp.sum(member, axis=1, keepdims=True)
    fine = total - total.astype(BF).astype(F32)
    tag = last.astype(F32) + 1.0
    row = lax.broadcasted_iota(jnp.int32, (PHI_PAD, LANES), 0)
    lane = lax.broadcasted_iota(jnp.int32, (PHI_PAD, LANES), 1)
    block = 256 if count % 256 == 0 else count
    for h in range(heads):
        at = h * HEAD
        key = ordered[:, at + FEAT : at + 2 * FEAT] * BF(0.25)
        value = ordered[:, at + 2 * FEAT : at + HEAD]
        at = low + h * HEAD
        query_t = ordered_t[at : at + FEAT, :]
        key_t = ordered_t[at + FEAT : at + 2 * FEAT, :]
        value_t = ordered_t[at + 2 * FEAT : at + HEAD, :]

        phi = (phi_of(key_t, left, right, cols) * member).astype(BF)
        summed = dot(phi, with_ones(value))
        summed = jnp.where((row == 0) & (lane == TAG), tag, summed)
        summed = jnp.where((row == 0) & (lane == REST), fine, summed)
        state[h] = summed.astype(BF)

        extended_t = with_ones_t(value_t)
        wide_key = key_t.astype(F32)
        wide_value = value_t.astype(F32)
        self_score = 0.25 * jnp.sum(wide_key * wide_key, axis=0, keepdims=True)
        self_value = jnp.sum(wide_value * wide_value, axis=0, keepdims=True)
        diagonal = (1.0 + self_score * (1.0 + 0.5 * self_score)) * self_value
        for begin in range(0, count, block):
            end = begin + block
            s = dot(key[:end], query_t[:, begin:end])
            w = (1.0 + s * (1.0 + 0.5 * s)) * mask[:end, begin:end]
            nd[h, :, begin:end] = dot(extended_t[:, :end], w.astype(BF))
            kk = dot(key[:end], key_t[:, begin:end])
            vv = dot(value[:end], value_t[:, begin:end])
            gram = (1.0 + kk * (1.0 + 0.5 * kk)) * vv * mask[:end, begin:end]
            below = jnp.sum(gram, axis=0, keepdims=True)
            squares[h : h + 1, begin:end] = 2.0 * below - diagonal[:, begin:end]
        sends.append(start(nd.at[h], nd_in.at[h], sems.at[1 + h]))
    for send in sends:
        send.wait()


def split3(x):
    a = x.astype(BF)
    rest = x - a.astype(F32)
    b = rest.astype(BF)
    return jnp.concatenate([a, b, (rest - b.astype(F32)).astype(BF)], axis=0)


def state_corner(state):
    corner = state[0, 0:1, :].astype(F32)
    return corner[:, TAG : TAG + 1], corner[:, ONE : ONE + 1] + corner[:, REST : REST + 1]


def shard_parts(offsets, own_shard, shards, w_t, up_t, inputs, held_out, outs, sems):
    width = w_t.shape[0] // shards
    inner = w_t.shape[1]
    pending = []
    for k, offset in enumerate(offsets):
        j = own_shard + offset
        there = (j >= 0) & (j < shards)

        @pl.when(there)
        def _(j=j, k=k):
            rows = pl.ds(pl.multiple_of(j * width, width), width)
            part = dot(w_t[rows, :], inputs[:inner, :]) + dot(up_t[rows, :], inputs[inner:, :])
            held_out[k] = part.astype(BF)
            start(held_out.at[k], outs[k], sems.at[k])

        pending.append((there, k))

    def finish():
        for there, k in pending:

            @pl.when(there)
            def _(k=k):
                pltpu.make_async_copy(held_out.at[k], outs[k], sems.at[k]).wait()

    return finish


def finish_kernel(
    low, heads, shards, ordered_t_in, nd_in, state_in, segrow, slotrow, left, right, cols, w_t_in, up_t_in, *refs
):
    far = far_offsets(shards)
    outs = refs[: len(far) - 1]
    outs = [outs[0], *outs]
    inputs_in, queries, nd, state, w_t, up_t, inputs, held_out, sems = refs[len(far) - 1 :]
    inner = heads * HD
    sem = iter(range(len(far), len(far) + heads + 6))
    fetches = [start(state_in, state, sems.at[next(sem)])]
    for h in range(heads):
        rows = pl.ds(low + h * HEAD, FEAT)
        fetches.append(start(ordered_t_in.at[rows], queries.at[h], sems.at[next(sem)]))
    fetches.append(start(nd_in, nd, sems.at[next(sem)]))
    fetches.append(start(ordered_t_in.at[pl.ds(0, low)], inputs.at[pl.ds(inner, low)], sems.at[next(sem)]))
    weights = [start(w_t_in, w_t, sems.at[next(sem)]), start(up_t_in, up_t, sems.at[next(sem)])]
    for fetch in fetches:
        fetch.wait()
    tag, _ = state_corner(state)
    carried = jnp.where(segrow[...].astype(F32) + 1.0 == tag, 1.0, 0.0)
    row_slot = lax.div(lax.broadcasted_iota(jnp.int32, (low, 1), 0), RANK)
    lowered = jnp.where(slotrow[...] == row_slot, inputs[inner:, :].astype(F32), 0.0)
    inputs[inner:, :] = lowered.astype(BF)
    for h in range(heads):
        cross = dot(state[h], phi_of(queries[h], left, right, cols).astype(BF), ((0,), (0,)))
        both = nd[h] + carried * cross
        inputs[h * HD : (h + 1) * HD, :] = (both[:HD, :] / both[ONE : ONE + 1, :]).astype(BF)
    for load in weights:
        load.wait()
    finish = shard_parts(far, lax.axis_index("mp"), shards, w_t, up_t, inputs, held_out, outs, sems)
    kept = start(inputs, inputs_in, sems.at[next(sem)])
    finish()
    kept.wait()


def far_offsets(shards):
    far = [shards - 1, 1 - shards]
    for distance in range(shards - 2, 1, -1):
        far += [distance, -distance]
    return far


def near_kernel(shards, w_t_in, up_t_in, inputs_in, *refs):
    outs = refs[: len(NEAR)]
    w_t, up_t, inputs, held_out, sems = refs[len(NEAR) :]
    loads = [
        start(source, target, sems.at[len(NEAR) + k])
        for k, (source, target) in enumerate([(w_t_in, w_t), (up_t_in, up_t), (inputs_in, inputs)])
    ]
    for load in loads:
        load.wait()
    shard_parts(NEAR, lax.axis_index("mp"), shards, w_t, up_t, inputs, held_out, outs, sems)()


def logits_kernel(dims, shards, width, table, arrived, inputs, out, vocab, both, wide, placed, seen):
    groups, per_group, per_peer, page_len = dims
    tall = per_peer * page_len
    inner = inputs.shape[0]
    rows = vocab.shape[0] // groups
    _, _, _, base = packing(rows, inner + width)
    for g in range(groups):
        unpack(arrived.at[g], 0, vocab, g * rows, rows, inner + width)
        unpack(arrived.at[g], base, wide, g * tall, tall, width)
    place_pages(table, lax.axis_index("group"), seen, wide, placed, groups, per_group, per_peer, page_len)
    both[:inner, :] = inputs[...]
    both[inner:, :] = jnp.transpose(placed[...]).astype(BF)
    block = inputs.shape[1] // shards
    scored = dot(vocab[...], both[...])
    for j in range(shards):
        out[j] = scored[:, j * block : (j + 1) * block].astype(BF)


def norms_kernel(low, heads, ordered_t, squares, state, segrow, left, right, cols, norms):
    count = segrow.shape[1]
    upto = same_upto(segrow).astype(BF)
    tag, held = state_corner(state)
    carried = jnp.where(segrow[...].astype(F32) + 1.0 == tag, 1.0, 0.0)
    value_lane = lax.broadcasted_iota(jnp.int32, (1, LANES), 1) < HD
    counted = carried * held + squares[heads : heads + 1, :]
    increments = []
    before = []
    for h in range(heads):
        at = low + h * HEAD
        held_state = state[h]
        key_t = ordered_t[at + FEAT : at + 2 * FEAT, :]
        value_t = ordered_t[at + 2 * FEAT : at + HEAD, :].astype(F32)
        against = dot(held_state, phi_of(key_t, left, right, cols).astype(BF), ((0,), (0,)))[:HD, :]
        along = jnp.sum(against * value_t, axis=0, keepdims=True)
        increments.append(squares[h : h + 1, :] + 2.0 * carried * along)
        wide_state = jnp.where(value_lane, held_state.astype(F32), 0.0)
        per_lane = jnp.sum(wide_state * wide_state, axis=0, keepdims=True)
        before.append(jnp.sum(per_lane, axis=1, keepdims=True))
    if heads % 8:
        increments.append(jnp.zeros((8 - heads % 8, count), F32))
    stacked = split3(jnp.concatenate(increments, axis=0))
    thrice = dot(stacked, upto)
    rows = thrice.shape[0] // 3
    summed = thrice[:rows] + thrice[rows : 2 * rows] + thrice[2 * rows :]
    for h in range(heads):
        total = carried * before[h] + summed[h : h + 1, :]
        norms[h : h + 1, :] = jnp.sqrt(total / (counted * float(FEAT * HD)))


def best_kernel(shards, pieces, best):
    whole = pieces[0].astype(F32)
    for i in range(1, shards):
        whole = whole + pieces[i].astype(F32)
    best[...] = jnp.max(whole, axis=0, keepdims=True)


def exchange(blocks, axis):
    return lax.all_to_all(blocks, axis, split_axis=0, concat_axis=0, tiled=True)


def ring_rows(values, axis):
    size = lax.axis_size(axis)
    steps = [lax.ppermute(values, axis, [(i, (i + by) % size) for i in range(size)]) for by in range(size - 1, 0, -1)]
    return jnp.concatenate([*steps, values], axis=0)


def line_sums(terms, axis):
    size = lax.axis_size(axis)

    def joined(*parts):
        return sum(part.astype(F32) for part in parts).astype(BF)

    def up(values, first, last):
        return lax.ppermute(values, axis, [(i, i + 1) for i in range(first, last)])

    def down(values, first, last):
        return lax.ppermute(values, axis, [(i, i - 1) for i in range(first, last)])

    if size == 4:
        relayed_up = up(terms[2], 0, size - 2)
        relayed_down = down(terms[-2], 2, size)
        far = lax.ppermute(terms[3], axis, [(0, 3), (3, 0)])
        near_up = up(joined(terms[1], relayed_up), 0, size - 1)
        near_down = down(joined(terms[-1], relayed_down), 1, size)
        return joined(terms[0], far, near_up, near_down)
    going_up = going_down = None
    for step in range(1, size):
        to_up = terms[size - step]
        to_down = terms[step - size]
        if step > 1:
            to_up = joined(to_up, going_up)
            to_down = joined(to_down, going_down)
        going_up = up(to_up, 0, step)
        going_down = down(to_down, size - step, size)
    return joined(terms[0], going_up, going_down)


def on_device(
    hidden,
    norm_gain,
    qkv_weight,
    out_weight,
    adapter_down,
    adapter_up,
    vocab_rows,
    segments,
    request_adapter,
    adapter_slot,
    page_table,
):
    groups = lax.axis_size("group")
    shards = lax.axis_size("mp")
    own_shard = lax.axis_index("mp")
    count, model_width = hidden.shape
    per_group = page_table.shape[0] // groups
    per_peer = per_group // groups
    page_len = count // per_group
    dims = (groups, per_group, per_peer, page_len)
    qkv_cols = qkv_weight.shape[1]
    heads = qkv_cols // HEAD
    low = adapter_down.shape[1]
    inner = heads * HD
    width = model_width // shards
    sent = low + qkv_cols
    tall = per_peer * page_len
    packed = packing(tall, sent)[-1]
    some = shards * vocab_rows.shape[0]
    scored = groups * some
    aside = packing(some, inner + low + width)[-1] + packing(tall, width)[-1]
    shape = jax.ShapeDtypeStruct
    dma = pltpu.SemaphoreType.DMA
    picked = pltpu.SMEM((groups * per_peer + 1,), jnp.int32)

    left, right, cols = [jnp.asarray(t) for t in feature_tables()]
    segrow = segments.reshape(1, count)
    request_ids = jnp.arange(request_adapter.shape[0], dtype=jnp.int32)
    adapter_ids = jnp.arange(adapter_slot.shape[0], dtype=jnp.int32)

    outgoing = kernel_call(
        functools.partial(project_kernel, dims),
        shape((groups, packed, LANES), BF),
        [SMEM, ANY, VMEM, ANY, ANY],
        ANY,
        [
            pltpu.VMEM((count, model_width), BF),
            pltpu.VMEM((qkv_cols, model_width), BF),
            pltpu.VMEM((model_width, low), BF),
            pltpu.VMEM((count, model_width), BF),
            pltpu.VMEM((count, sent), F32),
            pltpu.VMEM((groups, packed, LANES), BF),
            picked,
            dma((7 + groups,)),
        ],
        2 * count * model_width * sent,
        2 * (count * model_width + model_width * sent),
    )(page_table, hidden, norm_gain, qkv_weight.T, adapter_down)
    arrived = exchange(outgoing, "group")

    after_out, after_up, after_vocab, after_adapter, _ = lax.optimization_barrier(
        (out_weight, adapter_up, vocab_rows, request_adapter, outgoing)
    )
    w_t, up_t = after_out.T, after_up.T
    some_vocab = ring_rows(after_vocab, "mp")
    request_slot = jnp.sum(jnp.where(after_adapter[:, None] == adapter_ids[None, :], adapter_slot[None, :], 0), axis=1)
    slots = jnp.sum(jnp.where(segrow == request_ids[:, None], request_slot[:, None], 0), axis=0, keepdims=True)
    slotrow = slots - own_shard * (low // RANK)
    [beside] = staged_call(
        functools.partial(side_kernel, dims, shards),
        [shape((groups, aside, LANES), BF)],
        [page_table],
        [hidden, some_vocab, out_weight, adapter_up],
        [pltpu.VMEM((count, width), F32), pltpu.VMEM((some, inner + low + width), F32), picked],
        2 * some * model_width * (inner + low),
        2 * count * model_width,
    )
    arrived, beside, slotrow, w_t, up_t = lax.optimization_barrier((arrived, beside, slotrow, w_t, up_t))

    ordered_t, state, nd, squares = kernel_call(
        functools.partial(group_kernel, dims, low, heads),
        (
            shape((sent, count), BF),
            shape((heads, PHI_PAD, LANES), BF),
            shape((heads, LANES, count), F32),
            shape((8 * (heads // 8 + 1), count), F32),
        ),
        [SMEM, ANY] + [VMEM] * 4,
        (ANY, VMEM, ANY, VMEM),
        [
            pltpu.VMEM((groups, packed, LANES), BF),
            pltpu.VMEM((count, sent), F32),
            pltpu.VMEM((count, sent), F32),
            pltpu.VMEM((count, qkv_cols), BF),
            pltpu.VMEM((sent, count), BF),
            pltpu.VMEM((heads, LANES, count), F32),
            pltpu.VMEM((count, count), F32),
            pltpu.SMEM((groups,), jnp.int32),
            dma((max(groups, 1 + heads),)),
        ],
        heads * 2 * count * count * 512,
        6 * count * sent,
    )(page_table, arrived, segrow, left, right, cols)
    state = lax.ppermute(state, "group", [(i, i + 1) for i in range(groups - 1)])

    far = far_offsets(shards)
    part = shape((width, count), BF)
    w_buffers = [pltpu.VMEM((model_width, inner), BF), pltpu.VMEM((model_width, low), BF)]
    *far_terms, inputs = kernel_call(
        functools.partial(finish_kernel, low, heads, shards),
        [part] * (len(far) - 1) + [shape((inner + low, count), BF)],
        [ANY] * 3 + [VMEM] * 5 + [ANY] * 2,
        [ANY] * len(far),
        [
            pltpu.VMEM((heads, FEAT, count), BF),
            pltpu.VMEM((heads, LANES, count), F32),
            pltpu.VMEM((heads, PHI_PAD, LANES), BF),
            *w_buffers,
            pltpu.VMEM((inner + low, count), BF),
            pltpu.VMEM((len(far), width, count), BF),
            dma((len(far) + heads + 6,)),
        ],
        count * (inner + low) * model_width,
        2 * count * model_width,
    )(ordered_t, nd, state, segrow, slotrow, left, right, cols, w_t, up_t)
    near_terms = kernel_call(
        functools.partial(near_kernel, shards),
        [part] * len(NEAR),
        [ANY] * 3,
        [ANY] * len(NEAR),
        [
            *w_buffers,
            pltpu.VMEM((inner + low, count), BF),
            pltpu.VMEM((len(NEAR), width, count), BF),
            dma((len(NEAR) + 3,)),
        ],
        count * (inner + low) * model_width,
        2 * count * model_width,
    )(w_t, up_t, inputs)
    terms = dict(zip(NEAR, near_terms)) | dict(zip(far, [far_terms[0], *far_terms]))
    update = line_sums(terms, "mp")

    beside = exchange(beside, "group")
    [logits] = staged_call(
        functools.partial(logits_kernel, dims, shards, width),
        [shape((shards, scored, count // shards), BF)],
        [page_table],
        [beside, inputs],
        [
            pltpu.VMEM((scored, inner + low + width), BF),
            pltpu.VMEM((inner + low + width, count), BF),
            pltpu.VMEM((count, width), F32),
            pltpu.VMEM((count, width), F32),
            pltpu.SMEM((groups,), jnp.int32),
        ],
        2 * count * scored * (inner + low + width),
        4 * count * scored,
    )
    logits = exchange(logits, "mp")
    [state_norms] = staged_call(
        functools.partial(norms_kernel, low, heads),
        [shape((heads, count), F32)],
        [],
        [ordered_t, squares, state, segrow, left, right, cols],
        [],
        heads * 2 * count * count * 16,
        2 * sent * count,
    )
    [best] = staged_call(
        functools.partial(best_kernel, shards),
        [shape((1, count // shards), F32)],
        [],
        [logits],
        [],
        count * scored,
        2 * count * scored,
    )
    return update.T, state_norms, best.reshape(-1)


def solution(mesh):
    placed = (
        P("group", None),
        P(),
        P(None, "mp"),
        P("mp", None),
        P(None, "mp"),
        P("mp", None),
        P(("group", "mp"), None),
        P("group"),
        P(),
        P(),
        P(),
    )
    return jax.shard_map(
        on_device,
        mesh=mesh,
        in_specs=placed,
        out_specs=(P("group", "mp"), P("mp", "group"), P(("group", "mp"))),
        check_vma=False,
    )
```

```python
import functools

import jax
import jax.numpy as jnp
import numpy as np
from jax import lax
from jax.experimental import pallas as pl
from jax.experimental.pallas import tpu as pltpu
from jax.sharding import PartitionSpec as P

FEAT = 16
HD = 112
RANK = 16
EPSILON = 1e-05
HEAD = 2 * FEAT + HD
PHI = 1 + FEAT + FEAT * (FEAT + 1) // 2
PHI_PAD = 160
LANES = 128
ONE, TAG, REST = HD, HD + 1, HD + 2
NEAR = (0, 1, -1)
VMEM_LIMIT = 60 * 1024 * 1024

BF = jnp.bfloat16
F32 = jnp.float32
SMEM = pl.BlockSpec(memory_space=pltpu.SMEM)
VMEM = pl.BlockSpec(memory_space=pltpu.VMEM)
ANY = pl.BlockSpec(memory_space=pl.ANY)


def feature_tables():
    left = np.zeros((PHI_PAD, FEAT), np.float32)
    right = np.zeros((PHI_PAD, FEAT), np.float32)
    cols = np.zeros((PHI_PAD, 8), np.float32)
    cols[0, :3] = 1.0
    at = 1
    for i in range(FEAT):
        left[at, i] = 1.0
        cols[at, 1] = 1.0
        cols[at, 2] = FEAT**-0.25
        at += 1
    for i in range(FEAT):
        for j in range(i, FEAT):
            left[at, i] = 1.0
            right[at, j] = 1.0
            cols[at, 2] = (1.0 if i == j else 2.0**0.5) / (2.0 * FEAT) ** 0.5
            at += 1
    return left.astype(jnp.bfloat16), right.astype(jnp.bfloat16), cols


def dot(a, b, dims=((1,), (0,))):
    return lax.dot_general(a, b, (dims, ((), ())), preferred_element_type=F32)


def kernel_call(body, out_shape, in_specs, out_specs, scratch, flops, nbytes):
    return pl.pallas_call(
        body,
        out_shape=out_shape,
        in_specs=in_specs,
        out_specs=out_specs,
        scratch_shapes=scratch,
        compiler_params=pltpu.CompilerParams(vmem_limit_bytes=VMEM_LIMIT),
        cost_estimate=pl.CostEstimate(flops=flops, bytes_accessed=nbytes, transcendentals=0),
    )


def start(source, target, sem):
    copy = pltpu.make_async_copy(source, target, sem)
    copy.start()
    return copy


def packing(rows, columns):
    tiles, rest = divmod(columns, LANES)
    share = LANES // rest if rest and LANES % rest == 0 else 1
    if rows % (16 * share):
        share = 1
    return tiles, rest, share, tiles * rows + (rows // share if rest else 0)


def pack(block, target, base):
    rows = block.shape[0]
    tiles, rest, share, _ = packing(*block.shape)
    for t in range(tiles):
        target[base + t * rows : base + (t + 1) * rows, :] = block[:, t * LANES : (t + 1) * LANES].astype(BF)
    if rest:
        short = rows // share
        last = [block[q * short : (q + 1) * short, tiles * LANES :] for q in range(share)]
        if share * rest < LANES:
            last.append(jnp.zeros((short, LANES - share * rest), block.dtype))
        at = base + tiles * rows
        target[at : at + short, :] = jnp.concatenate(last, axis=1).astype(BF)


def unpack(source, base, target, row, rows, columns):
    tiles, rest, share, _ = packing(rows, columns)
    for t in range(tiles):
        piece = source[base + t * rows : base + (t + 1) * rows, :]
        target[row : row + rows, t * LANES : (t + 1) * LANES] = piece.astype(target.dtype)
    if rest:
        short = rows // share
        at = base + tiles * rows
        last = source[at : at + short, :].astype(F32)
        for q in range(share):
            piece = last[:, q * rest : (q + 1) * rest].astype(target.dtype)
            target[row + q * short : row + (q + 1) * short, tiles * LANES : columns] = piece


def staged_call(body, out_shape, scalars, operands, scratch, flops, nbytes, given=()):
    buffers = [pltpu.VMEM(x.shape, x.dtype) for x in list(operands) + list(out_shape)]
    ins, outs = len(operands), len(out_shape)

    def run(*refs):
        values, refs = refs[: len(scalars)], refs[len(scalars) :]
        ready, refs = refs[: len(given)], refs[len(given) :]
        far, refs = refs[: ins + outs], refs[ins + outs :]
        near, extra, sems = refs[: ins + outs], refs[ins + outs : -1], refs[-1]
        loads = [start(far[k], near[k], sems.at[k]) for k in range(ins)]
        for load in loads:
            load.wait()
        body(*values, *ready, *near, *extra)
        sends = [start(near[k], far[k], sems.at[k]) for k in range(ins, ins + outs)]
        for send in sends:
            send.wait()

    return kernel_call(
        run,
        list(out_shape),
        [SMEM] * len(scalars) + [VMEM] * len(given) + [ANY] * ins,
        [ANY] * outs,
        buffers + list(scratch) + [pltpu.SemaphoreType.DMA((ins + outs,))],
        flops,
        nbytes,
    )(*scalars, *given, *operands)


def pick_pages(table, own, picked, groups, per_group, per_peer):
    def one_group(g, carry):
        spot = g * per_peer
        for k in range(per_group):
            local = table[g * per_group + k] - own * per_group
            picked[spot] = local
            spot = spot + jnp.where((local >= 0) & (local < per_group), 1, 0)
        return carry

    lax.fori_loop(0, groups, one_group, 0)


def place_pages(table, own, seen, source, target, groups, per_group, per_peer, page_len):
    for g in range(groups):
        seen[g] = 0
    for k in range(per_group):
        holder = lax.div(table[own * per_group + k], per_group)
        slot = holder * per_peer + seen[holder]
        seen[holder] = seen[holder] + 1
        start = pl.multiple_of(slot * page_len, page_len)
        target[k * page_len : (k + 1) * page_len, :] = source[pl.ds(start, page_len), :]


def picked_rows(source, picked, g, per_peer, page_len):
    pages = []
    for b in range(per_peer):
        at = pl.multiple_of(picked[g * per_peer + b] * page_len, page_len)
        pages.append(source[pl.ds(at, page_len), :])
    return jnp.concatenate(pages, axis=0)


def project_kernel(
    dims, table, hidden_in, gain, wq_in, wd_in, out_in, hidden, wq, wd, normed, wide, out, picked, sems
):
    groups, per_group, per_peer, page_len = dims
    rows, model_width = hidden.shape
    low = wd.shape[1]
    pieces = 4
    part = rows // pieces
    strip = wq.shape[0] // 2
    loads = [
        start(hidden_in.at[pl.ds(k * part, part)], hidden.at[pl.ds(k * part, part)], sems.at[k]) for k in range(pieces)
    ]
    weights = [start(wd_in, wd, sems.at[pieces])]
    for k in range(2):
        half = pl.ds(k * strip, strip)
        weights.append(start(wq_in.at[half], wq.at[half], sems.at[pieces + 1 + k]))
    pick_pages(table, lax.axis_index("group"), picked, groups, per_group, per_peer)
    step = 32
    scale = gain[...].reshape(1, model_width)

    def norm_rows(i, carry):
        at = pl.ds(pl.multiple_of(i * step, step), step)
        x = hidden[at, :].astype(F32)
        meansq = jnp.mean(x * x, axis=-1, keepdims=True)
        normed[at, :] = (x * lax.rsqrt(meansq + EPSILON) * scale).astype(BF)
        return carry

    for k in range(pieces):
        loads[k].wait()
        lax.fori_loop(k * part // step, (k + 1) * part // step, norm_rows, 0, unroll=2)
    for load in weights:
        load.wait()
    wide[:, :low] = dot(normed[...], wd[...])
    wide[:, low:] = dot(normed[...], wq[...], ((1,), (1,)))
    sends = []
    for g in range(groups):
        pack(picked_rows(wide, picked, g, per_peer, page_len), out.at[g], 0)
        sends.append(start(out.at[g], out_in.at[g], sems.at[pieces + 3 + g]))
    for send in sends:
        send.wait()


def side_kernel(dims, shards, table, hidden, vocab, w_out, w_up, out, wide, products, picked):
    groups, per_group, per_peer, page_len = dims
    rows, model_width = hidden.shape
    width = model_width // shards
    inner, low = w_out.shape[0], w_up.shape[0]
    held = vocab.shape[0] // shards
    pick_pages(table, lax.axis_index("group"), picked, groups, per_group, per_peer)
    own_shard = lax.axis_index("mp")
    products[:, :inner] = dot(vocab[...], w_out[...], ((1,), (1,)))
    products[:, inner : inner + low] = dot(vocab[...], w_up[...], ((1,), (1,)))
    for j in range(shards):

        @pl.when(own_shard == j)
        def _(j=j):
            cols = slice(j * width, (j + 1) * width)
            wide[...] = hidden[:, cols].astype(F32)
            products[:, inner + low :] = vocab[:, cols].astype(F32)

    ordered = []
    for j in range(shards):
        at = lax.rem(j - own_shard + 2 * shards - 1, shards) * held
        ordered.append(products[pl.ds(pl.multiple_of(at, held), held), :])
    block = jnp.concatenate(ordered, axis=0)
    _, _, _, base = packing(*block.shape)
    for g in range(groups):
        pack(block, out.at[g], 0)
        pack(picked_rows(wide, picked, g, per_peer, page_len), out.at[g], base)


def phi_of(vectors, left, right, cols):
    first = dot(left[...], vectors) + cols[:, 0:1]
    second = dot(right[...], vectors) + cols[:, 1:2]
    return first * second * cols[:, 2:3]


def with_ones(values):
    lane = lax.broadcasted_iota(jnp.int32, (values.shape[0], LANES - HD), 1)
    return jnp.concatenate([values, jnp.where(lane == 0, 1.0, 0.0).astype(values.dtype)], axis=1)


def with_ones_t(values):
    row = lax.broadcasted_iota(jnp.int32, (LANES - HD, values.shape[1]), 0)
    return jnp.concatenate([values, jnp.where(row == 0, 1.0, 0.0).astype(values.dtype)], axis=0)


def same_upto(segrow):
    count = segrow.shape[1]
    ids = segrow[...].astype(F32)
    column = jnp.transpose(jnp.broadcast_to(ids, (8, count)))[:, 0:1]
    behind = lax.broadcasted_iota(jnp.int32, (count, count), 0)
    ahead = lax.broadcasted_iota(jnp.int32, (count, count), 1)
    return jnp.where((column == ids) & (behind <= ahead), 1.0, 0.0)


def group_kernel(
    dims, low, heads, table, arrived_in, segrow, left, right, cols, ordered_in, ordered_t_in, state, nd_in,
    arrived, wide, placed, ordered, ordered_t, nd, mask, seen, sems
):
    groups, per_group, per_peer, page_len = dims
    tall = per_peer * page_len
    count, sent = placed.shape
    loads = [start(arrived_in.at[g], arrived.at[g], sems.at[g]) for g in range(groups)]
    mask[...] = same_upto(segrow)
    for g in range(groups):
        loads[g].wait()
        unpack(arrived.at[g], 0, wide, g * tall, tall, sent)
    place_pages(table, lax.axis_index("group"), seen, wide, placed, groups, per_group, per_peer, page_len)
    ordered[...] = placed[:, low:].astype(BF)
    for at in range(0, sent, LANES):
        end = min(at + LANES, sent)
        ordered_t[at:end, :] = jnp.transpose(placed[:, at:end]).astype(BF)
    sends = [start(ordered_t, ordered_t_in, sems.at[0]), start(ordered, ordered_in, sems.at[1])]

    last = segrow[:, count - 1 : count]
    member = jnp.where(segrow[...] == last, 1.0, 0.0)
    total = jnp.sum(member, axis=1, keepdims=True)
    fine = total - total.astype(BF).astype(F32)
    tag = last.astype(F32) + 1.0
    row = lax.broadcasted_iota(jnp.int32, (PHI_PAD, LANES), 0)
    lane = lax.broadcasted_iota(jnp.int32, (PHI_PAD, LANES), 1)
    block = 256 if count % 256 == 0 else count
    for h in range(heads):
        at = h * HEAD
        key = ordered[:, at + FEAT : at + 2 * FEAT] * BF(0.25)
        value = ordered[:, at + 2 * FEAT : at + HEAD]
        at = low + h * HEAD
        query_t = ordered_t[at : at + FEAT, :]
        key_t = ordered_t[at + FEAT : at + 2 * FEAT, :]
        extended_t = with_ones_t(ordered_t[at + 2 * FEAT : at + HEAD, :])

        phi = (phi_of(key_t, left, right, cols) * member).astype(BF)
        summed = dot(phi, with_ones(value))
        summed = jnp.where((row == 0) & (lane == TAG), tag, summed)
        summed = jnp.where((row == 0) & (lane == REST), fine, summed)
        state[h] = summed.astype(BF)

        for begin in range(0, count, block):
            end = begin + block
            s = dot(key[:end], query_t[:, begin:end])
            w = (1.0 + s * (1.0 + 0.5 * s)) * mask[:end, begin:end]
            nd[h, :, begin:end] = dot(extended_t[:, :end], w.astype(BF))
        sends.append(start(nd.at[h], nd_in.at[h], sems.at[2 + h]))
    for send in sends:
        send.wait()


def split3(x):
    a = x.astype(BF)
    rest = x - a.astype(F32)
    b = rest.astype(BF)
    return jnp.concatenate([a, b, (rest - b.astype(F32)).astype(BF)], axis=0)


def state_corner(state):
    corner = state[0, 0:1, :].astype(F32)
    return corner[:, TAG : TAG + 1], corner[:, ONE : ONE + 1] + corner[:, REST : REST + 1]


def shard_parts(offsets, own_shard, shards, w_t, up_t, inputs, held_out, outs, sems):
    width = w_t.shape[0] // shards
    inner = w_t.shape[1]
    pending = []
    for k, offset in enumerate(offsets):
        j = own_shard + offset
        there = (j >= 0) & (j < shards)

        @pl.when(there)
        def _(j=j, k=k):
            rows = pl.ds(pl.multiple_of(j * width, width), width)
            part = dot(w_t[rows, :], inputs[:inner, :]) + dot(up_t[rows, :], inputs[inner:, :])
            held_out[k] = part.astype(BF)
            start(held_out.at[k], outs[k], sems.at[k])

        pending.append((there, k))

    def finish():
        for there, k in pending:

            @pl.when(there)
            def _(k=k):
                pltpu.make_async_copy(held_out.at[k], outs[k], sems.at[k]).wait()

    return finish


def finish_kernel(
    low, heads, shards, ordered_t_in, nd_in, state, segrow, slotrow, left, right, cols, w_t_in, up_t_in, *refs
):
    far = far_offsets(shards)
    outs = refs[: len(far) - 1]
    outs = [outs[0], *outs]
    inputs_in, queries, nd, w_t, up_t, inputs, held_out, sems = refs[len(far) - 1 :]
    inner = heads * HD
    sem = iter(range(len(far), len(far) + heads + 6))
    fetches = []
    for h in range(heads):
        rows = pl.ds(low + h * HEAD, FEAT)
        fetches.append(start(ordered_t_in.at[rows], queries.at[h], sems.at[next(sem)]))
    fetches.append(start(nd_in, nd, sems.at[next(sem)]))
    fetches.append(start(ordered_t_in.at[pl.ds(0, low)], inputs.at[pl.ds(inner, low)], sems.at[next(sem)]))
    weights = [start(w_t_in, w_t, sems.at[next(sem)]), start(up_t_in, up_t, sems.at[next(sem)])]
    for fetch in fetches:
        fetch.wait()
    tag, _ = state_corner(state)
    carried = jnp.where(segrow[...].astype(F32) + 1.0 == tag, 1.0, 0.0)
    row_slot = lax.div(lax.broadcasted_iota(jnp.int32, (low, 1), 0), RANK)
    lowered = jnp.where(slotrow[...] == row_slot, inputs[inner:, :].astype(F32), 0.0)
    inputs[inner:, :] = lowered.astype(BF)
    for h in range(heads):
        cross = dot(state[h], phi_of(queries[h], left, right, cols).astype(BF), ((0,), (0,)))
        both = nd[h] + carried * cross
        inputs[h * HD : (h + 1) * HD, :] = (both[:HD, :] / both[ONE : ONE + 1, :]).astype(BF)
    for load in weights:
        load.wait()
    finish = shard_parts(far, lax.axis_index("mp"), shards, w_t, up_t, inputs, held_out, outs, sems)
    kept = start(inputs, inputs_in, sems.at[next(sem)])
    finish()
    kept.wait()


def far_offsets(shards):
    far = [shards - 1, 1 - shards]
    for distance in range(shards - 2, 1, -1):
        far += [distance, -distance]
    return far


def near_kernel(shards, w_t_in, up_t_in, inputs_in, *refs):
    outs = refs[: len(NEAR)]
    w_t, up_t, inputs, held_out, sems = refs[len(NEAR) :]
    loads = [
        start(source, target, sems.at[len(NEAR) + k])
        for k, (source, target) in enumerate([(w_t_in, w_t), (up_t_in, up_t), (inputs_in, inputs)])
    ]
    for load in loads:
        load.wait()
    shard_parts(NEAR, lax.axis_index("mp"), shards, w_t, up_t, inputs, held_out, outs, sems)()


def logits_kernel(dims, shards, width, table, arrived, inputs, out, vocab, both, wide, placed, seen):
    groups, per_group, per_peer, page_len = dims
    tall = per_peer * page_len
    inner = inputs.shape[0]
    rows = vocab.shape[0] // groups
    _, _, _, base = packing(rows, inner + width)
    for g in range(groups):
        unpack(arrived.at[g], 0, vocab, g * rows, rows, inner + width)
        unpack(arrived.at[g], base, wide, g * tall, tall, width)
    place_pages(table, lax.axis_index("group"), seen, wide, placed, groups, per_group, per_peer, page_len)
    both[:inner, :] = inputs[...]
    both[inner:, :] = jnp.transpose(placed[...]).astype(BF)
    block = inputs.shape[1] // shards
    scored = dot(vocab[...], both[...])
    for j in range(shards):
        out[j] = scored[:, j * block : (j + 1) * block].astype(BF)


def norms_kernel(low, heads, ordered, ordered_t, state, segrow, left, right, cols, norms, mask):
    count = segrow.shape[1]
    mask[...] = same_upto(segrow)
    upto = mask[...].astype(BF)
    tag, held = state_corner(state)
    carried = jnp.where(segrow[...].astype(F32) + 1.0 == tag, 1.0, 0.0)
    value_lane = lax.broadcasted_iota(jnp.int32, (1, LANES), 1) < HD
    counted = carried * held + jnp.sum(mask[...], axis=0, keepdims=True)
    block = 256 if count % 256 == 0 else count
    increments = []
    before = []
    for h in range(heads):
        at = h * HEAD
        key = ordered[:, at + FEAT : at + 2 * FEAT] * BF(0.25)
        value = ordered[:, at + 2 * FEAT : at + HEAD]
        at = low + h * HEAD
        key_t = ordered_t[at + FEAT : at + 2 * FEAT, :]
        value_t = ordered_t[at + 2 * FEAT : at + HEAD, :]
        wide_key = key_t.astype(F32)
        wide_value = value_t.astype(F32)
        self_score = 0.25 * jnp.sum(wide_key * wide_key, axis=0, keepdims=True)
        self_value = jnp.sum(wide_value * wide_value, axis=0, keepdims=True)
        diagonal = (1.0 + self_score * (1.0 + 0.5 * self_score)) * self_value
        below = []
        for begin in range(0, count, block):
            end = begin + block
            kk = dot(key[:end], key_t[:, begin:end])
            vv = dot(value[:end], value_t[:, begin:end])
            gram = (1.0 + kk * (1.0 + 0.5 * kk)) * vv * mask[:end, begin:end]
            below.append(jnp.sum(gram, axis=0, keepdims=True))
        added = 2.0 * jnp.concatenate(below, axis=1) - diagonal
        held_state = state[h]
        against = dot(held_state, phi_of(key_t, left, right, cols).astype(BF), ((0,), (0,)))[:HD, :]
        along = jnp.sum(against * wide_value, axis=0, keepdims=True)
        increments.append(added + 2.0 * carried * along)
        wide_state = jnp.where(value_lane, held_state.astype(F32), 0.0)
        per_lane = jnp.sum(wide_state * wide_state, axis=0, keepdims=True)
        before.append(jnp.sum(per_lane, axis=1, keepdims=True))
    if heads % 8:
        increments.append(jnp.zeros((8 - heads % 8, count), F32))
    stacked = split3(jnp.concatenate(increments, axis=0))
    thrice = dot(stacked, upto)
    rows = thrice.shape[0] // 3
    summed = thrice[:rows] + thrice[rows : 2 * rows] + thrice[2 * rows :]
    for h in range(heads):
        total = carried * before[h] + summed[h : h + 1, :]
        norms[h : h + 1, :] = jnp.sqrt(total / (counted * float(FEAT * HD)))


def best_kernel(shards, pieces, best):
    whole = pieces[0].astype(F32)
    for i in range(1, shards):
        whole = whole + pieces[i].astype(F32)
    best[...] = jnp.max(whole, axis=0, keepdims=True)


def exchange(blocks, axis):
    return lax.all_to_all(blocks, axis, split_axis=0, concat_axis=0, tiled=True)


def ring_rows(values, axis):
    size = lax.axis_size(axis)
    steps = [lax.ppermute(values, axis, [(i, (i + by) % size) for i in range(size)]) for by in range(size - 1, 0, -1)]
    return jnp.concatenate([*steps, values], axis=0)


def line_sums(terms, axis):
    size = lax.axis_size(axis)

    def joined(*parts):
        return sum(part.astype(F32) for part in parts).astype(BF)

    def up(values, first, last):
        return lax.ppermute(values, axis, [(i, i + 1) for i in range(first, last)])

    def down(values, first, last):
        return lax.ppermute(values, axis, [(i, i - 1) for i in range(first, last)])

    if size == 4:
        relayed_up = up(terms[2], 0, size - 2)
        relayed_down = down(terms[-2], 2, size)
        far = lax.ppermute(terms[3], axis, [(0, 3), (3, 0)])
        near_up = up(joined(terms[1], relayed_up), 0, size - 1)
        near_down = down(joined(terms[-1], relayed_down), 1, size)
        return joined(terms[0], far, near_up, near_down)
    going_up = going_down = None
    for step in range(1, size):
        to_up = terms[size - step]
        to_down = terms[step - size]
        if step > 1:
            to_up = joined(to_up, going_up)
            to_down = joined(to_down, going_down)
        going_up = up(to_up, 0, step)
        going_down = down(to_down, size - step, size)
    return joined(terms[0], going_up, going_down)


def on_device(
    hidden,
    norm_gain,
    qkv_weight,
    out_weight,
    adapter_down,
    adapter_up,
    vocab_rows,
    segments,
    request_adapter,
    adapter_slot,
    page_table,
):
    groups = lax.axis_size("group")
    shards = lax.axis_size("mp")
    own_shard = lax.axis_index("mp")
    count, model_width = hidden.shape
    per_group = page_table.shape[0] // groups
    per_peer = per_group // groups
    page_len = count // per_group
    dims = (groups, per_group, per_peer, page_len)
    qkv_cols = qkv_weight.shape[1]
    heads = qkv_cols // HEAD
    low = adapter_down.shape[1]
    inner = heads * HD
    width = model_width // shards
    sent = low + qkv_cols
    tall = per_peer * page_len
    packed = packing(tall, sent)[-1]
    some = shards * vocab_rows.shape[0]
    scored = groups * some
    aside = packing(some, inner + low + width)[-1] + packing(tall, width)[-1]
    shape = jax.ShapeDtypeStruct
    dma = pltpu.SemaphoreType.DMA
    picked = pltpu.SMEM((groups * per_peer + 1,), jnp.int32)

    left, right, cols = [jnp.asarray(t) for t in feature_tables()]
    segrow = segments.reshape(1, count)
    request_ids = jnp.arange(request_adapter.shape[0], dtype=jnp.int32)
    adapter_ids = jnp.arange(adapter_slot.shape[0], dtype=jnp.int32)

    outgoing = kernel_call(
        functools.partial(project_kernel, dims),
        shape((groups, packed, LANES), BF),
        [SMEM, ANY, VMEM, ANY, ANY],
        ANY,
        [
            pltpu.VMEM((count, model_width), BF),
            pltpu.VMEM((qkv_cols, model_width), BF),
            pltpu.VMEM((model_width, low), BF),
            pltpu.VMEM((count, model_width), BF),
            pltpu.VMEM((count, sent), F32),
            pltpu.VMEM((groups, packed, LANES), BF),
            picked,
            dma((7 + groups,)),
        ],
        2 * count * model_width * sent,
        2 * (count * model_width + model_width * sent),
    )(page_table, hidden, norm_gain, qkv_weight.T, adapter_down)
    arrived = exchange(outgoing, "group")

    after_out, after_up, after_vocab, after_adapter, _ = lax.optimization_barrier(
        (out_weight, adapter_up, vocab_rows, request_adapter, outgoing)
    )
    w_t, up_t = after_out.T, after_up.T
    some_vocab = ring_rows(after_vocab, "mp")
    request_slot = jnp.sum(jnp.where(after_adapter[:, None] == adapter_ids[None, :], adapter_slot[None, :], 0), axis=1)
    slots = jnp.sum(jnp.where(segrow == request_ids[:, None], request_slot[:, None], 0), axis=0, keepdims=True)
    slotrow = slots - own_shard * (low // RANK)
    arrived, some_vocab, slotrow, w_t, up_t = lax.optimization_barrier((arrived, some_vocab, slotrow, w_t, up_t))

    ordered, ordered_t, state, nd = kernel_call(
        functools.partial(group_kernel, dims, low, heads),
        (
            shape((count, qkv_cols), BF),
            shape((sent, count), BF),
            shape((heads, PHI_PAD, LANES), BF),
            shape((heads, LANES, count), F32),
        ),
        [SMEM, ANY] + [VMEM] * 4,
        (ANY, ANY, VMEM, ANY),
        [
            pltpu.VMEM((groups, packed, LANES), BF),
            pltpu.VMEM((count, sent), F32),
            pltpu.VMEM((count, sent), F32),
            pltpu.VMEM((count, qkv_cols), BF),
            pltpu.VMEM((sent, count), BF),
            pltpu.VMEM((heads, LANES, count), F32),
            pltpu.VMEM((count, count), F32),
            pltpu.SMEM((groups,), jnp.int32),
            dma((max(groups, 2 + heads),)),
        ],
        heads * 2 * count * count * 512,
        6 * count * sent,
    )(page_table, arrived, segrow, left, right, cols)
    later_hidden, some_vocab, state = lax.optimization_barrier((hidden, some_vocab, state))
    state = lax.ppermute(state, "group", [(i, i + 1) for i in range(groups - 1)])
    [beside] = staged_call(
        functools.partial(side_kernel, dims, shards),
        [shape((groups, aside, LANES), BF)],
        [page_table],
        [later_hidden, some_vocab, out_weight, adapter_up],
        [pltpu.VMEM((count, width), F32), pltpu.VMEM((some, inner + low + width), F32), picked],
        2 * some * model_width * (inner + low),
        2 * count * model_width,
    )
    state, beside = lax.optimization_barrier((state, beside))

    far = far_offsets(shards)
    part = shape((width, count), BF)
    w_buffers = [pltpu.VMEM((model_width, inner), BF), pltpu.VMEM((model_width, low), BF)]
    *far_terms, inputs = kernel_call(
        functools.partial(finish_kernel, low, heads, shards),
        [part] * (len(far) - 1) + [shape((inner + low, count), BF)],
        [ANY] * 2 + [VMEM] * 6 + [ANY] * 2,
        [ANY] * len(far),
        [
            pltpu.VMEM((heads, FEAT, count), BF),
            pltpu.VMEM((heads, LANES, count), F32),
            *w_buffers,
            pltpu.VMEM((inner + low, count), BF),
            pltpu.VMEM((len(far), width, count), BF),
            dma((len(far) + heads + 6,)),
        ],
        count * (inner + low) * model_width,
        2 * count * model_width,
    )(ordered_t, nd, state, segrow, slotrow, left, right, cols, w_t, up_t)
    near_terms = kernel_call(
        functools.partial(near_kernel, shards),
        [part] * len(NEAR),
        [ANY] * 3,
        [ANY] * len(NEAR),
        [
            *w_buffers,
            pltpu.VMEM((inner + low, count), BF),
            pltpu.VMEM((len(NEAR), width, count), BF),
            dma((len(NEAR) + 3,)),
        ],
        count * (inner + low) * model_width,
        2 * count * model_width,
    )(w_t, up_t, inputs)
    terms = dict(zip(NEAR, near_terms)) | dict(zip(far, [far_terms[0], *far_terms]))
    update = line_sums(terms, "mp")

    beside, inputs = lax.optimization_barrier((beside, inputs))
    beside = exchange(beside, "group")
    [logits] = staged_call(
        functools.partial(logits_kernel, dims, shards, width),
        [shape((shards, scored, count // shards), BF)],
        [page_table],
        [inputs],
        [
            pltpu.VMEM((scored, inner + low + width), BF),
            pltpu.VMEM((inner + low + width, count), BF),
            pltpu.VMEM((count, width), F32),
            pltpu.VMEM((count, width), F32),
            pltpu.SMEM((groups,), jnp.int32),
        ],
        2 * count * scored * (inner + low + width),
        4 * count * scored,
        given=[beside],
    )
    logits = exchange(logits, "mp")
    [state_norms] = staged_call(
        functools.partial(norms_kernel, low, heads),
        [shape((heads, count), F32)],
        [],
        [ordered, ordered_t, state, segrow, left, right, cols],
        [pltpu.VMEM((count, count), F32)],
        heads * 2 * count * count * 256,
        2 * sent * count,
    )
    best = kernel_call(
        functools.partial(best_kernel, shards),
        shape((1, count // shards), F32),
        [VMEM],
        VMEM,
        [],
        count * scored,
        2 * count * scored,
    )(logits)
    return update.T, state_norms, best.reshape(-1)


def solution(mesh):
    placed = (
        P("group", None),
        P(),
        P(None, "mp"),
        P("mp", None),
        P(None, "mp"),
        P("mp", None),
        P(("group", "mp"), None),
        P("group"),
        P(),
        P(),
        P(),
    )
    return jax.shard_map(
        on_device,
        mesh=mesh,
        in_specs=placed,
        out_specs=(P("group", "mp"), P("mp", "group"), P(("group", "mp"))),
        check_vma=False,
    )
```

```python
import functools

import jax
import jax.numpy as jnp
import numpy as np
from jax import lax
from jax.experimental import pallas as pl
from jax.experimental.pallas import tpu as pltpu
from jax.sharding import PartitionSpec as P

FEAT = 16
HD = 112
RANK = 16
EPSILON = 1e-05
HEAD = 2 * FEAT + HD
PHI = 1 + FEAT + FEAT * (FEAT + 1) // 2
PHI_PAD = 160
LANES = 128
ONE, TAG, REST = HD, HD + 1, HD + 2
NEAR = (0, 1, -1)
MIB = 1024 * 1024
VMEM_LIMIT = 60 * MIB

BF = jnp.bfloat16
F32 = jnp.float32
SMEM = pl.BlockSpec(memory_space=pltpu.SMEM)
VMEM = pl.BlockSpec(memory_space=pltpu.VMEM)
ANY = pl.BlockSpec(memory_space=pltpu.HBM)


def feature_tables():
    left = np.zeros((PHI_PAD, FEAT), np.float32)
    right = np.zeros((PHI_PAD, FEAT), np.float32)
    cols = np.zeros((PHI_PAD, 8), np.float32)
    cols[0, :3] = 1.0
    at = 1
    for i in range(FEAT):
        left[at, i] = 1.0
        cols[at, 1] = 1.0
        cols[at, 2] = FEAT**-0.25
        at += 1
    for i in range(FEAT):
        for j in range(i, FEAT):
            left[at, i] = 1.0
            right[at, j] = 1.0
            cols[at, 2] = (1.0 if i == j else 2.0**0.5) / (2.0 * FEAT) ** 0.5
            at += 1
    return left.astype(jnp.bfloat16), right.astype(jnp.bfloat16), cols


def dot(a, b, dims=((1,), (0,))):
    return lax.dot_general(a, b, (dims, ((), ())), preferred_element_type=F32)


def kernel_call(body, out_shape, in_specs, out_specs, scratch, flops, nbytes, limit=VMEM_LIMIT):
    return pl.pallas_call(
        body,
        out_shape=out_shape,
        in_specs=in_specs,
        out_specs=out_specs,
        scratch_shapes=scratch,
        compiler_params=pltpu.CompilerParams(vmem_limit_bytes=limit),
        cost_estimate=pl.CostEstimate(flops=flops, bytes_accessed=nbytes, transcendentals=0),
    )


def start(source, target, sem):
    copy = pltpu.make_async_copy(source, target, sem)
    copy.start()
    return copy


def packing(rows, columns):
    tiles, rest = divmod(columns, LANES)
    share = LANES // rest if rest and LANES % rest == 0 else 1
    if rows % (16 * share):
        share = 1
    return tiles, rest, share, tiles * rows + (rows // share if rest else 0)


def pack(block, target, base):
    rows = block.shape[0]
    tiles, rest, share, _ = packing(*block.shape)
    for t in range(tiles):
        target[base + t * rows : base + (t + 1) * rows, :] = block[:, t * LANES : (t + 1) * LANES].astype(BF)
    if rest:
        short = rows // share
        last = [block[q * short : (q + 1) * short, tiles * LANES :] for q in range(share)]
        if share * rest < LANES:
            last.append(jnp.zeros((short, LANES - share * rest), block.dtype))
        at = base + tiles * rows
        target[at : at + short, :] = jnp.concatenate(last, axis=1).astype(BF)


def unpack(source, base, target, row, rows, columns):
    tiles, rest, share, _ = packing(rows, columns)
    for t in range(tiles):
        piece = source[base + t * rows : base + (t + 1) * rows, :]
        target[row : row + rows, t * LANES : (t + 1) * LANES] = piece.astype(target.dtype)
    if rest:
        short = rows // share
        at = base + tiles * rows
        last = source[at : at + short, :].astype(F32)
        for q in range(share):
            piece = last[:, q * rest : (q + 1) * rest].astype(target.dtype)
            target[row + q * short : row + (q + 1) * short, tiles * LANES : columns] = piece


def staged_call(body, out_shape, scalars, operands, scratch, flops, nbytes, given=(), limit=VMEM_LIMIT):
    buffers = [pltpu.VMEM(x.shape, x.dtype) for x in list(operands) + list(out_shape)]
    ins, outs = len(operands), len(out_shape)

    def run(*refs):
        values, refs = refs[: len(scalars)], refs[len(scalars) :]
        ready, refs = refs[: len(given)], refs[len(given) :]
        far, refs = refs[: ins + outs], refs[ins + outs :]
        near, extra, sems = refs[: ins + outs], refs[ins + outs : -1], refs[-1]
        loads = [start(far[k], near[k], sems.at[k]) for k in range(ins)]
        for load in loads:
            load.wait()
        body(*values, *ready, *near, *extra)
        sends = [start(near[k], far[k], sems.at[k]) for k in range(ins, ins + outs)]
        for send in sends:
            send.wait()

    return kernel_call(
        run,
        [pltpu.HBM(x.shape, x.dtype) for x in out_shape],
        [SMEM] * len(scalars) + [VMEM] * len(given) + [ANY] * ins,
        [ANY] * outs,
        buffers + list(scratch) + [pltpu.SemaphoreType.DMA((ins + outs,))],
        flops,
        nbytes,
        limit,
    )(*scalars, *given, *operands)


def pick_pages(table, own, picked, groups, per_group, per_peer):
    def one_group(g, carry):
        spot = g * per_peer
        for k in range(per_group):
            local = table[g * per_group + k] - own * per_group
            picked[spot] = local
            spot = spot + jnp.where((local >= 0) & (local < per_group), 1, 0)
        return carry

    lax.fori_loop(0, groups, one_group, 0)


def place_pages(table, own, seen, source, target, groups, per_group, per_peer, page_len):
    for g in range(groups):
        seen[g] = 0
    for k in range(per_group):
        holder = lax.div(table[own * per_group + k], per_group)
        slot = holder * per_peer + seen[holder]
        seen[holder] = seen[holder] + 1
        start = pl.multiple_of(slot * page_len, page_len)
        target[k * page_len : (k + 1) * page_len, :] = source[pl.ds(start, page_len), :]


def picked_rows(source, picked, g, per_peer, page_len):
    pages = []
    for b in range(per_peer):
        at = pl.multiple_of(picked[g * per_peer + b] * page_len, page_len)
        pages.append(source[pl.ds(at, page_len), :])
    return jnp.concatenate(pages, axis=0)


def project_kernel(
    dims, table, hidden_in, gain, wq_in, wd_in, out_in, hidden, wq, wd, normed, wide, out, picked, sems
):
    groups, per_group, per_peer, page_len = dims
    rows, model_width = hidden.shape
    low = wd.shape[1]
    pieces = 4
    part = rows // pieces
    strip = wq.shape[0] // 2
    loads = [
        start(hidden_in.at[pl.ds(k * part, part)], hidden.at[pl.ds(k * part, part)], sems.at[k]) for k in range(pieces)
    ]
    weights = [start(wd_in, wd, sems.at[pieces])]
    for k in range(2):
        half = pl.ds(k * strip, strip)
        weights.append(start(wq_in.at[half], wq.at[half], sems.at[pieces + 1 + k]))
    pick_pages(table, lax.axis_index("group"), picked, groups, per_group, per_peer)
    step = 32
    scale = gain[...].reshape(1, model_width)

    def norm_rows(i, carry):
        at = pl.ds(pl.multiple_of(i * step, step), step)
        x = hidden[at, :].astype(F32)
        meansq = jnp.mean(x * x, axis=-1, keepdims=True)
        normed[at, :] = (x * lax.rsqrt(meansq + EPSILON) * scale).astype(BF)
        return carry

    for k in range(pieces):
        loads[k].wait()
        lax.fori_loop(k * part // step, (k + 1) * part // step, norm_rows, 0, unroll=2)
    for load in weights:
        load.wait()
    wide[:, :low] = dot(normed[...], wd[...])
    wide[:, low:] = dot(normed[...], wq[...], ((1,), (1,)))
    sends = []
    for g in range(groups):
        pack(picked_rows(wide, picked, g, per_peer, page_len), out.at[g], 0)
        sends.append(start(out.at[g], out_in.at[g], sems.at[pieces + 3 + g]))
    for send in sends:
        send.wait()


def side_kernel(
    dims, shards, table, hidden_in, vocab_in, w_out_in, w_up_in, out_in,
    window, vocab, w_out, w_up, wide, products, shared, pages, picked, sems
):
    groups, per_group, per_peer, page_len = dims
    model_width = hidden_in.shape[1]
    width = model_width // shards
    inner, low = w_out.shape[0], w_up.shape[0]
    held = vocab.shape[0] // shards
    own_shard = lax.axis_index("mp")
    last = model_width - window.shape[1]
    first = jnp.minimum(lax.div(own_shard * width, LANES) * LANES, last)
    loads = [start(vocab_in, vocab, sems.at[0]), start(w_out_in, w_out, sems.at[1]), start(w_up_in, w_up, sems.at[2])]
    columns = pl.ds(pl.multiple_of(first, LANES), window.shape[1])
    load = start(hidden_in.at[:, columns], window, sems.at[3])
    pick_pages(table, lax.axis_index("group"), picked, groups, per_group, per_peer)
    load.wait()
    loads[0].wait()
    for j in range(shards):

        @pl.when(own_shard == j)
        def _(j=j):
            at = j * width - min(j * width // LANES * LANES, last)
            wide[...] = window[:, at : at + width].astype(F32)
            products[:, inner + low :] = vocab[:, j * width : (j + 1) * width].astype(F32)

    base = shared.shape[0]
    sends = []
    for g in range(groups):
        pack(picked_rows(wide, picked, g, per_peer, page_len), pages.at[g], 0)
        sends.append(start(pages.at[g], out_in.at[g, pl.ds(base, pages.shape[1])], sems.at[4 + g]))
    for load in loads[1:]:
        load.wait()
    products[:, :inner] = dot(vocab[...], w_out[...], ((1,), (1,)))
    products[:, inner : inner + low] = dot(vocab[...], w_up[...], ((1,), (1,)))
    ordered = []
    for j in range(shards):
        at = lax.rem(j - own_shard + 2 * shards - 1, shards) * held
        ordered.append(products[pl.ds(pl.multiple_of(at, held), held), :])
    pack(jnp.concatenate(ordered, axis=0), shared, 0)
    for g in range(groups):
        sends.append(start(shared, out_in.at[g, pl.ds(0, base)], sems.at[4 + groups + g]))
    for send in sends:
        send.wait()


def phi_of(vectors, left, right, cols):
    first = dot(left[...], vectors) + cols[:, 0:1]
    second = dot(right[...], vectors) + cols[:, 1:2]
    return first * second * cols[:, 2:3]


def with_ones(values):
    lane = lax.broadcasted_iota(jnp.int32, (values.shape[0], LANES - HD), 1)
    return jnp.concatenate([values, jnp.where(lane == 0, 1.0, 0.0).astype(values.dtype)], axis=1)


def with_ones_t(values):
    row = lax.broadcasted_iota(jnp.int32, (LANES - HD, values.shape[1]), 0)
    return jnp.concatenate([values, jnp.where(row == 0, 1.0, 0.0).astype(values.dtype)], axis=0)


def same_upto(segrow):
    count = segrow.shape[1]
    ids = segrow[...].astype(F32)
    column = jnp.transpose(jnp.broadcast_to(ids, (8, count)))[:, 0:1]
    behind = lax.broadcasted_iota(jnp.int32, (count, count), 0)
    ahead = lax.broadcasted_iota(jnp.int32, (count, count), 1)
    return jnp.where((column == ids) & (behind <= ahead), 1.0, 0.0)


def group_kernel(
    dims, low, heads, table, arrived, segrow, left, right, cols, ordered_in, ordered_t_in, state, nd_in,
    wide, placed, ordered, ordered_t, nd, mask, seen, sems
):
    groups, per_group, per_peer, page_len = dims
    tall = per_peer * page_len
    count, sent = placed.shape
    mask[...] = same_upto(segrow)
    for g in range(groups):
        unpack(arrived.at[g], 0, wide, g * tall, tall, sent)
    place_pages(table, lax.axis_index("group"), seen, wide, placed, groups, per_group, per_peer, page_len)
    ordered[...] = placed[:, low:].astype(BF)
    for at in range(0, sent, LANES):
        end = min(at + LANES, sent)
        ordered_t[at:end, :] = jnp.transpose(placed[:, at:end]).astype(BF)
    sends = [start(ordered_t, ordered_t_in, sems.at[0]), start(ordered, ordered_in, sems.at[1])]

    last = segrow[:, count - 1 : count]
    member = jnp.where(segrow[...] == last, 1.0, 0.0)
    total = jnp.sum(member, axis=1, keepdims=True)
    fine = total - total.astype(BF).astype(F32)
    tag = last.astype(F32) + 1.0
    row = lax.broadcasted_iota(jnp.int32, (PHI_PAD, LANES), 0)
    lane = lax.broadcasted_iota(jnp.int32, (PHI_PAD, LANES), 1)
    block = 256 if count % 256 == 0 else count
    for h in range(heads):
        at = h * HEAD
        key = ordered[:, at + FEAT : at + 2 * FEAT] * BF(0.25)
        value = ordered[:, at + 2 * FEAT : at + HEAD]
        at = low + h * HEAD
        query_t = ordered_t[at : at + FEAT, :]
        key_t = ordered_t[at + FEAT : at + 2 * FEAT, :]
        extended_t = with_ones_t(ordered_t[at + 2 * FEAT : at + HEAD, :])

        phi = (phi_of(key_t, left, right, cols) * member).astype(BF)
        summed = dot(phi, with_ones(value))
        summed = jnp.where((row == 0) & (lane == TAG), tag, summed)
        summed = jnp.where((row == 0) & (lane == REST), fine, summed)
        state[h] = summed.astype(BF)

        for begin in range(0, count, block):
            end = begin + block
            s = dot(key[:end], query_t[:, begin:end])
            w = (1.0 + s * (1.0 + 0.5 * s)) * mask[:end, begin:end]
            nd[h, :, begin:end] = dot(extended_t[:, :end], w.astype(BF))
        sends.append(start(nd.at[h], nd_in.at[h], sems.at[2 + h]))
    for send in sends:
        send.wait()


def split3(x):
    a = x.astype(BF)
    rest = x - a.astype(F32)
    b = rest.astype(BF)
    return jnp.concatenate([a, b, (rest - b.astype(F32)).astype(BF)], axis=0)


def state_corner(state):
    corner = state[0, 0:1, :].astype(F32)
    return corner[:, TAG : TAG + 1], corner[:, ONE : ONE + 1] + corner[:, REST : REST + 1]


def far_weights(offsets, own_shard, shards, sources, targets, sems):
    width = sources[0].shape[0] // shards
    copies = []
    for k, offset in enumerate(offsets):
        j = own_shard + offset
        rows = pl.ds(pl.multiple_of(jnp.clip(j, 0, shards - 1) * width, width), width)
        pairs = [(source.at[rows], target.at[rows]) for source, target in zip(sources, targets)]
        copies.append([pltpu.make_async_copy(*pair, sems.at[2 * k + i]) for i, pair in enumerate(pairs)])

        @pl.when((j >= 0) & (j < shards))
        def _(k=k):
            for copy in copies[k]:
                copy.start()

    return copies


def shard_parts(offsets, own_shard, shards, w_t, up_t, inputs, held_out, outs, sems, copies=None):
    width = w_t.shape[0] // shards
    inner = w_t.shape[1]
    pending = []
    for k, offset in enumerate(offsets):
        j = own_shard + offset
        there = (j >= 0) & (j < shards)

        @pl.when(there)
        def _(j=j, k=k):
            for copy in copies[k] if copies else ():
                copy.wait()
            rows = pl.ds(pl.multiple_of(j * width, width), width)
            part = dot(w_t[rows, :], inputs[:inner, :]) + dot(up_t[rows, :], inputs[inner:, :])
            held_out[k] = part.astype(BF)
            start(held_out.at[k], outs[k], sems.at[k])

        pending.append((there, k))

    def finish():
        for there, k in pending:

            @pl.when(there)
            def _(k=k):
                pltpu.make_async_copy(held_out.at[k], outs[k], sems.at[k]).wait()

    return finish


def finish_kernel(
    low, heads, shards, ordered_t_in, nd_in, state, segrow, slotrow, left, right, cols, w_t_in, up_t_in, *refs
):
    far = far_offsets(shards)
    outs = refs[: len(far) - 1]
    outs = [outs[0], *outs]
    inputs_in, queries, nd, w_t, up_t, inputs, held_out, sems, weight_sems = refs[len(far) - 1 :]
    inner = heads * HD
    sem = iter(range(len(far), len(far) + heads + 6))
    fetches = []
    for h in range(heads):
        rows = pl.ds(low + h * HEAD, FEAT)
        fetches.append(start(ordered_t_in.at[rows], queries.at[h], sems.at[next(sem)]))
    fetches.append(start(nd_in, nd, sems.at[next(sem)]))
    fetches.append(start(ordered_t_in.at[pl.ds(0, low)], inputs.at[pl.ds(inner, low)], sems.at[next(sem)]))
    own_shard = lax.axis_index("mp")
    copies = far_weights(far, own_shard, shards, (w_t_in, up_t_in), (w_t, up_t), weight_sems)
    for fetch in fetches:
        fetch.wait()
    tag, _ = state_corner(state)
    carried = jnp.where(segrow[...].astype(F32) + 1.0 == tag, 1.0, 0.0)
    row_slot = lax.div(lax.broadcasted_iota(jnp.int32, (low, 1), 0), RANK)
    lowered = jnp.where(slotrow[...] == row_slot, inputs[inner:, :].astype(F32), 0.0)
    inputs[inner:, :] = lowered.astype(BF)
    for h in range(heads):
        cross = dot(state[h], phi_of(queries[h], left, right, cols).astype(BF), ((0,), (0,)))
        both = nd[h] + carried * cross
        inputs[h * HD : (h + 1) * HD, :] = (both[:HD, :] / both[ONE : ONE + 1, :]).astype(BF)
    finish = shard_parts(far, own_shard, shards, w_t, up_t, inputs, held_out, outs, sems, copies)
    kept = start(inputs, inputs_in, sems.at[next(sem)])
    finish()
    kept.wait()


def far_offsets(shards):
    far = [shards - 1, 1 - shards]
    for distance in range(shards - 2, 1, -1):
        far += [distance, -distance]
    return far


def near_kernel(shards, w_t_in, up_t_in, inputs_in, *refs):
    outs = refs[: len(NEAR)]
    w_t, up_t, inputs, held_out, sems = refs[len(NEAR) :]
    loads = [
        start(source, target, sems.at[len(NEAR) + k])
        for k, (source, target) in enumerate([(w_t_in, w_t), (up_t_in, up_t), (inputs_in, inputs)])
    ]
    for load in loads:
        load.wait()
    shard_parts(NEAR, lax.axis_index("mp"), shards, w_t, up_t, inputs, held_out, outs, sems)()


def logits_kernel(dims, shards, width, table, arrived, inputs, out, vocab, both, wide, placed, seen):
    groups, per_group, per_peer, page_len = dims
    tall = per_peer * page_len
    inner = inputs.shape[0]
    rows = vocab.shape[0] // groups
    _, _, _, base = packing(rows, inner + width)
    for g in range(groups):
        unpack(arrived.at[g], 0, vocab, g * rows, rows, inner + width)
        unpack(arrived.at[g], base, wide, g * tall, tall, width)
    place_pages(table, lax.axis_index("group"), seen, wide, placed, groups, per_group, per_peer, page_len)
    both[:inner, :] = inputs[...]
    both[inner:, :] = jnp.transpose(placed[...]).astype(BF)
    block = inputs.shape[1] // shards
    scored = dot(vocab[...], both[...])
    for j in range(shards):
        out[j] = scored[:, j * block : (j + 1) * block].astype(BF)


def norms_kernel(low, heads, ordered, ordered_t, state, segrow, left, right, cols, norms, mask):
    count = segrow.shape[1]
    mask[...] = same_upto(segrow)
    upto = mask[...].astype(BF)
    tag, held = state_corner(state)
    carried = jnp.where(segrow[...].astype(F32) + 1.0 == tag, 1.0, 0.0)
    value_lane = lax.broadcasted_iota(jnp.int32, (1, LANES), 1) < HD
    counted = carried * held + jnp.sum(mask[...], axis=0, keepdims=True)
    block = 256 if count % 256 == 0 else count
    increments = []
    before = []
    for h in range(heads):
        at = h * HEAD
        key = ordered[:, at + FEAT : at + 2 * FEAT] * BF(0.25)
        value = ordered[:, at + 2 * FEAT : at + HEAD]
        at = low + h * HEAD
        key_t = ordered_t[at + FEAT : at + 2 * FEAT, :]
        value_t = ordered_t[at + 2 * FEAT : at + HEAD, :]
        wide_key = key_t.astype(F32)
        wide_value = value_t.astype(F32)
        self_score = 0.25 * jnp.sum(wide_key * wide_key, axis=0, keepdims=True)
        self_value = jnp.sum(wide_value * wide_value, axis=0, keepdims=True)
        diagonal = (1.0 + self_score * (1.0 + 0.5 * self_score)) * self_value
        below = []
        for begin in range(0, count, block):
            end = begin + block
            kk = dot(key[:end], key_t[:, begin:end])
            vv = dot(value[:end], value_t[:, begin:end])
            gram = (1.0 + kk * (1.0 + 0.5 * kk)) * vv * mask[:end, begin:end]
            below.append(jnp.sum(gram, axis=0, keepdims=True))
        added = 2.0 * jnp.concatenate(below, axis=1) - diagonal
        held_state = state[h]
        against = dot(held_state, phi_of(key_t, left, right, cols).astype(BF), ((0,), (0,)))[:HD, :]
        along = jnp.sum(against * wide_value, axis=0, keepdims=True)
        increments.append(added + 2.0 * carried * along)
        wide_state = jnp.where(value_lane, held_state.astype(F32), 0.0)
        per_lane = jnp.sum(wide_state * wide_state, axis=0, keepdims=True)
        before.append(jnp.sum(per_lane, axis=1, keepdims=True))
    if heads % 8:
        increments.append(jnp.zeros((8 - heads % 8, count), F32))
    stacked = split3(jnp.concatenate(increments, axis=0))
    thrice = dot(stacked, upto)
    rows = thrice.shape[0] // 3
    summed = thrice[:rows] + thrice[rows : 2 * rows] + thrice[2 * rows :]
    for h in range(heads):
        total = carried * before[h] + summed[h : h + 1, :]
        norms[h : h + 1, :] = jnp.sqrt(total / (counted * float(FEAT * HD)))


def best_kernel(shards, pieces, best):
    whole = pieces[0].astype(F32)
    for i in range(1, shards):
        whole = whole + pieces[i].astype(F32)
    best[...] = jnp.max(whole, axis=0, keepdims=True)


def exchange(blocks, axis):
    return lax.all_to_all(blocks, axis, split_axis=0, concat_axis=0, tiled=True)


def ring_rows(values, axis):
    size = lax.axis_size(axis)
    steps = [lax.ppermute(values, axis, [(i, (i + by) % size) for i in range(size)]) for by in range(size - 1, 0, -1)]
    return jnp.concatenate([*steps, values], axis=0)


def line_sums(terms, axis, beside):
    size = lax.axis_size(axis)

    def joined(*parts):
        return sum(part.astype(F32) for part in parts).astype(BF)

    def up(values, first, last):
        return lax.ppermute(values, axis, [(i, i + 1) for i in range(first, last)])

    def down(values, first, last):
        return lax.ppermute(values, axis, [(i, i - 1) for i in range(first, last)])

    if size == 4:
        relayed_up = up(terms[2], 0, size - 2)
        relayed_down = down(terms[-2], 2, size)
        far = lax.ppermute(terms[3], axis, [(0, 3), (3, 0)])
        to_up, to_down = joined(terms[1], relayed_up), joined(terms[-1], relayed_down)
        to_up, to_down, beside = lax.optimization_barrier((to_up, to_down, beside))
        near_up = up(to_up, 0, size - 1)
        near_down = down(to_down, 1, size)
        return joined(terms[0], far, near_up, near_down), beside
    going_up = going_down = None
    for step in range(1, size):
        to_up = terms[size - step]
        to_down = terms[step - size]
        if step > 1:
            to_up = joined(to_up, going_up)
            to_down = joined(to_down, going_down)
        going_up = up(to_up, 0, step)
        going_down = down(to_down, size - step, size)
    return joined(terms[0], going_up, going_down), beside


def on_device(
    hidden,
    norm_gain,
    qkv_weight,
    out_weight,
    adapter_down,
    adapter_up,
    vocab_rows,
    segments,
    request_adapter,
    adapter_slot,
    page_table,
):
    groups = lax.axis_size("group")
    shards = lax.axis_size("mp")
    own_shard = lax.axis_index("mp")
    count, model_width = hidden.shape
    per_group = page_table.shape[0] // groups
    per_peer = per_group // groups
    page_len = count // per_group
    dims = (groups, per_group, per_peer, page_len)
    qkv_cols = qkv_weight.shape[1]
    heads = qkv_cols // HEAD
    low = adapter_down.shape[1]
    inner = heads * HD
    width = model_width // shards
    sent = low + qkv_cols
    tall = per_peer * page_len
    packed = packing(tall, sent)[-1]
    some = shards * vocab_rows.shape[0]
    scored = groups * some
    aside = packing(some, inner + low + width)[-1] + packing(tall, width)[-1]
    shape = jax.ShapeDtypeStruct
    dma = pltpu.SemaphoreType.DMA
    picked = pltpu.SMEM((groups * per_peer + 1,), jnp.int32)

    left, right, cols = [jnp.asarray(t) for t in feature_tables()]
    segrow = segments.reshape(1, count)
    request_ids = jnp.arange(request_adapter.shape[0], dtype=jnp.int32)
    adapter_ids = jnp.arange(adapter_slot.shape[0], dtype=jnp.int32)

    outgoing = kernel_call(
        functools.partial(project_kernel, dims),
        pltpu.HBM((groups, packed, LANES), BF),
        [SMEM, ANY, VMEM, ANY, ANY],
        ANY,
        [
            pltpu.VMEM((count, model_width), BF),
            pltpu.VMEM((qkv_cols, model_width), BF),
            pltpu.VMEM((model_width, low), BF),
            pltpu.VMEM((count, model_width), BF),
            pltpu.VMEM((count, sent), F32),
            pltpu.VMEM((groups, packed, LANES), BF),
            picked,
            dma((7 + groups,)),
        ],
        2 * count * model_width * sent,
        2 * (count * model_width + model_width * sent),
    )(page_table, hidden, norm_gain, qkv_weight.T, adapter_down)
    arrived = exchange(outgoing, "group")

    after_out, after_up, after_vocab, after_adapter, _ = lax.optimization_barrier(
        (out_weight, adapter_up, vocab_rows, request_adapter, outgoing)
    )
    w_t, up_t = after_out.T, after_up.T
    some_vocab = ring_rows(after_vocab, "mp")
    request_slot = jnp.sum(jnp.where(after_adapter[:, None] == adapter_ids[None, :], adapter_slot[None, :], 0), axis=1)
    slots = jnp.sum(jnp.where(segrow == request_ids[:, None], request_slot[:, None], 0), axis=0, keepdims=True)
    slotrow = slots - own_shard * (low // RANK)
    arrived, some_vocab, slotrow, w_t, up_t = lax.optimization_barrier((arrived, some_vocab, slotrow, w_t, up_t))

    ordered, ordered_t, state, nd = kernel_call(
        functools.partial(group_kernel, dims, low, heads),
        (
            pltpu.HBM((count, qkv_cols), BF),
            pltpu.HBM((sent, count), BF),
            shape((heads, PHI_PAD, LANES), BF),
            pltpu.HBM((heads, LANES, count), F32),
        ),
        [SMEM] + [VMEM] * 5,
        (ANY, ANY, VMEM, ANY),
        [
            pltpu.VMEM((count, sent), F32),
            pltpu.VMEM((count, sent), F32),
            pltpu.VMEM((count, qkv_cols), BF),
            pltpu.VMEM((sent, count), BF),
            pltpu.VMEM((heads, LANES, count), F32),
            pltpu.VMEM((count, count), F32),
            pltpu.SMEM((groups,), jnp.int32),
            dma((2 + heads,)),
        ],
        heads * 2 * count * count * 512,
        6 * count * sent,
        56 * MIB,
    )(page_table, arrived, segrow, left, right, cols)
    later_hidden, some_vocab, state = lax.optimization_barrier((hidden, some_vocab, state))
    state = lax.ppermute(state, "group", [(i, i + 1) for i in range(groups - 1)])
    window = max(-(-(j * width % LANES + width) // LANES) * LANES for j in range(shards))
    beside = kernel_call(
        functools.partial(side_kernel, dims, shards),
        pltpu.HBM((groups, aside, LANES), BF),
        [SMEM] + [ANY] * 4,
        ANY,
        [
            pltpu.VMEM((count, window), BF),
            pltpu.VMEM((some, model_width), BF),
            pltpu.VMEM((inner, model_width), BF),
            pltpu.VMEM((low, model_width), BF),
            pltpu.VMEM((count, width), F32),
            pltpu.VMEM((some, inner + low + width), F32),
            pltpu.VMEM((packing(some, inner + low + width)[-1], LANES), BF),
            pltpu.VMEM((groups, packing(tall, width)[-1], LANES), BF),
            picked,
            dma((4 + 2 * groups,)),
        ],
        2 * some * model_width * (inner + low),
        2 * count * model_width,
    )(page_table, later_hidden, some_vocab, out_weight, adapter_up)
    state, beside = lax.optimization_barrier((state, beside))

    far = far_offsets(shards)
    part = pltpu.HBM((width, count), BF)
    w_buffers = [pltpu.VMEM((model_width, inner), BF), pltpu.VMEM((model_width, low), BF)]
    *far_terms, inputs = kernel_call(
        functools.partial(finish_kernel, low, heads, shards),
        [part] * (len(far) - 1) + [pltpu.HBM((inner + low, count), BF)],
        [ANY] * 2 + [VMEM] * 6 + [ANY] * 2,
        [ANY] * len(far),
        [
            pltpu.VMEM((heads, FEAT, count), BF),
            pltpu.VMEM((heads, LANES, count), F32),
            *w_buffers,
            pltpu.VMEM((inner + low, count), BF),
            pltpu.VMEM((len(far), width, count), BF),
            dma((len(far) + heads + 6,)),
            dma((2 * len(far),)),
        ],
        count * (inner + low) * model_width,
        2 * count * model_width,
    )(ordered_t, nd, state, segrow, slotrow, left, right, cols, w_t, up_t)
    near_terms = kernel_call(
        functools.partial(near_kernel, shards),
        [part] * len(NEAR),
        [ANY] * 3,
        [ANY] * len(NEAR),
        [
            *w_buffers,
            pltpu.VMEM((inner + low, count), BF),
            pltpu.VMEM((len(NEAR), width, count), BF),
            dma((len(NEAR) + 3,)),
        ],
        1,
        1,
    )(w_t, up_t, inputs)
    terms = dict(zip(NEAR, near_terms)) | dict(zip(far, [far_terms[0], *far_terms]))
    beside, inputs = lax.optimization_barrier((beside, inputs))
    update, beside = line_sums(terms, "mp", exchange(beside, "group"))
    [logits] = staged_call(
        functools.partial(logits_kernel, dims, shards, width),
        [shape((shards, scored, count // shards), BF)],
        [page_table],
        [inputs],
        [
            pltpu.VMEM((scored, inner + low + width), BF),
            pltpu.VMEM((inner + low + width, count), BF),
            pltpu.VMEM((count, width), F32),
            pltpu.VMEM((count, width), F32),
            pltpu.SMEM((groups,), jnp.int32),
        ],
        1,
        1,
        given=[beside],
        limit=56 * MIB,
    )
    logits = exchange(logits, "mp")
    [state_norms] = staged_call(
        functools.partial(norms_kernel, low, heads),
        [shape((heads, count), F32)],
        [],
        [ordered, ordered_t, state, segrow, left, right, cols],
        [pltpu.VMEM((count, count), F32)],
        1,
        1,
    )
    best = kernel_call(
        functools.partial(best_kernel, shards),
        shape((1, count // shards), F32),
        [VMEM],
        VMEM,
        [],
        1,
        1,
        32 * MIB,
    )(logits)
    return update.T, state_norms, best.reshape(-1)


def solution(mesh):
    placed = (
        P("group", None),
        P(),
        P(None, "mp"),
        P("mp", None),
        P(None, "mp"),
        P("mp", None),
        P(("group", "mp"), None),
        P("group"),
        P(),
        P(),
        P(),
    )
    return jax.shard_map(
        on_device,
        mesh=mesh,
        in_specs=placed,
        out_specs=(P("group", "mp"), P("mp", "group"), P(("group", "mp"))),
        check_vma=False,
    )
```

```python
import functools

import jax
import jax.numpy as jnp
import numpy as np
from jax import lax
from jax.experimental import pallas as pl
from jax.experimental.pallas import tpu as pltpu
from jax.sharding import PartitionSpec as P

FEAT = 16
HD = 112
RANK = 16
EPSILON = 1e-05
HEAD = 2 * FEAT + HD
PHI = 1 + FEAT + FEAT * (FEAT + 1) // 2
PHI_PAD = 160
LANES = 128
ONE, TAG, REST = HD, HD + 1, HD + 2
NEAR = (0, 1, -1)
MIB = 1024 * 1024
VMEM_LIMIT = 60 * MIB

BF = jnp.bfloat16
F32 = jnp.float32
SMEM = pl.BlockSpec(memory_space=pltpu.SMEM)
VMEM = pl.BlockSpec(memory_space=pltpu.VMEM)
ANY = pl.BlockSpec(memory_space=pltpu.HBM)


def feature_tables():
    left = np.zeros((PHI_PAD, FEAT), np.float32)
    right = np.zeros((PHI_PAD, FEAT), np.float32)
    cols = np.zeros((PHI_PAD, 8), np.float32)
    cols[0, :3] = 1.0
    at = 1
    for i in range(FEAT):
        left[at, i] = 1.0
        cols[at, 1] = 1.0
        cols[at, 2] = FEAT**-0.25
        at += 1
    for i in range(FEAT):
        for j in range(i, FEAT):
            left[at, i] = 1.0
            right[at, j] = 1.0
            cols[at, 2] = (1.0 if i == j else 2.0**0.5) / (2.0 * FEAT) ** 0.5
            at += 1
    return left.astype(jnp.bfloat16), right.astype(jnp.bfloat16), cols


def dot(a, b, dims=((1,), (0,))):
    return lax.dot_general(a, b, (dims, ((), ())), preferred_element_type=F32)


def kernel_call(body, out_shape, in_specs, out_specs, scratch, flops, nbytes, limit=VMEM_LIMIT):
    return pl.pallas_call(
        body,
        out_shape=out_shape,
        in_specs=in_specs,
        out_specs=out_specs,
        scratch_shapes=scratch,
        compiler_params=pltpu.CompilerParams(vmem_limit_bytes=limit),
        cost_estimate=pl.CostEstimate(flops=flops, bytes_accessed=nbytes, transcendentals=0),
    )


def start(source, target, sem):
    copy = pltpu.make_async_copy(source, target, sem)
    copy.start()
    return copy


def packing(rows, columns):
    tiles, rest = divmod(columns, LANES)
    share = LANES // rest if rest and LANES % rest == 0 else 1
    if rows % (16 * share):
        share = 1
    return tiles, rest, share, tiles * rows + (rows // share if rest else 0)


def pack(block, target, base):
    rows = block.shape[0]
    tiles, rest, share, _ = packing(*block.shape)
    for t in range(tiles):
        target[base + t * rows : base + (t + 1) * rows, :] = block[:, t * LANES : (t + 1) * LANES].astype(BF)
    if rest:
        short = rows // share
        last = [block[q * short : (q + 1) * short, tiles * LANES :] for q in range(share)]
        if share * rest < LANES:
            last.append(jnp.zeros((short, LANES - share * rest), block.dtype))
        at = base + tiles * rows
        target[at : at + short, :] = jnp.concatenate(last, axis=1).astype(BF)


def unpack(source, base, target, row, rows, columns):
    tiles, rest, share, _ = packing(rows, columns)
    for t in range(tiles):
        piece = source[base + t * rows : base + (t + 1) * rows, :]
        target[row : row + rows, t * LANES : (t + 1) * LANES] = piece.astype(target.dtype)
    if rest:
        short = rows // share
        at = base + tiles * rows
        last = source[at : at + short, :].astype(F32)
        for q in range(share):
            piece = last[:, q * rest : (q + 1) * rest].astype(target.dtype)
            target[row + q * short : row + (q + 1) * short, tiles * LANES : columns] = piece


def staged_call(body, out_shape, scalars, operands, scratch, flops, nbytes, given=(), limit=VMEM_LIMIT):
    buffers = [pltpu.VMEM(x.shape, x.dtype) for x in list(operands) + list(out_shape)]
    ins, outs = len(operands), len(out_shape)

    def run(*refs):
        values, refs = refs[: len(scalars)], refs[len(scalars) :]
        ready, refs = refs[: len(given)], refs[len(given) :]
        far, refs = refs[: ins + outs], refs[ins + outs :]
        near, extra, sems = refs[: ins + outs], refs[ins + outs : -1], refs[-1]
        loads = [start(far[k], near[k], sems.at[k]) for k in range(ins)]
        for load in loads:
            load.wait()
        body(*values, *ready, *near, *extra)
        sends = [start(near[k], far[k], sems.at[k]) for k in range(ins, ins + outs)]
        for send in sends:
            send.wait()

    return kernel_call(
        run,
        [pltpu.HBM(x.shape, x.dtype) for x in out_shape],
        [SMEM] * len(scalars) + [VMEM] * len(given) + [ANY] * ins,
        [ANY] * outs,
        buffers + list(scratch) + [pltpu.SemaphoreType.DMA((ins + outs,))],
        flops,
        nbytes,
        limit,
    )(*scalars, *given, *operands)


def pick_pages(table, own, picked, groups, per_group, per_peer):
    def one_group(g, carry):
        spot = g * per_peer
        for k in range(per_group):
            local = table[g * per_group + k] - own * per_group
            picked[spot] = local
            spot = spot + jnp.where((local >= 0) & (local < per_group), 1, 0)
        return carry

    lax.fori_loop(0, groups, one_group, 0)


def place_pages(table, own, seen, source, target, groups, per_group, per_peer, page_len):
    for g in range(groups):
        seen[g] = 0
    for k in range(per_group):
        holder = lax.div(table[own * per_group + k], per_group)
        slot = holder * per_peer + seen[holder]
        seen[holder] = seen[holder] + 1
        start = pl.multiple_of(slot * page_len, page_len)
        target[k * page_len : (k + 1) * page_len, :] = source[pl.ds(start, page_len), :]


def picked_rows(source, picked, g, per_peer, page_len):
    pages = []
    for b in range(per_peer):
        at = pl.multiple_of(picked[g * per_peer + b] * page_len, page_len)
        pages.append(source[pl.ds(at, page_len), :])
    return jnp.concatenate(pages, axis=0)


def project_kernel(
    dims, table, hidden_in, gain, wq_in, wd_in, out_in, hidden, wq, wd, normed, wide, out, picked, sems
):
    groups, per_group, per_peer, page_len = dims
    rows, model_width = hidden.shape
    low = wd.shape[1]
    pieces = 4
    part = rows // pieces
    strip = wq.shape[0] // 2
    loads = [
        start(hidden_in.at[pl.ds(k * part, part)], hidden.at[pl.ds(k * part, part)], sems.at[k]) for k in range(pieces)
    ]
    weights = [start(wd_in, wd, sems.at[pieces])]
    for k in range(2):
        half = pl.ds(k * strip, strip)
        weights.append(start(wq_in.at[half], wq.at[half], sems.at[pieces + 1 + k]))
    pick_pages(table, lax.axis_index("group"), picked, groups, per_group, per_peer)
    step = 32
    scale = gain[...].reshape(1, model_width)

    def norm_rows(i, carry):
        at = pl.ds(pl.multiple_of(i * step, step), step)
        x = hidden[at, :].astype(F32)
        meansq = jnp.mean(x * x, axis=-1, keepdims=True)
        normed[at, :] = (x * lax.rsqrt(meansq + EPSILON) * scale).astype(BF)
        return carry

    for k in range(pieces):
        loads[k].wait()
        lax.fori_loop(k * part // step, (k + 1) * part // step, norm_rows, 0, unroll=2)
    for load in weights:
        load.wait()
    wide[:, :low] = dot(normed[...], wd[...])
    wide[:, low:] = dot(normed[...], wq[...], ((1,), (1,)))
    sends = []
    for g in range(groups):
        pack(picked_rows(wide, picked, g, per_peer, page_len), out.at[g], 0)
        sends.append(start(out.at[g], out_in.at[g], sems.at[pieces + 3 + g]))
    for send in sends:
        send.wait()


def side_kernel(
    dims, shards, table, hidden_in, vocab_in, w_out_in, w_up_in, out_in,
    window, vocab, w_out, w_up, wide, products, shared, pages, picked, sems
):
    groups, per_group, per_peer, page_len = dims
    model_width = hidden_in.shape[1]
    width = model_width // shards
    inner, low = w_out.shape[0], w_up.shape[0]
    held = vocab.shape[0] // shards
    own_shard = lax.axis_index("mp")
    last = model_width - window.shape[1]
    first = jnp.minimum(lax.div(own_shard * width, LANES) * LANES, last)
    loads = [start(vocab_in, vocab, sems.at[0]), start(w_out_in, w_out, sems.at[1]), start(w_up_in, w_up, sems.at[2])]
    columns = pl.ds(pl.multiple_of(first, LANES), window.shape[1])
    load = start(hidden_in.at[:, columns], window, sems.at[3])
    pick_pages(table, lax.axis_index("group"), picked, groups, per_group, per_peer)
    load.wait()
    loads[0].wait()
    for j in range(shards):

        @pl.when(own_shard == j)
        def _(j=j):
            at = j * width - min(j * width // LANES * LANES, last)
            wide[...] = window[:, at : at + width].astype(F32)
            products[:, inner + low :] = vocab[:, j * width : (j + 1) * width].astype(F32)

    base = shared.shape[0]
    sends = []
    for g in range(groups):
        pack(picked_rows(wide, picked, g, per_peer, page_len), pages.at[g], 0)
        sends.append(start(pages.at[g], out_in.at[g, pl.ds(base, pages.shape[1])], sems.at[4 + g]))
    for load in loads[1:]:
        load.wait()
    products[:, :inner] = dot(vocab[...], w_out[...], ((1,), (1,)))
    products[:, inner : inner + low] = dot(vocab[...], w_up[...], ((1,), (1,)))
    ordered = []
    for j in range(shards):
        at = lax.rem(j - own_shard + 2 * shards - 1, shards) * held
        ordered.append(products[pl.ds(pl.multiple_of(at, held), held), :])
    pack(jnp.concatenate(ordered, axis=0), shared, 0)
    for g in range(groups):
        sends.append(start(shared, out_in.at[g, pl.ds(0, base)], sems.at[4 + groups + g]))
    for send in sends:
        send.wait()


def phi_of(vectors, left, right, cols):
    first = dot(left[...], vectors) + cols[:, 0:1]
    second = dot(right[...], vectors) + cols[:, 1:2]
    return first * second * cols[:, 2:3]


def with_ones(values):
    lane = lax.broadcasted_iota(jnp.int32, (values.shape[0], LANES - HD), 1)
    return jnp.concatenate([values, jnp.where(lane == 0, 1.0, 0.0).astype(values.dtype)], axis=1)


def with_ones_t(values):
    row = lax.broadcasted_iota(jnp.int32, (LANES - HD, values.shape[1]), 0)
    return jnp.concatenate([values, jnp.where(row == 0, 1.0, 0.0).astype(values.dtype)], axis=0)


def same_upto(segrow):
    count = segrow.shape[1]
    ids = segrow[...].astype(F32)
    column = jnp.transpose(jnp.broadcast_to(ids, (8, count)))[:, 0:1]
    behind = lax.broadcasted_iota(jnp.int32, (count, count), 0)
    ahead = lax.broadcasted_iota(jnp.int32, (count, count), 1)
    return jnp.where((column == ids) & (behind <= ahead), 1.0, 0.0)


def group_kernel(
    dims, low, heads, table, arrived, segrow, left, right, cols, ordered_in, ordered_t_in, state_in, nd_in,
    state, wide, placed, ordered, ordered_t, nd, mask, seen, sems
):
    groups, per_group, per_peer, page_len = dims
    tall = per_peer * page_len
    count, sent = placed.shape
    mask[...] = same_upto(segrow)
    for g in range(groups):
        unpack(arrived.at[g], 0, wide, g * tall, tall, sent)
    place_pages(table, lax.axis_index("group"), seen, wide, placed, groups, per_group, per_peer, page_len)
    ordered[...] = placed[:, low:].astype(BF)
    for at in range(0, sent, LANES):
        end = min(at + LANES, sent)
        ordered_t[at:end, :] = jnp.transpose(placed[:, at:end]).astype(BF)
    sends = [start(ordered_t, ordered_t_in, sems.at[0]), start(ordered, ordered_in, sems.at[1])]

    last = segrow[:, count - 1 : count]
    member = jnp.where(segrow[...] == last, 1.0, 0.0)
    total = jnp.sum(member, axis=1, keepdims=True)
    fine = total - total.astype(BF).astype(F32)
    tag = last.astype(F32) + 1.0
    row = lax.broadcasted_iota(jnp.int32, (PHI_PAD, LANES), 0)
    lane = lax.broadcasted_iota(jnp.int32, (PHI_PAD, LANES), 1)
    block = 256 if count % 256 == 0 else count
    for h in range(heads):
        at = h * HEAD
        key = ordered[:, at + FEAT : at + 2 * FEAT] * BF(0.25)
        value = ordered[:, at + 2 * FEAT : at + HEAD]
        at = low + h * HEAD
        query_t = ordered_t[at : at + FEAT, :]
        key_t = ordered_t[at + FEAT : at + 2 * FEAT, :]
        extended_t = with_ones_t(ordered_t[at + 2 * FEAT : at + HEAD, :])

        phi = (phi_of(key_t, left, right, cols) * member).astype(BF)
        summed = dot(phi, with_ones(value))
        summed = jnp.where((row == 0) & (lane == TAG), tag, summed)
        summed = jnp.where((row == 0) & (lane == REST), fine, summed)
        state[h] = summed.astype(BF)

        for begin in range(0, count, block):
            end = begin + block
            s = dot(key[:end], query_t[:, begin:end])
            w = (1.0 + s * (1.0 + 0.5 * s)) * mask[:end, begin:end]
            nd[h, :, begin:end] = dot(extended_t[:, :end], w.astype(BF))
        sends.append(start(nd.at[h], nd_in.at[h], sems.at[3 + h]))
    sends.append(start(state, state_in, sems.at[2]))
    for send in sends:
        send.wait()


def split3(x):
    a = x.astype(BF)
    rest = x - a.astype(F32)
    b = rest.astype(BF)
    return jnp.concatenate([a, b, (rest - b.astype(F32)).astype(BF)], axis=0)


def state_corner(state):
    corner = state[0, 0:1, :].astype(F32)
    return corner[:, TAG : TAG + 1], corner[:, ONE : ONE + 1] + corner[:, REST : REST + 1]


def far_weights(offsets, own_shard, shards, sources, targets, sems):
    width = sources[0].shape[0] // shards
    copies = []
    for k, offset in enumerate(offsets):
        j = own_shard + offset
        rows = pl.ds(pl.multiple_of(jnp.clip(j, 0, shards - 1) * width, width), width)
        pairs = [(source.at[rows], target.at[rows]) for source, target in zip(sources, targets)]
        copies.append([pltpu.make_async_copy(*pair, sems.at[2 * k + i]) for i, pair in enumerate(pairs)])

        @pl.when((j >= 0) & (j < shards))
        def _(k=k):
            for copy in copies[k]:
                copy.start()

    return copies


def shard_parts(offsets, own_shard, shards, w_t, up_t, inputs, held_out, outs, sems, copies=None):
    width = w_t.shape[0] // shards
    inner = w_t.shape[1]
    pending = []
    for k, offset in enumerate(offsets):
        j = own_shard + offset
        there = (j >= 0) & (j < shards)

        @pl.when(there)
        def _(j=j, k=k):
            for copy in copies[k] if copies else ():
                copy.wait()
            rows = pl.ds(pl.multiple_of(j * width, width), width)
            part = dot(w_t[rows, :], inputs[:inner, :]) + dot(up_t[rows, :], inputs[inner:, :])
            held_out[k] = part.astype(BF)
            start(held_out.at[k], outs[k], sems.at[k])

        pending.append((there, k))

    def finish():
        for there, k in pending:

            @pl.when(there)
            def _(k=k):
                pltpu.make_async_copy(held_out.at[k], outs[k], sems.at[k]).wait()

    return finish


def finish_kernel(
    low, heads, shards, ordered_t_in, nd_in, state, segrow, slotrow, left, right, cols, w_t_in, up_t_in, *refs
):
    far = far_offsets(shards)
    outs = refs[: len(far) - 1]
    outs = [outs[0], *outs]
    inputs_in, queries, nd, w_t, up_t, inputs, held_out, sems, weight_sems = refs[len(far) - 1 :]
    inner = heads * HD
    sem = iter(range(len(far), len(far) + heads + 6))
    fetches = []
    for h in range(heads):
        rows = pl.ds(low + h * HEAD, FEAT)
        fetches.append(start(ordered_t_in.at[rows], queries.at[h], sems.at[next(sem)]))
    fetches.append(start(nd_in, nd, sems.at[next(sem)]))
    fetches.append(start(ordered_t_in.at[pl.ds(0, low)], inputs.at[pl.ds(inner, low)], sems.at[next(sem)]))
    own_shard = lax.axis_index("mp")
    copies = far_weights(far, own_shard, shards, (w_t_in, up_t_in), (w_t, up_t), weight_sems)
    for fetch in fetches:
        fetch.wait()
    tag, _ = state_corner(state)
    carried = jnp.where(segrow[...].astype(F32) + 1.0 == tag, 1.0, 0.0)
    row_slot = lax.div(lax.broadcasted_iota(jnp.int32, (low, 1), 0), RANK)
    lowered = jnp.where(slotrow[...] == row_slot, inputs[inner:, :].astype(F32), 0.0)
    inputs[inner:, :] = lowered.astype(BF)
    for h in range(heads):
        cross = dot(state[h], phi_of(queries[h], left, right, cols).astype(BF), ((0,), (0,)))
        both = nd[h] + carried * cross
        inputs[h * HD : (h + 1) * HD, :] = (both[:HD, :] / both[ONE : ONE + 1, :]).astype(BF)
    finish = shard_parts(far, own_shard, shards, w_t, up_t, inputs, held_out, outs, sems, copies)
    kept = start(inputs, inputs_in, sems.at[next(sem)])
    finish()
    kept.wait()


def far_offsets(shards):
    far = [shards - 1, 1 - shards]
    for distance in range(shards - 2, 1, -1):
        far += [distance, -distance]
    return far


def near_kernel(shards, w_t_in, up_t_in, inputs_in, *refs):
    outs = refs[: len(NEAR)]
    w_t, up_t, inputs, held_out, sems = refs[len(NEAR) :]
    loads = [
        start(source, target, sems.at[len(NEAR) + k])
        for k, (source, target) in enumerate([(w_t_in, w_t), (up_t_in, up_t), (inputs_in, inputs)])
    ]
    for load in loads:
        load.wait()
    shard_parts(NEAR, lax.axis_index("mp"), shards, w_t, up_t, inputs, held_out, outs, sems)()


def logits_kernel(dims, shards, width, table, arrived, inputs, out, vocab, both, wide, placed, seen):
    groups, per_group, per_peer, page_len = dims
    tall = per_peer * page_len
    inner = inputs.shape[0]
    rows = vocab.shape[0] // groups
    _, _, _, base = packing(rows, inner + width)
    for g in range(groups):
        unpack(arrived.at[g], 0, vocab, g * rows, rows, inner + width)
        unpack(arrived.at[g], base, wide, g * tall, tall, width)
    place_pages(table, lax.axis_index("group"), seen, wide, placed, groups, per_group, per_peer, page_len)
    both[:inner, :] = inputs[...]
    both[inner:, :] = jnp.transpose(placed[...]).astype(BF)
    block = inputs.shape[1] // shards
    scored = dot(vocab[...], both[...])
    for j in range(shards):
        out[j] = scored[:, j * block : (j + 1) * block].astype(BF)


def norms_kernel(low, heads, ordered, ordered_t, state, segrow, left, right, cols, norms, mask):
    count = segrow.shape[1]
    mask[...] = same_upto(segrow)
    upto = mask[...].astype(BF)
    tag, held = state_corner(state)
    carried = jnp.where(segrow[...].astype(F32) + 1.0 == tag, 1.0, 0.0)
    value_lane = lax.broadcasted_iota(jnp.int32, (1, LANES), 1) < HD
    counted = carried * held + jnp.sum(mask[...], axis=0, keepdims=True)
    block = 256 if count % 256 == 0 else count
    increments = []
    before = []
    for h in range(heads):
        at = h * HEAD
        key = ordered[:, at + FEAT : at + 2 * FEAT] * BF(0.25)
        value = ordered[:, at + 2 * FEAT : at + HEAD]
        at = low + h * HEAD
        key_t = ordered_t[at + FEAT : at + 2 * FEAT, :]
        value_t = ordered_t[at + 2 * FEAT : at + HEAD, :]
        wide_key = key_t.astype(F32)
        wide_value = value_t.astype(F32)
        self_score = 0.25 * jnp.sum(wide_key * wide_key, axis=0, keepdims=True)
        self_value = jnp.sum(wide_value * wide_value, axis=0, keepdims=True)
        diagonal = (1.0 + self_score * (1.0 + 0.5 * self_score)) * self_value
        below = []
        for begin in range(0, count, block):
            end = begin + block
            kk = dot(key[:end], key_t[:, begin:end])
            vv = dot(value[:end], value_t[:, begin:end])
            gram = (1.0 + kk * (1.0 + 0.5 * kk)) * vv * mask[:end, begin:end]
            below.append(jnp.sum(gram, axis=0, keepdims=True))
        added = 2.0 * jnp.concatenate(below, axis=1) - diagonal
        held_state = state[h]
        against = dot(held_state, phi_of(key_t, left, right, cols).astype(BF), ((0,), (0,)))[:HD, :]
        along = jnp.sum(against * wide_value, axis=0, keepdims=True)
        increments.append(added + 2.0 * carried * along)
        wide_state = jnp.where(value_lane, held_state.astype(F32), 0.0)
        per_lane = jnp.sum(wide_state * wide_state, axis=0, keepdims=True)
        before.append(jnp.sum(per_lane, axis=1, keepdims=True))
    if heads % 8:
        increments.append(jnp.zeros((8 - heads % 8, count), F32))
    stacked = split3(jnp.concatenate(increments, axis=0))
    thrice = dot(stacked, upto)
    rows = thrice.shape[0] // 3
    summed = thrice[:rows] + thrice[rows : 2 * rows] + thrice[2 * rows :]
    for h in range(heads):
        total = carried * before[h] + summed[h : h + 1, :]
        norms[h : h + 1, :] = jnp.sqrt(total / (counted * float(FEAT * HD)))


def best_kernel(shards, pieces, best):
    whole = pieces[0].astype(F32)
    for i in range(1, shards):
        whole = whole + pieces[i].astype(F32)
    best[...] = jnp.max(whole, axis=0, keepdims=True)


def exchange(blocks, axis):
    return lax.all_to_all(blocks, axis, split_axis=0, concat_axis=0, tiled=True)


def ring_rows(values, axis):
    size = lax.axis_size(axis)
    steps = [lax.ppermute(values, axis, [(i, (i + by) % size) for i in range(size)]) for by in range(size - 1, 0, -1)]
    return jnp.concatenate([*steps, values], axis=0)


def line_sums(terms, axis, beside):
    size = lax.axis_size(axis)

    def joined(*parts):
        return sum(part.astype(F32) for part in parts).astype(BF)

    def up(values, first, last):
        return lax.ppermute(values, axis, [(i, i + 1) for i in range(first, last)])

    def down(values, first, last):
        return lax.ppermute(values, axis, [(i, i - 1) for i in range(first, last)])

    if size == 4:
        relayed_up = up(terms[2], 0, size - 2)
        relayed_down = down(terms[-2], 2, size)
        far = lax.ppermute(terms[3], axis, [(0, 3), (3, 0)])
        relayed_up, relayed_down, far, beside = lax.optimization_barrier((relayed_up, relayed_down, far, beside))
        near_up = up(joined(terms[1], relayed_up), 0, size - 1)
        near_down = down(joined(terms[-1], relayed_down), 1, size)
        return joined(terms[0], far, near_up, near_down), beside
    going_up = going_down = None
    for step in range(1, size):
        to_up = terms[size - step]
        to_down = terms[step - size]
        if step > 1:
            to_up = joined(to_up, going_up)
            to_down = joined(to_down, going_down)
        going_up = up(to_up, 0, step)
        going_down = down(to_down, size - step, size)
    return joined(terms[0], going_up, going_down), beside


def on_device(
    hidden,
    norm_gain,
    qkv_weight,
    out_weight,
    adapter_down,
    adapter_up,
    vocab_rows,
    segments,
    request_adapter,
    adapter_slot,
    page_table,
):
    groups = lax.axis_size("group")
    shards = lax.axis_size("mp")
    own_shard = lax.axis_index("mp")
    count, model_width = hidden.shape
    per_group = page_table.shape[0] // groups
    per_peer = per_group // groups
    page_len = count // per_group
    dims = (groups, per_group, per_peer, page_len)
    qkv_cols = qkv_weight.shape[1]
    heads = qkv_cols // HEAD
    low = adapter_down.shape[1]
    inner = heads * HD
    width = model_width // shards
    sent = low + qkv_cols
    tall = per_peer * page_len
    packed = packing(tall, sent)[-1]
    some = shards * vocab_rows.shape[0]
    scored = groups * some
    aside = packing(some, inner + low + width)[-1] + packing(tall, width)[-1]
    shape = jax.ShapeDtypeStruct
    dma = pltpu.SemaphoreType.DMA
    picked = pltpu.SMEM((groups * per_peer + 1,), jnp.int32)

    left, right, cols = [jnp.asarray(t) for t in feature_tables()]
    segrow = segments.reshape(1, count)
    request_ids = jnp.arange(request_adapter.shape[0], dtype=jnp.int32)
    adapter_ids = jnp.arange(adapter_slot.shape[0], dtype=jnp.int32)

    outgoing = kernel_call(
        functools.partial(project_kernel, dims),
        pltpu.HBM((groups, packed, LANES), BF),
        [SMEM, ANY, VMEM, ANY, ANY],
        ANY,
        [
            pltpu.VMEM((count, model_width), BF),
            pltpu.VMEM((qkv_cols, model_width), BF),
            pltpu.VMEM((model_width, low), BF),
            pltpu.VMEM((count, model_width), BF),
            pltpu.VMEM((count, sent), F32),
            pltpu.VMEM((groups, packed, LANES), BF),
            picked,
            dma((7 + groups,)),
        ],
        2 * count * model_width * sent,
        2 * (count * model_width + model_width * sent),
    )(page_table, hidden, norm_gain, qkv_weight.T, adapter_down)
    arrived = exchange(outgoing, "group")

    after_out, after_up, after_vocab, after_adapter, _ = lax.optimization_barrier(
        (out_weight, adapter_up, vocab_rows, request_adapter, outgoing)
    )
    w_t, up_t = after_out.T, after_up.T
    some_vocab = ring_rows(after_vocab, "mp")
    request_slot = jnp.sum(jnp.where(after_adapter[:, None] == adapter_ids[None, :], adapter_slot[None, :], 0), axis=1)
    slots = jnp.sum(jnp.where(segrow == request_ids[:, None], request_slot[:, None], 0), axis=0, keepdims=True)
    slotrow = slots - own_shard * (low // RANK)
    window = max(-(-(j * width % LANES + width) // LANES) * LANES for j in range(shards))
    beside = kernel_call(
        functools.partial(side_kernel, dims, shards),
        pltpu.HBM((groups, aside, LANES), BF),
        [SMEM] + [ANY] * 4,
        ANY,
        [
            pltpu.VMEM((count, window), BF),
            pltpu.VMEM((some, model_width), BF),
            pltpu.VMEM((inner, model_width), BF),
            pltpu.VMEM((low, model_width), BF),
            pltpu.VMEM((count, width), F32),
            pltpu.VMEM((some, inner + low + width), F32),
            pltpu.VMEM((packing(some, inner + low + width)[-1], LANES), BF),
            pltpu.VMEM((groups, packing(tall, width)[-1], LANES), BF),
            picked,
            dma((4 + 2 * groups,)),
        ],
        2 * some * model_width * (inner + low),
        2 * count * model_width,
    )(page_table, hidden, some_vocab, out_weight, adapter_up)
    arrived, beside, slotrow, w_t, up_t = lax.optimization_barrier((arrived, beside, slotrow, w_t, up_t))

    ordered, ordered_t, state, nd = kernel_call(
        functools.partial(group_kernel, dims, low, heads),
        (
            pltpu.HBM((count, qkv_cols), BF),
            pltpu.HBM((sent, count), BF),
            pltpu.HBM((heads, PHI_PAD, LANES), BF),
            pltpu.HBM((heads, LANES, count), F32),
        ),
        [SMEM] + [VMEM] * 5,
        (ANY, ANY, ANY, ANY),
        [
            pltpu.VMEM((heads, PHI_PAD, LANES), BF),
            pltpu.VMEM((count, sent), F32),
            pltpu.VMEM((count, sent), F32),
            pltpu.VMEM((count, qkv_cols), BF),
            pltpu.VMEM((sent, count), BF),
            pltpu.VMEM((heads, LANES, count), F32),
            pltpu.VMEM((count, count), F32),
            pltpu.SMEM((groups,), jnp.int32),
            dma((3 + heads,)),
        ],
        heads * 2 * count * count * 512,
        6 * count * sent,
        40 * MIB,
    )(page_table, arrived, segrow, left, right, cols)
    beside, state = lax.optimization_barrier((beside, state))
    beside = exchange(beside, "group")
    state = lax.ppermute(state, "group", [(i, i + 1) for i in range(groups - 1)])

    far = far_offsets(shards)
    part = pltpu.HBM((width, count), BF)
    w_buffers = [pltpu.VMEM((model_width, inner), BF), pltpu.VMEM((model_width, low), BF)]
    *far_terms, inputs = kernel_call(
        functools.partial(finish_kernel, low, heads, shards),
        [part] * (len(far) - 1) + [pltpu.HBM((inner + low, count), BF)],
        [ANY] * 2 + [VMEM] * 6 + [ANY] * 2,
        [ANY] * len(far),
        [
            pltpu.VMEM((heads, FEAT, count), BF),
            pltpu.VMEM((heads, LANES, count), F32),
            *w_buffers,
            pltpu.VMEM((inner + low, count), BF),
            pltpu.VMEM((len(far), width, count), BF),
            dma((len(far) + heads + 6,)),
            dma((2 * len(far),)),
        ],
        count * (inner + low) * model_width,
        2 * count * model_width,
    )(ordered_t, nd, state, segrow, slotrow, left, right, cols, w_t, up_t)
    near_terms = kernel_call(
        functools.partial(near_kernel, shards),
        [part] * len(NEAR),
        [ANY] * 3,
        [ANY] * len(NEAR),
        [
            *w_buffers,
            pltpu.VMEM((inner + low, count), BF),
            pltpu.VMEM((len(NEAR), width, count), BF),
            dma((len(NEAR) + 3,)),
        ],
        1,
        1,
    )(w_t, up_t, inputs)
    terms = dict(zip(NEAR, near_terms)) | dict(zip(far, [far_terms[0], *far_terms]))
    [logits] = staged_call(
        functools.partial(logits_kernel, dims, shards, width),
        [shape((shards, scored, count // shards), BF)],
        [page_table],
        [inputs],
        [
            pltpu.VMEM((scored, inner + low + width), BF),
            pltpu.VMEM((inner + low + width, count), BF),
            pltpu.VMEM((count, width), F32),
            pltpu.VMEM((count, width), F32),
            pltpu.SMEM((groups,), jnp.int32),
        ],
        1,
        1,
        given=[beside],
        limit=(40 if scored <= 512 else 56) * MIB,
    )
    [state_norms] = staged_call(
        functools.partial(norms_kernel, low, heads),
        [shape((heads, count), F32)],
        [],
        [ordered, ordered_t, state, segrow, left, right, cols],
        [pltpu.VMEM((count, count), F32)],
        1,
        1,
    )
    update, [state_norms, _] = line_sums(terms, "mp", [state_norms, logits])
    logits = exchange(logits, "mp")
    best = kernel_call(
        functools.partial(best_kernel, shards),
        shape((1, count // shards), F32),
        [VMEM],
        VMEM,
        [],
        1,
        1,
        32 * MIB,
    )(logits)
    return update.T, state_norms, best.reshape(-1)


def solution(mesh):
    placed = (
        P("group", None),
        P(),
        P(None, "mp"),
        P("mp", None),
        P(None, "mp"),
        P("mp", None),
        P(("group", "mp"), None),
        P("group"),
        P(),
        P(),
        P(),
    )
    return jax.shard_map(
        on_device,
        mesh=mesh,
        in_specs=placed,
        out_specs=(P("group", "mp"), P("mp", "group"), P(("group", "mp"))),
        check_vma=False,
    )
```

```python
import functools

import jax
import jax.numpy as jnp
import numpy as np
from jax import lax
from jax.experimental import pallas as pl
from jax.experimental.pallas import tpu as pltpu
from jax.sharding import PartitionSpec as P

FEAT = 16
HD = 112
RANK = 16
EPSILON = 1e-05
HEAD = 2 * FEAT + HD
PHI = 1 + FEAT + FEAT * (FEAT + 1) // 2
PHI_PAD = 160
LANES = 128
ONE, TAG, REST = HD, HD + 1, HD + 2
NEAR = (0, 1, -1)
MIB = 1024 * 1024
VMEM_LIMIT = 60 * MIB

BF = jnp.bfloat16
F32 = jnp.float32
SMEM = pl.BlockSpec(memory_space=pltpu.SMEM)
VMEM = pl.BlockSpec(memory_space=pltpu.VMEM)
ANY = pl.BlockSpec(memory_space=pltpu.HBM)


def feature_tables():
    left = np.zeros((PHI_PAD, FEAT), np.float32)
    right = np.zeros((PHI_PAD, FEAT), np.float32)
    cols = np.zeros((PHI_PAD, 8), np.float32)
    cols[0, :3] = 1.0
    at = 1
    for i in range(FEAT):
        left[at, i] = 1.0
        cols[at, 1] = 1.0
        cols[at, 2] = FEAT**-0.25
        at += 1
    for i in range(FEAT):
        for j in range(i, FEAT):
            left[at, i] = 1.0
            right[at, j] = 1.0
            cols[at, 2] = (1.0 if i == j else 2.0**0.5) / (2.0 * FEAT) ** 0.5
            at += 1
    return left.astype(jnp.bfloat16), right.astype(jnp.bfloat16), cols


def dot(a, b, dims=((1,), (0,))):
    return lax.dot_general(a, b, (dims, ((), ())), preferred_element_type=F32)


def kernel_call(body, out_shape, in_specs, out_specs, scratch, flops, nbytes, limit=VMEM_LIMIT):
    return pl.pallas_call(
        body,
        out_shape=out_shape,
        in_specs=in_specs,
        out_specs=out_specs,
        scratch_shapes=scratch,
        compiler_params=pltpu.CompilerParams(vmem_limit_bytes=limit),
        cost_estimate=pl.CostEstimate(flops=flops, bytes_accessed=nbytes, transcendentals=0),
    )


def start(source, target, sem):
    copy = pltpu.make_async_copy(source, target, sem)
    copy.start()
    return copy


def packing(rows, columns):
    tiles, rest = divmod(columns, LANES)
    share = LANES // rest if rest and LANES % rest == 0 else 1
    if rows % (16 * share):
        share = 1
    return tiles, rest, share, tiles * rows + (rows // share if rest else 0)


def pack(block, target, base):
    rows = block.shape[0]
    tiles, rest, share, _ = packing(*block.shape)
    for t in range(tiles):
        target[base + t * rows : base + (t + 1) * rows, :] = block[:, t * LANES : (t + 1) * LANES].astype(BF)
    if rest:
        short = rows // share
        last = [block[q * short : (q + 1) * short, tiles * LANES :] for q in range(share)]
        if share * rest < LANES:
            last.append(jnp.zeros((short, LANES - share * rest), block.dtype))
        at = base + tiles * rows
        target[at : at + short, :] = jnp.concatenate(last, axis=1).astype(BF)


def unpack(source, base, target, row, rows, columns):
    tiles, rest, share, _ = packing(rows, columns)
    for t in range(tiles):
        piece = source[base + t * rows : base + (t + 1) * rows, :]
        target[row : row + rows, t * LANES : (t + 1) * LANES] = piece.astype(target.dtype)
    if rest:
        short = rows // share
        at = base + tiles * rows
        last = source[at : at + short, :].astype(F32)
        for q in range(share):
            piece = last[:, q * rest : (q + 1) * rest].astype(target.dtype)
            target[row + q * short : row + (q + 1) * short, tiles * LANES : columns] = piece


def staged_call(body, out_shape, scalars, operands, scratch, flops, nbytes, given=(), limit=VMEM_LIMIT):
    buffers = [pltpu.VMEM(x.shape, x.dtype) for x in list(operands) + list(out_shape)]
    ins, outs = len(operands), len(out_shape)

    def run(*refs):
        values, refs = refs[: len(scalars)], refs[len(scalars) :]
        ready, refs = refs[: len(given)], refs[len(given) :]
        far, refs = refs[: ins + outs], refs[ins + outs :]
        near, extra, sems = refs[: ins + outs], refs[ins + outs : -1], refs[-1]
        loads = [start(far[k], near[k], sems.at[k]) for k in range(ins)]
        for load in loads:
            load.wait()
        body(*values, *ready, *near, *extra)
        sends = [start(near[k], far[k], sems.at[k]) for k in range(ins, ins + outs)]
        for send in sends:
            send.wait()

    return kernel_call(
        run,
        [pltpu.HBM(x.shape, x.dtype) for x in out_shape],
        [SMEM] * len(scalars) + [VMEM] * len(given) + [ANY] * ins,
        [ANY] * outs,
        buffers + list(scratch) + [pltpu.SemaphoreType.DMA((ins + outs,))],
        flops,
        nbytes,
        limit,
    )(*scalars, *given, *operands)


def pick_pages(table, own, picked, groups, per_group, per_peer):
    def one_group(g, carry):
        spot = g * per_peer
        for k in range(per_group):
            local = table[g * per_group + k] - own * per_group
            picked[spot] = local
            spot = spot + jnp.where((local >= 0) & (local < per_group), 1, 0)
        return carry

    lax.fori_loop(0, groups, one_group, 0)


def place_pages(table, own, seen, source, target, groups, per_group, per_peer, page_len):
    for g in range(groups):
        seen[g] = 0
    for k in range(per_group):
        holder = lax.div(table[own * per_group + k], per_group)
        slot = holder * per_peer + seen[holder]
        seen[holder] = seen[holder] + 1
        start = pl.multiple_of(slot * page_len, page_len)
        target[k * page_len : (k + 1) * page_len, :] = source[pl.ds(start, page_len), :]


def picked_rows(source, picked, g, per_peer, page_len):
    pages = []
    for b in range(per_peer):
        at = pl.multiple_of(picked[g * per_peer + b] * page_len, page_len)
        pages.append(source[pl.ds(at, page_len), :])
    return jnp.concatenate(pages, axis=0)


def project_kernel(
    dims, table, hidden_in, gain, wq_in, wd_in, out_in, hidden, wq, wd, normed, wide, out, picked, sems
):
    groups, per_group, per_peer, page_len = dims
    rows, model_width = hidden.shape
    low = wd.shape[1]
    pieces = 4
    part = rows // pieces
    strip = wq.shape[0] // 2
    loads = [
        start(hidden_in.at[pl.ds(k * part, part)], hidden.at[pl.ds(k * part, part)], sems.at[k]) for k in range(pieces)
    ]
    weights = [start(wd_in, wd, sems.at[pieces])]
    for k in range(2):
        half = pl.ds(k * strip, strip)
        weights.append(start(wq_in.at[half], wq.at[half], sems.at[pieces + 1 + k]))
    pick_pages(table, lax.axis_index("group"), picked, groups, per_group, per_peer)
    step = 32
    scale = gain[...].reshape(1, model_width)

    def norm_rows(i, carry):
        at = pl.ds(pl.multiple_of(i * step, step), step)
        x = hidden[at, :].astype(F32)
        meansq = jnp.mean(x * x, axis=-1, keepdims=True)
        normed[at, :] = (x * lax.rsqrt(meansq + EPSILON) * scale).astype(BF)
        return carry

    for k in range(pieces):
        loads[k].wait()
        lax.fori_loop(k * part // step, (k + 1) * part // step, norm_rows, 0, unroll=2)
    for load in weights:
        load.wait()
    wide[:, :low] = dot(normed[...], wd[...])
    wide[:, low:] = dot(normed[...], wq[...], ((1,), (1,)))
    sends = []
    for g in range(groups):
        pack(picked_rows(wide, picked, g, per_peer, page_len), out.at[g], 0)
        sends.append(start(out.at[g], out_in.at[g], sems.at[pieces + 3 + g]))
    for send in sends:
        send.wait()


def side_kernel(
    dims, shards, table, hidden_in, w_out_in, w_up_in, *refs
):
    groups, per_group, per_peer, page_len = dims
    vocab_in = refs[:shards]
    out_in, window, vocab, w_out, w_up, wide, products, shared, pages, picked, sems = refs[shards:]
    model_width = hidden_in.shape[1]
    width = model_width // shards
    inner, low = w_out.shape[0], w_up.shape[0]
    held = vocab.shape[0] // shards
    own_shard = lax.axis_index("mp")
    for j in range(shards):

        @pl.when(own_shard == j)
        def _(j=j):
            columns, _ = column_window(j, shards, model_width)
            start(hidden_in.at[:, columns], window, sems.at[2])

    loads = [start(w_out_in, w_out, sems.at[0]), start(w_up_in, w_up, sems.at[1])]
    base = shared.shape[0]
    spare = 3 + 2 * groups
    rows = [start(vocab_in[i], vocab.at[pl.ds(i * held, held)], sems.at[spare + i]) for i in range(shards)]
    pick_pages(table, lax.axis_index("group"), picked, groups, per_group, per_peer)
    pltpu.make_async_copy(hidden_in.at[:, 0 : window.shape[1]], window, sems.at[2]).wait()
    for load in rows:
        load.wait()
    for j in range(shards):

        @pl.when(own_shard == j)
        def _(j=j):
            _, at = column_window(j, shards, model_width)
            wide[...] = window[:, at : at + width].astype(F32)
            products[:, inner + low :] = vocab[:, j * width : (j + 1) * width].astype(F32)

    sends = []
    for g in range(groups):
        pack(picked_rows(wide, picked, g, per_peer, page_len), pages.at[g], 0)
        sends.append(start(pages.at[g], out_in.at[g, pl.ds(base, pages.shape[1])], sems.at[3 + g]))
    for load in loads:
        load.wait()
    products[:, :inner] = dot(vocab[...], w_out[...], ((1,), (1,)))
    products[:, inner : inner + low] = dot(vocab[...], w_up[...], ((1,), (1,)))
    ordered = []
    for j in range(shards):
        at = lax.rem(j - own_shard + 2 * shards - 1, shards) * held
        ordered.append(products[pl.ds(pl.multiple_of(at, held), held), :])
    pack(jnp.concatenate(ordered, axis=0), shared, 0)
    for g in range(groups):
        sends.append(start(shared, out_in.at[g, pl.ds(0, base)], sems.at[3 + groups + g]))
    for send in sends:
        send.wait()


def phi_of(vectors, left, right, cols):
    first = dot(left[...], vectors) + cols[:, 0:1]
    second = dot(right[...], vectors) + cols[:, 1:2]
    return first * second * cols[:, 2:3]


def with_ones(values):
    lane = lax.broadcasted_iota(jnp.int32, (values.shape[0], LANES - HD), 1)
    return jnp.concatenate([values, jnp.where(lane == 0, 1.0, 0.0).astype(values.dtype)], axis=1)


def with_ones_t(values):
    row = lax.broadcasted_iota(jnp.int32, (LANES - HD, values.shape[1]), 0)
    return jnp.concatenate([values, jnp.where(row == 0, 1.0, 0.0).astype(values.dtype)], axis=0)


def same_upto(segrow):
    count = segrow.shape[1]
    ids = segrow[...].astype(F32)
    column = jnp.transpose(jnp.broadcast_to(ids, (8, count)))[:, 0:1]
    behind = lax.broadcasted_iota(jnp.int32, (count, count), 0)
    ahead = lax.broadcasted_iota(jnp.int32, (count, count), 1)
    return jnp.where((column == ids) & (behind <= ahead), 1.0, 0.0)


def group_kernel(
    dims, low, heads, table, arrived, segrow, left, right, cols, ordered_in, ordered_t_in, state_in, nd_in,
    state, wide, placed, ordered, ordered_t, nd, mask, seen, sems
):
    groups, per_group, per_peer, page_len = dims
    tall = per_peer * page_len
    count, sent = placed.shape
    mask[...] = same_upto(segrow)
    for g in range(groups):
        unpack(arrived.at[g], 0, wide, g * tall, tall, sent)
    place_pages(table, lax.axis_index("group"), seen, wide, placed, groups, per_group, per_peer, page_len)
    ordered[...] = placed[:, low:].astype(BF)
    for at in range(0, sent, LANES):
        end = min(at + LANES, sent)
        ordered_t[at:end, :] = jnp.transpose(placed[:, at:end]).astype(BF)
    sends = [start(ordered_t, ordered_t_in, sems.at[0]), start(ordered, ordered_in, sems.at[1])]

    last = segrow[:, count - 1 : count]
    member = jnp.where(segrow[...] == last, 1.0, 0.0)
    total = jnp.sum(member, axis=1, keepdims=True)
    fine = total - total.astype(BF).astype(F32)
    tag = last.astype(F32) + 1.0
    row = lax.broadcasted_iota(jnp.int32, (PHI_PAD, LANES), 0)
    lane = lax.broadcasted_iota(jnp.int32, (PHI_PAD, LANES), 1)
    block = 256 if count % 256 == 0 else count
    for h in range(heads):
        at = h * HEAD
        key = ordered[:, at + FEAT : at + 2 * FEAT] * BF(0.25)
        value = ordered[:, at + 2 * FEAT : at + HEAD]
        at = low + h * HEAD
        query_t = ordered_t[at : at + FEAT, :]
        key_t = ordered_t[at + FEAT : at + 2 * FEAT, :]
        extended_t = with_ones_t(ordered_t[at + 2 * FEAT : at + HEAD, :])

        phi = (phi_of(key_t, left, right, cols) * member).astype(BF)
        summed = dot(phi, with_ones(value))
        summed = jnp.where((row == 0) & (lane == TAG), tag, summed)
        summed = jnp.where((row == 0) & (lane == REST), fine, summed)
        state[h] = summed.astype(BF)

        for begin in range(0, count, block):
            end = begin + block
            s = dot(key[:end], query_t[:, begin:end])
            w = (1.0 + s * (1.0 + 0.5 * s)) * mask[:end, begin:end]
            nd[h, :, begin:end] = dot(extended_t[:, :end], w.astype(BF))
        sends.append(start(nd.at[h], nd_in.at[h], sems.at[3 + h]))
    sends.append(start(state, state_in, sems.at[2]))
    for send in sends:
        send.wait()


def split3(x):
    a = x.astype(BF)
    rest = x - a.astype(F32)
    b = rest.astype(BF)
    return jnp.concatenate([a, b, (rest - b.astype(F32)).astype(BF)], axis=0)


def state_corner(state):
    corner = state[0, 0:1, :].astype(F32)
    return corner[:, TAG : TAG + 1], corner[:, ONE : ONE + 1] + corner[:, REST : REST + 1]


def column_window(j, shards, model_width):
    width = model_width // shards
    size = window_size(shards, model_width)
    first = min(j * width // LANES * LANES, model_width - size)
    return slice(first, first + size), j * width - first


def window_size(shards, model_width):
    width = model_width // shards
    return max(-(-(j * width % LANES + width) // LANES) * LANES for j in range(shards))


def each_shard(offsets, shards):
    for k, offset in enumerate(offsets):
        for own in range(shards):
            if 0 <= own + offset < shards:
                yield k, own, own + offset


def shard_parts(offsets, shards, w_out_in, w_up_in, weights, w_sems, inputs, held_out, outs, sems):
    own_shard = lax.axis_index("mp")
    inner, model_width = w_out_in.shape
    width = model_width // shards

    def copies(k, j):
        window, _ = column_window(j, shards, model_width)
        return (
            pltpu.make_async_copy(w_out_in.at[:, window], weights.at[k, pl.ds(0, inner)], w_sems.at[2 * k]),
            pltpu.make_async_copy(
                w_up_in.at[:, window], weights.at[k, pl.ds(inner, w_up_in.shape[0])], w_sems.at[2 * k + 1]
            ),
        )

    def fetch():
        for k, own, j in each_shard(offsets, shards):

            @pl.when(own_shard == own)
            def _(k=k, j=j):
                for copy in copies(k, j):
                    copy.start()

    def compute():
        for k, own, j in each_shard(offsets, shards):

            @pl.when(own_shard == own)
            def _(k=k, j=j):
                for copy in copies(k, j):
                    copy.wait()
                _, at = column_window(j, shards, model_width)
                held_out[k] = dot(weights[k, :, at : at + width], inputs[...], ((0,), (0,))).astype(BF)
                start(held_out.at[k], outs[k], sems.at[k])

    def finish():
        for k, own, j in each_shard(offsets, shards):

            @pl.when(own_shard == own)
            def _(k=k):
                pltpu.make_async_copy(held_out.at[k], outs[k], sems.at[k]).wait()

    return fetch, compute, finish


def finish_kernel(
    low, heads, shards, ordered_t_in, nd_in, state, segrow, slotrow, left, right, cols, w_out_in, w_up_in, *refs
):
    far = far_offsets(shards)
    outs = refs[: len(far) - 1]
    outs = [outs[0], *outs]
    inputs_in, queries, nd, weights, inputs, held_out, sems, w_sems = refs[len(far) - 1 :]
    inner = heads * HD
    sem = iter(range(len(far), len(far) + heads + 6))
    fetches = []
    for h in range(heads):
        rows = pl.ds(low + h * HEAD, FEAT)
        fetches.append(start(ordered_t_in.at[rows], queries.at[h], sems.at[next(sem)]))
    fetches.append(start(nd_in, nd, sems.at[next(sem)]))
    fetches.append(start(ordered_t_in.at[pl.ds(0, low)], inputs.at[pl.ds(inner, low)], sems.at[next(sem)]))
    fetch_weights, compute, finish = shard_parts(
        far, shards, w_out_in, w_up_in, weights, w_sems, inputs, held_out, outs, sems
    )
    fetch_weights()
    for fetch in fetches:
        fetch.wait()
    tag, _ = state_corner(state)
    carried = jnp.where(segrow[...].astype(F32) + 1.0 == tag, 1.0, 0.0)
    row_slot = lax.div(lax.broadcasted_iota(jnp.int32, (low, 1), 0), RANK)
    lowered = jnp.where(slotrow[...] == row_slot, inputs[inner:, :].astype(F32), 0.0)
    inputs[inner:, :] = lowered.astype(BF)
    for h in range(heads):
        cross = dot(state[h], phi_of(queries[h], left, right, cols).astype(BF), ((0,), (0,)))
        both = nd[h] + carried * cross
        inputs[h * HD : (h + 1) * HD, :] = (both[:HD, :] / both[ONE : ONE + 1, :]).astype(BF)
    compute()
    kept = start(inputs, inputs_in, sems.at[next(sem)])
    finish()
    kept.wait()


def far_offsets(shards):
    far = [shards - 1, 1 - shards]
    for distance in range(shards - 2, 1, -1):
        far += [distance, -distance]
    return far


def near_kernel(shards, w_out_in, w_up_in, inputs_in, *refs):
    outs = refs[: len(NEAR)]
    weights, inputs, held_out, sems, w_sems = refs[len(NEAR) :]
    load = start(inputs_in, inputs, sems.at[len(NEAR)])
    fetch, compute, finish = shard_parts(NEAR, shards, w_out_in, w_up_in, weights, w_sems, inputs, held_out, outs, sems)
    fetch()
    load.wait()
    compute()
    finish()


def logits_kernel(dims, shards, width, table, arrived, inputs, out, vocab, both, wide, placed, seen):
    groups, per_group, per_peer, page_len = dims
    tall = per_peer * page_len
    inner = inputs.shape[0]
    rows = vocab.shape[0] // groups
    _, _, _, base = packing(rows, inner + width)
    for g in range(groups):
        unpack(arrived.at[g], 0, vocab, g * rows, rows, inner + width)
        unpack(arrived.at[g], base, wide, g * tall, tall, width)
    place_pages(table, lax.axis_index("group"), seen, wide, placed, groups, per_group, per_peer, page_len)
    both[:inner, :] = inputs[...]
    both[inner:, :] = jnp.transpose(placed[...]).astype(BF)
    block = inputs.shape[1] // shards
    scored = dot(vocab[...], both[...])
    for j in range(shards):
        out[j] = scored[:, j * block : (j + 1) * block].astype(BF)


def norms_kernel(low, heads, ordered, ordered_t, state, segrow, left, right, cols, norms, mask):
    count = segrow.shape[1]
    mask[...] = same_upto(segrow)
    upto = mask[...].astype(BF)
    tag, held = state_corner(state)
    carried = jnp.where(segrow[...].astype(F32) + 1.0 == tag, 1.0, 0.0)
    value_lane = lax.broadcasted_iota(jnp.int32, (1, LANES), 1) < HD
    counted = carried * held + jnp.sum(mask[...], axis=0, keepdims=True)
    block = 256 if count % 256 == 0 else count
    increments = []
    before = []
    for h in range(heads):
        at = h * HEAD
        key = ordered[:, at + FEAT : at + 2 * FEAT] * BF(0.25)
        value = ordered[:, at + 2 * FEAT : at + HEAD]
        at = low + h * HEAD
        key_t = ordered_t[at + FEAT : at + 2 * FEAT, :]
        value_t = ordered_t[at + 2 * FEAT : at + HEAD, :]
        wide_key = key_t.astype(F32)
        wide_value = value_t.astype(F32)
        self_score = 0.25 * jnp.sum(wide_key * wide_key, axis=0, keepdims=True)
        self_value = jnp.sum(wide_value * wide_value, axis=0, keepdims=True)
        diagonal = (1.0 + self_score * (1.0 + 0.5 * self_score)) * self_value
        below = []
        for begin in range(0, count, block):
            end = begin + block
            kk = dot(key[:end], key_t[:, begin:end])
            vv = dot(value[:end], value_t[:, begin:end])
            gram = (1.0 + kk * (1.0 + 0.5 * kk)) * vv * mask[:end, begin:end]
            below.append(jnp.sum(gram, axis=0, keepdims=True))
        added = 2.0 * jnp.concatenate(below, axis=1) - diagonal
        held_state = state[h]
        against = dot(held_state, phi_of(key_t, left, right, cols).astype(BF), ((0,), (0,)))[:HD, :]
        along = jnp.sum(against * wide_value, axis=0, keepdims=True)
        increments.append(added + 2.0 * carried * along)
        wide_state = jnp.where(value_lane, held_state.astype(F32), 0.0)
        per_lane = jnp.sum(wide_state * wide_state, axis=0, keepdims=True)
        before.append(jnp.sum(per_lane, axis=1, keepdims=True))
    if heads % 8:
        increments.append(jnp.zeros((8 - heads % 8, count), F32))
    stacked = split3(jnp.concatenate(increments, axis=0))
    thrice = dot(stacked, upto)
    rows = thrice.shape[0] // 3
    summed = thrice[:rows] + thrice[rows : 2 * rows] + thrice[2 * rows :]
    for h in range(heads):
        total = carried * before[h] + summed[h : h + 1, :]
        norms[h : h + 1, :] = jnp.sqrt(total / (counted * float(FEAT * HD)))


def best_kernel(shards, pieces, best):
    whole = pieces[0].astype(F32)
    for i in range(1, shards):
        whole = whole + pieces[i].astype(F32)
    best[...] = jnp.max(whole, axis=0, keepdims=True)


def exchange(blocks, axis):
    return lax.all_to_all(blocks, axis, split_axis=0, concat_axis=0, tiled=True)


def ring_rows(values, axis):
    size = lax.axis_size(axis)
    steps = [lax.ppermute(values, axis, [(i, (i + by) % size) for i in range(size)]) for by in range(size - 1, 0, -1)]
    return [*steps, values]


def line_sums(terms, axis, beside):
    size = lax.axis_size(axis)

    def joined(*parts):
        return sum(part.astype(F32) for part in parts).astype(BF)

    def up(values, first, last):
        return lax.ppermute(values, axis, [(i, i + 1) for i in range(first, last)])

    def down(values, first, last):
        return lax.ppermute(values, axis, [(i, i - 1) for i in range(first, last)])

    if size == 4:
        relayed_up = up(terms[2], 0, size - 2)
        relayed_down = down(terms[-2], 2, size)
        far = lax.ppermute(terms[3], axis, [(0, 3), (3, 0)])
        relayed_up, relayed_down, far, beside = lax.optimization_barrier((relayed_up, relayed_down, far, beside))
        near_up = up(joined(terms[1], relayed_up), 0, size - 1)
        near_down = down(joined(terms[-1], relayed_down), 1, size)
        return joined(terms[0], far, near_up, near_down), beside
    going_up = going_down = None
    for step in range(1, size):
        to_up = terms[size - step]
        to_down = terms[step - size]
        if step > 1:
            to_up = joined(to_up, going_up)
            to_down = joined(to_down, going_down)
        going_up = up(to_up, 0, step)
        going_down = down(to_down, size - step, size)
    return joined(terms[0], going_up, going_down), beside


def on_device(
    hidden,
    norm_gain,
    qkv_weight,
    out_weight,
    adapter_down,
    adapter_up,
    vocab_rows,
    segments,
    request_adapter,
    adapter_slot,
    page_table,
):
    groups = lax.axis_size("group")
    shards = lax.axis_size("mp")
    own_shard = lax.axis_index("mp")
    count, model_width = hidden.shape
    per_group = page_table.shape[0] // groups
    per_peer = per_group // groups
    page_len = count // per_group
    dims = (groups, per_group, per_peer, page_len)
    qkv_cols = qkv_weight.shape[1]
    heads = qkv_cols // HEAD
    low = adapter_down.shape[1]
    inner = heads * HD
    width = model_width // shards
    sent = low + qkv_cols
    tall = per_peer * page_len
    packed = packing(tall, sent)[-1]
    some = shards * vocab_rows.shape[0]
    scored = groups * some
    aside = packing(some, inner + low + width)[-1] + packing(tall, width)[-1]
    shape = jax.ShapeDtypeStruct
    dma = pltpu.SemaphoreType.DMA
    picked = pltpu.SMEM((groups * per_peer + 1,), jnp.int32)

    left, right, cols = [jnp.asarray(t) for t in feature_tables()]
    segrow = segments.reshape(1, count)
    request_ids = jnp.arange(request_adapter.shape[0], dtype=jnp.int32)
    adapter_ids = jnp.arange(adapter_slot.shape[0], dtype=jnp.int32)

    outgoing = kernel_call(
        functools.partial(project_kernel, dims),
        pltpu.HBM((groups, packed, LANES), BF),
        [SMEM, ANY, VMEM, ANY, ANY],
        ANY,
        [
            pltpu.VMEM((count, model_width), BF),
            pltpu.VMEM((qkv_cols, model_width), BF),
            pltpu.VMEM((model_width, low), BF),
            pltpu.VMEM((count, model_width), BF),
            pltpu.VMEM((count, sent), F32),
            pltpu.VMEM((groups, packed, LANES), BF),
            picked,
            dma((7 + groups,)),
        ],
        2 * count * model_width * sent,
        2 * (count * model_width + model_width * sent),
    )(page_table, hidden, norm_gain, qkv_weight.T, adapter_down)
    arrived = exchange(outgoing, "group")

    after_vocab, after_adapter, _ = lax.optimization_barrier((vocab_rows, request_adapter, outgoing))
    some_vocab = ring_rows(after_vocab, "mp")
    request_slot = jnp.sum(jnp.where(after_adapter[:, None] == adapter_ids[None, :], adapter_slot[None, :], 0), axis=1)
    slots = jnp.sum(jnp.where(segrow == request_ids[:, None], request_slot[:, None], 0), axis=0, keepdims=True)
    slotrow = slots - own_shard * (low // RANK)
    window = window_size(shards, model_width)
    beside = kernel_call(
        functools.partial(side_kernel, dims, shards),
        pltpu.HBM((groups, aside, LANES), BF),
        [SMEM] + [ANY] * (3 + shards),
        ANY,
        [
            pltpu.VMEM((count, window), BF),
            pltpu.VMEM((some, model_width), BF),
            pltpu.VMEM((inner, model_width), BF),
            pltpu.VMEM((low, model_width), BF),
            pltpu.VMEM((count, width), F32),
            pltpu.VMEM((some, inner + low + width), F32),
            pltpu.VMEM((packing(some, inner + low + width)[-1], LANES), BF),
            pltpu.VMEM((groups, packing(tall, width)[-1], LANES), BF),
            picked,
            dma((3 + 2 * groups + shards,)),
        ],
        2 * some * model_width * (inner + low),
        2 * count * model_width,
    )(page_table, hidden, out_weight, adapter_up, *some_vocab)
    arrived, beside, slotrow = lax.optimization_barrier((arrived, beside, slotrow))

    ordered, ordered_t, state, nd = kernel_call(
        functools.partial(group_kernel, dims, low, heads),
        (
            pltpu.HBM((count, qkv_cols), BF),
            pltpu.HBM((sent, count), BF),
            pltpu.HBM((heads, PHI_PAD, LANES), BF),
            pltpu.HBM((heads, LANES, count), F32),
        ),
        [SMEM] + [VMEM] * 5,
        (ANY, ANY, ANY, ANY),
        [
            pltpu.VMEM((heads, PHI_PAD, LANES), BF),
            pltpu.VMEM((count, sent), F32),
            pltpu.VMEM((count, sent), F32),
            pltpu.VMEM((count, qkv_cols), BF),
            pltpu.VMEM((sent, count), BF),
            pltpu.VMEM((heads, LANES, count), F32),
            pltpu.VMEM((count, count), F32),
            pltpu.SMEM((groups,), jnp.int32),
            dma((3 + heads,)),
        ],
        heads * 2 * count * count * 512,
        6 * count * sent,
        40 * MIB,
    )(page_table, arrived, segrow, left, right, cols)
    beside, state = lax.optimization_barrier((beside, state))
    beside = exchange(beside, "group")
    state = lax.ppermute(state, "group", [(i, i + 1) for i in range(groups - 1)])

    far = far_offsets(shards)
    part = pltpu.HBM((width, count), BF)
    *far_terms, inputs = kernel_call(
        functools.partial(finish_kernel, low, heads, shards),
        [part] * (len(far) - 1) + [pltpu.HBM((inner + low, count), BF)],
        [ANY] * 2 + [VMEM] * 6 + [ANY] * 2,
        [ANY] * len(far),
        [
            pltpu.VMEM((heads, FEAT, count), BF),
            pltpu.VMEM((heads, LANES, count), F32),
            pltpu.VMEM((len(far), inner + low, window), BF),
            pltpu.VMEM((inner + low, count), BF),
            pltpu.VMEM((len(far), width, count), BF),
            dma((len(far) + heads + 6,)),
            dma((2 * len(far),)),
        ],
        20 * count * (inner + low) * model_width,
        40 * count * model_width,
    )(ordered_t, nd, state, segrow, slotrow, left, right, cols, out_weight, adapter_up)
    near_terms = kernel_call(
        functools.partial(near_kernel, shards),
        [part] * len(NEAR),
        [ANY] * 3,
        [ANY] * len(NEAR),
        [
            pltpu.VMEM((len(NEAR), inner + low, window), BF),
            pltpu.VMEM((inner + low, count), BF),
            pltpu.VMEM((len(NEAR), width, count), BF),
            dma((len(NEAR) + 1,)),
            dma((2 * len(NEAR),)),
        ],
        1,
        1,
    )(out_weight, adapter_up, inputs)
    terms = dict(zip(NEAR, near_terms)) | dict(zip(far, [far_terms[0], *far_terms]))
    [logits] = staged_call(
        functools.partial(logits_kernel, dims, shards, width),
        [shape((shards, scored, count // shards), BF)],
        [page_table],
        [inputs],
        [
            pltpu.VMEM((scored, inner + low + width), BF),
            pltpu.VMEM((inner + low + width, count), BF),
            pltpu.VMEM((count, width), F32),
            pltpu.VMEM((count, width), F32),
            pltpu.SMEM((groups,), jnp.int32),
        ],
        1,
        1,
        given=[beside],
        limit=(40 if scored <= 512 else 56) * MIB,
    )
    [state_norms] = staged_call(
        functools.partial(norms_kernel, low, heads),
        [shape((heads, count), F32)],
        [],
        [ordered, ordered_t, state, segrow, left, right, cols],
        [pltpu.VMEM((count, count), F32)],
        1,
        1,
    )
    update, [state_norms, _] = line_sums(terms, "mp", [state_norms, logits])
    logits = exchange(logits, "mp")
    best = kernel_call(
        functools.partial(best_kernel, shards),
        shape((1, count // shards), F32),
        [VMEM],
        VMEM,
        [],
        1,
        1,
        32 * MIB,
    )(logits)
    return update.T, state_norms, best.reshape(-1)


def solution(mesh):
    placed = (
        P("group", None),
        P(),
        P(None, "mp"),
        P("mp", None),
        P(None, "mp"),
        P("mp", None),
        P(("group", "mp"), None),
        P("group"),
        P(),
        P(),
        P(),
    )
    return jax.shard_map(
        on_device,
        mesh=mesh,
        in_specs=placed,
        out_specs=(P("group", "mp"), P("mp", "group"), P(("group", "mp"))),
        check_vma=False,
    )
```

```python
import functools

import jax
import jax.numpy as jnp
import numpy as np
from jax import lax
from jax.experimental import pallas as pl
from jax.experimental.pallas import tpu as pltpu
from jax.sharding import PartitionSpec as P

FEAT = 16
HD = 112
RANK = 16
EPSILON = 1e-05
HEAD = 2 * FEAT + HD
PHI = 1 + FEAT + FEAT * (FEAT + 1) // 2
PHI_PAD = 160
LANES = 128
ONE, TAG, REST = HD, HD + 1, HD + 2
NEAR = (0, 1, -1)
MIB = 1024 * 1024
VMEM_LIMIT = 60 * MIB

BF = jnp.bfloat16
F32 = jnp.float32
SMEM = pl.BlockSpec(memory_space=pltpu.SMEM)
VMEM = pl.BlockSpec(memory_space=pltpu.VMEM)
ANY = pl.BlockSpec(memory_space=pltpu.HBM)


def feature_tables():
    left = np.zeros((PHI_PAD, FEAT), np.float32)
    right = np.zeros((PHI_PAD, FEAT), np.float32)
    cols = np.zeros((PHI_PAD, 8), np.float32)
    cols[0, :3] = 1.0
    at = 1
    for i in range(FEAT):
        left[at, i] = 1.0
        cols[at, 1] = 1.0
        cols[at, 2] = FEAT**-0.25
        at += 1
    for i in range(FEAT):
        for j in range(i, FEAT):
            left[at, i] = 1.0
            right[at, j] = 1.0
            cols[at, 2] = (1.0 if i == j else 2.0**0.5) / (2.0 * FEAT) ** 0.5
            at += 1
    return left.astype(jnp.bfloat16), right.astype(jnp.bfloat16), cols


def dot(a, b, dims=((1,), (0,))):
    return lax.dot_general(a, b, (dims, ((), ())), preferred_element_type=F32)


def kernel_call(body, out_shape, in_specs, out_specs, scratch, flops, nbytes, limit=VMEM_LIMIT, aliases=None):
    return pl.pallas_call(
        body,
        out_shape=out_shape,
        in_specs=in_specs,
        out_specs=out_specs,
        scratch_shapes=scratch,
        input_output_aliases=aliases or {},
        compiler_params=pltpu.CompilerParams(vmem_limit_bytes=limit),
        cost_estimate=pl.CostEstimate(flops=flops, bytes_accessed=nbytes, transcendentals=0),
    )


def start(source, target, sem):
    copy = pltpu.make_async_copy(source, target, sem)
    copy.start()
    return copy


def packing(rows, columns):
    tiles, rest = divmod(columns, LANES)
    share = LANES // rest if rest and LANES % rest == 0 else 1
    if rows % (16 * share):
        share = 1
    return tiles, rest, share, tiles * rows + (rows // share if rest else 0)


def pack(block, target, base):
    rows = block.shape[0]
    tiles, rest, share, _ = packing(*block.shape)
    for t in range(tiles):
        target[base + t * rows : base + (t + 1) * rows, :] = block[:, t * LANES : (t + 1) * LANES].astype(BF)
    if rest:
        short = rows // share
        last = [block[q * short : (q + 1) * short, tiles * LANES :] for q in range(share)]
        if share * rest < LANES:
            last.append(jnp.zeros((short, LANES - share * rest), block.dtype))
        at = base + tiles * rows
        target[at : at + short, :] = jnp.concatenate(last, axis=1).astype(BF)


def unpack(source, base, target, row, rows, columns):
    tiles, rest, share, _ = packing(rows, columns)
    for t in range(tiles):
        piece = source[base + t * rows : base + (t + 1) * rows, :]
        target[row : row + rows, t * LANES : (t + 1) * LANES] = piece.astype(target.dtype)
    if rest:
        short = rows // share
        at = base + tiles * rows
        last = source[at : at + short, :].astype(F32)
        for q in range(share):
            piece = last[:, q * rest : (q + 1) * rest].astype(target.dtype)
            target[row + q * short : row + (q + 1) * short, tiles * LANES : columns] = piece


def staged_call(body, out_shape, scalars, operands, scratch, flops, nbytes, given=(), limit=VMEM_LIMIT):
    buffers = [pltpu.VMEM(x.shape, x.dtype) for x in list(operands) + list(out_shape)]
    ins, outs = len(operands), len(out_shape)

    def run(*refs):
        values, refs = refs[: len(scalars)], refs[len(scalars) :]
        ready, refs = refs[: len(given)], refs[len(given) :]
        far, refs = refs[: ins + outs], refs[ins + outs :]
        near, extra, sems = refs[: ins + outs], refs[ins + outs : -1], refs[-1]
        loads = [start(far[k], near[k], sems.at[k]) for k in range(ins)]
        for load in loads:
            load.wait()
        body(*values, *ready, *near, *extra)
        sends = [start(near[k], far[k], sems.at[k]) for k in range(ins, ins + outs)]
        for send in sends:
            send.wait()

    return kernel_call(
        run,
        [pltpu.HBM(x.shape, x.dtype) for x in out_shape],
        [SMEM] * len(scalars) + [VMEM] * len(given) + [ANY] * ins,
        [ANY] * outs,
        buffers + list(scratch) + [pltpu.SemaphoreType.DMA((ins + outs,))],
        flops,
        nbytes,
        limit,
    )(*scalars, *given, *operands)


def pick_pages(table, own, picked, groups, per_group, per_peer):
    def one_group(g, carry):
        spot = g * per_peer
        for k in range(per_group):
            local = table[g * per_group + k] - own * per_group
            picked[spot] = local
            spot = spot + jnp.where((local >= 0) & (local < per_group), 1, 0)
        return carry

    lax.fori_loop(0, groups, one_group, 0)


def place_pages(table, own, seen, source, target, groups, per_group, per_peer, page_len):
    for g in range(groups):
        seen[g] = 0
    for k in range(per_group):
        holder = lax.div(table[own * per_group + k], per_group)
        slot = holder * per_peer + seen[holder]
        seen[holder] = seen[holder] + 1
        start = pl.multiple_of(slot * page_len, page_len)
        target[k * page_len : (k + 1) * page_len, :] = source[pl.ds(start, page_len), :]


def picked_rows(source, picked, g, per_peer, page_len):
    pages = []
    for b in range(per_peer):
        at = pl.multiple_of(picked[g * per_peer + b] * page_len, page_len)
        pages.append(source[pl.ds(at, page_len), :])
    return jnp.concatenate(pages, axis=0)


def project_kernel(
    dims, table, hidden_in, gain, wq_in, wd_in, out_in, hidden, wq, wd, normed, wide, out, picked, sems
):
    groups, per_group, per_peer, page_len = dims
    rows, model_width = hidden.shape
    low = wd.shape[1]
    pieces = 4
    part = rows // pieces
    strip = wq.shape[0] // 2
    loads = [
        start(hidden_in.at[pl.ds(k * part, part)], hidden.at[pl.ds(k * part, part)], sems.at[k]) for k in range(pieces)
    ]
    weights = [start(wd_in, wd, sems.at[pieces])]
    for k in range(2):
        half = pl.ds(k * strip, strip)
        weights.append(start(wq_in.at[half], wq.at[half], sems.at[pieces + 1 + k]))
    pick_pages(table, lax.axis_index("group"), picked, groups, per_group, per_peer)
    step = 32
    scale = gain[...].reshape(1, model_width)

    def norm_rows(i, carry):
        at = pl.ds(pl.multiple_of(i * step, step), step)
        x = hidden[at, :].astype(F32)
        meansq = jnp.mean(x * x, axis=-1, keepdims=True)
        normed[at, :] = (x * lax.rsqrt(meansq + EPSILON) * scale).astype(BF)
        return carry

    for k in range(pieces):
        loads[k].wait()
        lax.fori_loop(k * part // step, (k + 1) * part // step, norm_rows, 0, unroll=2)
    for load in weights:
        load.wait()
    wide[:, :low] = dot(normed[...], wd[...])
    wide[:, low:] = dot(normed[...], wq[...], ((1,), (1,)))
    sends = []
    for g in range(groups):
        pack(picked_rows(wide, picked, g, per_peer, page_len), out.at[g], 0)
        sends.append(start(out.at[g], out_in.at[g], sems.at[pieces + 3 + g]))
    for send in sends:
        send.wait()


def residual_kernel(dims, shards, base, table, hidden_in, out_in, window, wide, pages, picked, sems):
    groups, per_group, per_peer, page_len = dims
    own_shard = lax.axis_index("mp")
    for j in range(shards):

        @pl.when(own_shard == j)
        def _(j=j):
            columns, _ = column_window(j, shards, hidden_in.shape[1])
            start(hidden_in.at[:, columns], window, sems.at[groups])

    pick_pages(table, lax.axis_index("group"), picked, groups, per_group, per_peer)
    pltpu.make_async_copy(hidden_in.at[:, 0 : window.shape[1]], window, sems.at[groups]).wait()
    for j in range(shards):

        @pl.when(own_shard == j)
        def _(j=j):
            _, at = column_window(j, shards, hidden_in.shape[1])
            wide[...] = window[:, at : at + wide.shape[1]].astype(F32)

    sends = []
    for g in range(groups):
        pack(picked_rows(wide, picked, g, per_peer, page_len), pages.at[g], 0)
        sends.append(start(pages.at[g], out_in.at[g, pl.ds(base, pages.shape[1])], sems.at[g]))
    for send in sends:
        send.wait()


def products_kernel(groups, shards, w_out_in, w_up_in, *refs):
    blocks = refs[:shards]
    _, out_in, vocab, w_out, w_up, products, shared, sems = refs[shards:]
    inner, model_width = w_out.shape
    low = w_up.shape[0]
    width = model_width // shards
    held = blocks[0].shape[0]
    loads = [start(w_up_in, w_up, sems.at[groups])]
    for k in range(inner // HD):
        rows = pl.ds(k * HD, HD)
        loads.append(start(w_out_in.at[rows], w_out.at[rows], sems.at[groups + 1 + k]))
    own_shard = lax.axis_index("mp")
    for i in range(shards):
        at = lax.rem(own_shard + i + 1, shards) * held
        vocab[pl.ds(pl.multiple_of(at, held), held), :] = blocks[i][...]
    for load in loads:
        load.wait()
    products[:, :inner] = dot(vocab[...], w_out[...], ((1,), (1,)))
    products[:, inner : inner + low] = dot(vocab[...], w_up[...], ((1,), (1,)))
    for j in range(shards):

        @pl.when(own_shard == j)
        def _(j=j):
            products[:, inner + low :] = vocab[:, j * width : (j + 1) * width].astype(F32)

    pack(products[...], shared, 0)
    sends = [start(shared, out_in.at[g, pl.ds(0, shared.shape[0])], sems.at[g]) for g in range(groups)]
    for send in sends:
        send.wait()


def phi_of(vectors, left, right, cols):
    first = dot(left[...], vectors) + cols[:, 0:1]
    second = dot(right[...], vectors) + cols[:, 1:2]
    return first * second * cols[:, 2:3]


def with_ones(values):
    lane = lax.broadcasted_iota(jnp.int32, (values.shape[0], LANES - HD), 1)
    return jnp.concatenate([values, jnp.where(lane == 0, 1.0, 0.0).astype(values.dtype)], axis=1)


def with_ones_t(values):
    row = lax.broadcasted_iota(jnp.int32, (LANES - HD, values.shape[1]), 0)
    return jnp.concatenate([values, jnp.where(row == 0, 1.0, 0.0).astype(values.dtype)], axis=0)


def same_upto(segrow):
    count = segrow.shape[1]
    ids = segrow[...].astype(F32)
    column = jnp.transpose(jnp.broadcast_to(ids, (8, count)))[:, 0:1]
    behind = lax.broadcasted_iota(jnp.int32, (count, count), 0)
    ahead = lax.broadcasted_iota(jnp.int32, (count, count), 1)
    return jnp.where((column == ids) & (behind <= ahead), 1.0, 0.0)


def group_kernel(
    dims, low, heads, table, arrived, segrow, left, right, cols, ordered_in, ordered_t_in, state_in, nd_in,
    state, wide, placed, ordered, ordered_t, nd, mask, seen, sems
):
    groups, per_group, per_peer, page_len = dims
    tall = per_peer * page_len
    count, sent = placed.shape
    mask[...] = same_upto(segrow)
    for g in range(groups):
        unpack(arrived.at[g], 0, wide, g * tall, tall, sent)
    place_pages(table, lax.axis_index("group"), seen, wide, placed, groups, per_group, per_peer, page_len)
    ordered[...] = placed[:, low:].astype(BF)
    for at in range(0, sent, LANES):
        end = min(at + LANES, sent)
        ordered_t[at:end, :] = jnp.transpose(placed[:, at:end]).astype(BF)
    sends = [start(ordered_t, ordered_t_in, sems.at[0]), start(ordered, ordered_in, sems.at[1])]

    last = segrow[:, count - 1 : count]
    member = jnp.where(segrow[...] == last, 1.0, 0.0)
    total = jnp.sum(member, axis=1, keepdims=True)
    fine = total - total.astype(BF).astype(F32)
    tag = last.astype(F32) + 1.0
    row = lax.broadcasted_iota(jnp.int32, (PHI_PAD, LANES), 0)
    lane = lax.broadcasted_iota(jnp.int32, (PHI_PAD, LANES), 1)
    block = 256 if count % 256 == 0 else count
    for h in range(heads):
        at = h * HEAD
        key = ordered[:, at + FEAT : at + 2 * FEAT] * BF(0.25)
        value = ordered[:, at + 2 * FEAT : at + HEAD]
        at = low + h * HEAD
        query_t = ordered_t[at : at + FEAT, :]
        key_t = ordered_t[at + FEAT : at + 2 * FEAT, :]
        extended_t = with_ones_t(ordered_t[at + 2 * FEAT : at + HEAD, :])

        phi = (phi_of(key_t, left, right, cols) * member).astype(BF)
        summed = dot(phi, with_ones(value))
        summed = jnp.where((row == 0) & (lane == TAG), tag, summed)
        summed = jnp.where((row == 0) & (lane == REST), fine, summed)
        state[h] = summed.astype(BF)

        for begin in range(0, count, block):
            end = begin + block
            s = dot(key[:end], query_t[:, begin:end])
            w = (1.0 + s * (1.0 + 0.5 * s)) * mask[:end, begin:end]
            nd[h, :, begin:end] = dot(extended_t[:, :end], w.astype(BF))
        sends.append(start(nd.at[h], nd_in.at[h], sems.at[3 + h]))
    sends.append(start(state, state_in, sems.at[2]))
    for send in sends:
        send.wait()


def split3(x):
    a = x.astype(BF)
    rest = x - a.astype(F32)
    b = rest.astype(BF)
    return jnp.concatenate([a, b, (rest - b.astype(F32)).astype(BF)], axis=0)


def state_corner(state):
    corner = state[0, 0:1, :].astype(F32)
    return corner[:, TAG : TAG + 1], corner[:, ONE : ONE + 1] + corner[:, REST : REST + 1]


def column_window(j, shards, model_width):
    width = model_width // shards
    size = window_size(shards, model_width)
    first = min(j * width // LANES * LANES, model_width - size)
    return slice(first, first + size), j * width - first


def window_size(shards, model_width):
    width = model_width // shards
    return max(-(-(j * width % LANES + width) // LANES) * LANES for j in range(shards))


def each_shard(offsets, shards):
    for k, offset in enumerate(offsets):
        for own in range(shards):
            if 0 <= own + offset < shards:
                yield k, own, own + offset


def shard_parts(offsets, shards, w_out_in, w_up_in, weights, w_sems, inputs, held_out, outs, sems):
    own_shard = lax.axis_index("mp")
    inner, model_width = w_out_in.shape
    width = model_width // shards

    def copies(k, j):
        window, _ = column_window(j, shards, model_width)
        return (
            pltpu.make_async_copy(w_out_in.at[:, window], weights.at[k, pl.ds(0, inner)], w_sems.at[2 * k]),
            pltpu.make_async_copy(
                w_up_in.at[:, window], weights.at[k, pl.ds(inner, w_up_in.shape[0])], w_sems.at[2 * k + 1]
            ),
        )

    def fetch():
        for k, own, j in each_shard(offsets, shards):

            @pl.when(own_shard == own)
            def _(k=k, j=j):
                for copy in copies(k, j):
                    copy.start()

    def compute():
        for k, own, j in each_shard(offsets, shards):

            @pl.when(own_shard == own)
            def _(k=k, j=j):
                for copy in copies(k, j):
                    copy.wait()
                _, at = column_window(j, shards, model_width)
                held_out[k] = dot(weights[k, :, at : at + width], inputs[...], ((0,), (0,))).astype(BF)
                start(held_out.at[k], outs[k], sems.at[k])

    def finish():
        for k, own, j in each_shard(offsets, shards):

            @pl.when(own_shard == own)
            def _(k=k):
                pltpu.make_async_copy(held_out.at[k], outs[k], sems.at[k]).wait()

    return fetch, compute, finish


def finish_kernel(
    low, heads, shards, ordered_t_in, nd_in, state, segrow, slotrow, left, right, cols, w_out_in, w_up_in, *refs
):
    far = far_offsets(shards)
    outs = refs[: len(far) - 1]
    outs = [outs[0], *outs]
    inputs_in, queries, nd, weights, inputs, held_out, sems, w_sems = refs[len(far) - 1 :]
    inner = heads * HD
    sem = iter(range(len(far), len(far) + 2 * heads + 2))
    lows = start(ordered_t_in.at[pl.ds(0, low)], inputs.at[pl.ds(inner, low)], sems.at[next(sem)])
    fetches = []
    for h in range(heads):
        rows = pl.ds(low + h * HEAD, FEAT)
        fetches.append(start(ordered_t_in.at[rows], queries.at[h], sems.at[next(sem)]))
        fetches.append(start(nd_in.at[h], nd.at[h], sems.at[next(sem)]))
    fetch_weights, compute, finish = shard_parts(
        far, shards, w_out_in, w_up_in, weights, w_sems, inputs, held_out, outs, sems
    )
    fetch_weights()
    tag, _ = state_corner(state)
    carried = jnp.where(segrow[...].astype(F32) + 1.0 == tag, 1.0, 0.0)
    row_slot = lax.div(lax.broadcasted_iota(jnp.int32, (low, 1), 0), RANK)
    lows.wait()
    lowered = jnp.where(slotrow[...] == row_slot, inputs[inner:, :].astype(F32), 0.0)
    inputs[inner:, :] = lowered.astype(BF)
    for h in range(heads):
        fetches[2 * h].wait()
        fetches[2 * h + 1].wait()
        cross = dot(state[h], phi_of(queries[h], left, right, cols).astype(BF), ((0,), (0,)))
        both = nd[h] + carried * cross
        inputs[h * HD : (h + 1) * HD, :] = (both[:HD, :] / both[ONE : ONE + 1, :]).astype(BF)
    compute()
    kept = start(inputs, inputs_in, sems.at[next(sem)])
    finish()
    kept.wait()


def far_offsets(shards):
    far = [shards - 1, 1 - shards]
    for distance in range(shards - 2, 1, -1):
        far += [distance, -distance]
    return far


def near_kernel(shards, w_out_in, w_up_in, inputs_in, *refs):
    outs = refs[: len(NEAR)]
    weights, inputs, held_out, sems, w_sems = refs[len(NEAR) :]
    load = start(inputs_in, inputs, sems.at[len(NEAR)])
    fetch, compute, finish = shard_parts(NEAR, shards, w_out_in, w_up_in, weights, w_sems, inputs, held_out, outs, sems)
    fetch()
    load.wait()
    compute()
    finish()


def logits_kernel(dims, shards, width, table, arrived, inputs, out, vocab, both, wide, placed, seen):
    groups, per_group, per_peer, page_len = dims
    tall = per_peer * page_len
    inner = inputs.shape[0]
    rows = vocab.shape[0] // groups
    _, _, _, base = packing(rows, inner + width)
    for g in range(groups):
        unpack(arrived.at[g], 0, vocab, g * rows, rows, inner + width)
        unpack(arrived.at[g], base, wide, g * tall, tall, width)
    place_pages(table, lax.axis_index("group"), seen, wide, placed, groups, per_group, per_peer, page_len)
    both[:inner, :] = inputs[...]
    both[inner:, :] = jnp.transpose(placed[...]).astype(BF)
    block = inputs.shape[1] // shards
    scored = dot(vocab[...], both[...])
    for j in range(shards):
        out[j] = scored[:, j * block : (j + 1) * block].astype(BF)


def norms_kernel(low, heads, ordered, ordered_t, state, segrow, left, right, cols, norms, mask):
    count = segrow.shape[1]
    mask[...] = same_upto(segrow)
    upto = mask[...].astype(BF)
    tag, held = state_corner(state)
    carried = jnp.where(segrow[...].astype(F32) + 1.0 == tag, 1.0, 0.0)
    value_lane = lax.broadcasted_iota(jnp.int32, (1, LANES), 1) < HD
    counted = carried * held + jnp.sum(mask[...], axis=0, keepdims=True)
    block = 256 if count % 256 == 0 else count
    increments = []
    before = []
    for h in range(heads):
        at = h * HEAD
        key = ordered[:, at + FEAT : at + 2 * FEAT] * BF(0.25)
        value = ordered[:, at + 2 * FEAT : at + HEAD]
        at = low + h * HEAD
        key_t = ordered_t[at + FEAT : at + 2 * FEAT, :]
        value_t = ordered_t[at + 2 * FEAT : at + HEAD, :]
        wide_key = key_t.astype(F32)
        wide_value = value_t.astype(F32)
        self_score = 0.25 * jnp.sum(wide_key * wide_key, axis=0, keepdims=True)
        self_value = jnp.sum(wide_value * wide_value, axis=0, keepdims=True)
        diagonal = (1.0 + self_score * (1.0 + 0.5 * self_score)) * self_value
        below = []
        for begin in range(0, count, block):
            end = begin + block
            kk = dot(key[:end], key_t[:, begin:end])
            vv = dot(value[:end], value_t[:, begin:end])
            gram = (1.0 + kk * (1.0 + 0.5 * kk)) * vv * mask[:end, begin:end]
            below.append(jnp.sum(gram, axis=0, keepdims=True))
        added = 2.0 * jnp.concatenate(below, axis=1) - diagonal
        held_state = state[h]
        against = dot(held_state, phi_of(key_t, left, right, cols).astype(BF), ((0,), (0,)))[:HD, :]
        along = jnp.sum(against * wide_value, axis=0, keepdims=True)
        increments.append(added + 2.0 * carried * along)
        wide_state = jnp.where(value_lane, held_state.astype(F32), 0.0)
        per_lane = jnp.sum(wide_state * wide_state, axis=0, keepdims=True)
        before.append(jnp.sum(per_lane, axis=1, keepdims=True))
    if heads % 8:
        increments.append(jnp.zeros((8 - heads % 8, count), F32))
    stacked = split3(jnp.concatenate(increments, axis=0))
    thrice = dot(stacked, upto)
    rows = thrice.shape[0] // 3
    summed = thrice[:rows] + thrice[rows : 2 * rows] + thrice[2 * rows :]
    for h in range(heads):
        total = carried * before[h] + summed[h : h + 1, :]
        norms[h : h + 1, :] = jnp.sqrt(total / (counted * float(FEAT * HD)))


def best_kernel(shards, pieces, best):
    whole = pieces[0].astype(F32)
    for i in range(1, shards):
        whole = whole + pieces[i].astype(F32)
    best[...] = jnp.max(whole, axis=0, keepdims=True)


def exchange(blocks, axis):
    return lax.all_to_all(blocks, axis, split_axis=0, concat_axis=0, tiled=True)


def ring_rows(values, axis):
    size = lax.axis_size(axis)
    steps = [lax.ppermute(values, axis, [(i, (i + by) % size) for i in range(size)]) for by in range(size - 1, 0, -1)]
    return [*steps, values]


def line_sums(terms, axis, beside):
    size = lax.axis_size(axis)

    def joined(*parts):
        return sum(part.astype(F32) for part in parts).astype(BF)

    def up(values, first, last):
        return lax.ppermute(values, axis, [(i, i + 1) for i in range(first, last)])

    def down(values, first, last):
        return lax.ppermute(values, axis, [(i, i - 1) for i in range(first, last)])

    if size == 4:
        relayed_up = up(terms[2], 0, size - 2)
        relayed_down = down(terms[-2], 2, size)
        far = lax.ppermute(terms[3], axis, [(0, 3), (3, 0)])
        relayed_up, relayed_down, far, beside = lax.optimization_barrier((relayed_up, relayed_down, far, beside))
        near_up = up(joined(terms[1], relayed_up), 0, size - 1)
        near_down = down(joined(terms[-1], relayed_down), 1, size)
        return joined(terms[0], far, near_up, near_down), beside
    going_up = going_down = None
    for step in range(1, size):
        to_up = terms[size - step]
        to_down = terms[step - size]
        if step > 1:
            to_up = joined(to_up, going_up)
            to_down = joined(to_down, going_down)
        going_up = up(to_up, 0, step)
        going_down = down(to_down, size - step, size)
    return joined(terms[0], going_up, going_down), beside


def on_device(
    hidden,
    norm_gain,
    qkv_weight,
    out_weight,
    adapter_down,
    adapter_up,
    vocab_rows,
    segments,
    request_adapter,
    adapter_slot,
    page_table,
):
    groups = lax.axis_size("group")
    shards = lax.axis_size("mp")
    own_shard = lax.axis_index("mp")
    count, model_width = hidden.shape
    per_group = page_table.shape[0] // groups
    per_peer = per_group // groups
    page_len = count // per_group
    dims = (groups, per_group, per_peer, page_len)
    qkv_cols = qkv_weight.shape[1]
    heads = qkv_cols // HEAD
    low = adapter_down.shape[1]
    inner = heads * HD
    width = model_width // shards
    sent = low + qkv_cols
    tall = per_peer * page_len
    packed = packing(tall, sent)[-1]
    some = shards * vocab_rows.shape[0]
    scored = groups * some
    aside = packing(some, inner + low + width)[-1] + packing(tall, width)[-1]
    shape = jax.ShapeDtypeStruct
    dma = pltpu.SemaphoreType.DMA
    picked = pltpu.SMEM((groups * per_peer + 1,), jnp.int32)

    left, right, cols = [jnp.asarray(t) for t in feature_tables()]
    segrow = segments.reshape(1, count)
    request_ids = jnp.arange(request_adapter.shape[0], dtype=jnp.int32)
    adapter_ids = jnp.arange(adapter_slot.shape[0], dtype=jnp.int32)

    outgoing = kernel_call(
        functools.partial(project_kernel, dims),
        pltpu.HBM((groups, packed, LANES), BF),
        [SMEM, ANY, VMEM, ANY, ANY],
        ANY,
        [
            pltpu.VMEM((count, model_width), BF),
            pltpu.VMEM((qkv_cols, model_width), BF),
            pltpu.VMEM((model_width, low), BF),
            pltpu.VMEM((count, model_width), BF),
            pltpu.VMEM((count, sent), F32),
            pltpu.VMEM((groups, packed, LANES), BF),
            picked,
            dma((7 + groups,)),
        ],
        2 * count * model_width * sent,
        2 * (count * model_width + model_width * sent),
    )(page_table, hidden, norm_gain, qkv_weight.T, adapter_down)
    arrived = exchange(outgoing, "group")

    after_vocab, after_adapter, later_hidden, _ = lax.optimization_barrier(
        (vocab_rows, request_adapter, hidden, outgoing)
    )
    some_vocab = ring_rows(after_vocab, "mp")
    request_slot = jnp.sum(jnp.where(after_adapter[:, None] == adapter_ids[None, :], adapter_slot[None, :], 0), axis=1)
    slots = jnp.sum(jnp.where(segrow == request_ids[:, None], request_slot[:, None], 0), axis=0, keepdims=True)
    slotrow = slots - own_shard * (low // RANK)
    window = window_size(shards, model_width)
    ahead = packing(some, inner + low + width)[-1]
    beside = kernel_call(
        functools.partial(residual_kernel, dims, shards, ahead),
        pltpu.HBM((groups, aside, LANES), BF),
        [SMEM, ANY],
        ANY,
        [
            pltpu.VMEM((count, window), BF),
            pltpu.VMEM((count, width), F32),
            pltpu.VMEM((groups, packing(tall, width)[-1], LANES), BF),
            picked,
            dma((groups + 1,)),
        ],
        1,
        1,
    )(page_table, later_hidden)
    beside = kernel_call(
        functools.partial(products_kernel, groups, shards),
        pltpu.HBM((groups, aside, LANES), BF),
        [ANY, ANY] + [VMEM] * shards + [ANY],
        ANY,
        [
            pltpu.VMEM((some, model_width), BF),
            pltpu.VMEM((inner, model_width), BF),
            pltpu.VMEM((low, model_width), BF),
            pltpu.VMEM((some, inner + low + width), F32),
            pltpu.VMEM((ahead, LANES), BF),
            dma((groups + 1 + heads,)),
        ],
        2 * some * model_width * (inner + low),
        2 * count * model_width,
        44 * MIB,
        {2 + shards: 0},
    )(out_weight, adapter_up, *some_vocab, beside)
    arrived, beside, slotrow = lax.optimization_barrier((arrived, beside, slotrow))

    ordered, ordered_t, state, nd = kernel_call(
        functools.partial(group_kernel, dims, low, heads),
        (
            pltpu.HBM((count, qkv_cols), BF),
            pltpu.HBM((sent, count), BF),
            pltpu.HBM((heads, PHI_PAD, LANES), BF),
            pltpu.HBM((heads, LANES, count), F32),
        ),
        [SMEM] + [VMEM] * 5,
        (ANY, ANY, ANY, ANY),
        [
            pltpu.VMEM((heads, PHI_PAD, LANES), BF),
            pltpu.VMEM((count, sent), F32),
            pltpu.VMEM((count, sent), F32),
            pltpu.VMEM((count, qkv_cols), BF),
            pltpu.VMEM((sent, count), BF),
            pltpu.VMEM((heads, LANES, count), F32),
            pltpu.VMEM((count, count), F32),
            pltpu.SMEM((groups,), jnp.int32),
            dma((3 + heads,)),
        ],
        heads * 2 * count * count * 512,
        6 * count * sent,
        40 * MIB,
    )(page_table, arrived, segrow, left, right, cols)
    beside, state = lax.optimization_barrier((beside, state))
    beside = exchange(beside, "group")
    state = lax.ppermute(state, "group", [(i, i + 1) for i in range(groups - 1)])

    far = far_offsets(shards)
    part = pltpu.HBM((width, count), BF)
    *far_terms, inputs = kernel_call(
        functools.partial(finish_kernel, low, heads, shards),
        [part] * (len(far) - 1) + [pltpu.HBM((inner + low, count), BF)],
        [ANY] * 2 + [VMEM] * 6 + [ANY] * 2,
        [ANY] * len(far),
        [
            pltpu.VMEM((heads, FEAT, count), BF),
            pltpu.VMEM((heads, LANES, count), F32),
            pltpu.VMEM((len(far), inner + low, window), BF),
            pltpu.VMEM((inner + low, count), BF),
            pltpu.VMEM((len(far), width, count), BF),
            dma((len(far) + 2 * heads + 2,)),
            dma((2 * len(far),)),
        ],
        20 * count * (inner + low) * model_width,
        40 * count * model_width,
    )(ordered_t, nd, state, segrow, slotrow, left, right, cols, out_weight, adapter_up)
    near_terms = kernel_call(
        functools.partial(near_kernel, shards),
        [part] * len(NEAR),
        [ANY] * 3,
        [ANY] * len(NEAR),
        [
            pltpu.VMEM((len(NEAR), inner + low, window), BF),
            pltpu.VMEM((inner + low, count), BF),
            pltpu.VMEM((len(NEAR), width, count), BF),
            dma((len(NEAR) + 1,)),
            dma((2 * len(NEAR),)),
        ],
        1,
        1,
    )(out_weight, adapter_up, inputs)
    terms = dict(zip(NEAR, near_terms)) | dict(zip(far, [far_terms[0], *far_terms]))
    [logits] = staged_call(
        functools.partial(logits_kernel, dims, shards, width),
        [shape((shards, scored, count // shards), BF)],
        [page_table],
        [inputs],
        [
            pltpu.VMEM((scored, inner + low + width), BF),
            pltpu.VMEM((inner + low + width, count), BF),
            pltpu.VMEM((count, width), F32),
            pltpu.VMEM((count, width), F32),
            pltpu.SMEM((groups,), jnp.int32),
        ],
        1,
        1,
        given=[beside],
        limit=(40 if scored <= 512 else 56) * MIB,
    )
    [state_norms] = staged_call(
        functools.partial(norms_kernel, low, heads),
        [shape((heads, count), F32)],
        [],
        [ordered, ordered_t, state, segrow, left, right, cols],
        [pltpu.VMEM((count, count), F32)],
        1,
        1,
    )
    update, [state_norms, _] = line_sums(terms, "mp", [state_norms, logits])
    logits = exchange(logits, "mp")
    best = kernel_call(
        functools.partial(best_kernel, shards),
        shape((1, count // shards), F32),
        [VMEM],
        VMEM,
        [],
        1,
        1,
        32 * MIB,
    )(logits)
    return update.T, state_norms, best.reshape(-1)


def solution(mesh):
    placed = (
        P("group", None),
        P(),
        P(None, "mp"),
        P("mp", None),
        P(None, "mp"),
        P("mp", None),
        P(("group", "mp"), None),
        P("group"),
        P(),
        P(),
        P(),
    )
    return jax.shard_map(
        on_device,
        mesh=mesh,
        in_specs=placed,
        out_specs=(P("group", "mp"), P("mp", "group"), P(("group", "mp"))),
        check_vma=False,
    )
```

```python
import functools

import jax
import jax.numpy as jnp
import numpy as np
from jax import lax
from jax.experimental import pallas as pl
from jax.experimental.pallas import tpu as pltpu
from jax.sharding import PartitionSpec as P

FEAT = 16
HD = 112
RANK = 16
EPSILON = 1e-05
HEAD = 2 * FEAT + HD
PHI = 1 + FEAT + FEAT * (FEAT + 1) // 2
PHI_PAD = 160
LANES = 128
ONE, TAG, REST = HD, HD + 1, HD + 2
MIB = 1024 * 1024
VMEM_LIMIT = 60 * MIB

BF = jnp.bfloat16
F32 = jnp.float32
SMEM = pl.BlockSpec(memory_space=pltpu.SMEM)
VMEM = pl.BlockSpec(memory_space=pltpu.VMEM)
ANY = pl.BlockSpec(memory_space=pltpu.HBM)


def feature_tables():
    left = np.zeros((PHI_PAD, FEAT), np.float32)
    right = np.zeros((PHI_PAD, FEAT), np.float32)
    cols = np.zeros((PHI_PAD, 8), np.float32)
    cols[0, :3] = 1.0
    at = 1
    for i in range(FEAT):
        left[at, i] = 1.0
        cols[at, 1] = 1.0
        cols[at, 2] = FEAT**-0.25
        at += 1
    for i in range(FEAT):
        for j in range(i, FEAT):
            left[at, i] = 1.0
            right[at, j] = 1.0
            cols[at, 2] = (1.0 if i == j else 2.0**0.5) / (2.0 * FEAT) ** 0.5
            at += 1
    return left.astype(jnp.bfloat16), right.astype(jnp.bfloat16), cols


def dot(a, b, dims=((1,), (0,))):
    return lax.dot_general(a, b, (dims, ((), ())), preferred_element_type=F32)


def kernel_call(body, out_shape, in_specs, out_specs, scratch, flops, nbytes, limit=VMEM_LIMIT, aliases=None):
    return pl.pallas_call(
        body,
        out_shape=out_shape,
        in_specs=in_specs,
        out_specs=out_specs,
        scratch_shapes=scratch,
        input_output_aliases=aliases or {},
        compiler_params=pltpu.CompilerParams(vmem_limit_bytes=limit),
        cost_estimate=pl.CostEstimate(flops=flops, bytes_accessed=nbytes, transcendentals=0),
    )


def start(source, target, sem):
    copy = pltpu.make_async_copy(source, target, sem)
    copy.start()
    return copy


def packing(rows, columns):
    tiles, rest = divmod(columns, LANES)
    share = LANES // rest if rest and LANES % rest == 0 else 1
    if rows % (16 * share):
        share = 1
    return tiles, rest, share, tiles * rows + (rows // share if rest else 0)


def pack(block, target, base):
    rows = block.shape[0]
    tiles, rest, share, _ = packing(*block.shape)
    for t in range(tiles):
        target[base + t * rows : base + (t + 1) * rows, :] = block[:, t * LANES : (t + 1) * LANES].astype(BF)
    if rest:
        short = rows // share
        last = [block[q * short : (q + 1) * short, tiles * LANES :] for q in range(share)]
        if share * rest < LANES:
            last.append(jnp.zeros((short, LANES - share * rest), block.dtype))
        at = base + tiles * rows
        target[at : at + short, :] = jnp.concatenate(last, axis=1).astype(BF)


def unpack(source, base, target, row, rows, columns):
    tiles, rest, share, _ = packing(rows, columns)
    for t in range(tiles):
        piece = source[base + t * rows : base + (t + 1) * rows, :]
        target[row : row + rows, t * LANES : (t + 1) * LANES] = piece.astype(target.dtype)
    if rest:
        short = rows // share
        at = base + tiles * rows
        last = source[at : at + short, :].astype(F32)
        for q in range(share):
            piece = last[:, q * rest : (q + 1) * rest].astype(target.dtype)
            target[row + q * short : row + (q + 1) * short, tiles * LANES : columns] = piece


def staged_call(body, out_shape, scalars, operands, scratch, flops, nbytes, given=(), limit=VMEM_LIMIT):
    buffers = [pltpu.VMEM(x.shape, x.dtype) for x in list(operands) + list(out_shape)]
    ins, outs = len(operands), len(out_shape)

    def run(*refs):
        values, refs = refs[: len(scalars)], refs[len(scalars) :]
        ready, refs = refs[: len(given)], refs[len(given) :]
        far, refs = refs[: ins + outs], refs[ins + outs :]
        near, extra, sems = refs[: ins + outs], refs[ins + outs : -1], refs[-1]
        loads = [start(far[k], near[k], sems.at[k]) for k in range(ins)]
        for load in loads:
            load.wait()
        body(*values, *ready, *near, *extra)
        sends = [start(near[k], far[k], sems.at[k]) for k in range(ins, ins + outs)]
        for send in sends:
            send.wait()

    return kernel_call(
        run,
        [pltpu.HBM(x.shape, x.dtype) for x in out_shape],
        [SMEM] * len(scalars) + [VMEM] * len(given) + [ANY] * ins,
        [ANY] * outs,
        buffers + list(scratch) + [pltpu.SemaphoreType.DMA((ins + outs,))],
        flops,
        nbytes,
        limit,
    )(*scalars, *given, *operands)


def pick_pages(table, own, picked, groups, per_group, per_peer):
    def one_group(g, carry):
        spot = g * per_peer
        for k in range(per_group):
            local = table[g * per_group + k] - own * per_group
            picked[spot] = local
            spot = spot + jnp.where((local >= 0) & (local < per_group), 1, 0)
        return carry

    lax.fori_loop(0, groups, one_group, 0)


def place_pages(table, own, seen, source, target, groups, per_group, per_peer, page_len):
    for g in range(groups):
        seen[g] = 0
    for k in range(per_group):
        holder = lax.div(table[own * per_group + k], per_group)
        slot = holder * per_peer + seen[holder]
        seen[holder] = seen[holder] + 1
        start = pl.multiple_of(slot * page_len, page_len)
        target[k * page_len : (k + 1) * page_len, :] = source[pl.ds(start, page_len), :]


def picked_rows(source, picked, g, per_peer, page_len):
    pages = []
    for b in range(per_peer):
        at = pl.multiple_of(picked[g * per_peer + b] * page_len, page_len)
        pages.append(source[pl.ds(at, page_len), :])
    return jnp.concatenate(pages, axis=0)


def project_kernel(
    dims, table, hidden_in, gain, wq_in, wd_in, out_in, hidden, wq, wd, normed, wide, out, picked, sems
):
    groups, per_group, per_peer, page_len = dims
    rows, model_width = hidden.shape
    low = wd.shape[1]
    pieces = 4
    part = rows // pieces
    strip = wq.shape[0] // 2
    loads = [
        start(hidden_in.at[pl.ds(k * part, part)], hidden.at[pl.ds(k * part, part)], sems.at[k]) for k in range(pieces)
    ]
    weights = [start(wd_in, wd, sems.at[pieces])]
    for k in range(2):
        half = pl.ds(k * strip, strip)
        weights.append(start(wq_in.at[half], wq.at[half], sems.at[pieces + 1 + k]))
    pick_pages(table, lax.axis_index("group"), picked, groups, per_group, per_peer)
    step = 32
    scale = gain[...].reshape(1, model_width)

    def norm_rows(i, carry):
        at = pl.ds(pl.multiple_of(i * step, step), step)
        x = hidden[at, :].astype(F32)
        meansq = jnp.mean(x * x, axis=-1, keepdims=True)
        normed[at, :] = (x * lax.rsqrt(meansq + EPSILON) * scale).astype(BF)
        return carry

    for k in range(pieces):
        loads[k].wait()
        lax.fori_loop(k * part // step, (k + 1) * part // step, norm_rows, 0, unroll=2)
    for load in weights:
        load.wait()
    wide[:, :low] = dot(normed[...], wd[...])
    wide[:, low:] = dot(normed[...], wq[...], ((1,), (1,)))
    sends = []
    for g in range(groups):
        pack(picked_rows(wide, picked, g, per_peer, page_len), out.at[g], 0)
        sends.append(start(out.at[g], out_in.at[g], sems.at[pieces + 3 + g]))
    for send in sends:
        send.wait()


def residual_kernel(dims, shards, base, table, hidden_in, out_in, window, wide, pages, picked, sems):
    groups, per_group, per_peer, page_len = dims
    own_shard = lax.axis_index("mp")
    for j in range(shards):

        @pl.when(own_shard == j)
        def _(j=j):
            columns, _ = column_window(j, shards, hidden_in.shape[1])
            start(hidden_in.at[:, columns], window, sems.at[groups])

    pick_pages(table, lax.axis_index("group"), picked, groups, per_group, per_peer)
    pltpu.make_async_copy(hidden_in.at[:, 0 : window.shape[1]], window, sems.at[groups]).wait()
    for j in range(shards):

        @pl.when(own_shard == j)
        def _(j=j):
            _, at = column_window(j, shards, hidden_in.shape[1])
            wide[...] = window[:, at : at + wide.shape[1]].astype(F32)

    sends = []
    for g in range(groups):
        pack(picked_rows(wide, picked, g, per_peer, page_len), pages.at[g], 0)
        sends.append(start(pages.at[g], out_in.at[g, pl.ds(base, pages.shape[1])], sems.at[g]))
    for send in sends:
        send.wait()


def products_kernel(groups, shards, w_out_in, w_up_in, *refs):
    blocks = refs[:shards]
    _, out_in, vocab, w_out, w_up, products, shared, sems = refs[shards:]
    inner, model_width = w_out.shape
    low = w_up.shape[0]
    width = model_width // shards
    held = blocks[0].shape[0]
    loads = [start(w_up_in, w_up, sems.at[groups])]
    for k in range(inner // HD):
        rows = pl.ds(k * HD, HD)
        loads.append(start(w_out_in.at[rows], w_out.at[rows], sems.at[groups + 1 + k]))
    own_shard = lax.axis_index("mp")
    for i in range(shards):
        at = lax.rem(own_shard + i + 1, shards) * held
        vocab[pl.ds(pl.multiple_of(at, held), held), :] = blocks[i][...]
    for load in loads:
        load.wait()
    products[:, :inner] = dot(vocab[...], w_out[...], ((1,), (1,)))
    products[:, inner : inner + low] = dot(vocab[...], w_up[...], ((1,), (1,)))
    for j in range(shards):

        @pl.when(own_shard == j)
        def _(j=j):
            products[:, inner + low :] = vocab[:, j * width : (j + 1) * width].astype(F32)

    pack(products[...], shared, 0)
    sends = [start(shared, out_in.at[g, pl.ds(0, shared.shape[0])], sems.at[g]) for g in range(groups)]
    for send in sends:
        send.wait()


def phi_of(vectors, left, right, cols):
    first = dot(left[...], vectors) + cols[:, 0:1]
    second = dot(right[...], vectors) + cols[:, 1:2]
    return first * second * cols[:, 2:3]


def with_ones(values):
    lane = lax.broadcasted_iota(jnp.int32, (values.shape[0], LANES - HD), 1)
    return jnp.concatenate([values, jnp.where(lane == 0, 1.0, 0.0).astype(values.dtype)], axis=1)


def with_ones_t(values):
    row = lax.broadcasted_iota(jnp.int32, (LANES - HD, values.shape[1]), 0)
    return jnp.concatenate([values, jnp.where(row == 0, 1.0, 0.0).astype(values.dtype)], axis=0)


def same_upto(segrow):
    count = segrow.shape[1]
    ids = segrow[...].astype(F32)
    column = jnp.transpose(jnp.broadcast_to(ids, (8, count)))[:, 0:1]
    behind = lax.broadcasted_iota(jnp.int32, (count, count), 0)
    ahead = lax.broadcasted_iota(jnp.int32, (count, count), 1)
    return jnp.where((column == ids) & (behind <= ahead), 1.0, 0.0)


def group_kernel(
    dims, low, heads, table, arrived, segrow, left, right, cols, ordered_in, ordered_t_in, state_in, nd_in,
    state, wide, placed, ordered, ordered_t, nd, mask, seen, sems
):
    groups, per_group, per_peer, page_len = dims
    tall = per_peer * page_len
    count, sent = placed.shape
    mask[...] = same_upto(segrow)
    for g in range(groups):
        unpack(arrived.at[g], 0, wide, g * tall, tall, sent)
    place_pages(table, lax.axis_index("group"), seen, wide, placed, groups, per_group, per_peer, page_len)
    ordered[...] = placed[:, low:].astype(BF)
    for at in range(0, sent, LANES):
        end = min(at + LANES, sent)
        ordered_t[at:end, :] = jnp.transpose(placed[:, at:end]).astype(BF)
    sends = [start(ordered_t, ordered_t_in, sems.at[0]), start(ordered, ordered_in, sems.at[1])]

    last = segrow[:, count - 1 : count]
    member = jnp.where(segrow[...] == last, 1.0, 0.0)
    total = jnp.sum(member, axis=1, keepdims=True)
    fine = total - total.astype(BF).astype(F32)
    tag = last.astype(F32) + 1.0
    row = lax.broadcasted_iota(jnp.int32, (PHI_PAD, LANES), 0)
    lane = lax.broadcasted_iota(jnp.int32, (PHI_PAD, LANES), 1)
    block = 256 if count % 256 == 0 else count
    for h in range(heads):
        at = h * HEAD
        key = ordered[:, at + FEAT : at + 2 * FEAT] * BF(0.25)
        value = ordered[:, at + 2 * FEAT : at + HEAD]
        at = low + h * HEAD
        query_t = ordered_t[at : at + FEAT, :]
        key_t = ordered_t[at + FEAT : at + 2 * FEAT, :]
        extended_t = with_ones_t(ordered_t[at + 2 * FEAT : at + HEAD, :])

        phi = (phi_of(key_t, left, right, cols) * member).astype(BF)
        summed = dot(phi, with_ones(value))
        summed = jnp.where((row == 0) & (lane == TAG), tag, summed)
        summed = jnp.where((row == 0) & (lane == REST), fine, summed)
        state[h] = summed.astype(BF)

        for begin in range(0, count, block):
            end = begin + block
            s = dot(key[:end], query_t[:, begin:end])
            w = (1.0 + s * (1.0 + 0.5 * s)) * mask[:end, begin:end]
            nd[h, :, begin:end] = dot(extended_t[:, :end], w.astype(BF))
        sends.append(start(nd.at[h], nd_in.at[h], sems.at[3 + h]))
    sends.append(start(state, state_in, sems.at[2]))
    for send in sends:
        send.wait()


def split3(x):
    a = x.astype(BF)
    rest = x - a.astype(F32)
    b = rest.astype(BF)
    return jnp.concatenate([a, b, (rest - b.astype(F32)).astype(BF)], axis=0)


def state_corner(state):
    corner = state[0, 0:1, :].astype(F32)
    return corner[:, TAG : TAG + 1], corner[:, ONE : ONE + 1] + corner[:, REST : REST + 1]


def column_window(j, shards, model_width):
    width = model_width // shards
    size = window_size(shards, model_width)
    first = min(j * width // LANES * LANES, model_width - size)
    return slice(first, first + size), j * width - first


def window_size(shards, model_width):
    width = model_width // shards
    return max(-(-(j * width % LANES + width) // LANES) * LANES for j in range(shards))


def far_tables(shards):
    if shards == 4:
        return [(3, 3, 0, 0), (2, None, None, 1)]
    tables = [tuple({0: shards - 1, shards - 1: 0}.get(own) for own in range(shards))]
    for distance in range(shards - 2, 1, -1):
        tables += [offset_table(distance, shards), offset_table(-distance, shards)]
    return tables


def near_tables(shards):
    if shards == 4:
        return [(0, 1, 2, 3), (1, 0, 3, 2), (None, 2, 1, None)]
    return [offset_table(offset, shards) for offset in (0, 1, -1)]


def offset_table(offset, shards):
    return tuple(own + offset if 0 <= own + offset < shards else None for own in range(shards))


def each_shard(tables):
    for k, table in enumerate(tables):
        for own, j in enumerate(table):
            if j is not None:
                yield k, own, j


def shard_parts(tables, w_out_in, w_up_in, weights, w_sems, inputs, held_out, outs, sems):
    own_shard = lax.axis_index("mp")
    shards = len(tables[0])
    inner, model_width = w_out_in.shape
    width = model_width // shards

    def copies(k, j):
        window, _ = column_window(j, shards, model_width)
        return (
            pltpu.make_async_copy(w_out_in.at[:, window], weights.at[k, pl.ds(0, inner)], w_sems.at[2 * k]),
            pltpu.make_async_copy(
                w_up_in.at[:, window], weights.at[k, pl.ds(inner, w_up_in.shape[0])], w_sems.at[2 * k + 1]
            ),
        )

    def fetch():
        for k, own, j in each_shard(tables):

            @pl.when(own_shard == own)
            def _(k=k, j=j):
                for copy in copies(k, j):
                    copy.start()

    def compute():
        for k, own, j in each_shard(tables):

            @pl.when(own_shard == own)
            def _(k=k, j=j):
                for copy in copies(k, j):
                    copy.wait()
                _, at = column_window(j, shards, model_width)
                held_out[k] = dot(weights[k, :, at : at + width], inputs[...], ((0,), (0,))).astype(BF)
                start(held_out.at[k], outs[k], sems.at[k])

    def finish():
        for k, own, j in each_shard(tables):

            @pl.when(own_shard == own)
            def _(k=k):
                pltpu.make_async_copy(held_out.at[k], outs[k], sems.at[k]).wait()

    return fetch, compute, finish


def finish_kernel(
    low, heads, shards, ordered_t_in, nd_in, state, segrow, slotrow, left, right, cols, w_out_in, w_up_in, *refs
):
    far = far_tables(shards)
    outs = refs[: len(far)]
    inputs_in, state_in, queries, nd, weights, inputs, held_out, sems, w_sems = refs[len(far) :]
    inner = heads * HD
    sem = iter(range(len(far), len(far) + 2 * heads + 3))
    lows = start(ordered_t_in.at[pl.ds(0, low)], inputs.at[pl.ds(inner, low)], sems.at[next(sem)])
    fetches = []
    for h in range(heads):
        rows = pl.ds(low + h * HEAD, FEAT)
        fetches.append(start(ordered_t_in.at[rows], queries.at[h], sems.at[next(sem)]))
        fetches.append(start(nd_in.at[h], nd.at[h], sems.at[next(sem)]))
    fetch_weights, compute, finish = shard_parts(
        far, w_out_in, w_up_in, weights, w_sems, inputs, held_out, outs, sems
    )
    fetch_weights()
    tag, _ = state_corner(state)
    carried = jnp.where(segrow[...].astype(F32) + 1.0 == tag, 1.0, 0.0)
    row_slot = lax.div(lax.broadcasted_iota(jnp.int32, (low, 1), 0), RANK)
    lows.wait()
    lowered = jnp.where(slotrow[...] == row_slot, inputs[inner:, :].astype(F32), 0.0)
    inputs[inner:, :] = lowered.astype(BF)
    for h in range(heads):
        fetches[2 * h].wait()
        fetches[2 * h + 1].wait()
        cross = dot(state[h], phi_of(queries[h], left, right, cols).astype(BF), ((0,), (0,)))
        both = nd[h] + carried * cross
        inputs[h * HD : (h + 1) * HD, :] = (both[:HD, :] / both[ONE : ONE + 1, :]).astype(BF)
    compute()
    kept = [start(inputs, inputs_in, sems.at[next(sem)]), start(state, state_in, sems.at[next(sem)])]
    finish()
    for copy in kept:
        copy.wait()


def near_kernel(shards, w_out_in, w_up_in, inputs_in, *refs):
    near = near_tables(shards)
    outs = refs[: len(near)]
    weights, inputs, held_out, sems, w_sems = refs[len(near) :]
    load = start(inputs_in, inputs, sems.at[len(near)])
    fetch, compute, finish = shard_parts(near, w_out_in, w_up_in, weights, w_sems, inputs, held_out, outs, sems)
    fetch()
    load.wait()
    compute()
    finish()


def logits_kernel(dims, shards, width, table, arrived, inputs, out, vocab, both, wide, placed, seen):
    groups, per_group, per_peer, page_len = dims
    tall = per_peer * page_len
    inner = inputs.shape[0]
    rows = vocab.shape[0] // groups
    _, _, _, base = packing(rows, inner + width)
    for g in range(groups):
        unpack(arrived.at[g], 0, vocab, g * rows, rows, inner + width)
        unpack(arrived.at[g], base, wide, g * tall, tall, width)
    place_pages(table, lax.axis_index("group"), seen, wide, placed, groups, per_group, per_peer, page_len)
    both[:inner, :] = inputs[...]
    both[inner:, :] = jnp.transpose(placed[...]).astype(BF)
    block = inputs.shape[1] // shards
    scored = dot(vocab[...], both[...])
    for j in range(shards):
        out[j] = scored[:, j * block : (j + 1) * block].astype(BF)


def norms_kernel(low, heads, ordered, ordered_t, state, segrow, left, right, cols, norms, mask):
    count = segrow.shape[1]
    mask[...] = same_upto(segrow)
    upto = mask[...].astype(BF)
    tag, held = state_corner(state)
    carried = jnp.where(segrow[...].astype(F32) + 1.0 == tag, 1.0, 0.0)
    value_lane = lax.broadcasted_iota(jnp.int32, (1, LANES), 1) < HD
    counted = carried * held + jnp.sum(mask[...], axis=0, keepdims=True)
    block = 256 if count % 256 == 0 else count
    increments = []
    before = []
    for h in range(heads):
        at = h * HEAD
        key = ordered[:, at + FEAT : at + 2 * FEAT] * BF(0.25)
        value = ordered[:, at + 2 * FEAT : at + HEAD]
        at = low + h * HEAD
        key_t = ordered_t[at + FEAT : at + 2 * FEAT, :]
        value_t = ordered_t[at + 2 * FEAT : at + HEAD, :]
        wide_key = key_t.astype(F32)
        wide_value = value_t.astype(F32)
        self_score = 0.25 * jnp.sum(wide_key * wide_key, axis=0, keepdims=True)
        self_value = jnp.sum(wide_value * wide_value, axis=0, keepdims=True)
        diagonal = (1.0 + self_score * (1.0 + 0.5 * self_score)) * self_value
        below = []
        for begin in range(0, count, block):
            end = begin + block
            kk = dot(key[:end], key_t[:, begin:end])
            vv = dot(value[:end], value_t[:, begin:end])
            gram = (1.0 + kk * (1.0 + 0.5 * kk)) * vv * mask[:end, begin:end]
            below.append(jnp.sum(gram, axis=0, keepdims=True))
        added = 2.0 * jnp.concatenate(below, axis=1) - diagonal
        held_state = state[h]
        against = dot(held_state, phi_of(key_t, left, right, cols).astype(BF), ((0,), (0,)))[:HD, :]
        along = jnp.sum(against * wide_value, axis=0, keepdims=True)
        increments.append(added + 2.0 * carried * along)
        wide_state = jnp.where(value_lane, held_state.astype(F32), 0.0)
        per_lane = jnp.sum(wide_state * wide_state, axis=0, keepdims=True)
        before.append(jnp.sum(per_lane, axis=1, keepdims=True))
    if heads % 8:
        increments.append(jnp.zeros((8 - heads % 8, count), F32))
    stacked = split3(jnp.concatenate(increments, axis=0))
    thrice = dot(stacked, upto)
    rows = thrice.shape[0] // 3
    summed = thrice[:rows] + thrice[rows : 2 * rows] + thrice[2 * rows :]
    for h in range(heads):
        total = carried * before[h] + summed[h : h + 1, :]
        norms[h : h + 1, :] = jnp.sqrt(total / (counted * float(FEAT * HD)))


def best_kernel(shards, pieces, best):
    whole = pieces[0].astype(F32)
    for i in range(1, shards):
        whole = whole + pieces[i].astype(F32)
    best[...] = jnp.max(whole, axis=0, keepdims=True)


def exchange(blocks, axis):
    return lax.all_to_all(blocks, axis, split_axis=0, concat_axis=0, tiled=True)


def ring_rows(values, axis):
    size = lax.axis_size(axis)
    steps = [lax.ppermute(values, axis, [(i, (i + by) % size) for i in range(size)]) for by in range(size - 1, 0, -1)]
    return [*steps, values]


def line_sums(far_terms, near_terms, axis, beside):
    size = lax.axis_size(axis)

    def joined(*parts):
        return sum(part.astype(F32) for part in parts).astype(BF)

    def send(values, *pairs):
        return lax.ppermute(values, axis, pairs)

    own_term = near_terms[0]
    if size == 4:
        here = lax.axis_index(axis)
        middle = (here == 1) | (here == 2)
        across = send(far_terms[0], (1, 2), (2, 1), (0, 3), (3, 0))
        inward = send(far_terms[1], (0, 1), (3, 2))
        across, inward, beside = lax.optimization_barrier((across, inward, beside))
        relayed = jnp.where(middle, across, 0)
        paired = send(joined(near_terms[1], relayed), (0, 1), (1, 0), (2, 3), (3, 2))
        centre = send(joined(near_terms[2], inward), (1, 2), (2, 1))
        return joined(own_term, jnp.where(middle, centre, across), paired), beside
    terms = {1: near_terms[1], -1: near_terms[2], size - 1: far_terms[0], 1 - size: far_terms[0]}
    for distance in range(size - 2, 1, -1):
        terms[distance], terms[-distance] = far_terms[2 * (size - 1 - distance) - 1 :][:2]
    going_up = going_down = None
    for step in range(1, size):
        to_up = terms[size - step]
        to_down = terms[step - size]
        if step > 1:
            to_up = joined(to_up, going_up)
            to_down = joined(to_down, going_down)
        going_up = send(to_up, *[(i, i + 1) for i in range(step)])
        going_down = send(to_down, *[(i, i - 1) for i in range(size - step, size)])
    return joined(own_term, going_up, going_down), beside


def on_device(
    hidden,
    norm_gain,
    qkv_weight,
    out_weight,
    adapter_down,
    adapter_up,
    vocab_rows,
    segments,
    request_adapter,
    adapter_slot,
    page_table,
):
    groups = lax.axis_size("group")
    shards = lax.axis_size("mp")
    own_shard = lax.axis_index("mp")
    count, model_width = hidden.shape
    per_group = page_table.shape[0] // groups
    per_peer = per_group // groups
    page_len = count // per_group
    dims = (groups, per_group, per_peer, page_len)
    qkv_cols = qkv_weight.shape[1]
    heads = qkv_cols // HEAD
    low = adapter_down.shape[1]
    inner = heads * HD
    width = model_width // shards
    sent = low + qkv_cols
    tall = per_peer * page_len
    packed = packing(tall, sent)[-1]
    some = shards * vocab_rows.shape[0]
    scored = groups * some
    aside = packing(some, inner + low + width)[-1] + packing(tall, width)[-1]
    shape = jax.ShapeDtypeStruct
    dma = pltpu.SemaphoreType.DMA
    picked = pltpu.SMEM((groups * per_peer + 1,), jnp.int32)

    left, right, cols = [jnp.asarray(t) for t in feature_tables()]
    segrow = segments.reshape(1, count)
    request_ids = jnp.arange(request_adapter.shape[0], dtype=jnp.int32)
    adapter_ids = jnp.arange(adapter_slot.shape[0], dtype=jnp.int32)

    outgoing = kernel_call(
        functools.partial(project_kernel, dims),
        pltpu.HBM((groups, packed, LANES), BF),
        [SMEM, ANY, VMEM, ANY, ANY],
        ANY,
        [
            pltpu.VMEM((count, model_width), BF),
            pltpu.VMEM((qkv_cols, model_width), BF),
            pltpu.VMEM((model_width, low), BF),
            pltpu.VMEM((count, model_width), BF),
            pltpu.VMEM((count, sent), F32),
            pltpu.VMEM((groups, packed, LANES), BF),
            picked,
            dma((7 + groups,)),
        ],
        2 * count * model_width * sent,
        2 * (count * model_width + model_width * sent),
    )(page_table, hidden, norm_gain, qkv_weight.T, adapter_down)
    arrived = exchange(outgoing, "group")

    after_vocab, after_adapter, later_hidden, _ = lax.optimization_barrier(
        (vocab_rows, request_adapter, hidden, outgoing)
    )
    some_vocab = ring_rows(after_vocab, "mp")
    request_slot = jnp.sum(jnp.where(after_adapter[:, None] == adapter_ids[None, :], adapter_slot[None, :], 0), axis=1)
    slots = jnp.sum(jnp.where(segrow == request_ids[:, None], request_slot[:, None], 0), axis=0, keepdims=True)
    slotrow = slots - own_shard * (low // RANK)
    window = window_size(shards, model_width)
    ahead = packing(some, inner + low + width)[-1]
    beside = kernel_call(
        functools.partial(residual_kernel, dims, shards, ahead),
        pltpu.HBM((groups, aside, LANES), BF),
        [SMEM, ANY],
        ANY,
        [
            pltpu.VMEM((count, window), BF),
            pltpu.VMEM((count, width), F32),
            pltpu.VMEM((groups, packing(tall, width)[-1], LANES), BF),
            picked,
            dma((groups + 1,)),
        ],
        1,
        1,
    )(page_table, later_hidden)
    beside = kernel_call(
        functools.partial(products_kernel, groups, shards),
        pltpu.HBM((groups, aside, LANES), BF),
        [ANY, ANY] + [VMEM] * shards + [ANY],
        ANY,
        [
            pltpu.VMEM((some, model_width), BF),
            pltpu.VMEM((inner, model_width), BF),
            pltpu.VMEM((low, model_width), BF),
            pltpu.VMEM((some, inner + low + width), F32),
            pltpu.VMEM((ahead, LANES), BF),
            dma((groups + 1 + heads,)),
        ],
        2 * some * model_width * (inner + low),
        2 * count * model_width,
        44 * MIB,
        {2 + shards: 0},
    )(out_weight, adapter_up, *some_vocab, beside)
    arrived, beside, slotrow = lax.optimization_barrier((arrived, beside, slotrow))

    ordered, ordered_t, state, nd = kernel_call(
        functools.partial(group_kernel, dims, low, heads),
        (
            pltpu.HBM((count, qkv_cols), BF),
            pltpu.HBM((sent, count), BF),
            pltpu.HBM((heads, PHI_PAD, LANES), BF),
            pltpu.HBM((heads, LANES, count), F32),
        ),
        [SMEM] + [VMEM] * 5,
        (ANY, ANY, ANY, ANY),
        [
            pltpu.VMEM((heads, PHI_PAD, LANES), BF),
            pltpu.VMEM((count, sent), F32),
            pltpu.VMEM((count, sent), F32),
            pltpu.VMEM((count, qkv_cols), BF),
            pltpu.VMEM((sent, count), BF),
            pltpu.VMEM((heads, LANES, count), F32),
            pltpu.VMEM((count, count), F32),
            pltpu.SMEM((groups,), jnp.int32),
            dma((3 + heads,)),
        ],
        heads * 2 * count * count * 512,
        6 * count * sent,
        40 * MIB,
    )(page_table, arrived, segrow, left, right, cols)
    beside, state = lax.optimization_barrier((beside, state))
    beside = exchange(beside, "group")
    state = lax.ppermute(state, "group", [(i, i + 1) for i in range(groups - 1)])

    far, near = len(far_tables(shards)), len(near_tables(shards))
    part = pltpu.HBM((width, count), BF)
    *far_terms, inputs, kept_state = kernel_call(
        functools.partial(finish_kernel, low, heads, shards),
        [part] * far + [pltpu.HBM((inner + low, count), BF), pltpu.HBM((heads, PHI_PAD, LANES), BF)],
        [ANY] * 2 + [VMEM] * 6 + [ANY] * 2,
        [ANY] * (far + 2),
        [
            pltpu.VMEM((heads, FEAT, count), BF),
            pltpu.VMEM((heads, LANES, count), F32),
            pltpu.VMEM((far, inner + low, window), BF),
            pltpu.VMEM((inner + low, count), BF),
            pltpu.VMEM((far, width, count), BF),
            dma((far + 2 * heads + 3,)),
            dma((2 * far,)),
        ],
        20 * count * (inner + low) * model_width,
        40 * count * model_width,
    )(ordered_t, nd, state, segrow, slotrow, left, right, cols, out_weight, adapter_up)
    near_terms = kernel_call(
        functools.partial(near_kernel, shards),
        [part] * near,
        [ANY] * 3,
        [ANY] * near,
        [
            pltpu.VMEM((near, inner + low, window), BF),
            pltpu.VMEM((inner + low, count), BF),
            pltpu.VMEM((near, width, count), BF),
            dma((near + 1,)),
            dma((2 * near,)),
        ],
        1,
        1,
    )(out_weight, adapter_up, inputs)

    [logits] = staged_call(
        functools.partial(logits_kernel, dims, shards, width),
        [shape((shards, scored, count // shards), BF)],
        [page_table],
        [inputs],
        [
            pltpu.VMEM((scored, inner + low + width), BF),
            pltpu.VMEM((inner + low + width, count), BF),
            pltpu.VMEM((count, width), F32),
            pltpu.VMEM((count, width), F32),
            pltpu.SMEM((groups,), jnp.int32),
        ],
        1,
        1,
        given=[beside],
        limit=(40 if scored <= 512 else 56) * MIB,
    )
    [state_norms] = staged_call(
        functools.partial(norms_kernel, low, heads),
        [shape((heads, count), F32)],
        [],
        [ordered, ordered_t, kept_state, segrow, left, right, cols],
        [pltpu.VMEM((count, count), F32)],
        1,
        1,
    )
    update, [state_norms, _] = line_sums(far_terms, near_terms, "mp", [state_norms, logits])
    logits = exchange(logits, "mp")
    best = kernel_call(
        functools.partial(best_kernel, shards),
        shape((1, count // shards), F32),
        [VMEM],
        VMEM,
        [],
        1,
        1,
        32 * MIB,
    )(logits)
    return update.T, state_norms, best.reshape(-1)


def solution(mesh):
    placed = (
        P("group", None),
        P(),
        P(None, "mp"),
        P("mp", None),
        P(None, "mp"),
        P("mp", None),
        P(("group", "mp"), None),
        P("group"),
        P(),
        P(),
        P(),
    )
    return jax.shard_map(
        on_device,
        mesh=mesh,
        in_specs=placed,
        out_specs=(P("group", "mp"), P("mp", "group"), P(("group", "mp"))),
        check_vma=False,
    )
```

```python
import functools

import jax
import jax.numpy as jnp
import numpy as np
from jax import lax
from jax.experimental import pallas as pl
from jax.experimental.pallas import tpu as pltpu
from jax.sharding import PartitionSpec as P

FEAT = 16
HD = 112
RANK = 16
EPSILON = 1e-05
HEAD = 2 * FEAT + HD
PHI = 1 + FEAT + FEAT * (FEAT + 1) // 2
PHI_PAD = 160
LANES = 128
ONE, TAG, REST = HD, HD + 1, HD + 2
MIB = 1024 * 1024
VMEM_LIMIT = 60 * MIB

BF = jnp.bfloat16
F32 = jnp.float32
SMEM = pl.BlockSpec(memory_space=pltpu.SMEM)
VMEM = pl.BlockSpec(memory_space=pltpu.VMEM)
ANY = pl.BlockSpec(memory_space=pltpu.HBM)


def feature_tables():
    left = np.zeros((PHI_PAD, FEAT), np.float32)
    right = np.zeros((PHI_PAD, FEAT), np.float32)
    cols = np.zeros((PHI_PAD, 8), np.float32)
    cols[0, :3] = 1.0
    at = 1
    for i in range(FEAT):
        left[at, i] = 1.0
        cols[at, 1] = 1.0
        cols[at, 2] = FEAT**-0.25
        at += 1
    for i in range(FEAT):
        for j in range(i, FEAT):
            left[at, i] = 1.0
            right[at, j] = 1.0
            cols[at, 2] = (1.0 if i == j else 2.0**0.5) / (2.0 * FEAT) ** 0.5
            at += 1
    return left.astype(jnp.bfloat16), right.astype(jnp.bfloat16), cols


def dot(a, b, dims=((1,), (0,))):
    return lax.dot_general(a, b, (dims, ((), ())), preferred_element_type=F32)


def kernel_call(body, out_shape, in_specs, out_specs, scratch, flops, nbytes, limit=VMEM_LIMIT, aliases=None):
    return pl.pallas_call(
        body,
        out_shape=out_shape,
        in_specs=in_specs,
        out_specs=out_specs,
        scratch_shapes=scratch,
        input_output_aliases=aliases or {},
        compiler_params=pltpu.CompilerParams(vmem_limit_bytes=limit),
        cost_estimate=pl.CostEstimate(flops=flops, bytes_accessed=nbytes, transcendentals=0),
    )


def start(source, target, sem):
    copy = pltpu.make_async_copy(source, target, sem)
    copy.start()
    return copy


def packing(rows, columns):
    tiles, rest = divmod(columns, LANES)
    share = LANES // rest if rest and LANES % rest == 0 else 1
    if rows % (16 * share):
        share = 1
    return tiles, rest, share, tiles * rows + (rows // share if rest else 0)


def pack(block, target, base):
    rows = block.shape[0]
    tiles, rest, share, _ = packing(*block.shape)
    for t in range(tiles):
        target[base + t * rows : base + (t + 1) * rows, :] = block[:, t * LANES : (t + 1) * LANES].astype(BF)
    if rest:
        short = rows // share
        last = [block[q * short : (q + 1) * short, tiles * LANES :] for q in range(share)]
        if share * rest < LANES:
            last.append(jnp.zeros((short, LANES - share * rest), block.dtype))
        at = base + tiles * rows
        target[at : at + short, :] = jnp.concatenate(last, axis=1).astype(BF)


def unpack(source, base, target, row, rows, columns):
    tiles, rest, share, _ = packing(rows, columns)
    for t in range(tiles):
        piece = source[base + t * rows : base + (t + 1) * rows, :]
        target[row : row + rows, t * LANES : (t + 1) * LANES] = piece.astype(target.dtype)
    if rest:
        short = rows // share
        at = base + tiles * rows
        last = source[at : at + short, :].astype(F32)
        for q in range(share):
            piece = last[:, q * rest : (q + 1) * rest].astype(target.dtype)
            target[row + q * short : row + (q + 1) * short, tiles * LANES : columns] = piece


def staged_call(body, out_shape, scalars, operands, scratch, flops, nbytes, given=(), limit=VMEM_LIMIT):
    buffers = [pltpu.VMEM(x.shape, x.dtype) for x in list(operands) + list(out_shape)]
    ins, outs = len(operands), len(out_shape)

    def run(*refs):
        values, refs = refs[: len(scalars)], refs[len(scalars) :]
        ready, refs = refs[: len(given)], refs[len(given) :]
        far, refs = refs[: ins + outs], refs[ins + outs :]
        near, extra, sems = refs[: ins + outs], refs[ins + outs : -1], refs[-1]
        loads = [start(far[k], near[k], sems.at[k]) for k in range(ins)]
        for load in loads:
            load.wait()
        body(*values, *ready, *near, *extra)
        sends = [start(near[k], far[k], sems.at[k]) for k in range(ins, ins + outs)]
        for send in sends:
            send.wait()

    return kernel_call(
        run,
        [pltpu.HBM(x.shape, x.dtype) for x in out_shape],
        [SMEM] * len(scalars) + [VMEM] * len(given) + [ANY] * ins,
        [ANY] * outs,
        buffers + list(scratch) + [pltpu.SemaphoreType.DMA((ins + outs,))],
        flops,
        nbytes,
        limit,
    )(*scalars, *given, *operands)


def pick_pages(table, own, picked, groups, per_group, per_peer):
    def one_group(g, carry):
        spot = g * per_peer
        for k in range(per_group):
            local = table[g * per_group + k] - own * per_group
            picked[spot] = local
            spot = spot + jnp.where((local >= 0) & (local < per_group), 1, 0)
        return carry

    lax.fori_loop(0, groups, one_group, 0)


def place_pages(table, own, seen, source, target, groups, per_group, per_peer, page_len):
    for g in range(groups):
        seen[g] = 0
    for k in range(per_group):
        holder = lax.div(table[own * per_group + k], per_group)
        slot = holder * per_peer + seen[holder]
        seen[holder] = seen[holder] + 1
        start = pl.multiple_of(slot * page_len, page_len)
        target[k * page_len : (k + 1) * page_len, :] = source[pl.ds(start, page_len), :]


def picked_rows(source, picked, g, per_peer, page_len):
    pages = []
    for b in range(per_peer):
        at = pl.multiple_of(picked[g * per_peer + b] * page_len, page_len)
        pages.append(source[pl.ds(at, page_len), :])
    return jnp.concatenate(pages, axis=0)


def project_kernel(
    dims, table, hidden_in, gain, wq_in, wd_in, out_in, hidden, wq, wd, normed, wide, out, picked, sems
):
    groups, per_group, per_peer, page_len = dims
    rows, model_width = hidden.shape
    low = wd.shape[1]
    pieces = 4
    part = rows // pieces
    strip = wq.shape[0] // 2
    loads = [
        start(hidden_in.at[pl.ds(k * part, part)], hidden.at[pl.ds(k * part, part)], sems.at[k]) for k in range(pieces)
    ]
    weights = [start(wd_in, wd, sems.at[pieces])]
    for k in range(2):
        half = pl.ds(k * strip, strip)
        weights.append(start(wq_in.at[half], wq.at[half], sems.at[pieces + 1 + k]))
    pick_pages(table, lax.axis_index("group"), picked, groups, per_group, per_peer)
    step = 32
    scale = gain[...].reshape(1, model_width)

    def norm_rows(i, carry):
        at = pl.ds(pl.multiple_of(i * step, step), step)
        x = hidden[at, :].astype(F32)
        meansq = jnp.mean(x * x, axis=-1, keepdims=True)
        normed[at, :] = (x * lax.rsqrt(meansq + EPSILON) * scale).astype(BF)
        return carry

    for k in range(pieces):
        loads[k].wait()
        lax.fori_loop(k * part // step, (k + 1) * part // step, norm_rows, 0, unroll=2)
    for load in weights:
        load.wait()
    wide[:, :low] = dot(normed[...], wd[...])
    wide[:, low:] = dot(normed[...], wq[...], ((1,), (1,)))
    sends = []
    for g in range(groups):
        pack(picked_rows(wide, picked, g, per_peer, page_len), out.at[g], 0)
        sends.append(start(out.at[g], out_in.at[g], sems.at[pieces + 3 + g]))
    for send in sends:
        send.wait()


def residual_kernel(dims, shards, base, table, hidden_in, out_in, window, wide, pages, picked, sems):
    groups, per_group, per_peer, page_len = dims
    own_shard = lax.axis_index("mp")
    for j in range(shards):

        @pl.when(own_shard == j)
        def _(j=j):
            columns, _ = column_window(j, shards, hidden_in.shape[1])
            start(hidden_in.at[:, columns], window, sems.at[groups])

    pick_pages(table, lax.axis_index("group"), picked, groups, per_group, per_peer)
    pltpu.make_async_copy(hidden_in.at[:, 0 : window.shape[1]], window, sems.at[groups]).wait()
    for j in range(shards):

        @pl.when(own_shard == j)
        def _(j=j):
            _, at = column_window(j, shards, hidden_in.shape[1])
            wide[...] = window[:, at : at + wide.shape[1]].astype(F32)

    sends = []
    for g in range(groups):
        pack(picked_rows(wide, picked, g, per_peer, page_len), pages.at[g], 0)
        sends.append(start(pages.at[g], out_in.at[g, pl.ds(base, pages.shape[1])], sems.at[g]))
    for send in sends:
        send.wait()


def products_kernel(groups, shards, w_out_in, w_up_in, *refs):
    blocks = refs[:shards]
    _, out_in, vocab, w_out, w_up, products, shared, sems = refs[shards:]
    inner, model_width = w_out.shape
    low = w_up.shape[0]
    width = model_width // shards
    held = blocks[0].shape[0]
    loads = [start(w_up_in, w_up, sems.at[groups])]
    for k in range(inner // HD):
        rows = pl.ds(k * HD, HD)
        loads.append(start(w_out_in.at[rows], w_out.at[rows], sems.at[groups + 1 + k]))
    own_shard = lax.axis_index("mp")
    for i in range(shards):
        at = lax.rem(own_shard + i + 1, shards) * held
        vocab[pl.ds(pl.multiple_of(at, held), held), :] = blocks[i][...]
    for load in loads:
        load.wait()
    products[:, :inner] = dot(vocab[...], w_out[...], ((1,), (1,)))
    products[:, inner : inner + low] = dot(vocab[...], w_up[...], ((1,), (1,)))
    for j in range(shards):

        @pl.when(own_shard == j)
        def _(j=j):
            products[:, inner + low :] = vocab[:, j * width : (j + 1) * width].astype(F32)

    pack(products[...], shared, 0)
    sends = [start(shared, out_in.at[g, pl.ds(0, shared.shape[0])], sems.at[g]) for g in range(groups)]
    for send in sends:
        send.wait()


def phi_of(vectors, left, right, cols):
    first = dot(left[...], vectors) + cols[:, 0:1]
    second = dot(right[...], vectors) + cols[:, 1:2]
    return first * second * cols[:, 2:3]


def with_ones(values):
    lane = lax.broadcasted_iota(jnp.int32, (values.shape[0], LANES - HD), 1)
    return jnp.concatenate([values, jnp.where(lane == 0, 1.0, 0.0).astype(values.dtype)], axis=1)


def with_ones_t(values):
    row = lax.broadcasted_iota(jnp.int32, (LANES - HD, values.shape[1]), 0)
    return jnp.concatenate([values, jnp.where(row == 0, 1.0, 0.0).astype(values.dtype)], axis=0)


def same_upto(segrow):
    count = segrow.shape[1]
    ids = segrow[...].astype(F32)
    column = jnp.transpose(jnp.broadcast_to(ids, (8, count)))[:, 0:1]
    behind = lax.broadcasted_iota(jnp.int32, (count, count), 0)
    ahead = lax.broadcasted_iota(jnp.int32, (count, count), 1)
    return jnp.where((column == ids) & (behind <= ahead), 1.0, 0.0)


def group_kernel(
    dims, low, heads, table, arrived, segrow, left, right, cols, ordered_in, ordered_t_in, state_in, nd_in,
    state, wide, placed, ordered, ordered_t, nd, mask, seen, sems
):
    groups, per_group, per_peer, page_len = dims
    tall = per_peer * page_len
    count, sent = placed.shape
    mask[...] = same_upto(segrow)
    for g in range(groups):
        unpack(arrived.at[g], 0, wide, g * tall, tall, sent)
    place_pages(table, lax.axis_index("group"), seen, wide, placed, groups, per_group, per_peer, page_len)
    ordered[...] = placed[:, low:].astype(BF)
    for at in range(0, sent, LANES):
        end = min(at + LANES, sent)
        ordered_t[at:end, :] = jnp.transpose(placed[:, at:end]).astype(BF)
    sends = [start(ordered_t, ordered_t_in, sems.at[0]), start(ordered, ordered_in, sems.at[1])]

    last = segrow[:, count - 1 : count]
    member = jnp.where(segrow[...] == last, 1.0, 0.0)
    total = jnp.sum(member, axis=1, keepdims=True)
    fine = total - total.astype(BF).astype(F32)
    tag = last.astype(F32) + 1.0
    row = lax.broadcasted_iota(jnp.int32, (PHI_PAD, LANES), 0)
    lane = lax.broadcasted_iota(jnp.int32, (PHI_PAD, LANES), 1)
    block = 256 if count % 256 == 0 else count
    for h in range(heads):
        at = h * HEAD
        key = ordered[:, at + FEAT : at + 2 * FEAT] * BF(0.25)
        value = ordered[:, at + 2 * FEAT : at + HEAD]
        at = low + h * HEAD
        query_t = ordered_t[at : at + FEAT, :]
        key_t = ordered_t[at + FEAT : at + 2 * FEAT, :]
        extended_t = with_ones_t(ordered_t[at + 2 * FEAT : at + HEAD, :])

        phi = (phi_of(key_t, left, right, cols) * member).astype(BF)
        summed = dot(phi, with_ones(value))
        summed = jnp.where((row == 0) & (lane == TAG), tag, summed)
        summed = jnp.where((row == 0) & (lane == REST), fine, summed)
        state[h] = summed.astype(BF)

        for begin in range(0, count, block):
            end = begin + block
            s = dot(key[:end], query_t[:, begin:end])
            w = (1.0 + s * (1.0 + 0.5 * s)) * mask[:end, begin:end]
            nd[h, :, begin:end] = dot(extended_t[:, :end], w.astype(BF))
        sends.append(start(nd.at[h], nd_in.at[h], sems.at[3 + h]))
    sends.append(start(state, state_in, sems.at[2]))
    for send in sends:
        send.wait()


def split3(x):
    a = x.astype(BF)
    rest = x - a.astype(F32)
    b = rest.astype(BF)
    return jnp.concatenate([a, b, (rest - b.astype(F32)).astype(BF)], axis=0)


def state_corner(state):
    corner = state[0, 0:1, :].astype(F32)
    return corner[:, TAG : TAG + 1], corner[:, ONE : ONE + 1] + corner[:, REST : REST + 1]


def column_window(j, shards, model_width):
    width = model_width // shards
    size = window_size(shards, model_width)
    first = min(j * width // LANES * LANES, model_width - size)
    return slice(first, first + size), j * width - first


def window_size(shards, model_width):
    width = model_width // shards
    return max(-(-(j * width % LANES + width) // LANES) * LANES for j in range(shards))


def far_tables(shards):
    if shards == 4:
        return [(3, 3, 0, 0), (2, None, None, 1)]
    tables = [tuple({0: shards - 1, shards - 1: 0}.get(own) for own in range(shards))]
    for distance in range(shards - 2, 1, -1):
        tables += [offset_table(distance, shards), offset_table(-distance, shards)]
    return tables


def near_tables(shards):
    if shards == 4:
        return [(0, 1, 2, 3), (1, 0, 3, 2), (None, 2, 1, None)]
    return [offset_table(offset, shards) for offset in (0, 1, -1)]


def offset_table(offset, shards):
    return tuple(own + offset if 0 <= own + offset < shards else None for own in range(shards))


def each_shard(tables):
    for k, table in enumerate(tables):
        for own, j in enumerate(table):
            if j is not None:
                yield k, own, j


def shard_parts(tables, w_out_in, w_up_in, weights, w_sems, inputs, held_out, outs, sems):
    own_shard = lax.axis_index("mp")
    shards = len(tables[0])
    inner, model_width = w_out_in.shape
    width = model_width // shards

    def copies(k, j):
        window, _ = column_window(j, shards, model_width)
        return (
            pltpu.make_async_copy(w_out_in.at[:, window], weights.at[k, pl.ds(0, inner)], w_sems.at[2 * k]),
            pltpu.make_async_copy(
                w_up_in.at[:, window], weights.at[k, pl.ds(inner, w_up_in.shape[0])], w_sems.at[2 * k + 1]
            ),
        )

    def fetch():
        for k, own, j in each_shard(tables):

            @pl.when(own_shard == own)
            def _(k=k, j=j):
                for copy in copies(k, j):
                    copy.start()

    def compute():
        for k, own, j in each_shard(tables):

            @pl.when(own_shard == own)
            def _(k=k, j=j):
                for copy in copies(k, j):
                    copy.wait()
                _, at = column_window(j, shards, model_width)
                held_out[k] = dot(weights[k, :, at : at + width], inputs[...], ((0,), (0,))).astype(BF)
                start(held_out.at[k], outs[k], sems.at[k])

    def finish():
        for k, own, j in each_shard(tables):

            @pl.when(own_shard == own)
            def _(k=k):
                pltpu.make_async_copy(held_out.at[k], outs[k], sems.at[k]).wait()

    return fetch, compute, finish


def finish_kernel(
    low, heads, shards, ordered_t_in, nd_in, state, segrow, slotrow, left, right, cols, w_out_in, w_up_in, *refs
):
    far = far_tables(shards)
    outs = refs[: len(far)]
    inputs_in, state_in, queries, nd, weights, inputs, held_out, sems, w_sems = refs[len(far) :]
    inner = heads * HD
    sem = iter(range(len(far), len(far) + 2 * heads + 3))
    lows = start(ordered_t_in.at[pl.ds(0, low)], inputs.at[pl.ds(inner, low)], sems.at[next(sem)])
    fetches = []
    for h in range(heads):
        rows = pl.ds(low + h * HEAD, FEAT)
        fetches.append(start(ordered_t_in.at[rows], queries.at[h], sems.at[next(sem)]))
        fetches.append(start(nd_in.at[h], nd.at[h], sems.at[next(sem)]))
    fetch_weights, compute, finish = shard_parts(
        far, w_out_in, w_up_in, weights, w_sems, inputs, held_out, outs, sems
    )
    fetch_weights()
    tag, _ = state_corner(state)
    carried = jnp.where(segrow[...].astype(F32) + 1.0 == tag, 1.0, 0.0)
    row_slot = lax.div(lax.broadcasted_iota(jnp.int32, (low, 1), 0), RANK)
    lows.wait()
    lowered = jnp.where(slotrow[...] == row_slot, inputs[inner:, :].astype(F32), 0.0)
    inputs[inner:, :] = lowered.astype(BF)
    for h in range(heads):
        fetches[2 * h].wait()
        fetches[2 * h + 1].wait()
        cross = dot(state[h], phi_of(queries[h], left, right, cols).astype(BF), ((0,), (0,)))
        both = nd[h] + carried * cross
        inputs[h * HD : (h + 1) * HD, :] = (both[:HD, :] / both[ONE : ONE + 1, :]).astype(BF)
    compute()
    kept = [start(inputs, inputs_in, sems.at[next(sem)]), start(state, state_in, sems.at[next(sem)])]
    finish()
    for copy in kept:
        copy.wait()


def near_kernel(shards, w_out_in, w_up_in, inputs_in, *refs):
    near = near_tables(shards)
    outs = refs[: len(near)]
    weights, inputs, held_out, sems, w_sems = refs[len(near) :]
    load = start(inputs_in, inputs, sems.at[len(near)])
    fetch, compute, finish = shard_parts(near, w_out_in, w_up_in, weights, w_sems, inputs, held_out, outs, sems)
    fetch()
    load.wait()
    compute()
    finish()


def logits_kernel(dims, shards, width, table, arrived, inputs, out, vocab, both, wide, placed, seen):
    groups, per_group, per_peer, page_len = dims
    tall = per_peer * page_len
    inner = inputs.shape[0]
    rows = vocab.shape[0] // groups
    _, _, _, base = packing(rows, inner + width)
    for g in range(groups):
        unpack(arrived.at[g], 0, vocab, g * rows, rows, inner + width)
        unpack(arrived.at[g], base, wide, g * tall, tall, width)
    place_pages(table, lax.axis_index("group"), seen, wide, placed, groups, per_group, per_peer, page_len)
    both[:inner, :] = inputs[...]
    both[inner:, :] = jnp.transpose(placed[...]).astype(BF)
    block = inputs.shape[1] // shards
    scored = dot(vocab[...], both[...])
    for j in range(shards):
        out[j] = scored[:, j * block : (j + 1) * block].astype(BF)


def norms_kernel(low, heads, ordered, ordered_t, state, segrow, left, right, cols, norms, mask):
    count = segrow.shape[1]
    mask[...] = same_upto(segrow)
    upto = mask[...].astype(BF)
    tag, held = state_corner(state)
    carried = jnp.where(segrow[...].astype(F32) + 1.0 == tag, 1.0, 0.0)
    value_lane = lax.broadcasted_iota(jnp.int32, (1, LANES), 1) < HD
    counted = carried * held + jnp.sum(mask[...], axis=0, keepdims=True)
    block = 256 if count % 256 == 0 else count
    increments = []
    before = []
    for h in range(heads):
        at = h * HEAD
        key = ordered[:, at + FEAT : at + 2 * FEAT] * BF(0.25)
        value = ordered[:, at + 2 * FEAT : at + HEAD]
        at = low + h * HEAD
        key_t = ordered_t[at + FEAT : at + 2 * FEAT, :]
        value_t = ordered_t[at + 2 * FEAT : at + HEAD, :]
        wide_key = key_t.astype(F32)
        wide_value = value_t.astype(F32)
        self_score = 0.25 * jnp.sum(wide_key * wide_key, axis=0, keepdims=True)
        self_value = jnp.sum(wide_value * wide_value, axis=0, keepdims=True)
        diagonal = (1.0 + self_score * (1.0 + 0.5 * self_score)) * self_value
        below = []
        for begin in range(0, count, block):
            end = begin + block
            kk = dot(key[:end], key_t[:, begin:end])
            vv = dot(value[:end], value_t[:, begin:end])
            gram = (1.0 + kk * (1.0 + 0.5 * kk)) * vv * mask[:end, begin:end]
            below.append(jnp.sum(gram, axis=0, keepdims=True))
        added = 2.0 * jnp.concatenate(below, axis=1) - diagonal
        held_state = state[h]
        against = dot(held_state, phi_of(key_t, left, right, cols).astype(BF), ((0,), (0,)))[:HD, :]
        along = jnp.sum(against * wide_value, axis=0, keepdims=True)
        increments.append(added + 2.0 * carried * along)
        wide_state = jnp.where(value_lane, held_state.astype(F32), 0.0)
        per_lane = jnp.sum(wide_state * wide_state, axis=0, keepdims=True)
        before.append(jnp.sum(per_lane, axis=1, keepdims=True))
    if heads % 8:
        increments.append(jnp.zeros((8 - heads % 8, count), F32))
    stacked = split3(jnp.concatenate(increments, axis=0))
    thrice = dot(stacked, upto)
    rows = thrice.shape[0] // 3
    summed = thrice[:rows] + thrice[rows : 2 * rows] + thrice[2 * rows :]
    for h in range(heads):
        total = carried * before[h] + summed[h : h + 1, :]
        norms[h : h + 1, :] = jnp.sqrt(total / (counted * float(FEAT * HD)))


def best_kernel(shards, pieces, best):
    whole = pieces[0].astype(F32)
    for i in range(1, shards):
        whole = whole + pieces[i].astype(F32)
    best[...] = jnp.max(whole, axis=0, keepdims=True)


def exchange(blocks, axis):
    return lax.all_to_all(blocks, axis, split_axis=0, concat_axis=0, tiled=True)


def ring_rows(values, axis):
    size = lax.axis_size(axis)
    steps = [lax.ppermute(values, axis, [(i, (i + by) % size) for i in range(size)]) for by in range(size - 1, 0, -1)]
    return [*steps, values]


def joined(*parts):
    return sum(part.astype(F32) for part in parts).astype(BF)


def line_sums(far_terms, near_terms, axis, beside):
    size = lax.axis_size(axis)

    def send(values, *pairs):
        return lax.ppermute(values, axis, pairs)

    own_term = near_terms[0]
    if size == 4:
        outward = send(far_terms[0], (1, 2), (2, 1))
        inward = send(far_terms[1], (0, 1), (3, 2))
        ends, _ = lax.optimization_barrier((far_terms[0], own_term))
        across = send(ends, (0, 3), (3, 0))
        outward, inward, first = lax.optimization_barrier((outward, inward, beside))
        paired = send(joined(near_terms[1], outward), (0, 1), (1, 0), (2, 3), (3, 2))
        centre = send(joined(near_terms[2], inward), (1, 2), (2, 1))
        across, beside = lax.optimization_barrier((across, [first[0], beside[1]]))
        return (own_term, across, paired, centre), beside
    terms = {1: near_terms[1], -1: near_terms[2], size - 1: far_terms[0], 1 - size: far_terms[0]}
    for distance in range(size - 2, 1, -1):
        terms[distance], terms[-distance] = far_terms[2 * (size - 1 - distance) - 1 :][:2]
    going_up = going_down = None
    for step in range(1, size):
        to_up = terms[size - step]
        to_down = terms[step - size]
        if step > 1:
            to_up = joined(to_up, going_up)
            to_down = joined(to_down, going_down)
        going_up = send(to_up, *[(i, i + 1) for i in range(step)])
        going_down = send(to_down, *[(i, i - 1) for i in range(size - step, size)])
    return (own_term, going_up, going_down), beside


def on_device(
    hidden,
    norm_gain,
    qkv_weight,
    out_weight,
    adapter_down,
    adapter_up,
    vocab_rows,
    segments,
    request_adapter,
    adapter_slot,
    page_table,
):
    groups = lax.axis_size("group")
    shards = lax.axis_size("mp")
    own_shard = lax.axis_index("mp")
    count, model_width = hidden.shape
    per_group = page_table.shape[0] // groups
    per_peer = per_group // groups
    page_len = count // per_group
    dims = (groups, per_group, per_peer, page_len)
    qkv_cols = qkv_weight.shape[1]
    heads = qkv_cols // HEAD
    low = adapter_down.shape[1]
    inner = heads * HD
    width = model_width // shards
    sent = low + qkv_cols
    tall = per_peer * page_len
    packed = packing(tall, sent)[-1]
    some = shards * vocab_rows.shape[0]
    scored = groups * some
    aside = packing(some, inner + low + width)[-1] + packing(tall, width)[-1]
    shape = jax.ShapeDtypeStruct
    dma = pltpu.SemaphoreType.DMA
    picked = pltpu.SMEM((groups * per_peer + 1,), jnp.int32)

    left, right, cols = [jnp.asarray(t) for t in feature_tables()]
    segrow = segments.reshape(1, count)
    request_ids = jnp.arange(request_adapter.shape[0], dtype=jnp.int32)
    adapter_ids = jnp.arange(adapter_slot.shape[0], dtype=jnp.int32)

    outgoing = kernel_call(
        functools.partial(project_kernel, dims),
        pltpu.HBM((groups, packed, LANES), BF),
        [SMEM, ANY, VMEM, ANY, ANY],
        ANY,
        [
            pltpu.VMEM((count, model_width), BF),
            pltpu.VMEM((qkv_cols, model_width), BF),
            pltpu.VMEM((model_width, low), BF),
            pltpu.VMEM((count, model_width), BF),
            pltpu.VMEM((count, sent), F32),
            pltpu.VMEM((groups, packed, LANES), BF),
            picked,
            dma((7 + groups,)),
        ],
        2 * count * model_width * sent,
        2 * (count * model_width + model_width * sent),
    )(page_table, hidden, norm_gain, qkv_weight.T, adapter_down)
    arrived = exchange(outgoing, "group")

    after_vocab, after_adapter, later_hidden, _ = lax.optimization_barrier(
        (vocab_rows, request_adapter, hidden, outgoing)
    )
    some_vocab = ring_rows(after_vocab, "mp")
    request_slot = jnp.sum(jnp.where(after_adapter[:, None] == adapter_ids[None, :], adapter_slot[None, :], 0), axis=1)
    slots = jnp.sum(jnp.where(segrow == request_ids[:, None], request_slot[:, None], 0), axis=0, keepdims=True)
    slotrow = slots - own_shard * (low // RANK)
    window = window_size(shards, model_width)
    ahead = packing(some, inner + low + width)[-1]
    beside = kernel_call(
        functools.partial(residual_kernel, dims, shards, ahead),
        pltpu.HBM((groups, aside, LANES), BF),
        [SMEM, ANY],
        ANY,
        [
            pltpu.VMEM((count, window), BF),
            pltpu.VMEM((count, width), F32),
            pltpu.VMEM((groups, packing(tall, width)[-1], LANES), BF),
            picked,
            dma((groups + 1,)),
        ],
        1,
        1,
    )(page_table, later_hidden)
    beside = kernel_call(
        functools.partial(products_kernel, groups, shards),
        pltpu.HBM((groups, aside, LANES), BF),
        [ANY, ANY] + [VMEM] * shards + [ANY],
        ANY,
        [
            pltpu.VMEM((some, model_width), BF),
            pltpu.VMEM((inner, model_width), BF),
            pltpu.VMEM((low, model_width), BF),
            pltpu.VMEM((some, inner + low + width), F32),
            pltpu.VMEM((ahead, LANES), BF),
            dma((groups + 1 + heads,)),
        ],
        2 * some * model_width * (inner + low),
        2 * count * model_width,
        44 * MIB,
        {2 + shards: 0},
    )(out_weight, adapter_up, *some_vocab, beside)
    arrived, beside, slotrow = lax.optimization_barrier((arrived, beside, slotrow))

    ordered, ordered_t, state, nd = kernel_call(
        functools.partial(group_kernel, dims, low, heads),
        (
            pltpu.HBM((count, qkv_cols), BF),
            pltpu.HBM((sent, count), BF),
            pltpu.HBM((heads, PHI_PAD, LANES), BF),
            pltpu.HBM((heads, LANES, count), F32),
        ),
        [SMEM] + [VMEM] * 5,
        (ANY, ANY, ANY, ANY),
        [
            pltpu.VMEM((heads, PHI_PAD, LANES), BF),
            pltpu.VMEM((count, sent), F32),
            pltpu.VMEM((count, sent), F32),
            pltpu.VMEM((count, qkv_cols), BF),
            pltpu.VMEM((sent, count), BF),
            pltpu.VMEM((heads, LANES, count), F32),
            pltpu.VMEM((count, count), F32),
            pltpu.SMEM((groups,), jnp.int32),
            dma((3 + heads,)),
        ],
        heads * 2 * count * count * 512,
        6 * count * sent,
        40 * MIB,
    )(page_table, arrived, segrow, left, right, cols)
    beside, state = lax.optimization_barrier((beside, state))
    beside = exchange(beside, "group")
    state = lax.ppermute(state, "group", [(i, i + 1) for i in range(groups - 1)])

    far, near = len(far_tables(shards)), len(near_tables(shards))
    part = pltpu.HBM((width, count), BF)
    *far_terms, inputs, kept_state = kernel_call(
        functools.partial(finish_kernel, low, heads, shards),
        [part] * far + [pltpu.HBM((inner + low, count), BF), pltpu.HBM((heads, PHI_PAD, LANES), BF)],
        [ANY] * 2 + [VMEM] * 6 + [ANY] * 2,
        [ANY] * (far + 2),
        [
            pltpu.VMEM((heads, FEAT, count), BF),
            pltpu.VMEM((heads, LANES, count), F32),
            pltpu.VMEM((far, inner + low, window), BF),
            pltpu.VMEM((inner + low, count), BF),
            pltpu.VMEM((far, width, count), BF),
            dma((far + 2 * heads + 3,)),
            dma((2 * far,)),
        ],
        20 * count * (inner + low) * model_width,
        40 * count * model_width,
    )(ordered_t, nd, state, segrow, slotrow, left, right, cols, out_weight, adapter_up)
    near_terms = kernel_call(
        functools.partial(near_kernel, shards),
        [part] * near,
        [ANY] * 3,
        [ANY] * near,
        [
            pltpu.VMEM((near, inner + low, window), BF),
            pltpu.VMEM((inner + low, count), BF),
            pltpu.VMEM((near, width, count), BF),
            dma((near + 1,)),
            dma((2 * near,)),
        ],
        1,
        1,
    )(out_weight, adapter_up, inputs)

    [logits] = staged_call(
        functools.partial(logits_kernel, dims, shards, width),
        [shape((shards, scored, count // shards), BF)],
        [page_table],
        [inputs],
        [
            pltpu.VMEM((scored, inner + low + width), BF),
            pltpu.VMEM((inner + low + width, count), BF),
            pltpu.VMEM((count, width), F32),
            pltpu.VMEM((count, width), F32),
            pltpu.SMEM((groups,), jnp.int32),
        ],
        1,
        1,
        given=[beside],
        limit=(40 if scored <= 512 else 56) * MIB,
    )
    [state_norms] = staged_call(
        functools.partial(norms_kernel, low, heads),
        [shape((heads, count), F32)],
        [],
        [ordered, ordered_t, kept_state, segrow, left, right, cols],
        [pltpu.VMEM((count, count), F32)],
        1,
        1,
    )
    terms, [state_norms, logits] = line_sums(far_terms, near_terms, "mp", [state_norms, logits])
    logits = exchange(logits, "mp")
    best = kernel_call(
        functools.partial(best_kernel, shards),
        shape((1, count // shards), F32),
        [VMEM],
        VMEM,
        [],
        1,
        1,
        32 * MIB,
    )(logits)
    terms, best = lax.optimization_barrier((terms, best))
    return joined(*terms).T, state_norms, best.reshape(-1)


def solution(mesh):
    placed = (
        P("group", None),
        P(),
        P(None, "mp"),
        P("mp", None),
        P(None, "mp"),
        P("mp", None),
        P(("group", "mp"), None),
        P("group"),
        P(),
        P(),
        P(),
    )
    return jax.shard_map(
        on_device,
        mesh=mesh,
        in_specs=placed,
        out_specs=(P("group", "mp"), P("mp", "group"), P(("group", "mp"))),
        check_vma=False,
    )
```

```python
import functools

import jax
import jax.numpy as jnp
import numpy as np
from jax import lax
from jax.experimental import pallas as pl
from jax.experimental.pallas import tpu as pltpu
from jax.sharding import PartitionSpec as P

FEAT = 16
HD = 112
RANK = 16
EPSILON = 1e-05
HEAD = 2 * FEAT + HD
PHI = 1 + FEAT + FEAT * (FEAT + 1) // 2
PHI_PAD = 160
LANES = 128
ONE, TAG, REST = HD, HD + 1, HD + 2
MIB = 1024 * 1024
VMEM_LIMIT = 60 * MIB

BF = jnp.bfloat16
F32 = jnp.float32
SMEM = pl.BlockSpec(memory_space=pltpu.SMEM)
VMEM = pl.BlockSpec(memory_space=pltpu.VMEM)
ANY = pl.BlockSpec(memory_space=pltpu.HBM)


def feature_tables():
    left = np.zeros((PHI_PAD, FEAT), np.float32)
    right = np.zeros((PHI_PAD, FEAT), np.float32)
    cols = np.zeros((PHI_PAD, 8), np.float32)
    cols[0, :3] = 1.0
    at = 1
    for i in range(FEAT):
        left[at, i] = 1.0
        cols[at, 1] = 1.0
        cols[at, 2] = FEAT**-0.25
        at += 1
    for i in range(FEAT):
        for j in range(i, FEAT):
            left[at, i] = 1.0
            right[at, j] = 1.0
            cols[at, 2] = (1.0 if i == j else 2.0**0.5) / (2.0 * FEAT) ** 0.5
            at += 1
    return left.astype(jnp.bfloat16), right.astype(jnp.bfloat16), cols


def dot(a, b, dims=((1,), (0,))):
    return lax.dot_general(a, b, (dims, ((), ())), preferred_element_type=F32)


def kernel_call(body, out_shape, in_specs, out_specs, scratch, flops, nbytes, limit=VMEM_LIMIT, aliases=None):
    return pl.pallas_call(
        body,
        out_shape=out_shape,
        in_specs=in_specs,
        out_specs=out_specs,
        scratch_shapes=scratch,
        input_output_aliases=aliases or {},
        compiler_params=pltpu.CompilerParams(vmem_limit_bytes=limit),
        cost_estimate=pl.CostEstimate(flops=flops, bytes_accessed=nbytes, transcendentals=0),
    )


def start(source, target, sem):
    copy = pltpu.make_async_copy(source, target, sem)
    copy.start()
    return copy


def packing(rows, columns):
    tiles, rest = divmod(columns, LANES)
    share = LANES // rest if rest and LANES % rest == 0 else 1
    if rows % (16 * share):
        share = 1
    return tiles, rest, share, tiles * rows + (rows // share if rest else 0)


def pack(block, target, base):
    rows = block.shape[0]
    tiles, rest, share, _ = packing(*block.shape)
    for t in range(tiles):
        target[base + t * rows : base + (t + 1) * rows, :] = block[:, t * LANES : (t + 1) * LANES].astype(BF)
    if rest:
        short = rows // share
        last = [block[q * short : (q + 1) * short, tiles * LANES :] for q in range(share)]
        if share * rest < LANES:
            last.append(jnp.zeros((short, LANES - share * rest), block.dtype))
        at = base + tiles * rows
        target[at : at + short, :] = jnp.concatenate(last, axis=1).astype(BF)


def unpack(source, base, target, row, rows, columns):
    tiles, rest, share, _ = packing(rows, columns)
    for t in range(tiles):
        piece = source[base + t * rows : base + (t + 1) * rows, :]
        target[row : row + rows, t * LANES : (t + 1) * LANES] = piece.astype(target.dtype)
    if rest:
        short = rows // share
        at = base + tiles * rows
        last = source[at : at + short, :].astype(F32)
        for q in range(share):
            piece = last[:, q * rest : (q + 1) * rest].astype(target.dtype)
            target[row + q * short : row + (q + 1) * short, tiles * LANES : columns] = piece


def staged_call(body, out_shape, scalars, operands, scratch, flops, nbytes, given=(), limit=VMEM_LIMIT):
    buffers = [pltpu.VMEM(x.shape, x.dtype) for x in list(operands) + list(out_shape)]
    ins, outs = len(operands), len(out_shape)

    def run(*refs):
        values, refs = refs[: len(scalars)], refs[len(scalars) :]
        ready, refs = refs[: len(given)], refs[len(given) :]
        far, refs = refs[: ins + outs], refs[ins + outs :]
        near, extra, sems = refs[: ins + outs], refs[ins + outs : -1], refs[-1]
        loads = [start(far[k], near[k], sems.at[k]) for k in range(ins)]
        for load in loads:
            load.wait()
        body(*values, *ready, *near, *extra)
        sends = [start(near[k], far[k], sems.at[k]) for k in range(ins, ins + outs)]
        for send in sends:
            send.wait()

    return kernel_call(
        run,
        [pltpu.HBM(x.shape, x.dtype) for x in out_shape],
        [SMEM] * len(scalars) + [VMEM] * len(given) + [ANY] * ins,
        [ANY] * outs,
        buffers + list(scratch) + [pltpu.SemaphoreType.DMA((ins + outs,))],
        flops,
        nbytes,
        limit,
    )(*scalars, *given, *operands)


def pick_pages(table, own, picked, groups, per_group, per_peer):
    def one_group(g, carry):
        spot = g * per_peer
        for k in range(per_group):
            local = table[g * per_group + k] - own * per_group
            picked[spot] = local
            spot = spot + jnp.where((local >= 0) & (local < per_group), 1, 0)
        return carry

    lax.fori_loop(0, groups, one_group, 0)


def place_pages(table, own, seen, source, target, groups, per_group, per_peer, page_len):
    for g in range(groups):
        seen[g] = 0
    for k in range(per_group):
        holder = lax.div(table[own * per_group + k], per_group)
        slot = holder * per_peer + seen[holder]
        seen[holder] = seen[holder] + 1
        start = pl.multiple_of(slot * page_len, page_len)
        target[k * page_len : (k + 1) * page_len, :] = source[pl.ds(start, page_len), :]


def picked_rows(source, picked, g, per_peer, page_len):
    pages = []
    for b in range(per_peer):
        at = pl.multiple_of(picked[g * per_peer + b] * page_len, page_len)
        pages.append(source[pl.ds(at, page_len), :])
    return jnp.concatenate(pages, axis=0)


def project_kernel(
    dims, table, hidden_in, gain, wq_in, wd_in, out_in, hidden, wq, wd, normed, wide, out, picked, sems
):
    groups, per_group, per_peer, page_len = dims
    rows, model_width = hidden.shape
    low = wd.shape[1]
    pieces = 4
    part = rows // pieces
    strip = wq.shape[0] // 2
    loads = [
        start(hidden_in.at[pl.ds(k * part, part)], hidden.at[pl.ds(k * part, part)], sems.at[k]) for k in range(pieces)
    ]
    weights = [start(wd_in, wd, sems.at[pieces])]
    for k in range(2):
        half = pl.ds(k * strip, strip)
        weights.append(start(wq_in.at[half], wq.at[half], sems.at[pieces + 1 + k]))
    pick_pages(table, lax.axis_index("group"), picked, groups, per_group, per_peer)
    step = 32
    scale = gain[...].reshape(1, model_width)

    def norm_rows(i, carry):
        at = pl.ds(pl.multiple_of(i * step, step), step)
        x = hidden[at, :].astype(F32)
        meansq = jnp.mean(x * x, axis=-1, keepdims=True)
        normed[at, :] = (x * lax.rsqrt(meansq + EPSILON) * scale).astype(BF)
        return carry

    for k in range(pieces):
        loads[k].wait()
        lax.fori_loop(k * part // step, (k + 1) * part // step, norm_rows, 0, unroll=2)
    for load in weights:
        load.wait()
    wide[:, :low] = dot(normed[...], wd[...]).astype(wide.dtype)
    wide[:, low:] = dot(normed[...], wq[...], ((1,), (1,))).astype(wide.dtype)
    sends = []
    for g in range(groups):
        pack(picked_rows(wide, picked, g, per_peer, page_len), out.at[g], 0)
        sends.append(start(out.at[g], out_in.at[g], sems.at[pieces + 3 + g]))
    for send in sends:
        send.wait()


def residual_kernel(dims, shards, base, table, hidden_in, out_in, window, wide, pages, picked, sems):
    groups, per_group, per_peer, page_len = dims
    own_shard = lax.axis_index("mp")
    for j in range(shards):

        @pl.when(own_shard == j)
        def _(j=j):
            columns, _ = column_window(j, shards, hidden_in.shape[1])
            start(hidden_in.at[:, columns], window, sems.at[groups])

    pick_pages(table, lax.axis_index("group"), picked, groups, per_group, per_peer)
    pltpu.make_async_copy(hidden_in.at[:, 0 : window.shape[1]], window, sems.at[groups]).wait()
    for j in range(shards):

        @pl.when(own_shard == j)
        def _(j=j):
            _, at = column_window(j, shards, hidden_in.shape[1])
            wide[...] = window[:, at : at + wide.shape[1]].astype(F32)

    sends = []
    for g in range(groups):
        pack(picked_rows(wide, picked, g, per_peer, page_len), pages.at[g], 0)
        sends.append(start(pages.at[g], out_in.at[g, pl.ds(base, pages.shape[1])], sems.at[g]))
    for send in sends:
        send.wait()


def products_kernel(groups, shards, w_out_in, w_up_in, *refs):
    blocks = refs[:shards]
    _, out_in, vocab, w_out, w_up, products, shared, sems = refs[shards:]
    inner, model_width = w_out.shape
    low = w_up.shape[0]
    width = model_width // shards
    held = blocks[0].shape[0]
    loads = [start(w_up_in, w_up, sems.at[groups])]
    for k in range(inner // HD):
        rows = pl.ds(k * HD, HD)
        loads.append(start(w_out_in.at[rows], w_out.at[rows], sems.at[groups + 1 + k]))
    own_shard = lax.axis_index("mp")
    for i in range(shards):
        at = lax.rem(own_shard + i + 1, shards) * held
        vocab[pl.ds(pl.multiple_of(at, held), held), :] = blocks[i][...]
    for load in loads:
        load.wait()
    products[:, :inner] = dot(vocab[...], w_out[...], ((1,), (1,)))
    products[:, inner : inner + low] = dot(vocab[...], w_up[...], ((1,), (1,)))
    for j in range(shards):

        @pl.when(own_shard == j)
        def _(j=j):
            products[:, inner + low :] = vocab[:, j * width : (j + 1) * width].astype(F32)

    pack(products[...], shared, 0)
    sends = [start(shared, out_in.at[g, pl.ds(0, shared.shape[0])], sems.at[g]) for g in range(groups)]
    for send in sends:
        send.wait()


def phi_of(vectors, left, right, cols):
    first = dot(left[...], vectors) + cols[:, 0:1]
    second = dot(right[...], vectors) + cols[:, 1:2]
    return first * second * cols[:, 2:3]


def with_ones(values):
    lane = lax.broadcasted_iota(jnp.int32, (values.shape[0], LANES - HD), 1)
    return jnp.concatenate([values, jnp.where(lane == 0, 1.0, 0.0).astype(values.dtype)], axis=1)


def with_ones_t(values):
    row = lax.broadcasted_iota(jnp.int32, (LANES - HD, values.shape[1]), 0)
    return jnp.concatenate([values, jnp.where(row == 0, 1.0, 0.0).astype(values.dtype)], axis=0)


def same_upto(segrow):
    count = segrow.shape[1]
    ids = segrow[...].astype(F32)
    column = jnp.transpose(jnp.broadcast_to(ids, (8, count)))[:, 0:1]
    behind = lax.broadcasted_iota(jnp.int32, (count, count), 0)
    ahead = lax.broadcasted_iota(jnp.int32, (count, count), 1)
    return jnp.where((column == ids) & (behind <= ahead), 1.0, 0.0)


def group_kernel(
    dims, low, heads, table, arrived, segrow, left, right, cols, ordered_in, ordered_t_in, state_in, nd_in,
    state, wide, placed, ordered, ordered_t, nd, mask, seen, sems
):
    groups, per_group, per_peer, page_len = dims
    tall = per_peer * page_len
    count, sent = placed.shape
    mask[...] = same_upto(segrow)
    for g in range(groups):
        unpack(arrived.at[g], 0, wide, g * tall, tall, sent)
    place_pages(table, lax.axis_index("group"), seen, wide, placed, groups, per_group, per_peer, page_len)
    ordered[...] = placed[:, low:].astype(BF)
    for at in range(0, sent, LANES):
        end = min(at + LANES, sent)
        ordered_t[at:end, :] = jnp.transpose(placed[:, at:end]).astype(BF)
    sends = [start(ordered_t, ordered_t_in, sems.at[0]), start(ordered, ordered_in, sems.at[1])]

    last = segrow[:, count - 1 : count]
    member = jnp.where(segrow[...] == last, 1.0, 0.0)
    total = jnp.sum(member, axis=1, keepdims=True)
    fine = total - total.astype(BF).astype(F32)
    tag = last.astype(F32) + 1.0
    row = lax.broadcasted_iota(jnp.int32, (PHI_PAD, LANES), 0)
    lane = lax.broadcasted_iota(jnp.int32, (PHI_PAD, LANES), 1)
    block = 256 if count % 256 == 0 else count
    for h in range(heads):
        at = h * HEAD
        key = ordered[:, at + FEAT : at + 2 * FEAT] * BF(0.25)
        value = ordered[:, at + 2 * FEAT : at + HEAD]
        at = low + h * HEAD
        query_t = ordered_t[at : at + FEAT, :]
        key_t = ordered_t[at + FEAT : at + 2 * FEAT, :]
        extended_t = with_ones_t(ordered_t[at + 2 * FEAT : at + HEAD, :])

        phi = (phi_of(key_t, left, right, cols) * member).astype(BF)
        summed = dot(phi, with_ones(value))
        summed = jnp.where((row == 0) & (lane == TAG), tag, summed)
        summed = jnp.where((row == 0) & (lane == REST), fine, summed)
        state[h] = summed.astype(BF)

        for begin in range(0, count, block):
            end = begin + block
            s = dot(key[:end], query_t[:, begin:end])
            w = (1.0 + s * (1.0 + 0.5 * s)) * mask[:end, begin:end]
            nd[h, :, begin:end] = dot(extended_t[:, :end], w.astype(BF))
        sends.append(start(nd.at[h], nd_in.at[h], sems.at[3 + h]))
    sends.append(start(state, state_in, sems.at[2]))
    for send in sends:
        send.wait()


def split3(x):
    a = x.astype(BF)
    rest = x - a.astype(F32)
    b = rest.astype(BF)
    return jnp.concatenate([a, b, (rest - b.astype(F32)).astype(BF)], axis=0)


def state_corner(state):
    corner = state[0, 0:1, :].astype(F32)
    return corner[:, TAG : TAG + 1], corner[:, ONE : ONE + 1] + corner[:, REST : REST + 1]


def column_window(j, shards, model_width):
    width = model_width // shards
    size = window_size(shards, model_width)
    first = min(j * width // LANES * LANES, model_width - size)
    return slice(first, first + size), j * width - first


def window_size(shards, model_width):
    width = model_width // shards
    return max(-(-(j * width % LANES + width) // LANES) * LANES for j in range(shards))


def far_tables(shards):
    if shards == 4:
        return [(3, 3, 0, 0), (2, None, None, 1)]
    tables = [tuple({0: shards - 1, shards - 1: 0}.get(own) for own in range(shards))]
    for distance in range(shards - 2, 1, -1):
        tables += [offset_table(distance, shards), offset_table(-distance, shards)]
    return tables


def near_tables(shards):
    if shards == 4:
        return [(0, 1, 2, 3), (1, 0, 3, 2), (None, 2, 1, None)]
    return [offset_table(offset, shards) for offset in (0, 1, -1)]


def offset_table(offset, shards):
    return tuple(own + offset if 0 <= own + offset < shards else None for own in range(shards))


def each_shard(tables):
    for k, table in enumerate(tables):
        for own, j in enumerate(table):
            if j is not None:
                yield k, own, j


def shard_parts(tables, w_out_in, w_up_in, weights, w_sems, inputs, held_out, outs, sems):
    own_shard = lax.axis_index("mp")
    shards = len(tables[0])
    inner, model_width = w_out_in.shape
    width = model_width // shards

    def copies(k, j):
        window, _ = column_window(j, shards, model_width)
        return (
            pltpu.make_async_copy(w_out_in.at[:, window], weights.at[k, pl.ds(0, inner)], w_sems.at[2 * k]),
            pltpu.make_async_copy(
                w_up_in.at[:, window], weights.at[k, pl.ds(inner, w_up_in.shape[0])], w_sems.at[2 * k + 1]
            ),
        )

    def fetch():
        for k, own, j in each_shard(tables):

            @pl.when(own_shard == own)
            def _(k=k, j=j):
                for copy in copies(k, j):
                    copy.start()

    def compute():
        for k, own, j in each_shard(tables):

            @pl.when(own_shard == own)
            def _(k=k, j=j):
                for copy in copies(k, j):
                    copy.wait()
                _, at = column_window(j, shards, model_width)
                held_out[k] = dot(weights[k, :, at : at + width], inputs[...], ((0,), (0,))).astype(BF)
                start(held_out.at[k], outs[k], sems.at[k])

    def finish():
        for k, own, j in each_shard(tables):

            @pl.when(own_shard == own)
            def _(k=k):
                pltpu.make_async_copy(held_out.at[k], outs[k], sems.at[k]).wait()

    return fetch, compute, finish


def finish_kernel(
    low, heads, shards, ordered_t_in, nd_in, state, segrow, slotrow, left, right, cols, w_out_in, w_up_in, *refs
):
    far = far_tables(shards)
    outs = refs[: len(far)]
    inputs_in, state_in, queries, nd, weights, inputs, held_out, sems, w_sems = refs[len(far) :]
    inner = heads * HD
    sem = iter(range(len(far), len(far) + 2 * heads + 3))
    lows = start(ordered_t_in.at[pl.ds(0, low)], inputs.at[pl.ds(inner, low)], sems.at[next(sem)])
    fetches = []
    for h in range(heads):
        rows = pl.ds(low + h * HEAD, FEAT)
        fetches.append(start(ordered_t_in.at[rows], queries.at[h], sems.at[next(sem)]))
        fetches.append(start(nd_in.at[h], nd.at[h], sems.at[next(sem)]))
    fetch_weights, compute, finish = shard_parts(
        far, w_out_in, w_up_in, weights, w_sems, inputs, held_out, outs, sems
    )
    fetch_weights()
    tag, _ = state_corner(state)
    carried = jnp.where(segrow[...].astype(F32) + 1.0 == tag, 1.0, 0.0)
    row_slot = lax.div(lax.broadcasted_iota(jnp.int32, (low, 1), 0), RANK)
    lows.wait()
    lowered = jnp.where(slotrow[...] == row_slot, inputs[inner:, :].astype(F32), 0.0)
    inputs[inner:, :] = lowered.astype(BF)
    for h in range(heads):
        fetches[2 * h].wait()
        fetches[2 * h + 1].wait()
        cross = dot(state[h], phi_of(queries[h], left, right, cols).astype(BF), ((0,), (0,)))
        both = nd[h] + carried * cross
        inputs[h * HD : (h + 1) * HD, :] = (both[:HD, :] * (1.0 / both[ONE : ONE + 1, :])).astype(BF)
    compute()
    kept = [start(inputs, inputs_in, sems.at[next(sem)]), start(state, state_in, sems.at[next(sem)])]
    finish()
    for copy in kept:
        copy.wait()


def near_kernel(shards, w_out_in, w_up_in, inputs_in, *refs):
    near = near_tables(shards)
    outs = refs[: len(near)]
    weights, inputs, held_out, sems, w_sems = refs[len(near) :]
    load = start(inputs_in, inputs, sems.at[len(near)])
    fetch, compute, finish = shard_parts(near, w_out_in, w_up_in, weights, w_sems, inputs, held_out, outs, sems)
    fetch()
    load.wait()
    compute()
    finish()


def logits_kernel(dims, shards, width, table, arrived, inputs, out, vocab, both, wide, placed, seen):
    groups, per_group, per_peer, page_len = dims
    tall = per_peer * page_len
    inner = inputs.shape[0]
    rows = vocab.shape[0] // groups
    _, _, _, base = packing(rows, inner + width)
    for g in range(groups):
        unpack(arrived.at[g], 0, vocab, g * rows, rows, inner + width)
        unpack(arrived.at[g], base, wide, g * tall, tall, width)
    place_pages(table, lax.axis_index("group"), seen, wide, placed, groups, per_group, per_peer, page_len)
    both[:inner, :] = inputs[...]
    both[inner:, :] = jnp.transpose(placed[...]).astype(BF)
    block = inputs.shape[1] // shards
    scored = dot(vocab[...], both[...])
    for j in range(shards):
        out[j] = scored[:, j * block : (j + 1) * block].astype(BF)


def norms_kernel(low, heads, ordered, ordered_t, state, segrow, left, right, cols, norms, mask):
    count = segrow.shape[1]
    mask[...] = same_upto(segrow)
    upto = mask[...].astype(BF)
    tag, held = state_corner(state)
    carried = jnp.where(segrow[...].astype(F32) + 1.0 == tag, 1.0, 0.0)
    value_lane = lax.broadcasted_iota(jnp.int32, (1, LANES), 1) < HD
    counted = carried * held + jnp.sum(mask[...], axis=0, keepdims=True)
    block = 256 if count % 256 == 0 else count
    increments = []
    before = []
    for h in range(heads):
        at = h * HEAD
        key = ordered[:, at + FEAT : at + 2 * FEAT] * BF(0.25)
        value = ordered[:, at + 2 * FEAT : at + HEAD]
        at = low + h * HEAD
        key_t = ordered_t[at + FEAT : at + 2 * FEAT, :]
        value_t = ordered_t[at + 2 * FEAT : at + HEAD, :]
        wide_key = key_t.astype(F32)
        wide_value = value_t.astype(F32)
        self_score = 0.25 * jnp.sum(wide_key * wide_key, axis=0, keepdims=True)
        self_value = jnp.sum(wide_value * wide_value, axis=0, keepdims=True)
        diagonal = (1.0 + self_score * (1.0 + 0.5 * self_score)) * self_value
        below = []
        for begin in range(0, count, block):
            end = begin + block
            kk = dot(key[:end], key_t[:, begin:end])
            vv = dot(value[:end], value_t[:, begin:end])
            gram = (1.0 + kk * (1.0 + 0.5 * kk)) * vv * mask[:end, begin:end]
            below.append(jnp.sum(gram, axis=0, keepdims=True))
        added = 2.0 * jnp.concatenate(below, axis=1) - diagonal
        held_state = state[h]
        against = dot(held_state, phi_of(key_t, left, right, cols).astype(BF), ((0,), (0,)))[:HD, :]
        along = jnp.sum(against * wide_value, axis=0, keepdims=True)
        increments.append(added + 2.0 * carried * along)
        wide_state = jnp.where(value_lane, held_state.astype(F32), 0.0)
        per_lane = jnp.sum(wide_state * wide_state, axis=0, keepdims=True)
        before.append(jnp.sum(per_lane, axis=1, keepdims=True))
    if heads % 8:
        increments.append(jnp.zeros((8 - heads % 8, count), F32))
    stacked = split3(jnp.concatenate(increments, axis=0))
    thrice = dot(stacked, upto)
    rows = thrice.shape[0] // 3
    summed = thrice[:rows] + thrice[rows : 2 * rows] + thrice[2 * rows :]
    for h in range(heads):
        total = carried * before[h] + summed[h : h + 1, :]
        norms[h : h + 1, :] = jnp.sqrt(total / (counted * float(FEAT * HD)))


def best_kernel(*refs):
    *pieces, best = refs
    whole = pieces[0][...].astype(F32)
    for piece in pieces[1:]:
        whole = whole + piece[...].astype(F32)
    best[...] = jnp.max(whole, axis=0, keepdims=True)


def exchange(blocks, axis):
    return lax.all_to_all(blocks, axis, split_axis=0, concat_axis=0, tiled=True)


def ring_rows(values, axis):
    size = lax.axis_size(axis)
    steps = [lax.ppermute(values, axis, [(i, (i + by) % size) for i in range(size)]) for by in range(size - 1, 0, -1)]
    return [*steps, values]


def joined(*parts):
    return sum(part.astype(F32) for part in parts).astype(BF)


def line_total(terms, axis):
    if lax.axis_size(axis) != 4:
        return joined(*terms)
    own_term, across, paired, centre = terms
    return joined(own_term, jnp.where(on_middle(axis), centre, across), paired)


def on_middle(axis):
    here = lax.axis_index(axis)
    return (here == 1) | (here == 2)


def pair_blocks(blocks, axis):
    size = lax.axis_size(axis)
    here = lax.axis_index(axis)

    def block(at):
        return lax.dynamic_index_in_dim(blocks, at, 0, keepdims=False)

    received = [block(here)]
    for by in range(1, size):
        received.append(lax.ppermute(block(here ^ by), axis, [(i, i ^ by) for i in range(size)]))
    return received


def line_sums(far_terms, near_terms, axis, beside):
    size = lax.axis_size(axis)

    def send(values, *pairs):
        return lax.ppermute(values, axis, pairs)

    own_term = near_terms[0]
    if size == 4:
        across = send(far_terms[0], (1, 2), (2, 1), (0, 3), (3, 0))
        inward = send(far_terms[1], (0, 1), (3, 2))
        across, inward, beside = lax.optimization_barrier((across, inward, beside))
        relayed = jnp.where(on_middle(axis), across, 0)
        paired = send(joined(near_terms[1], relayed), (0, 1), (1, 0), (2, 3), (3, 2))
        centre = send(joined(near_terms[2], inward), (1, 2), (2, 1))
        return (own_term, across, paired, centre), beside
    terms = {1: near_terms[1], -1: near_terms[2], size - 1: far_terms[0], 1 - size: far_terms[0]}
    for distance in range(size - 2, 1, -1):
        terms[distance], terms[-distance] = far_terms[2 * (size - 1 - distance) - 1 :][:2]
    going_up = going_down = None
    for step in range(1, size):
        to_up = terms[size - step]
        to_down = terms[step - size]
        if step > 1:
            to_up = joined(to_up, going_up)
            to_down = joined(to_down, going_down)
        going_up = send(to_up, *[(i, i + 1) for i in range(step)])
        going_down = send(to_down, *[(i, i - 1) for i in range(size - step, size)])
    return (own_term, going_up, going_down), beside


def on_device(
    hidden,
    norm_gain,
    qkv_weight,
    out_weight,
    adapter_down,
    adapter_up,
    vocab_rows,
    segments,
    request_adapter,
    adapter_slot,
    page_table,
):
    groups = lax.axis_size("group")
    shards = lax.axis_size("mp")
    own_shard = lax.axis_index("mp")
    count, model_width = hidden.shape
    per_group = page_table.shape[0] // groups
    per_peer = per_group // groups
    page_len = count // per_group
    dims = (groups, per_group, per_peer, page_len)
    qkv_cols = qkv_weight.shape[1]
    heads = qkv_cols // HEAD
    low = adapter_down.shape[1]
    inner = heads * HD
    width = model_width // shards
    sent = low + qkv_cols
    tall = per_peer * page_len
    packed = packing(tall, sent)[-1]
    some = shards * vocab_rows.shape[0]
    scored = groups * some
    aside = packing(some, inner + low + width)[-1] + packing(tall, width)[-1]
    shape = jax.ShapeDtypeStruct
    dma = pltpu.SemaphoreType.DMA
    picked = pltpu.SMEM((groups * per_peer + 1,), jnp.int32)

    left, right, cols = [jnp.asarray(t) for t in feature_tables()]
    segrow = segments.reshape(1, count)
    request_ids = jnp.arange(request_adapter.shape[0], dtype=jnp.int32)
    adapter_ids = jnp.arange(adapter_slot.shape[0], dtype=jnp.int32)

    outgoing = kernel_call(
        functools.partial(project_kernel, dims),
        pltpu.HBM((groups, packed, LANES), BF),
        [SMEM, ANY, VMEM, ANY, ANY],
        ANY,
        [
            pltpu.VMEM((count, model_width), BF),
            pltpu.VMEM((qkv_cols, model_width), BF),
            pltpu.VMEM((model_width, low), BF),
            pltpu.VMEM((count, model_width), BF),
            pltpu.VMEM((count, sent), F32 if page_len % 16 else BF),
            pltpu.VMEM((groups, packed, LANES), BF),
            picked,
            dma((7 + groups,)),
        ],
        2 * count * model_width * sent,
        2 * (count * model_width + model_width * sent),
    )(page_table, hidden, norm_gain, qkv_weight.T, adapter_down)
    arrived = exchange(outgoing, "group")

    after_vocab, after_adapter, later_hidden, _ = lax.optimization_barrier(
        (vocab_rows, request_adapter, hidden, outgoing)
    )
    some_vocab = ring_rows(after_vocab, "mp")
    request_slot = jnp.sum(jnp.where(after_adapter[:, None] == adapter_ids[None, :], adapter_slot[None, :], 0), axis=1)
    slots = jnp.sum(jnp.where(segrow == request_ids[:, None], request_slot[:, None], 0), axis=0, keepdims=True)
    slotrow = slots - own_shard * (low // RANK)
    window = window_size(shards, model_width)
    ahead = packing(some, inner + low + width)[-1]
    beside = kernel_call(
        functools.partial(residual_kernel, dims, shards, ahead),
        pltpu.HBM((groups, aside, LANES), BF),
        [SMEM, ANY],
        ANY,
        [
            pltpu.VMEM((count, window), BF),
            pltpu.VMEM((count, width), F32),
            pltpu.VMEM((groups, packing(tall, width)[-1], LANES), BF),
            picked,
            dma((groups + 1,)),
        ],
        1,
        1,
    )(page_table, later_hidden)
    beside = kernel_call(
        functools.partial(products_kernel, groups, shards),
        pltpu.HBM((groups, aside, LANES), BF),
        [ANY, ANY] + [VMEM] * shards + [ANY],
        ANY,
        [
            pltpu.VMEM((some, model_width), BF),
            pltpu.VMEM((inner, model_width), BF),
            pltpu.VMEM((low, model_width), BF),
            pltpu.VMEM((some, inner + low + width), F32),
            pltpu.VMEM((ahead, LANES), BF),
            dma((groups + 1 + heads,)),
        ],
        2 * some * model_width * (inner + low),
        2 * count * model_width,
        44 * MIB,
        {2 + shards: 0},
    )(out_weight, adapter_up, *some_vocab, beside)
    arrived, beside, slotrow = lax.optimization_barrier((arrived, beside, slotrow))

    ordered, ordered_t, state, nd = kernel_call(
        functools.partial(group_kernel, dims, low, heads),
        (
            pltpu.HBM((count, qkv_cols), BF),
            pltpu.HBM((sent, count), BF),
            pltpu.HBM((heads, PHI_PAD, LANES), BF),
            pltpu.HBM((heads, LANES, count), F32),
        ),
        [SMEM] + [VMEM] * 5,
        (ANY, ANY, ANY, ANY),
        [
            pltpu.VMEM((heads, PHI_PAD, LANES), BF),
            pltpu.VMEM((count, sent), F32),
            pltpu.VMEM((count, sent), F32),
            pltpu.VMEM((count, qkv_cols), BF),
            pltpu.VMEM((sent, count), BF),
            pltpu.VMEM((heads, LANES, count), F32),
            pltpu.VMEM((count, count), F32),
            pltpu.SMEM((groups,), jnp.int32),
            dma((3 + heads,)),
        ],
        heads * 2 * count * count * 512,
        6 * count * sent,
        40 * MIB,
    )(page_table, arrived, segrow, left, right, cols)
    beside, state = lax.optimization_barrier((beside, state))
    beside = exchange(beside, "group")
    state = lax.ppermute(state, "group", [(i, i + 1) for i in range(groups - 1)])

    far, near = len(far_tables(shards)), len(near_tables(shards))
    part = pltpu.HBM((width, count), BF)
    *far_terms, inputs, kept_state = kernel_call(
        functools.partial(finish_kernel, low, heads, shards),
        [part] * far + [pltpu.HBM((inner + low, count), BF), pltpu.HBM((heads, PHI_PAD, LANES), BF)],
        [ANY] * 2 + [VMEM] * 6 + [ANY] * 2,
        [ANY] * (far + 2),
        [
            pltpu.VMEM((heads, FEAT, count), BF),
            pltpu.VMEM((heads, LANES, count), F32),
            pltpu.VMEM((far, inner + low, window), BF),
            pltpu.VMEM((inner + low, count), BF),
            pltpu.VMEM((far, width, count), BF),
            dma((far + 2 * heads + 3,)),
            dma((2 * far,)),
        ],
        20 * count * (inner + low) * model_width,
        40 * count * model_width,
    )(ordered_t, nd, state, segrow, slotrow, left, right, cols, out_weight, adapter_up)
    near_terms = kernel_call(
        functools.partial(near_kernel, shards),
        [part] * near,
        [ANY] * 3,
        [ANY] * near,
        [
            pltpu.VMEM((near, inner + low, window), BF),
            pltpu.VMEM((inner + low, count), BF),
            pltpu.VMEM((near, width, count), BF),
            dma((near + 1,)),
            dma((2 * near,)),
        ],
        1,
        1,
    )(out_weight, adapter_up, inputs)

    [logits] = staged_call(
        functools.partial(logits_kernel, dims, shards, width),
        [shape((shards, scored, count // shards), BF)],
        [page_table],
        [inputs],
        [
            pltpu.VMEM((scored, inner + low + width), BF),
            pltpu.VMEM((inner + low + width, count), BF),
            pltpu.VMEM((count, width), F32),
            pltpu.VMEM((count, width), F32),
            pltpu.SMEM((groups,), jnp.int32),
        ],
        1,
        1,
        given=[beside],
        limit=(40 if scored <= 512 else 56) * MIB,
    )
    [state_norms] = staged_call(
        functools.partial(norms_kernel, low, heads),
        [shape((heads, count), F32)],
        [],
        [ordered, ordered_t, kept_state, segrow, left, right, cols],
        [pltpu.VMEM((count, count), F32)],
        1,
        1,
    )
    terms, [state_norms, _] = line_sums(far_terms, near_terms, "mp", [state_norms, logits])
    blocks = pair_blocks(logits, "mp")
    best = kernel_call(
        best_kernel,
        shape((1, count // shards), F32),
        [VMEM] * shards,
        VMEM,
        [],
        1,
        1,
        32 * MIB,
    )(*blocks)
    terms, best = lax.optimization_barrier((terms, best))
    return line_total(terms, "mp").T, state_norms, best.reshape(-1)


def solution(mesh):
    placed = (
        P("group", None),
        P(),
        P(None, "mp"),
        P("mp", None),
        P(None, "mp"),
        P("mp", None),
        P(("group", "mp"), None),
        P("group"),
        P(),
        P(),
        P(),
    )
    return jax.shard_map(
        on_device,
        mesh=mesh,
        in_specs=placed,
        out_specs=(P("group", "mp"), P("mp", "group"), P(("group", "mp"))),
        check_vma=False,
    )
```

```python
import functools

import jax
import jax.numpy as jnp
import numpy as np
from jax import lax
from jax.experimental import pallas as pl
from jax.experimental.pallas import tpu as pltpu
from jax.sharding import PartitionSpec as P

FEAT = 16
HD = 112
RANK = 16
EPSILON = 1e-05
HEAD = 2 * FEAT + HD
PHI = 1 + FEAT + FEAT * (FEAT + 1) // 2
PHI_PAD = 160
LANES = 128
ONE, TAG, REST = HD, HD + 1, HD + 2
HALVES = 2
MIB = 1024 * 1024
VMEM_LIMIT = 60 * MIB

BF = jnp.bfloat16
F32 = jnp.float32
SMEM = pl.BlockSpec(memory_space=pltpu.SMEM)
VMEM = pl.BlockSpec(memory_space=pltpu.VMEM)
ANY = pl.BlockSpec(memory_space=pltpu.HBM)


def feature_tables():
    left = np.zeros((PHI_PAD, FEAT), np.float32)
    right = np.zeros((PHI_PAD, FEAT), np.float32)
    cols = np.zeros((PHI_PAD, 8), np.float32)
    cols[0, :3] = 1.0
    at = 1
    for i in range(FEAT):
        left[at, i] = 1.0
        cols[at, 1] = 1.0
        cols[at, 2] = FEAT**-0.25
        at += 1
    for i in range(FEAT):
        for j in range(i, FEAT):
            left[at, i] = 1.0
            right[at, j] = 1.0
            cols[at, 2] = (1.0 if i == j else 2.0**0.5) / (2.0 * FEAT) ** 0.5
            at += 1
    return left.astype(jnp.bfloat16), right.astype(jnp.bfloat16), cols


def dot(a, b, dims=((1,), (0,))):
    return lax.dot_general(a, b, (dims, ((), ())), preferred_element_type=F32)


def kernel_call(body, out_shape, in_specs, out_specs, scratch, flops, nbytes, limit=VMEM_LIMIT, aliases=None):
    return pl.pallas_call(
        body,
        out_shape=out_shape,
        in_specs=in_specs,
        out_specs=out_specs,
        scratch_shapes=scratch,
        input_output_aliases=aliases or {},
        compiler_params=pltpu.CompilerParams(vmem_limit_bytes=limit),
        cost_estimate=pl.CostEstimate(flops=flops, bytes_accessed=nbytes, transcendentals=0),
    )


def start(source, target, sem):
    copy = pltpu.make_async_copy(source, target, sem)
    copy.start()
    return copy


def packing(rows, columns):
    tiles, rest = divmod(columns, LANES)
    share = LANES // rest if rest and LANES % rest == 0 else 1
    if rows % (16 * share):
        share = 1
    return tiles, rest, share, tiles * rows + (rows // share if rest else 0)


def pack(block, target, base):
    rows = block.shape[0]
    tiles, rest, share, _ = packing(*block.shape)
    for t in range(tiles):
        target[base + t * rows : base + (t + 1) * rows, :] = block[:, t * LANES : (t + 1) * LANES].astype(BF)
    if rest:
        short = rows // share
        last = [block[q * short : (q + 1) * short, tiles * LANES :] for q in range(share)]
        if share * rest < LANES:
            last.append(jnp.zeros((short, LANES - share * rest), block.dtype))
        at = base + tiles * rows
        target[at : at + short, :] = jnp.concatenate(last, axis=1).astype(BF)


def unpack(source, base, target, row, rows, columns):
    tiles, rest, share, _ = packing(rows, columns)
    for t in range(tiles):
        piece = source[base + t * rows : base + (t + 1) * rows, :]
        target[row : row + rows, t * LANES : (t + 1) * LANES] = piece.astype(target.dtype)
    if rest:
        short = rows // share
        at = base + tiles * rows
        last = source[at : at + short, :].astype(F32)
        for q in range(share):
            piece = last[:, q * rest : (q + 1) * rest].astype(target.dtype)
            target[row + q * short : row + (q + 1) * short, tiles * LANES : columns] = piece


def staged_call(body, out_shape, scalars, operands, scratch, flops, nbytes, given=(), limit=VMEM_LIMIT):
    buffers = [pltpu.VMEM(x.shape, x.dtype) for x in list(operands) + list(out_shape)]
    ins, outs = len(operands), len(out_shape)

    def run(*refs):
        values, refs = refs[: len(scalars)], refs[len(scalars) :]
        ready, refs = refs[: len(given)], refs[len(given) :]
        far, refs = refs[: ins + outs], refs[ins + outs :]
        near, extra, sems = refs[: ins + outs], refs[ins + outs : -1], refs[-1]
        loads = [start(far[k], near[k], sems.at[k]) for k in range(ins)]
        for load in loads:
            load.wait()
        body(*values, *ready, *near, *extra)
        sends = [start(near[k], far[k], sems.at[k]) for k in range(ins, ins + outs)]
        for send in sends:
            send.wait()

    return kernel_call(
        run,
        [pltpu.HBM(x.shape, x.dtype) for x in out_shape],
        [SMEM] * len(scalars) + [VMEM] * len(given) + [ANY] * ins,
        [ANY] * outs,
        buffers + list(scratch) + [pltpu.SemaphoreType.DMA((ins + outs,))],
        flops,
        nbytes,
        limit,
    )(*scalars, *given, *operands)


def pick_pages(table, own, picked, groups, per_group, per_peer):
    def one_group(g, carry):
        spot = g * per_peer
        for k in range(per_group):
            local = table[g * per_group + k] - own * per_group
            picked[spot] = local
            spot = spot + jnp.where((local >= 0) & (local < per_group), 1, 0)
        return carry

    lax.fori_loop(0, groups, one_group, 0)


def place_pages(table, own, seen, source, target, groups, per_group, per_peer, page_len):
    for g in range(groups):
        seen[g] = 0
    for k in range(per_group):
        holder = lax.div(table[own * per_group + k], per_group)
        slot = holder * per_peer + seen[holder]
        seen[holder] = seen[holder] + 1
        start = pl.multiple_of(slot * page_len, page_len)
        target[k * page_len : (k + 1) * page_len, :] = source[pl.ds(start, page_len), :]


def picked_rows(source, picked, g, per_peer, page_len):
    pages = []
    for b in range(per_peer):
        at = pl.multiple_of(picked[g * per_peer + b] * page_len, page_len)
        pages.append(source[pl.ds(at, page_len), :])
    return jnp.concatenate(pages, axis=0)


def project_kernel(
    dims, table, hidden_in, gain, wq_in, wd_in, out_in, hidden, wq, wd, normed, wide, out, picked, sems
):
    groups, per_group, per_peer, page_len = dims
    rows, model_width = hidden.shape
    low = wd.shape[1]
    pieces = 4
    part = rows // pieces
    strip = wq.shape[0] // 2
    loads = [
        start(hidden_in.at[pl.ds(k * part, part)], hidden.at[pl.ds(k * part, part)], sems.at[k]) for k in range(pieces)
    ]
    weights = [start(wd_in, wd, sems.at[pieces])]
    for k in range(2):
        half = pl.ds(k * strip, strip)
        weights.append(start(wq_in.at[half], wq.at[half], sems.at[pieces + 1 + k]))
    pick_pages(table, lax.axis_index("group"), picked, groups, per_group, per_peer)
    step = 32
    scale = gain[...].reshape(1, model_width)

    def norm_rows(i, carry):
        at = pl.ds(pl.multiple_of(i * step, step), step)
        x = hidden[at, :].astype(F32)
        meansq = jnp.mean(x * x, axis=-1, keepdims=True)
        normed[at, :] = (x * lax.rsqrt(meansq + EPSILON) * scale).astype(BF)
        return carry

    for k in range(pieces):
        loads[k].wait()
        lax.fori_loop(k * part // step, (k + 1) * part // step, norm_rows, 0, unroll=2)
    for load in weights:
        load.wait()
    wide[:, :low] = dot(normed[...], wd[...]).astype(wide.dtype)
    wide[:, low:] = dot(normed[...], wq[...], ((1,), (1,))).astype(wide.dtype)
    sends = []
    for g in range(groups):
        pack(picked_rows(wide, picked, g, per_peer, page_len), out.at[g], 0)
        sends.append(start(out.at[g], out_in.at[g], sems.at[pieces + 3 + g]))
    for send in sends:
        send.wait()


def residual_kernel(dims, shards, base, table, hidden_in, out_in, window, wide, pages, picked, sems):
    groups, per_group, per_peer, page_len = dims
    own_shard = lax.axis_index("mp")
    for j in range(shards):

        @pl.when(own_shard == j)
        def _(j=j):
            columns, _ = column_window(j, shards, hidden_in.shape[1])
            start(hidden_in.at[:, columns], window, sems.at[groups])

    pick_pages(table, lax.axis_index("group"), picked, groups, per_group, per_peer)
    pltpu.make_async_copy(hidden_in.at[:, 0 : window.shape[1]], window, sems.at[groups]).wait()
    for j in range(shards):

        @pl.when(own_shard == j)
        def _(j=j):
            _, at = column_window(j, shards, hidden_in.shape[1])
            wide[...] = window[:, at : at + wide.shape[1]].astype(F32)

    sends = []
    for g in range(groups):
        pack(picked_rows(wide, picked, g, per_peer, page_len), pages.at[g], 0)
        sends.append(start(pages.at[g], out_in.at[g, pl.ds(base, pages.shape[1])], sems.at[g]))
    for send in sends:
        send.wait()


def products_kernel(groups, shards, w_out_in, w_up_in, *refs):
    blocks = refs[:shards]
    _, out_in, vocab, w_out, w_up, products, shared, sems = refs[shards:]
    inner, model_width = w_out.shape
    low = w_up.shape[0]
    width = model_width // shards
    held = blocks[0].shape[0]
    loads = [start(w_up_in, w_up, sems.at[groups])]
    for k in range(inner // HD):
        rows = pl.ds(k * HD, HD)
        loads.append(start(w_out_in.at[rows], w_out.at[rows], sems.at[groups + 1 + k]))
    own_shard = lax.axis_index("mp")
    for i in range(shards):
        at = lax.rem(own_shard + i + 1, shards) * held
        vocab[pl.ds(pl.multiple_of(at, held), held), :] = blocks[i][...]
    for load in loads:
        load.wait()
    products[:, :inner] = dot(vocab[...], w_out[...], ((1,), (1,)))
    products[:, inner : inner + low] = dot(vocab[...], w_up[...], ((1,), (1,)))
    for j in range(shards):

        @pl.when(own_shard == j)
        def _(j=j):
            products[:, inner + low :] = vocab[:, j * width : (j + 1) * width].astype(F32)

    pack(products[...], shared, 0)
    sends = [start(shared, out_in.at[g, pl.ds(0, shared.shape[0])], sems.at[g]) for g in range(groups)]
    for send in sends:
        send.wait()


def phi_of(vectors, left, right, cols):
    first = dot(left[...], vectors) + cols[:, 0:1]
    second = dot(right[...], vectors) + cols[:, 1:2]
    return first * second * cols[:, 2:3]


def with_ones(values):
    lane = lax.broadcasted_iota(jnp.int32, (values.shape[0], LANES - HD), 1)
    return jnp.concatenate([values, jnp.where(lane == 0, 1.0, 0.0).astype(values.dtype)], axis=1)


def with_ones_t(values):
    row = lax.broadcasted_iota(jnp.int32, (LANES - HD, values.shape[1]), 0)
    return jnp.concatenate([values, jnp.where(row == 0, 1.0, 0.0).astype(values.dtype)], axis=0)


def same_upto(segrow):
    count = segrow.shape[1]
    ids = segrow[...].astype(F32)
    column = jnp.transpose(jnp.broadcast_to(ids, (8, count)))[:, 0:1]
    behind = lax.broadcasted_iota(jnp.int32, (count, count), 0)
    ahead = lax.broadcasted_iota(jnp.int32, (count, count), 1)
    return jnp.where((column == ids) & (behind <= ahead), 1.0, 0.0)


def group_kernel(
    dims, low, heads, table, arrived, segrow, left, right, cols, ordered_in, ordered_t_in, state_in, nd_in,
    state, wide, placed, ordered, ordered_t, nd, mask, seen, sems
):
    groups, per_group, per_peer, page_len = dims
    tall = per_peer * page_len
    count, sent = placed.shape
    mask[...] = same_upto(segrow)
    for g in range(groups):
        unpack(arrived.at[g], 0, wide, g * tall, tall, sent)
    place_pages(table, lax.axis_index("group"), seen, wide, placed, groups, per_group, per_peer, page_len)
    ordered[...] = placed[:, low:].astype(BF)
    for at in range(0, sent, LANES):
        end = min(at + LANES, sent)
        ordered_t[at:end, :] = jnp.transpose(placed[:, at:end]).astype(BF)
    sends = [start(ordered_t, ordered_t_in, sems.at[0]), start(ordered, ordered_in, sems.at[1])]

    last = segrow[:, count - 1 : count]
    member = jnp.where(segrow[...] == last, 1.0, 0.0)
    total = jnp.sum(member, axis=1, keepdims=True)
    fine = total - total.astype(BF).astype(F32)
    tag = last.astype(F32) + 1.0
    row = lax.broadcasted_iota(jnp.int32, (PHI_PAD, LANES), 0)
    lane = lax.broadcasted_iota(jnp.int32, (PHI_PAD, LANES), 1)
    block = 256 if count % 256 == 0 else count
    for h in range(heads):
        at = h * HEAD
        key = ordered[:, at + FEAT : at + 2 * FEAT] * BF(0.25)
        value = ordered[:, at + 2 * FEAT : at + HEAD]
        at = low + h * HEAD
        query_t = ordered_t[at : at + FEAT, :]
        key_t = ordered_t[at + FEAT : at + 2 * FEAT, :]
        extended_t = with_ones_t(ordered_t[at + 2 * FEAT : at + HEAD, :])

        phi = (phi_of(key_t, left, right, cols) * member).astype(BF)
        summed = dot(phi, with_ones(value))
        summed = jnp.where((row == 0) & (lane == TAG), tag, summed)
        summed = jnp.where((row == 0) & (lane == REST), fine, summed)
        state[h] = summed.astype(BF)

        for begin in range(0, count, block):
            end = begin + block
            s = dot(key[:end], query_t[:, begin:end])
            w = (1.0 + s * (1.0 + 0.5 * s)) * mask[:end, begin:end]
            nd[h, :, begin:end] = dot(extended_t[:, :end], w.astype(BF))
        sends.append(start(nd.at[h], nd_in.at[h], sems.at[3 + h]))
    sends.append(start(state, state_in, sems.at[2]))
    for send in sends:
        send.wait()


def split3(x):
    a = x.astype(BF)
    rest = x - a.astype(F32)
    b = rest.astype(BF)
    return jnp.concatenate([a, b, (rest - b.astype(F32)).astype(BF)], axis=0)


def state_corner(state):
    corner = state[0, 0:1, :].astype(F32)
    return corner[:, TAG : TAG + 1], corner[:, ONE : ONE + 1] + corner[:, REST : REST + 1]


def column_window(j, shards, model_width):
    width = model_width // shards
    size = window_size(shards, model_width)
    first = min(j * width // LANES * LANES, model_width - size)
    return slice(first, first + size), j * width - first


def window_size(shards, model_width):
    width = model_width // shards
    return max(-(-(j * width % LANES + width) // LANES) * LANES for j in range(shards))


def far_tables(shards):
    if shards == 4:
        return [(3, 3, 0, 0), (2, None, None, 1)]
    tables = [tuple({0: shards - 1, shards - 1: 0}.get(own) for own in range(shards))]
    for distance in range(shards - 2, 1, -1):
        tables += [offset_table(distance, shards), offset_table(-distance, shards)]
    return tables


def near_tables(shards):
    if shards == 4:
        return [(0, 1, 2, 3), (1, 0, 3, 2), (None, 2, 1, None)]
    return [offset_table(offset, shards) for offset in (0, 1, -1)]


def offset_table(offset, shards):
    return tuple(own + offset if 0 <= own + offset < shards else None for own in range(shards))


def each_shard(tables):
    for k, table in enumerate(tables):
        for own, j in enumerate(table):
            if j is not None:
                yield k, own, j


def shard_parts(tables, w_out_in, w_up_in, weights, w_sems, inputs, held_out, outs, sems):
    own_shard = lax.axis_index("mp")
    shards = len(tables[0])
    inner, model_width = w_out_in.shape
    width = model_width // shards

    def copies(k, j):
        window, _ = column_window(j, shards, model_width)
        return (
            pltpu.make_async_copy(w_out_in.at[:, window], weights.at[k, pl.ds(0, inner)], w_sems.at[2 * k]),
            pltpu.make_async_copy(
                w_up_in.at[:, window], weights.at[k, pl.ds(inner, w_up_in.shape[0])], w_sems.at[2 * k + 1]
            ),
        )

    def sends(k):
        rows = [pl.ds(h * (width // HALVES), width // HALVES) for h in range(HALVES)]
        targets = [(HALVES * k + h, outs[HALVES * k + h]) for h in range(HALVES)]
        return [
            pltpu.make_async_copy(held_out.at[k, part], target, sems.at[at]) for part, (at, target) in zip(rows, targets)
        ]

    def fetch():
        for k, own, j in each_shard(tables):

            @pl.when(own_shard == own)
            def _(k=k, j=j):
                for copy in copies(k, j):
                    copy.start()

    def compute():
        for k, own, j in each_shard(tables):

            @pl.when(own_shard == own)
            def _(k=k, j=j):
                for copy in copies(k, j):
                    copy.wait()
                _, at = column_window(j, shards, model_width)
                held_out[k] = dot(weights[k, :, at : at + width], inputs[...], ((0,), (0,))).astype(BF)
                for copy in sends(k):
                    copy.start()

    def finish():
        for k, own, j in each_shard(tables):

            @pl.when(own_shard == own)
            def _(k=k):
                for copy in sends(k):
                    copy.wait()

    return fetch, compute, finish


def finish_kernel(
    low, heads, shards, ordered_t_in, nd_in, state, segrow, slotrow, left, right, cols, w_out_in, w_up_in, *refs
):
    far = far_tables(shards)
    arrays = HALVES * len(far)
    outs = refs[:arrays]
    inputs_in, state_in, queries, nd, weights, inputs, held_out, sems, w_sems = refs[arrays:]
    inner = heads * HD
    sem = iter(range(arrays, arrays + 2 * heads + 3))
    lows = start(ordered_t_in.at[pl.ds(0, low)], inputs.at[pl.ds(inner, low)], sems.at[next(sem)])
    fetches = []
    for h in range(heads):
        rows = pl.ds(low + h * HEAD, FEAT)
        fetches.append(start(ordered_t_in.at[rows], queries.at[h], sems.at[next(sem)]))
        fetches.append(start(nd_in.at[h], nd.at[h], sems.at[next(sem)]))
    fetch_weights, compute, finish = shard_parts(
        far, w_out_in, w_up_in, weights, w_sems, inputs, held_out, outs, sems
    )
    fetch_weights()
    tag, _ = state_corner(state)
    carried = jnp.where(segrow[...].astype(F32) + 1.0 == tag, 1.0, 0.0)
    row_slot = lax.div(lax.broadcasted_iota(jnp.int32, (low, 1), 0), RANK)
    lows.wait()
    lowered = jnp.where(slotrow[...] == row_slot, inputs[inner:, :].astype(F32), 0.0)
    inputs[inner:, :] = lowered.astype(BF)
    for h in range(heads):
        fetches[2 * h].wait()
        fetches[2 * h + 1].wait()
        cross = dot(state[h], phi_of(queries[h], left, right, cols).astype(BF), ((0,), (0,)))
        both = nd[h] + carried * cross
        inputs[h * HD : (h + 1) * HD, :] = (both[:HD, :] * (1.0 / both[ONE : ONE + 1, :])).astype(BF)
    compute()
    kept = [start(inputs, inputs_in, sems.at[next(sem)]), start(state, state_in, sems.at[next(sem)])]
    finish()
    for copy in kept:
        copy.wait()


def near_kernel(shards, w_out_in, w_up_in, inputs_in, *refs):
    near = near_tables(shards)
    own_out, outs = refs[0], refs[1 : 1 + HALVES * (len(near) - 1)]
    weights, inputs, held_out, sems, w_sems = refs[1 + len(outs) :]
    rows = held_out.shape[1] // HALVES
    outs = [own_out.at[pl.ds(h * rows, rows)] for h in range(HALVES)] + list(outs)
    load = start(inputs_in, inputs, sems.at[len(outs)])
    fetch, compute, finish = shard_parts(near, w_out_in, w_up_in, weights, w_sems, inputs, held_out, outs, sems)
    fetch()
    load.wait()
    compute()
    finish()


def logits_kernel(dims, shards, width, table, arrived, inputs, out, vocab, both, wide, placed, seen):
    groups, per_group, per_peer, page_len = dims
    tall = per_peer * page_len
    inner = inputs.shape[0]
    rows = vocab.shape[0] // groups
    _, _, _, base = packing(rows, inner + width)
    for g in range(groups):
        unpack(arrived.at[g], 0, vocab, g * rows, rows, inner + width)
        unpack(arrived.at[g], base, wide, g * tall, tall, width)
    place_pages(table, lax.axis_index("group"), seen, wide, placed, groups, per_group, per_peer, page_len)
    both[:inner, :] = inputs[...]
    both[inner:, :] = jnp.transpose(placed[...]).astype(BF)
    block = inputs.shape[1] // shards
    scored = dot(vocab[...], both[...])
    for j in range(shards):
        out[j] = scored[:, j * block : (j + 1) * block].astype(BF)


def norms_kernel(low, heads, ordered, ordered_t, state, segrow, left, right, cols, norms, mask):
    count = segrow.shape[1]
    mask[...] = same_upto(segrow)
    upto = mask[...].astype(BF)
    tag, held = state_corner(state)
    carried = jnp.where(segrow[...].astype(F32) + 1.0 == tag, 1.0, 0.0)
    value_lane = lax.broadcasted_iota(jnp.int32, (1, LANES), 1) < HD
    counted = carried * held + jnp.sum(mask[...], axis=0, keepdims=True)
    block = 256 if count % 256 == 0 else count
    increments = []
    before = []
    for h in range(heads):
        at = h * HEAD
        key = ordered[:, at + FEAT : at + 2 * FEAT] * BF(0.25)
        value = ordered[:, at + 2 * FEAT : at + HEAD]
        at = low + h * HEAD
        key_t = ordered_t[at + FEAT : at + 2 * FEAT, :]
        value_t = ordered_t[at + 2 * FEAT : at + HEAD, :]
        wide_key = key_t.astype(F32)
        wide_value = value_t.astype(F32)
        self_score = 0.25 * jnp.sum(wide_key * wide_key, axis=0, keepdims=True)
        self_value = jnp.sum(wide_value * wide_value, axis=0, keepdims=True)
        diagonal = (1.0 + self_score * (1.0 + 0.5 * self_score)) * self_value
        below = []
        for begin in range(0, count, block):
            end = begin + block
            kk = dot(key[:end], key_t[:, begin:end])
            vv = dot(value[:end], value_t[:, begin:end])
            gram = (1.0 + kk * (1.0 + 0.5 * kk)) * vv * mask[:end, begin:end]
            below.append(jnp.sum(gram, axis=0, keepdims=True))
        added = 2.0 * jnp.concatenate(below, axis=1) - diagonal
        held_state = state[h]
        against = dot(held_state, phi_of(key_t, left, right, cols).astype(BF), ((0,), (0,)))[:HD, :]
        along = jnp.sum(against * wide_value, axis=0, keepdims=True)
        increments.append(added + 2.0 * carried * along)
        wide_state = jnp.where(value_lane, held_state.astype(F32), 0.0)
        per_lane = jnp.sum(wide_state * wide_state, axis=0, keepdims=True)
        before.append(jnp.sum(per_lane, axis=1, keepdims=True))
    if heads % 8:
        increments.append(jnp.zeros((8 - heads % 8, count), F32))
    stacked = split3(jnp.concatenate(increments, axis=0))
    thrice = dot(stacked, upto)
    rows = thrice.shape[0] // 3
    summed = thrice[:rows] + thrice[rows : 2 * rows] + thrice[2 * rows :]
    for h in range(heads):
        total = carried * before[h] + summed[h : h + 1, :]
        norms[h : h + 1, :] = jnp.sqrt(total / (counted * float(FEAT * HD)))


def best_kernel(shards, pieces, best):
    whole = pieces[0].astype(F32)
    for i in range(1, shards):
        whole = whole + pieces[i].astype(F32)
    best[...] = jnp.max(whole, axis=0, keepdims=True)


def total_kernel(shards, own_terms, *refs):
    *terms, out = refs
    each = len(terms) // HALVES
    rows = out.shape[0] // HALVES

    def put(chosen):
        for h in range(HALVES):
            part = slice(h * rows, (h + 1) * rows)
            total = own_terms[part, :].astype(F32)
            for k in chosen:
                total = total + terms[h * each + k][...].astype(F32)
            out[part, :] = total.astype(BF)

    if shards != 4:
        return put(range(each))
    here = lax.axis_index("mp")
    middle = (here == 1) | (here == 2)
    pl.when(middle)(lambda: put((1, 2)))
    pl.when(jnp.logical_not(middle))(lambda: put((0, 1)))


def exchange(blocks, axis):
    return lax.all_to_all(blocks, axis, split_axis=0, concat_axis=0, tiled=True)


def ring_rows(values, axis):
    size = lax.axis_size(axis)
    steps = [lax.ppermute(values, axis, [(i, (i + by) % size) for i in range(size)]) for by in range(size - 1, 0, -1)]
    return [*steps, values]


def joined(*parts):
    return sum(part.astype(F32) for part in parts).astype(BF)


def on_middle(axis):
    here = lax.axis_index(axis)
    return (here == 1) | (here == 2)


def line_sums(far_terms, near_terms, axis, beside):
    size = lax.axis_size(axis)

    def send(values, *pairs):
        return lax.ppermute(values, axis, pairs)

    if size == 4:
        across = send(far_terms[0], (1, 2), (2, 1), (0, 3), (3, 0))
        inward = send(far_terms[1], (0, 1), (3, 2))
        across, inward, _ = lax.optimization_barrier((across, inward, beside))
        relayed = jnp.where(on_middle(axis), across, 0)
        paired = send(joined(near_terms[0], relayed), (0, 1), (1, 0), (2, 3), (3, 2))
        centre = send(joined(near_terms[1], inward), (1, 2), (2, 1))
        return [across, paired, centre]
    terms = {1: near_terms[0], -1: near_terms[1], size - 1: far_terms[0], 1 - size: far_terms[0]}
    for distance in range(size - 2, 1, -1):
        terms[distance], terms[-distance] = far_terms[2 * (size - 1 - distance) - 1 :][:2]
    going_up = going_down = None
    for step in range(1, size):
        to_up = terms[size - step]
        to_down = terms[step - size]
        if step > 1:
            to_up = joined(to_up, going_up)
            to_down = joined(to_down, going_down)
        going_up = send(to_up, *[(i, i + 1) for i in range(step)])
        going_down = send(to_down, *[(i, i - 1) for i in range(size - step, size)])
    return [going_up, going_down]


def on_device(
    hidden,
    norm_gain,
    qkv_weight,
    out_weight,
    adapter_down,
    adapter_up,
    vocab_rows,
    segments,
    request_adapter,
    adapter_slot,
    page_table,
):
    groups = lax.axis_size("group")
    shards = lax.axis_size("mp")
    own_shard = lax.axis_index("mp")
    count, model_width = hidden.shape
    per_group = page_table.shape[0] // groups
    per_peer = per_group // groups
    page_len = count // per_group
    dims = (groups, per_group, per_peer, page_len)
    qkv_cols = qkv_weight.shape[1]
    heads = qkv_cols // HEAD
    low = adapter_down.shape[1]
    inner = heads * HD
    width = model_width // shards
    sent = low + qkv_cols
    tall = per_peer * page_len
    packed = packing(tall, sent)[-1]
    some = shards * vocab_rows.shape[0]
    scored = groups * some
    aside = packing(some, inner + low + width)[-1] + packing(tall, width)[-1]
    shape = jax.ShapeDtypeStruct
    dma = pltpu.SemaphoreType.DMA
    picked = pltpu.SMEM((groups * per_peer + 1,), jnp.int32)

    left, right, cols = [jnp.asarray(t) for t in feature_tables()]
    segrow = segments.reshape(1, count)
    request_ids = jnp.arange(request_adapter.shape[0], dtype=jnp.int32)
    adapter_ids = jnp.arange(adapter_slot.shape[0], dtype=jnp.int32)

    outgoing = kernel_call(
        functools.partial(project_kernel, dims),
        pltpu.HBM((groups, packed, LANES), BF),
        [SMEM, ANY, VMEM, ANY, ANY],
        ANY,
        [
            pltpu.VMEM((count, model_width), BF),
            pltpu.VMEM((qkv_cols, model_width), BF),
            pltpu.VMEM((model_width, low), BF),
            pltpu.VMEM((count, model_width), BF),
            pltpu.VMEM((count, sent), F32 if page_len % 16 else BF),
            pltpu.VMEM((groups, packed, LANES), BF),
            picked,
            dma((7 + groups,)),
        ],
        2 * count * model_width * sent,
        2 * (count * model_width + model_width * sent),
    )(page_table, hidden, norm_gain, qkv_weight.T, adapter_down)
    arrived = exchange(outgoing, "group")

    after_vocab, after_adapter, later_hidden, _ = lax.optimization_barrier(
        (vocab_rows, request_adapter, hidden, outgoing)
    )
    some_vocab = ring_rows(after_vocab, "mp")
    request_slot = jnp.sum(jnp.where(after_adapter[:, None] == adapter_ids[None, :], adapter_slot[None, :], 0), axis=1)
    slots = jnp.sum(jnp.where(segrow == request_ids[:, None], request_slot[:, None], 0), axis=0, keepdims=True)
    slotrow = slots - own_shard * (low // RANK)
    window = window_size(shards, model_width)
    ahead = packing(some, inner + low + width)[-1]
    beside = kernel_call(
        functools.partial(residual_kernel, dims, shards, ahead),
        pltpu.HBM((groups, aside, LANES), BF),
        [SMEM, ANY],
        ANY,
        [
            pltpu.VMEM((count, window), BF),
            pltpu.VMEM((count, width), F32),
            pltpu.VMEM((groups, packing(tall, width)[-1], LANES), BF),
            picked,
            dma((groups + 1,)),
        ],
        1,
        1,
    )(page_table, later_hidden)
    beside = kernel_call(
        functools.partial(products_kernel, groups, shards),
        pltpu.HBM((groups, aside, LANES), BF),
        [ANY, ANY] + [VMEM] * shards + [ANY],
        ANY,
        [
            pltpu.VMEM((some, model_width), BF),
            pltpu.VMEM((inner, model_width), BF),
            pltpu.VMEM((low, model_width), BF),
            pltpu.VMEM((some, inner + low + width), F32),
            pltpu.VMEM((ahead, LANES), BF),
            dma((groups + 1 + heads,)),
        ],
        2 * some * model_width * (inner + low),
        2 * count * model_width,
        44 * MIB,
        {2 + shards: 0},
    )(out_weight, adapter_up, *some_vocab, beside)
    arrived, beside, slotrow = lax.optimization_barrier((arrived, beside, slotrow))

    ordered, ordered_t, state, nd = kernel_call(
        functools.partial(group_kernel, dims, low, heads),
        (
            pltpu.HBM((count, qkv_cols), BF),
            pltpu.HBM((sent, count), BF),
            pltpu.HBM((heads, PHI_PAD, LANES), BF),
            pltpu.HBM((heads, LANES, count), F32),
        ),
        [SMEM] + [VMEM] * 5,
        (ANY, ANY, ANY, ANY),
        [
            pltpu.VMEM((heads, PHI_PAD, LANES), BF),
            pltpu.VMEM((count, sent), F32),
            pltpu.VMEM((count, sent), F32),
            pltpu.VMEM((count, qkv_cols), BF),
            pltpu.VMEM((sent, count), BF),
            pltpu.VMEM((heads, LANES, count), F32),
            pltpu.VMEM((count, count), F32),
            pltpu.SMEM((groups,), jnp.int32),
            dma((3 + heads,)),
        ],
        heads * 2 * count * count * 512,
        6 * count * sent,
        40 * MIB,
    )(page_table, arrived, segrow, left, right, cols)
    beside, state = lax.optimization_barrier((beside, state))
    beside = exchange(beside, "group")
    state = lax.ppermute(state, "group", [(i, i + 1) for i in range(groups - 1)])

    far, near = len(far_tables(shards)), len(near_tables(shards))
    part = pltpu.HBM((width // HALVES, count), BF)
    *far_terms, inputs, kept_state = kernel_call(
        functools.partial(finish_kernel, low, heads, shards),
        [part] * (HALVES * far) + [pltpu.HBM((inner + low, count), BF), pltpu.HBM((heads, PHI_PAD, LANES), BF)],
        [ANY] * 2 + [VMEM] * 6 + [ANY] * 2,
        [ANY] * (HALVES * far + 2),
        [
            pltpu.VMEM((heads, FEAT, count), BF),
            pltpu.VMEM((heads, LANES, count), F32),
            pltpu.VMEM((far, inner + low, window), BF),
            pltpu.VMEM((inner + low, count), BF),
            pltpu.VMEM((far, width, count), BF),
            dma((HALVES * far + 2 * heads + 3,)),
            dma((2 * far,)),
        ],
        20 * count * (inner + low) * model_width,
        40 * count * model_width,
    )(ordered_t, nd, state, segrow, slotrow, left, right, cols, out_weight, adapter_up)
    own_term, *near_terms = kernel_call(
        functools.partial(near_kernel, shards),
        [pltpu.HBM((width, count), BF)] + [part] * (HALVES * (near - 1)),
        [ANY] * 3,
        [ANY] * (1 + HALVES * (near - 1)),
        [
            pltpu.VMEM((near, inner + low, window), BF),
            pltpu.VMEM((inner + low, count), BF),
            pltpu.VMEM((near, width, count), BF),
            dma((HALVES * near + 1,)),
            dma((2 * near,)),
        ],
        1,
        1,
    )(out_weight, adapter_up, inputs)

    [logits] = staged_call(
        functools.partial(logits_kernel, dims, shards, width),
        [shape((shards, scored, count // shards), BF)],
        [page_table],
        [inputs],
        [
            pltpu.VMEM((scored, inner + low + width), BF),
            pltpu.VMEM((inner + low + width, count), BF),
            pltpu.VMEM((count, width), F32),
            pltpu.VMEM((count, width), F32),
            pltpu.SMEM((groups,), jnp.int32),
        ],
        1,
        1,
        given=[beside],
        limit=(40 if scored <= 512 else 56) * MIB,
    )
    [state_norms] = staged_call(
        functools.partial(norms_kernel, low, heads),
        [shape((heads, count), F32)],
        [],
        [ordered, ordered_t, kept_state, segrow, left, right, cols],
        [pltpu.VMEM((count, count), F32)],
        1,
        1,
    )
    terms = []
    for h in range(HALVES):
        terms += line_sums(far_terms[h::HALVES], near_terms[h::HALVES], "mp", [state_norms, logits])
    logits = exchange(logits, "mp")
    best = kernel_call(
        functools.partial(best_kernel, shards),
        shape((1, count // shards), F32),
        [VMEM],
        VMEM,
        [],
        1,
        1,
        32 * MIB,
    )(logits)
    terms, best = lax.optimization_barrier((terms, best))
    update = kernel_call(
        functools.partial(total_kernel, shards),
        shape((width, count), BF),
        [VMEM] * (1 + len(terms)),
        VMEM,
        [],
        1,
        1,
        32 * MIB,
    )(own_term, *terms)
    return update.T, state_norms, best.reshape(-1)


def solution(mesh):
    placed = (
        P("group", None),
        P(),
        P(None, "mp"),
        P("mp", None),
        P(None, "mp"),
        P("mp", None),
        P(("group", "mp"), None),
        P("group"),
        P(),
        P(),
        P(),
    )
    return jax.shard_map(
        on_device,
        mesh=mesh,
        in_specs=placed,
        out_specs=(P("group", "mp"), P("mp", "group"), P(("group", "mp"))),
        check_vma=False,
    )
```

```python
import functools

import jax
import jax.numpy as jnp
import numpy as np
from jax import lax
from jax.experimental import pallas as pl
from jax.experimental.pallas import tpu as pltpu
from jax.sharding import PartitionSpec as P

FEAT = 16
HD = 112
RANK = 16
EPSILON = 1e-05
HEAD = 2 * FEAT + HD
PHI = 1 + FEAT + FEAT * (FEAT + 1) // 2
PHI_PAD = 160
LANES = 128
ONE, TAG, REST = HD, HD + 1, HD + 2
MIB = 1024 * 1024
VMEM_LIMIT = 60 * MIB

BF = jnp.bfloat16
F32 = jnp.float32
SMEM = pl.BlockSpec(memory_space=pltpu.SMEM)
VMEM = pl.BlockSpec(memory_space=pltpu.VMEM)
ANY = pl.BlockSpec(memory_space=pltpu.HBM)


def feature_tables():
    left = np.zeros((PHI_PAD, FEAT), np.float32)
    right = np.zeros((PHI_PAD, FEAT), np.float32)
    cols = np.zeros((PHI_PAD, 8), np.float32)
    cols[0, :3] = 1.0
    at = 1
    for i in range(FEAT):
        left[at, i] = 1.0
        cols[at, 1] = 1.0
        cols[at, 2] = FEAT**-0.25
        at += 1
    for i in range(FEAT):
        for j in range(i, FEAT):
            left[at, i] = 1.0
            right[at, j] = 1.0
            cols[at, 2] = (1.0 if i == j else 2.0**0.5) / (2.0 * FEAT) ** 0.5
            at += 1
    return left.astype(jnp.bfloat16), right.astype(jnp.bfloat16), cols


def dot(a, b, dims=((1,), (0,))):
    return lax.dot_general(a, b, (dims, ((), ())), preferred_element_type=F32)


def kernel_call(body, out_shape, in_specs, out_specs, scratch, flops, nbytes, limit=VMEM_LIMIT, aliases=None):
    return pl.pallas_call(
        body,
        out_shape=out_shape,
        in_specs=in_specs,
        out_specs=out_specs,
        scratch_shapes=scratch,
        input_output_aliases=aliases or {},
        compiler_params=pltpu.CompilerParams(vmem_limit_bytes=limit),
        cost_estimate=pl.CostEstimate(flops=flops, bytes_accessed=nbytes, transcendentals=0),
    )


def start(source, target, sem):
    copy = pltpu.make_async_copy(source, target, sem)
    copy.start()
    return copy


def packing(rows, columns):
    tiles, rest = divmod(columns, LANES)
    share = LANES // rest if rest and LANES % rest == 0 else 1
    if rows % (16 * share):
        share = 1
    return tiles, rest, share, tiles * rows + (rows // share if rest else 0)


def pack(block, target, base):
    rows = block.shape[0]
    tiles, rest, share, _ = packing(*block.shape)
    for t in range(tiles):
        target[base + t * rows : base + (t + 1) * rows, :] = block[:, t * LANES : (t + 1) * LANES].astype(BF)
    if rest:
        short = rows // share
        last = [block[q * short : (q + 1) * short, tiles * LANES :] for q in range(share)]
        if share * rest < LANES:
            last.append(jnp.zeros((short, LANES - share * rest), block.dtype))
        at = base + tiles * rows
        target[at : at + short, :] = jnp.concatenate(last, axis=1).astype(BF)


def unpack(source, base, target, row, rows, columns):
    tiles, rest, share, _ = packing(rows, columns)
    for t in range(tiles):
        piece = source[base + t * rows : base + (t + 1) * rows, :]
        target[row : row + rows, t * LANES : (t + 1) * LANES] = piece.astype(target.dtype)
    if rest:
        short = rows // share
        at = base + tiles * rows
        last = source[at : at + short, :].astype(F32)
        for q in range(share):
            piece = last[:, q * rest : (q + 1) * rest].astype(target.dtype)
            target[row + q * short : row + (q + 1) * short, tiles * LANES : columns] = piece


def staged_call(body, out_shape, scalars, operands, scratch, flops, nbytes, given=(), limit=VMEM_LIMIT):
    buffers = [pltpu.VMEM(x.shape, x.dtype) for x in list(operands) + list(out_shape)]
    ins, outs = len(operands), len(out_shape)

    def run(*refs):
        values, refs = refs[: len(scalars)], refs[len(scalars) :]
        ready, refs = refs[: len(given)], refs[len(given) :]
        far, refs = refs[: ins + outs], refs[ins + outs :]
        near, extra, sems = refs[: ins + outs], refs[ins + outs : -1], refs[-1]
        loads = [start(far[k], near[k], sems.at[k]) for k in range(ins)]
        for load in loads:
            load.wait()
        body(*values, *ready, *near, *extra)
        sends = [start(near[k], far[k], sems.at[k]) for k in range(ins, ins + outs)]
        for send in sends:
            send.wait()

    return kernel_call(
        run,
        [pltpu.HBM(x.shape, x.dtype) for x in out_shape],
        [SMEM] * len(scalars) + [VMEM] * len(given) + [ANY] * ins,
        [ANY] * outs,
        buffers + list(scratch) + [pltpu.SemaphoreType.DMA((ins + outs,))],
        flops,
        nbytes,
        limit,
    )(*scalars, *given, *operands)


def pick_pages(table, own, picked, groups, per_group, per_peer):
    def one_group(g, carry):
        spot = g * per_peer
        for k in range(per_group):
            local = table[g * per_group + k] - own * per_group
            picked[spot] = local
            spot = spot + jnp.where((local >= 0) & (local < per_group), 1, 0)
        return carry

    lax.fori_loop(0, groups, one_group, 0)


def place_pages(table, own, seen, source, target, groups, per_group, per_peer, page_len):
    for g in range(groups):
        seen[g] = 0
    for k in range(per_group):
        holder = lax.div(table[own * per_group + k], per_group)
        slot = holder * per_peer + seen[holder]
        seen[holder] = seen[holder] + 1
        start = pl.multiple_of(slot * page_len, page_len)
        target[k * page_len : (k + 1) * page_len, :] = source[pl.ds(start, page_len), :]


def picked_rows(source, picked, g, per_peer, page_len):
    pages = []
    for b in range(per_peer):
        at = pl.multiple_of(picked[g * per_peer + b] * page_len, page_len)
        pages.append(source[pl.ds(at, page_len), :])
    return jnp.concatenate(pages, axis=0)


def project_kernel(
    dims, table, hidden_in, gain, wq_in, wd_in, out_in, hidden, wq, wd, normed, wide, out, picked, sems
):
    groups, per_group, per_peer, page_len = dims
    rows, model_width = hidden.shape
    low = wd.shape[1]
    pieces = 4
    part = rows // pieces
    strip = wq.shape[0] // 2
    loads = [
        start(hidden_in.at[pl.ds(k * part, part)], hidden.at[pl.ds(k * part, part)], sems.at[k]) for k in range(pieces)
    ]
    weights = [start(wd_in, wd, sems.at[pieces])]
    for k in range(2):
        half = pl.ds(k * strip, strip)
        weights.append(start(wq_in.at[half], wq.at[half], sems.at[pieces + 1 + k]))
    pick_pages(table, lax.axis_index("group"), picked, groups, per_group, per_peer)
    step = 32
    scale = gain[...].reshape(1, model_width)

    def norm_rows(i, carry):
        at = pl.ds(pl.multiple_of(i * step, step), step)
        x = hidden[at, :].astype(F32)
        meansq = jnp.mean(x * x, axis=-1, keepdims=True)
        normed[at, :] = (x * lax.rsqrt(meansq + EPSILON) * scale).astype(BF)
        return carry

    for k in range(pieces):
        loads[k].wait()
        lax.fori_loop(k * part // step, (k + 1) * part // step, norm_rows, 0, unroll=2)
    for load in weights:
        load.wait()
    wide[:, :low] = dot(normed[...], wd[...]).astype(wide.dtype)
    wide[:, low:] = dot(normed[...], wq[...], ((1,), (1,))).astype(wide.dtype)
    sends = []
    for g in range(groups):
        pack(picked_rows(wide, picked, g, per_peer, page_len), out.at[g], 0)
        sends.append(start(out.at[g], out_in.at[g], sems.at[pieces + 3 + g]))
    for send in sends:
        send.wait()


def residual_kernel(dims, shards, base, table, hidden_in, out_in, window, wide, pages, picked, sems):
    groups, per_group, per_peer, page_len = dims
    own_shard = lax.axis_index("mp")
    for j in range(shards):

        @pl.when(own_shard == j)
        def _(j=j):
            columns, _ = column_window(j, shards, hidden_in.shape[1])
            start(hidden_in.at[:, columns], window, sems.at[groups])

    pick_pages(table, lax.axis_index("group"), picked, groups, per_group, per_peer)
    pltpu.make_async_copy(hidden_in.at[:, 0 : window.shape[1]], window, sems.at[groups]).wait()
    for j in range(shards):

        @pl.when(own_shard == j)
        def _(j=j):
            _, at = column_window(j, shards, hidden_in.shape[1])
            wide[...] = window[:, at : at + wide.shape[1]].astype(F32)

    sends = []
    for g in range(groups):
        pack(picked_rows(wide, picked, g, per_peer, page_len), pages.at[g], 0)
        sends.append(start(pages.at[g], out_in.at[g, pl.ds(base, pages.shape[1])], sems.at[g]))
    for send in sends:
        send.wait()


def products_kernel(groups, shards, w_out_in, w_up_in, *refs):
    blocks = refs[:shards]
    _, out_in, vocab, w_out, w_up, products, shared, sems = refs[shards:]
    inner, model_width = w_out.shape
    low = w_up.shape[0]
    width = model_width // shards
    held = blocks[0].shape[0]
    loads = [start(w_up_in, w_up, sems.at[groups])]
    for k in range(inner // HD):
        rows = pl.ds(k * HD, HD)
        loads.append(start(w_out_in.at[rows], w_out.at[rows], sems.at[groups + 1 + k]))
    own_shard = lax.axis_index("mp")
    for i in range(shards):
        at = lax.rem(own_shard + i + 1, shards) * held
        vocab[pl.ds(pl.multiple_of(at, held), held), :] = blocks[i][...]
    for load in loads:
        load.wait()
    products[:, :inner] = dot(vocab[...], w_out[...], ((1,), (1,)))
    products[:, inner : inner + low] = dot(vocab[...], w_up[...], ((1,), (1,)))
    for j in range(shards):

        @pl.when(own_shard == j)
        def _(j=j):
            products[:, inner + low :] = vocab[:, j * width : (j + 1) * width].astype(F32)

    pack(products[...], shared, 0)
    sends = [start(shared, out_in.at[g, pl.ds(0, shared.shape[0])], sems.at[g]) for g in range(groups)]
    for send in sends:
        send.wait()


def phi_of(vectors, left, right, cols):
    first = dot(left[...], vectors) + cols[:, 0:1]
    second = dot(right[...], vectors) + cols[:, 1:2]
    return first * second * cols[:, 2:3]


def with_ones(values):
    lane = lax.broadcasted_iota(jnp.int32, (values.shape[0], LANES - HD), 1)
    return jnp.concatenate([values, jnp.where(lane == 0, 1.0, 0.0).astype(values.dtype)], axis=1)


def with_ones_t(values):
    row = lax.broadcasted_iota(jnp.int32, (LANES - HD, values.shape[1]), 0)
    return jnp.concatenate([values, jnp.where(row == 0, 1.0, 0.0).astype(values.dtype)], axis=0)


def same_upto(segrow):
    count = segrow.shape[1]
    ids = segrow[...].astype(F32)
    column = jnp.transpose(jnp.broadcast_to(ids, (8, count)))[:, 0:1]
    behind = lax.broadcasted_iota(jnp.int32, (count, count), 0)
    ahead = lax.broadcasted_iota(jnp.int32, (count, count), 1)
    return jnp.where((column == ids) & (behind <= ahead), 1.0, 0.0)


def group_kernel(
    dims, low, heads, table, arrived, segrow, left, right, cols, ordered_in, ordered_t_in, state_in, nd_in,
    state, wide, placed, ordered, ordered_t, nd, mask, seen, sems
):
    groups, per_group, per_peer, page_len = dims
    tall = per_peer * page_len
    count, sent = placed.shape
    mask[...] = same_upto(segrow)
    for g in range(groups):
        unpack(arrived.at[g], 0, wide, g * tall, tall, sent)
    place_pages(table, lax.axis_index("group"), seen, wide, placed, groups, per_group, per_peer, page_len)
    ordered[...] = placed[:, low:].astype(BF)
    for at in range(0, sent, LANES):
        end = min(at + LANES, sent)
        ordered_t[at:end, :] = jnp.transpose(placed[:, at:end]).astype(BF)
    sends = [start(ordered_t, ordered_t_in, sems.at[0]), start(ordered, ordered_in, sems.at[1])]

    last = segrow[:, count - 1 : count]
    member = jnp.where(segrow[...] == last, 1.0, 0.0)
    total = jnp.sum(member, axis=1, keepdims=True)
    fine = total - total.astype(BF).astype(F32)
    tag = last.astype(F32) + 1.0
    row = lax.broadcasted_iota(jnp.int32, (PHI_PAD, LANES), 0)
    lane = lax.broadcasted_iota(jnp.int32, (PHI_PAD, LANES), 1)
    block = 256 if count % 256 == 0 else count
    for h in range(heads):
        at = h * HEAD
        key = ordered[:, at + FEAT : at + 2 * FEAT] * BF(0.25)
        value = ordered[:, at + 2 * FEAT : at + HEAD]
        at = low + h * HEAD
        query_t = ordered_t[at : at + FEAT, :]
        key_t = ordered_t[at + FEAT : at + 2 * FEAT, :]
        extended_t = with_ones_t(ordered_t[at + 2 * FEAT : at + HEAD, :])

        phi = (phi_of(key_t, left, right, cols) * member).astype(BF)
        summed = dot(phi, with_ones(value))
        summed = jnp.where((row == 0) & (lane == TAG), tag, summed)
        summed = jnp.where((row == 0) & (lane == REST), fine, summed)
        state[h] = summed.astype(BF)

        for begin in range(0, count, block):
            end = begin + block
            s = dot(key[:end], query_t[:, begin:end])
            w = (1.0 + s * (1.0 + 0.5 * s)) * mask[:end, begin:end]
            nd[h, :, begin:end] = dot(extended_t[:, :end], w.astype(BF))
        sends.append(start(nd.at[h], nd_in.at[h], sems.at[3 + h]))
    sends.append(start(state, state_in, sems.at[2]))
    for send in sends:
        send.wait()


def split3(x):
    a = x.astype(BF)
    rest = x - a.astype(F32)
    b = rest.astype(BF)
    return jnp.concatenate([a, b, (rest - b.astype(F32)).astype(BF)], axis=0)


def state_corner(state):
    corner = state[0, 0:1, :].astype(F32)
    return corner[:, TAG : TAG + 1], corner[:, ONE : ONE + 1] + corner[:, REST : REST + 1]


def column_window(j, shards, model_width):
    width = model_width // shards
    size = window_size(shards, model_width)
    first = min(j * width // LANES * LANES, model_width - size)
    return slice(first, first + size), j * width - first


def window_size(shards, model_width):
    width = model_width // shards
    return max(-(-(j * width % LANES + width) // LANES) * LANES for j in range(shards))


def far_tables(shards):
    if shards == 4:
        return [(3, 3, 0, 0), (2, None, None, 1)]
    tables = [tuple({0: shards - 1, shards - 1: 0}.get(own) for own in range(shards))]
    for distance in range(shards - 2, 1, -1):
        tables += [offset_table(distance, shards), offset_table(-distance, shards)]
    return tables


def near_tables(shards):
    if shards == 4:
        return [(0, 1, 2, 3), (1, 0, 3, 2), (None, 2, 1, None)]
    return [offset_table(offset, shards) for offset in (0, 1, -1)]


def offset_table(offset, shards):
    return tuple(own + offset if 0 <= own + offset < shards else None for own in range(shards))


def each_shard(tables):
    for k, table in enumerate(tables):
        for own, j in enumerate(table):
            if j is not None:
                yield k, own, j


def shard_parts(tables, w_out_in, w_up_in, weights, w_sems, inputs, held_out, outs, sems):
    own_shard = lax.axis_index("mp")
    shards = len(tables[0])
    inner, model_width = w_out_in.shape
    width = model_width // shards

    def copies(k, j):
        window, _ = column_window(j, shards, model_width)
        return (
            pltpu.make_async_copy(w_out_in.at[:, window], weights.at[k, pl.ds(0, inner)], w_sems.at[2 * k]),
            pltpu.make_async_copy(
                w_up_in.at[:, window], weights.at[k, pl.ds(inner, w_up_in.shape[0])], w_sems.at[2 * k + 1]
            ),
        )

    def fetch():
        for k, own, j in each_shard(tables):

            @pl.when(own_shard == own)
            def _(k=k, j=j):
                for copy in copies(k, j):
                    copy.start()

    def compute():
        for k, own, j in each_shard(tables):

            @pl.when(own_shard == own)
            def _(k=k, j=j):
                for copy in copies(k, j):
                    copy.wait()
                _, at = column_window(j, shards, model_width)
                held_out[k] = dot(weights[k, :, at : at + width], inputs[...], ((0,), (0,))).astype(BF)
                start(held_out.at[k], outs[k], sems.at[k])

    def finish():
        for k, own, j in each_shard(tables):

            @pl.when(own_shard == own)
            def _(k=k):
                pltpu.make_async_copy(held_out.at[k], outs[k], sems.at[k]).wait()

    return fetch, compute, finish


def finish_kernel(
    low, heads, shards, ordered_t_in, nd_in, state, segrow, slotrow, left, right, cols, w_out_in, w_up_in, *refs
):
    far = far_tables(shards)
    outs = refs[: len(far)]
    inputs_in, state_in, queries, nd, weights, inputs, held_out, sems, w_sems = refs[len(far) :]
    inner = heads * HD
    sem = iter(range(len(far), len(far) + 2 * heads + 3))
    lows = start(ordered_t_in.at[pl.ds(0, low)], inputs.at[pl.ds(inner, low)], sems.at[next(sem)])
    fetches = []
    for h in range(heads):
        rows = pl.ds(low + h * HEAD, FEAT)
        fetches.append(start(ordered_t_in.at[rows], queries.at[h], sems.at[next(sem)]))
        fetches.append(start(nd_in.at[h], nd.at[h], sems.at[next(sem)]))
    fetch_weights, compute, finish = shard_parts(
        far, w_out_in, w_up_in, weights, w_sems, inputs, held_out, outs, sems
    )
    fetch_weights()
    tag, _ = state_corner(state)
    carried = jnp.where(segrow[...].astype(F32) + 1.0 == tag, 1.0, 0.0)
    row_slot = lax.div(lax.broadcasted_iota(jnp.int32, (low, 1), 0), RANK)
    lows.wait()
    lowered = jnp.where(slotrow[...] == row_slot, inputs[inner:, :].astype(F32), 0.0)
    inputs[inner:, :] = lowered.astype(BF)
    for h in range(heads):
        fetches[2 * h].wait()
        fetches[2 * h + 1].wait()
        cross = dot(state[h], phi_of(queries[h], left, right, cols).astype(BF), ((0,), (0,)))
        both = nd[h] + carried * cross
        inputs[h * HD : (h + 1) * HD, :] = (both[:HD, :] * (1.0 / both[ONE : ONE + 1, :])).astype(BF)
    compute()
    kept = [start(inputs, inputs_in, sems.at[next(sem)]), start(state, state_in, sems.at[next(sem)])]
    finish()
    for copy in kept:
        copy.wait()


def near_kernel(shards, w_out_in, w_up_in, inputs_in, *refs):
    near = near_tables(shards)
    outs = refs[: len(near)]
    weights, inputs, held_out, sems, w_sems = refs[len(near) :]
    load = start(inputs_in, inputs, sems.at[len(near)])
    fetch, compute, finish = shard_parts(near, w_out_in, w_up_in, weights, w_sems, inputs, held_out, outs, sems)
    fetch()
    load.wait()
    compute()
    finish()


def logits_kernel(dims, shards, width, table, arrived, inputs, out, vocab, both, wide, placed, seen):
    groups, per_group, per_peer, page_len = dims
    tall = per_peer * page_len
    inner = inputs.shape[0]
    rows = vocab.shape[0] // groups
    _, _, _, base = packing(rows, inner + width)
    for g in range(groups):
        unpack(arrived.at[g], 0, vocab, g * rows, rows, inner + width)
        unpack(arrived.at[g], base, wide, g * tall, tall, width)
    place_pages(table, lax.axis_index("group"), seen, wide, placed, groups, per_group, per_peer, page_len)
    both[:inner, :] = inputs[...]
    both[inner:, :] = jnp.transpose(placed[...]).astype(BF)
    block = inputs.shape[1] // shards
    scored = dot(vocab[...], both[...])
    for j in range(shards):
        out[j] = scored[:, j * block : (j + 1) * block].astype(BF)


def norms_kernel(low, heads, ordered, ordered_t, state, segrow, left, right, cols, norms, mask):
    count = segrow.shape[1]
    mask[...] = same_upto(segrow)
    upto = mask[...].astype(BF)
    tag, held = state_corner(state)
    carried = jnp.where(segrow[...].astype(F32) + 1.0 == tag, 1.0, 0.0)
    value_lane = lax.broadcasted_iota(jnp.int32, (1, LANES), 1) < HD
    counted = carried * held + jnp.sum(mask[...], axis=0, keepdims=True)
    block = 256 if count % 256 == 0 else count
    increments = []
    before = []
    for h in range(heads):
        at = h * HEAD
        key = ordered[:, at + FEAT : at + 2 * FEAT] * BF(0.25)
        value = ordered[:, at + 2 * FEAT : at + HEAD]
        at = low + h * HEAD
        key_t = ordered_t[at + FEAT : at + 2 * FEAT, :]
        value_t = ordered_t[at + 2 * FEAT : at + HEAD, :]
        wide_key = key_t.astype(F32)
        wide_value = value_t.astype(F32)
        self_score = 0.25 * jnp.sum(wide_key * wide_key, axis=0, keepdims=True)
        self_value = jnp.sum(wide_value * wide_value, axis=0, keepdims=True)
        diagonal = (1.0 + self_score * (1.0 + 0.5 * self_score)) * self_value
        below = []
        for begin in range(0, count, block):
            end = begin + block
            kk = dot(key[:end], key_t[:, begin:end])
            vv = dot(value[:end], value_t[:, begin:end])
            gram = (1.0 + kk * (1.0 + 0.5 * kk)) * vv * mask[:end, begin:end]
            below.append(jnp.sum(gram, axis=0, keepdims=True))
        added = 2.0 * jnp.concatenate(below, axis=1) - diagonal
        held_state = state[h]
        against = dot(held_state, phi_of(key_t, left, right, cols).astype(BF), ((0,), (0,)))[:HD, :]
        along = jnp.sum(against * wide_value, axis=0, keepdims=True)
        increments.append(added + 2.0 * carried * along)
        wide_state = jnp.where(value_lane, held_state.astype(F32), 0.0)
        per_lane = jnp.sum(wide_state * wide_state, axis=0, keepdims=True)
        before.append(jnp.sum(per_lane, axis=1, keepdims=True))
    if heads % 8:
        increments.append(jnp.zeros((8 - heads % 8, count), F32))
    stacked = split3(jnp.concatenate(increments, axis=0))
    thrice = dot(stacked, upto)
    rows = thrice.shape[0] // 3
    summed = thrice[:rows] + thrice[rows : 2 * rows] + thrice[2 * rows :]
    for h in range(heads):
        total = carried * before[h] + summed[h : h + 1, :]
        norms[h : h + 1, :] = jnp.sqrt(total / (counted * float(FEAT * HD)))


def best_kernel(shards, pieces, best):
    whole = pieces[0].astype(F32)
    for i in range(1, shards):
        whole = whole + pieces[i].astype(F32)
    best[...] = jnp.max(whole, axis=0, keepdims=True)


def exchange(blocks, axis):
    return lax.all_to_all(blocks, axis, split_axis=0, concat_axis=0, tiled=True)


def ring_rows(values, axis):
    size = lax.axis_size(axis)
    steps = [lax.ppermute(values, axis, [(i, (i + by) % size) for i in range(size)]) for by in range(size - 1, 0, -1)]
    return [*steps, values]


def joined(*parts):
    return sum(part.astype(F32) for part in parts).astype(BF)


def line_sums(far_terms, near_terms, axis, beside):
    size = lax.axis_size(axis)

    def send(values, *pairs):
        return lax.ppermute(values, axis, pairs)

    own_term = near_terms[0]
    if size == 4:
        here = lax.axis_index(axis)
        middle = (here == 1) | (here == 2)
        across = send(far_terms[0], (1, 2), (2, 1), (0, 3), (3, 0))
        inward = send(far_terms[1], (0, 1), (3, 2))
        across, inward, beside = lax.optimization_barrier((across, inward, beside))
        relayed = jnp.where(middle, across, 0)
        paired = send(joined(near_terms[1], relayed), (0, 1), (1, 0), (2, 3), (3, 2))
        centre = send(joined(near_terms[2], inward), (1, 2), (2, 1))
        return (own_term, jnp.where(middle, centre, across), paired), beside
    terms = {1: near_terms[1], -1: near_terms[2], size - 1: far_terms[0], 1 - size: far_terms[0]}
    for distance in range(size - 2, 1, -1):
        terms[distance], terms[-distance] = far_terms[2 * (size - 1 - distance) - 1 :][:2]
    going_up = going_down = None
    for step in range(1, size):
        to_up = terms[size - step]
        to_down = terms[step - size]
        if step > 1:
            to_up = joined(to_up, going_up)
            to_down = joined(to_down, going_down)
        going_up = send(to_up, *[(i, i + 1) for i in range(step)])
        going_down = send(to_down, *[(i, i - 1) for i in range(size - step, size)])
    return (own_term, going_up, going_down), beside


def on_device(
    hidden,
    norm_gain,
    qkv_weight,
    out_weight,
    adapter_down,
    adapter_up,
    vocab_rows,
    segments,
    request_adapter,
    adapter_slot,
    page_table,
):
    groups = lax.axis_size("group")
    shards = lax.axis_size("mp")
    own_shard = lax.axis_index("mp")
    count, model_width = hidden.shape
    per_group = page_table.shape[0] // groups
    per_peer = per_group // groups
    page_len = count // per_group
    dims = (groups, per_group, per_peer, page_len)
    qkv_cols = qkv_weight.shape[1]
    heads = qkv_cols // HEAD
    low = adapter_down.shape[1]
    inner = heads * HD
    width = model_width // shards
    sent = low + qkv_cols
    tall = per_peer * page_len
    packed = packing(tall, sent)[-1]
    some = shards * vocab_rows.shape[0]
    scored = groups * some
    aside = packing(some, inner + low + width)[-1] + packing(tall, width)[-1]
    shape = jax.ShapeDtypeStruct
    dma = pltpu.SemaphoreType.DMA
    picked = pltpu.SMEM((groups * per_peer + 1,), jnp.int32)

    left, right, cols = [jnp.asarray(t) for t in feature_tables()]
    segrow = segments.reshape(1, count)
    request_ids = jnp.arange(request_adapter.shape[0], dtype=jnp.int32)
    adapter_ids = jnp.arange(adapter_slot.shape[0], dtype=jnp.int32)

    outgoing = kernel_call(
        functools.partial(project_kernel, dims),
        pltpu.HBM((groups, packed, LANES), BF),
        [SMEM, ANY, VMEM, ANY, ANY],
        ANY,
        [
            pltpu.VMEM((count, model_width), BF),
            pltpu.VMEM((qkv_cols, model_width), BF),
            pltpu.VMEM((model_width, low), BF),
            pltpu.VMEM((count, model_width), BF),
            pltpu.VMEM((count, sent), F32 if page_len % 16 else BF),
            pltpu.VMEM((groups, packed, LANES), BF),
            picked,
            dma((7 + groups,)),
        ],
        2 * count * model_width * sent,
        2 * (count * model_width + model_width * sent),
    )(page_table, hidden, norm_gain, qkv_weight.T, adapter_down)
    arrived = exchange(outgoing, "group")

    after_vocab, after_adapter, later_hidden, _ = lax.optimization_barrier(
        (vocab_rows, request_adapter, hidden, outgoing)
    )
    some_vocab = ring_rows(after_vocab, "mp")
    request_slot = jnp.sum(jnp.where(after_adapter[:, None] == adapter_ids[None, :], adapter_slot[None, :], 0), axis=1)
    slots = jnp.sum(jnp.where(segrow == request_ids[:, None], request_slot[:, None], 0), axis=0, keepdims=True)
    slotrow = slots - own_shard * (low // RANK)
    window = window_size(shards, model_width)
    ahead = packing(some, inner + low + width)[-1]
    beside = kernel_call(
        functools.partial(residual_kernel, dims, shards, ahead),
        pltpu.HBM((groups, aside, LANES), BF),
        [SMEM, ANY],
        ANY,
        [
            pltpu.VMEM((count, window), BF),
            pltpu.VMEM((count, width), F32),
            pltpu.VMEM((groups, packing(tall, width)[-1], LANES), BF),
            picked,
            dma((groups + 1,)),
        ],
        1,
        1,
    )(page_table, later_hidden)
    beside = kernel_call(
        functools.partial(products_kernel, groups, shards),
        pltpu.HBM((groups, aside, LANES), BF),
        [ANY, ANY] + [VMEM] * shards + [ANY],
        ANY,
        [
            pltpu.VMEM((some, model_width), BF),
            pltpu.VMEM((inner, model_width), BF),
            pltpu.VMEM((low, model_width), BF),
            pltpu.VMEM((some, inner + low + width), F32),
            pltpu.VMEM((ahead, LANES), BF),
            dma((groups + 1 + heads,)),
        ],
        2 * some * model_width * (inner + low),
        2 * count * model_width,
        44 * MIB,
        {2 + shards: 0},
    )(out_weight, adapter_up, *some_vocab, beside)
    arrived, beside, slotrow = lax.optimization_barrier((arrived, beside, slotrow))

    ordered, ordered_t, state, nd = kernel_call(
        functools.partial(group_kernel, dims, low, heads),
        (
            pltpu.HBM((count, qkv_cols), BF),
            pltpu.HBM((sent, count), BF),
            pltpu.HBM((heads, PHI_PAD, LANES), BF),
            pltpu.HBM((heads, LANES, count), F32),
        ),
        [SMEM] + [VMEM] * 5,
        (ANY, ANY, ANY, ANY),
        [
            pltpu.VMEM((heads, PHI_PAD, LANES), BF),
            pltpu.VMEM((count, sent), F32),
            pltpu.VMEM((count, sent), F32),
            pltpu.VMEM((count, qkv_cols), BF),
            pltpu.VMEM((sent, count), BF),
            pltpu.VMEM((heads, LANES, count), F32),
            pltpu.VMEM((count, count), F32),
            pltpu.SMEM((groups,), jnp.int32),
            dma((3 + heads,)),
        ],
        heads * 2 * count * count * 512,
        6 * count * sent,
        40 * MIB,
    )(page_table, arrived, segrow, left, right, cols)
    beside, state = lax.optimization_barrier((beside, state))
    beside = exchange(beside, "group")
    state = lax.ppermute(state, "group", [(i, i + 1) for i in range(groups - 1)])

    far, near = len(far_tables(shards)), len(near_tables(shards))
    part = pltpu.HBM((width, count), BF)
    *far_terms, inputs, kept_state = kernel_call(
        functools.partial(finish_kernel, low, heads, shards),
        [part] * far + [pltpu.HBM((inner + low, count), BF), pltpu.HBM((heads, PHI_PAD, LANES), BF)],
        [ANY] * 2 + [VMEM] * 6 + [ANY] * 2,
        [ANY] * (far + 2),
        [
            pltpu.VMEM((heads, FEAT, count), BF),
            pltpu.VMEM((heads, LANES, count), F32),
            pltpu.VMEM((far, inner + low, window), BF),
            pltpu.VMEM((inner + low, count), BF),
            pltpu.VMEM((far, width, count), BF),
            dma((far + 2 * heads + 3,)),
            dma((2 * far,)),
        ],
        20 * count * (inner + low) * model_width,
        40 * count * model_width,
    )(ordered_t, nd, state, segrow, slotrow, left, right, cols, out_weight, adapter_up)
    near_terms = kernel_call(
        functools.partial(near_kernel, shards),
        [part] * near,
        [ANY] * 3,
        [ANY] * near,
        [
            pltpu.VMEM((near, inner + low, window), BF),
            pltpu.VMEM((inner + low, count), BF),
            pltpu.VMEM((near, width, count), BF),
            dma((near + 1,)),
            dma((2 * near,)),
        ],
        1,
        1,
    )(out_weight, adapter_up, inputs)

    [logits] = staged_call(
        functools.partial(logits_kernel, dims, shards, width),
        [shape((shards, scored, count // shards), BF)],
        [page_table],
        [inputs],
        [
            pltpu.VMEM((scored, inner + low + width), BF),
            pltpu.VMEM((inner + low + width, count), BF),
            pltpu.VMEM((count, width), F32),
            pltpu.VMEM((count, width), F32),
            pltpu.SMEM((groups,), jnp.int32),
        ],
        1,
        1,
        given=[beside],
        limit=(40 if scored <= 512 else 56) * MIB,
    )
    [state_norms] = staged_call(
        functools.partial(norms_kernel, low, heads),
        [shape((heads, count), F32)],
        [],
        [ordered, ordered_t, kept_state, segrow, left, right, cols],
        [pltpu.VMEM((count, count), F32)],
        1,
        1,
    )
    (own_term, *others), [state_norms, _] = line_sums(far_terms, near_terms, "mp", [state_norms, logits])
    logits = exchange(logits, "mp")
    best = kernel_call(
        functools.partial(best_kernel, shards),
        shape((1, count // shards), F32),
        [VMEM],
        VMEM,
        [],
        1,
        1,
        32 * MIB,
    )(logits)
    own_term, best = lax.optimization_barrier((own_term, best))
    return joined(own_term, *others).T, state_norms, best.reshape(-1)


def solution(mesh):
    placed = (
        P("group", None),
        P(),
        P(None, "mp"),
        P("mp", None),
        P(None, "mp"),
        P("mp", None),
        P(("group", "mp"), None),
        P("group"),
        P(),
        P(),
        P(),
    )
    return jax.shard_map(
        on_device,
        mesh=mesh,
        in_specs=placed,
        out_specs=(P("group", "mp"), P("mp", "group"), P(("group", "mp"))),
        check_vma=False,
    )
```

```python
import functools

import jax
import jax.numpy as jnp
import numpy as np
from jax import lax
from jax.experimental import pallas as pl
from jax.experimental.pallas import tpu as pltpu
from jax.sharding import PartitionSpec as P

FEAT = 16
HD = 112
RANK = 16
EPSILON = 1e-05
HEAD = 2 * FEAT + HD
PHI = 1 + FEAT + FEAT * (FEAT + 1) // 2
PHI_PAD = 160
LANES = 128
ONE, TAG, REST = HD, HD + 1, HD + 2
MIB = 1024 * 1024
VMEM_LIMIT = 60 * MIB

BF = jnp.bfloat16
F32 = jnp.float32
SMEM = pl.BlockSpec(memory_space=pltpu.SMEM)
VMEM = pl.BlockSpec(memory_space=pltpu.VMEM)
ANY = pl.BlockSpec(memory_space=pltpu.HBM)


def feature_tables():
    left = np.zeros((PHI_PAD, FEAT), np.float32)
    right = np.zeros((PHI_PAD, FEAT), np.float32)
    cols = np.zeros((PHI_PAD, 8), np.float32)
    cols[0, :3] = 1.0
    at = 1
    for i in range(FEAT):
        left[at, i] = 1.0
        cols[at, 1] = 1.0
        cols[at, 2] = FEAT**-0.25
        at += 1
    for i in range(FEAT):
        for j in range(i, FEAT):
            left[at, i] = 1.0
            right[at, j] = 1.0
            cols[at, 2] = (1.0 if i == j else 2.0**0.5) / (2.0 * FEAT) ** 0.5
            at += 1
    return left.astype(jnp.bfloat16), right.astype(jnp.bfloat16), cols


def dot(a, b, dims=((1,), (0,))):
    return lax.dot_general(a, b, (dims, ((), ())), preferred_element_type=F32)


def kernel_call(body, out_shape, in_specs, out_specs, scratch, flops, nbytes, limit=VMEM_LIMIT, aliases=None):
    return pl.pallas_call(
        body,
        out_shape=out_shape,
        in_specs=in_specs,
        out_specs=out_specs,
        scratch_shapes=scratch,
        input_output_aliases=aliases or {},
        compiler_params=pltpu.CompilerParams(vmem_limit_bytes=limit),
        cost_estimate=pl.CostEstimate(flops=flops, bytes_accessed=nbytes, transcendentals=0),
    )


def start(source, target, sem):
    copy = pltpu.make_async_copy(source, target, sem)
    copy.start()
    return copy


def packing(rows, columns):
    tiles, rest = divmod(columns, LANES)
    share = LANES // rest if rest and LANES % rest == 0 else 1
    if rows % (16 * share):
        share = 1
    return tiles, rest, share, tiles * rows + (rows // share if rest else 0)


def pack(block, target, base):
    rows = block.shape[0]
    tiles, rest, share, _ = packing(*block.shape)
    for t in range(tiles):
        target[base + t * rows : base + (t + 1) * rows, :] = block[:, t * LANES : (t + 1) * LANES].astype(BF)
    if rest:
        short = rows // share
        last = [block[q * short : (q + 1) * short, tiles * LANES :] for q in range(share)]
        if share * rest < LANES:
            last.append(jnp.zeros((short, LANES - share * rest), block.dtype))
        at = base + tiles * rows
        target[at : at + short, :] = jnp.concatenate(last, axis=1).astype(BF)


def unpack(source, base, target, row, rows, columns):
    tiles, rest, share, _ = packing(rows, columns)
    for t in range(tiles):
        piece = source[base + t * rows : base + (t + 1) * rows, :]
        target[row : row + rows, t * LANES : (t + 1) * LANES] = piece.astype(target.dtype)
    if rest:
        short = rows // share
        at = base + tiles * rows
        last = source[at : at + short, :].astype(F32)
        for q in range(share):
            piece = last[:, q * rest : (q + 1) * rest].astype(target.dtype)
            target[row + q * short : row + (q + 1) * short, tiles * LANES : columns] = piece


def staged_call(body, out_shape, scalars, operands, scratch, flops, nbytes, given=(), limit=VMEM_LIMIT):
    buffers = [pltpu.VMEM(x.shape, x.dtype) for x in list(operands) + list(out_shape)]
    ins, outs = len(operands), len(out_shape)

    def run(*refs):
        values, refs = refs[: len(scalars)], refs[len(scalars) :]
        ready, refs = refs[: len(given)], refs[len(given) :]
        far, refs = refs[: ins + outs], refs[ins + outs :]
        near, extra, sems = refs[: ins + outs], refs[ins + outs : -1], refs[-1]
        loads = [start(far[k], near[k], sems.at[k]) for k in range(ins)]
        for load in loads:
            load.wait()
        body(*values, *ready, *near, *extra)
        sends = [start(near[k], far[k], sems.at[k]) for k in range(ins, ins + outs)]
        for send in sends:
            send.wait()

    return kernel_call(
        run,
        [pltpu.HBM(x.shape, x.dtype) for x in out_shape],
        [SMEM] * len(scalars) + [VMEM] * len(given) + [ANY] * ins,
        [ANY] * outs,
        buffers + list(scratch) + [pltpu.SemaphoreType.DMA((ins + outs,))],
        flops,
        nbytes,
        limit,
    )(*scalars, *given, *operands)


def pick_pages(table, own, picked, groups, per_group, per_peer):
    def one_group(g, carry):
        spot = g * per_peer
        for k in range(per_group):
            local = table[g * per_group + k] - own * per_group
            picked[spot] = local
            spot = spot + jnp.where((local >= 0) & (local < per_group), 1, 0)
        return carry

    lax.fori_loop(0, groups, one_group, 0)


def place_pages(table, own, seen, source, target, groups, per_group, per_peer, page_len):
    for g in range(groups):
        seen[g] = 0
    for k in range(per_group):
        holder = lax.div(table[own * per_group + k], per_group)
        slot = holder * per_peer + seen[holder]
        seen[holder] = seen[holder] + 1
        start = pl.multiple_of(slot * page_len, page_len)
        target[k * page_len : (k + 1) * page_len, :] = source[pl.ds(start, page_len), :]


def picked_rows(source, picked, g, per_peer, page_len):
    pages = []
    for b in range(per_peer):
        at = pl.multiple_of(picked[g * per_peer + b] * page_len, page_len)
        pages.append(source[pl.ds(at, page_len), :])
    return jnp.concatenate(pages, axis=0)


def project_kernel(
    dims, table, hidden_in, gain, wq_in, wd_in, out_in, hidden, wq, wd, normed, wide, out, picked, sems
):
    groups, per_group, per_peer, page_len = dims
    rows, model_width = hidden.shape
    low = wd.shape[1]
    pieces = 4
    part = rows // pieces
    strip = wq.shape[0] // 2
    loads = [
        start(hidden_in.at[pl.ds(k * part, part)], hidden.at[pl.ds(k * part, part)], sems.at[k]) for k in range(pieces)
    ]
    weights = [start(wd_in, wd, sems.at[pieces])]
    for k in range(2):
        half = pl.ds(k * strip, strip)
        weights.append(start(wq_in.at[half], wq.at[half], sems.at[pieces + 1 + k]))
    pick_pages(table, lax.axis_index("group"), picked, groups, per_group, per_peer)
    step = 32
    scale = gain[...].reshape(1, model_width)

    def norm_rows(i, carry):
        at = pl.ds(pl.multiple_of(i * step, step), step)
        x = hidden[at, :].astype(F32)
        meansq = jnp.mean(x * x, axis=-1, keepdims=True)
        normed[at, :] = (x * lax.rsqrt(meansq + EPSILON) * scale).astype(BF)
        return carry

    for k in range(pieces):
        loads[k].wait()
        lax.fori_loop(k * part // step, (k + 1) * part // step, norm_rows, 0, unroll=2)
    for load in weights:
        load.wait()
    wide[:, :low] = dot(normed[...], wd[...]).astype(wide.dtype)
    wide[:, low:] = dot(normed[...], wq[...], ((1,), (1,))).astype(wide.dtype)
    sends = []
    for g in range(groups):
        pack(picked_rows(wide, picked, g, per_peer, page_len), out.at[g], 0)
        sends.append(start(out.at[g], out_in.at[g], sems.at[pieces + 3 + g]))
    for send in sends:
        send.wait()


def residual_kernel(dims, shards, base, table, hidden_in, out_in, window, wide, pages, picked, sems):
    groups, per_group, per_peer, page_len = dims
    own_shard = lax.axis_index("mp")
    for j in range(shards):

        @pl.when(own_shard == j)
        def _(j=j):
            columns, _ = column_window(j, shards, hidden_in.shape[1])
            start(hidden_in.at[:, columns], window, sems.at[groups])

    pick_pages(table, lax.axis_index("group"), picked, groups, per_group, per_peer)
    pltpu.make_async_copy(hidden_in.at[:, 0 : window.shape[1]], window, sems.at[groups]).wait()
    for j in range(shards):

        @pl.when(own_shard == j)
        def _(j=j):
            _, at = column_window(j, shards, hidden_in.shape[1])
            wide[...] = window[:, at : at + wide.shape[1]].astype(F32)

    sends = []
    for g in range(groups):
        pack(picked_rows(wide, picked, g, per_peer, page_len), pages.at[g], 0)
        sends.append(start(pages.at[g], out_in.at[g, pl.ds(base, pages.shape[1])], sems.at[g]))
    for send in sends:
        send.wait()


def products_kernel(groups, shards, w_out_in, w_up_in, *refs):
    blocks = refs[:shards]
    _, out_in, vocab, w_out, w_up, products, shared, sems = refs[shards:]
    inner, model_width = w_out.shape
    low = w_up.shape[0]
    width = model_width // shards
    held = blocks[0].shape[0]
    loads = [start(w_up_in, w_up, sems.at[groups])]
    for k in range(inner // HD):
        rows = pl.ds(k * HD, HD)
        loads.append(start(w_out_in.at[rows], w_out.at[rows], sems.at[groups + 1 + k]))
    own_shard = lax.axis_index("mp")
    for i in range(shards):
        at = lax.rem(own_shard + i + 1, shards) * held
        vocab[pl.ds(pl.multiple_of(at, held), held), :] = blocks[i][...]
    for load in loads:
        load.wait()
    products[:, :inner] = dot(vocab[...], w_out[...], ((1,), (1,)))
    products[:, inner : inner + low] = dot(vocab[...], w_up[...], ((1,), (1,)))
    for j in range(shards):

        @pl.when(own_shard == j)
        def _(j=j):
            products[:, inner + low :] = vocab[:, j * width : (j + 1) * width].astype(F32)

    pack(products[...], shared, 0)
    sends = [start(shared, out_in.at[g, pl.ds(0, shared.shape[0])], sems.at[g]) for g in range(groups)]
    for send in sends:
        send.wait()


def phi_of(vectors, left, right, cols):
    first = dot(left[...], vectors) + cols[:, 0:1]
    second = dot(right[...], vectors) + cols[:, 1:2]
    return first * second * cols[:, 2:3]


def with_ones(values):
    lane = lax.broadcasted_iota(jnp.int32, (values.shape[0], LANES - HD), 1)
    return jnp.concatenate([values, jnp.where(lane == 0, 1.0, 0.0).astype(values.dtype)], axis=1)


def with_ones_t(values):
    row = lax.broadcasted_iota(jnp.int32, (LANES - HD, values.shape[1]), 0)
    return jnp.concatenate([values, jnp.where(row == 0, 1.0, 0.0).astype(values.dtype)], axis=0)


def same_upto(segrow):
    count = segrow.shape[1]
    ids = segrow[...].astype(F32)
    column = jnp.transpose(jnp.broadcast_to(ids, (8, count)))[:, 0:1]
    behind = lax.broadcasted_iota(jnp.int32, (count, count), 0)
    ahead = lax.broadcasted_iota(jnp.int32, (count, count), 1)
    return jnp.where((column == ids) & (behind <= ahead), 1.0, 0.0)


def group_kernel(
    dims, low, heads, table, arrived, segrow, left, right, cols, ordered_in, ordered_t_in, state_in, nd_in,
    state, wide, placed, ordered, ordered_t, nd, mask, seen, sems
):
    groups, per_group, per_peer, page_len = dims
    tall = per_peer * page_len
    count, sent = placed.shape
    mask[...] = same_upto(segrow)
    for g in range(groups):
        unpack(arrived.at[g], 0, wide, g * tall, tall, sent)
    place_pages(table, lax.axis_index("group"), seen, wide, placed, groups, per_group, per_peer, page_len)
    ordered[...] = placed[:, low:].astype(BF)
    for at in range(0, sent, LANES):
        end = min(at + LANES, sent)
        ordered_t[at:end, :] = jnp.transpose(placed[:, at:end]).astype(BF)
    sends = [start(ordered_t, ordered_t_in, sems.at[0]), start(ordered, ordered_in, sems.at[1])]

    last = segrow[:, count - 1 : count]
    member = jnp.where(segrow[...] == last, 1.0, 0.0)
    total = jnp.sum(member, axis=1, keepdims=True)
    fine = total - total.astype(BF).astype(F32)
    tag = last.astype(F32) + 1.0
    row = lax.broadcasted_iota(jnp.int32, (PHI_PAD, LANES), 0)
    lane = lax.broadcasted_iota(jnp.int32, (PHI_PAD, LANES), 1)
    block = 256 if count % 256 == 0 else count
    for h in range(heads):
        at = h * HEAD
        key = ordered[:, at + FEAT : at + 2 * FEAT] * BF(0.25)
        value = ordered[:, at + 2 * FEAT : at + HEAD]
        at = low + h * HEAD
        query_t = ordered_t[at : at + FEAT, :]
        key_t = ordered_t[at + FEAT : at + 2 * FEAT, :]
        extended_t = with_ones_t(ordered_t[at + 2 * FEAT : at + HEAD, :])

        phi = (phi_of(key_t, left, right, cols) * member).astype(BF)
        summed = dot(phi, with_ones(value))
        summed = jnp.where((row == 0) & (lane == TAG), tag, summed)
        summed = jnp.where((row == 0) & (lane == REST), fine, summed)
        state[h] = summed.astype(BF)

        for begin in range(0, count, block):
            end = begin + block
            s = dot(key[:end], query_t[:, begin:end])
            w = (1.0 + s * (1.0 + 0.5 * s)) * mask[:end, begin:end]
            nd[h, :, begin:end] = dot(extended_t[:, :end], w.astype(BF))
        sends.append(start(nd.at[h], nd_in.at[h], sems.at[3 + h]))
    sends.append(start(state, state_in, sems.at[2]))
    for send in sends:
        send.wait()


def split3(x):
    a = x.astype(BF)
    rest = x - a.astype(F32)
    b = rest.astype(BF)
    return jnp.concatenate([a, b, (rest - b.astype(F32)).astype(BF)], axis=0)


def state_corner(state):
    corner = state[0, 0:1, :].astype(F32)
    return corner[:, TAG : TAG + 1], corner[:, ONE : ONE + 1] + corner[:, REST : REST + 1]


def column_window(j, shards, model_width):
    width = model_width // shards
    size = window_size(shards, model_width)
    first = min(j * width // LANES * LANES, model_width - size)
    return slice(first, first + size), j * width - first


def window_size(shards, model_width):
    width = model_width // shards
    return max(-(-(j * width % LANES + width) // LANES) * LANES for j in range(shards))


def far_tables(shards):
    if shards == 4:
        return [(3, 3, 0, 0), (2, None, None, 1)]
    tables = [tuple({0: shards - 1, shards - 1: 0}.get(own) for own in range(shards))]
    for distance in range(shards - 2, 1, -1):
        tables += [offset_table(distance, shards), offset_table(-distance, shards)]
    return tables


def near_tables(shards):
    if shards == 4:
        return [(0, 1, 2, 3), (1, 0, 3, 2), (None, 2, 1, None)]
    return [offset_table(offset, shards) for offset in (0, 1, -1)]


def offset_table(offset, shards):
    return tuple(own + offset if 0 <= own + offset < shards else None for own in range(shards))


def each_shard(tables):
    for k, table in enumerate(tables):
        for own, j in enumerate(table):
            if j is not None:
                yield k, own, j


def shard_parts(tables, w_out_in, w_up_in, weights, w_sems, inputs, held_out, outs, sems):
    own_shard = lax.axis_index("mp")
    shards = len(tables[0])
    inner, model_width = w_out_in.shape
    width = model_width // shards

    def copies(k, j):
        window, _ = column_window(j, shards, model_width)
        return (
            pltpu.make_async_copy(w_out_in.at[:, window], weights.at[k, pl.ds(0, inner)], w_sems.at[2 * k]),
            pltpu.make_async_copy(
                w_up_in.at[:, window], weights.at[k, pl.ds(inner, w_up_in.shape[0])], w_sems.at[2 * k + 1]
            ),
        )

    def fetch():
        for k, own, j in each_shard(tables):

            @pl.when(own_shard == own)
            def _(k=k, j=j):
                for copy in copies(k, j):
                    copy.start()

    def compute():
        for k, own, j in each_shard(tables):

            @pl.when(own_shard == own)
            def _(k=k, j=j):
                for copy in copies(k, j):
                    copy.wait()
                _, at = column_window(j, shards, model_width)
                held_out[k] = dot(weights[k, :, at : at + width], inputs[...], ((0,), (0,))).astype(BF)
                start(held_out.at[k], outs[k], sems.at[k])

    def finish():
        for k, own, j in each_shard(tables):

            @pl.when(own_shard == own)
            def _(k=k):
                pltpu.make_async_copy(held_out.at[k], outs[k], sems.at[k]).wait()

    return fetch, compute, finish


def finish_kernel(
    low, heads, shards, ordered_t_in, nd_in, state, segrow, slotrow, left, right, cols, w_out_in, w_up_in, *refs
):
    far = far_tables(shards)
    outs = refs[: len(far)]
    inputs_in, state_in, queries, nd, weights, inputs, held_out, sems, w_sems = refs[len(far) :]
    inner = heads * HD
    sem = iter(range(len(far), len(far) + 2 * heads + 3))
    lows = start(ordered_t_in.at[pl.ds(0, low)], inputs.at[pl.ds(inner, low)], sems.at[next(sem)])
    fetches = []
    for h in range(heads):
        rows = pl.ds(low + h * HEAD, FEAT)
        fetches.append(start(ordered_t_in.at[rows], queries.at[h], sems.at[next(sem)]))
        fetches.append(start(nd_in.at[h], nd.at[h], sems.at[next(sem)]))
    fetch_weights, compute, finish = shard_parts(
        far, w_out_in, w_up_in, weights, w_sems, inputs, held_out, outs, sems
    )
    fetch_weights()
    tag, _ = state_corner(state)
    carried = jnp.where(segrow[...].astype(F32) + 1.0 == tag, 1.0, 0.0)
    row_slot = lax.div(lax.broadcasted_iota(jnp.int32, (low, 1), 0), RANK)
    lows.wait()
    lowered = jnp.where(slotrow[...] == row_slot, inputs[inner:, :].astype(F32), 0.0)
    inputs[inner:, :] = lowered.astype(BF)
    for h in range(heads):
        fetches[2 * h].wait()
        fetches[2 * h + 1].wait()
        cross = dot(state[h], phi_of(queries[h], left, right, cols).astype(BF), ((0,), (0,)))
        both = nd[h] + carried * cross
        inputs[h * HD : (h + 1) * HD, :] = (both[:HD, :] * (1.0 / both[ONE : ONE + 1, :])).astype(BF)
    compute()
    kept = [start(inputs, inputs_in, sems.at[next(sem)]), start(state, state_in, sems.at[next(sem)])]
    finish()
    for copy in kept:
        copy.wait()


def near_kernel(shards, w_out_in, w_up_in, inputs_in, *refs):
    near = near_tables(shards)
    outs = refs[: len(near)]
    weights, inputs, held_out, sems, w_sems = refs[len(near) :]
    load = start(inputs_in, inputs, sems.at[len(near)])
    fetch, compute, finish = shard_parts(near, w_out_in, w_up_in, weights, w_sems, inputs, held_out, outs, sems)
    fetch()
    load.wait()
    compute()
    finish()


def logits_kernel(dims, shards, width, table, arrived, inputs, out, vocab, both, wide, placed, seen):
    groups, per_group, per_peer, page_len = dims
    tall = per_peer * page_len
    inner = inputs.shape[0]
    rows = vocab.shape[0] // groups
    _, _, _, base = packing(rows, inner + width)
    for g in range(groups):
        unpack(arrived.at[g], 0, vocab, g * rows, rows, inner + width)
        unpack(arrived.at[g], base, wide, g * tall, tall, width)
    place_pages(table, lax.axis_index("group"), seen, wide, placed, groups, per_group, per_peer, page_len)
    both[:inner, :] = inputs[...]
    both[inner:, :] = jnp.transpose(placed[...]).astype(BF)
    block = inputs.shape[1] // shards
    scored = dot(vocab[...], both[...])
    for j in range(shards):
        out[j] = scored[:, j * block : (j + 1) * block].astype(BF)


def norms_kernel(low, heads, ordered, ordered_t, state, segrow, left, right, cols, norms, mask):
    count = segrow.shape[1]
    mask[...] = same_upto(segrow)
    upto = mask[...].astype(BF)
    tag, held = state_corner(state)
    carried = jnp.where(segrow[...].astype(F32) + 1.0 == tag, 1.0, 0.0)
    value_lane = lax.broadcasted_iota(jnp.int32, (1, LANES), 1) < HD
    counted = carried * held + jnp.sum(mask[...], axis=0, keepdims=True)
    block = 256 if count % 256 == 0 else count
    increments = []
    before = []
    for h in range(heads):
        at = h * HEAD
        key = ordered[:, at + FEAT : at + 2 * FEAT] * BF(0.25)
        value = ordered[:, at + 2 * FEAT : at + HEAD]
        at = low + h * HEAD
        key_t = ordered_t[at + FEAT : at + 2 * FEAT, :]
        value_t = ordered_t[at + 2 * FEAT : at + HEAD, :]
        wide_key = key_t.astype(F32)
        wide_value = value_t.astype(F32)
        self_score = 0.25 * jnp.sum(wide_key * wide_key, axis=0, keepdims=True)
        self_value = jnp.sum(wide_value * wide_value, axis=0, keepdims=True)
        diagonal = (1.0 + self_score * (1.0 + 0.5 * self_score)) * self_value
        below = []
        for begin in range(0, count, block):
            end = begin + block
            kk = dot(key[:end], key_t[:, begin:end])
            vv = dot(value[:end], value_t[:, begin:end])
            gram = (1.0 + kk * (1.0 + 0.5 * kk)) * vv * mask[:end, begin:end]
            below.append(jnp.sum(gram, axis=0, keepdims=True))
        added = 2.0 * jnp.concatenate(below, axis=1) - diagonal
        held_state = state[h]
        against = dot(held_state, phi_of(key_t, left, right, cols).astype(BF), ((0,), (0,)))[:HD, :]
        along = jnp.sum(against * wide_value, axis=0, keepdims=True)
        increments.append(added + 2.0 * carried * along)
        wide_state = jnp.where(value_lane, held_state.astype(F32), 0.0)
        per_lane = jnp.sum(wide_state * wide_state, axis=0, keepdims=True)
        before.append(jnp.sum(per_lane, axis=1, keepdims=True))
    if heads % 8:
        increments.append(jnp.zeros((8 - heads % 8, count), F32))
    stacked = split3(jnp.concatenate(increments, axis=0))
    thrice = dot(stacked, upto)
    rows = thrice.shape[0] // 3
    summed = thrice[:rows] + thrice[rows : 2 * rows] + thrice[2 * rows :]
    for h in range(heads):
        total = carried * before[h] + summed[h : h + 1, :]
        norms[h : h + 1, :] = jnp.sqrt(total / (counted * float(FEAT * HD)))


def relay_kernel(across, inward, paired_in, centre_in, to_pair_in, to_centre_in, paired, centre, sems):
    loads = [start(paired_in, paired, sems.at[0]), start(centre_in, centre, sems.at[1])]
    here = lax.axis_index("mp")
    middle = (here == 1) | (here == 2)
    for load in loads:
        load.wait()

    @pl.when(middle)
    def _():
        paired[...] = (paired[...].astype(F32) + across[...].astype(F32)).astype(BF)

    sends = [start(paired, to_pair_in, sems.at[2])]

    @pl.when(middle)
    def _():
        centre[...] = (centre[...].astype(F32) + inward[...].astype(F32)).astype(BF)

    sends.append(start(centre, to_centre_in, sems.at[3]))
    for copy in sends:
        copy.wait()


def best_kernel(shards, pieces, best):
    whole = pieces[0].astype(F32)
    for i in range(1, shards):
        whole = whole + pieces[i].astype(F32)
    best[...] = jnp.max(whole, axis=0, keepdims=True)


def exchange(blocks, axis):
    return lax.all_to_all(blocks, axis, split_axis=0, concat_axis=0, tiled=True)


def ring_rows(values, axis):
    size = lax.axis_size(axis)
    steps = [lax.ppermute(values, axis, [(i, (i + by) % size) for i in range(size)]) for by in range(size - 1, 0, -1)]
    return [*steps, values]


def joined(*parts):
    return sum(part.astype(F32) for part in parts).astype(BF)


def line_sums(far_terms, near_terms, axis, beside):
    size = lax.axis_size(axis)

    def send(values, *pairs):
        return lax.ppermute(values, axis, pairs)

    own_term = near_terms[0]
    if size == 4:
        here = lax.axis_index(axis)
        middle = (here == 1) | (here == 2)
        across = send(far_terms[0], (1, 2), (2, 1), (0, 3), (3, 0))
        inward = send(far_terms[1], (0, 1), (3, 2))
        across, inward, beside = lax.optimization_barrier((across, inward, beside))
        whole = own_term.shape
        to_pair, to_centre = kernel_call(
            relay_kernel,
            [pltpu.HBM(whole, BF)] * 2,
            [VMEM, VMEM, ANY, ANY],
            [ANY, ANY],
            [pltpu.VMEM(whole, BF), pltpu.VMEM(whole, BF), pltpu.SemaphoreType.DMA((4,))],
            1,
            1,
            VMEM_LIMIT - 416 * 1024,
        )(across, inward, near_terms[1], near_terms[2])
        paired = send(to_pair, (0, 1), (1, 0), (2, 3), (3, 2))
        centre = send(to_centre, (1, 2), (2, 1))
        return (own_term, jnp.where(middle, centre, across), paired), beside
    terms = {1: near_terms[1], -1: near_terms[2], size - 1: far_terms[0], 1 - size: far_terms[0]}
    for distance in range(size - 2, 1, -1):
        terms[distance], terms[-distance] = far_terms[2 * (size - 1 - distance) - 1 :][:2]
    going_up = going_down = None
    for step in range(1, size):
        to_up = terms[size - step]
        to_down = terms[step - size]
        if step > 1:
            to_up = joined(to_up, going_up)
            to_down = joined(to_down, going_down)
        going_up = send(to_up, *[(i, i + 1) for i in range(step)])
        going_down = send(to_down, *[(i, i - 1) for i in range(size - step, size)])
    return (own_term, going_up, going_down), beside


def on_device(
    hidden,
    norm_gain,
    qkv_weight,
    out_weight,
    adapter_down,
    adapter_up,
    vocab_rows,
    segments,
    request_adapter,
    adapter_slot,
    page_table,
):
    groups = lax.axis_size("group")
    shards = lax.axis_size("mp")
    own_shard = lax.axis_index("mp")
    count, model_width = hidden.shape
    per_group = page_table.shape[0] // groups
    per_peer = per_group // groups
    page_len = count // per_group
    dims = (groups, per_group, per_peer, page_len)
    qkv_cols = qkv_weight.shape[1]
    heads = qkv_cols // HEAD
    low = adapter_down.shape[1]
    inner = heads * HD
    width = model_width // shards
    sent = low + qkv_cols
    tall = per_peer * page_len
    packed = packing(tall, sent)[-1]
    some = shards * vocab_rows.shape[0]
    scored = groups * some
    aside = packing(some, inner + low + width)[-1] + packing(tall, width)[-1]
    shape = jax.ShapeDtypeStruct
    dma = pltpu.SemaphoreType.DMA
    picked = pltpu.SMEM((groups * per_peer + 1,), jnp.int32)

    left, right, cols = [jnp.asarray(t) for t in feature_tables()]
    segrow = segments.reshape(1, count)
    request_ids = jnp.arange(request_adapter.shape[0], dtype=jnp.int32)
    adapter_ids = jnp.arange(adapter_slot.shape[0], dtype=jnp.int32)

    outgoing = kernel_call(
        functools.partial(project_kernel, dims),
        pltpu.HBM((groups, packed, LANES), BF),
        [SMEM, ANY, VMEM, ANY, ANY],
        ANY,
        [
            pltpu.VMEM((count, model_width), BF),
            pltpu.VMEM((qkv_cols, model_width), BF),
            pltpu.VMEM((model_width, low), BF),
            pltpu.VMEM((count, model_width), BF),
            pltpu.VMEM((count, sent), F32 if page_len % 16 else BF),
            pltpu.VMEM((groups, packed, LANES), BF),
            picked,
            dma((7 + groups,)),
        ],
        2 * count * model_width * sent,
        2 * (count * model_width + model_width * sent),
    )(page_table, hidden, norm_gain, qkv_weight.T, adapter_down)
    arrived = exchange(outgoing, "group")

    after_vocab, after_adapter, later_hidden, _ = lax.optimization_barrier(
        (vocab_rows, request_adapter, hidden, outgoing)
    )
    some_vocab = ring_rows(after_vocab, "mp")
    request_slot = jnp.sum(jnp.where(after_adapter[:, None] == adapter_ids[None, :], adapter_slot[None, :], 0), axis=1)
    slots = jnp.sum(jnp.where(segrow == request_ids[:, None], request_slot[:, None], 0), axis=0, keepdims=True)
    slotrow = slots - own_shard * (low // RANK)
    window = window_size(shards, model_width)
    ahead = packing(some, inner + low + width)[-1]
    beside = kernel_call(
        functools.partial(residual_kernel, dims, shards, ahead),
        pltpu.HBM((groups, aside, LANES), BF),
        [SMEM, ANY],
        ANY,
        [
            pltpu.VMEM((count, window), BF),
            pltpu.VMEM((count, width), F32),
            pltpu.VMEM((groups, packing(tall, width)[-1], LANES), BF),
            picked,
            dma((groups + 1,)),
        ],
        1,
        1,
    )(page_table, later_hidden)
    beside = kernel_call(
        functools.partial(products_kernel, groups, shards),
        pltpu.HBM((groups, aside, LANES), BF),
        [ANY, ANY] + [VMEM] * shards + [ANY],
        ANY,
        [
            pltpu.VMEM((some, model_width), BF),
            pltpu.VMEM((inner, model_width), BF),
            pltpu.VMEM((low, model_width), BF),
            pltpu.VMEM((some, inner + low + width), F32),
            pltpu.VMEM((ahead, LANES), BF),
            dma((groups + 1 + heads,)),
        ],
        2 * some * model_width * (inner + low),
        2 * count * model_width,
        44 * MIB,
        {2 + shards: 0},
    )(out_weight, adapter_up, *some_vocab, beside)
    arrived, beside, slotrow = lax.optimization_barrier((arrived, beside, slotrow))

    ordered, ordered_t, state, nd = kernel_call(
        functools.partial(group_kernel, dims, low, heads),
        (
            pltpu.HBM((count, qkv_cols), BF),
            pltpu.HBM((sent, count), BF),
            pltpu.HBM((heads, PHI_PAD, LANES), BF),
            pltpu.HBM((heads, LANES, count), F32),
        ),
        [SMEM] + [VMEM] * 5,
        (ANY, ANY, ANY, ANY),
        [
            pltpu.VMEM((heads, PHI_PAD, LANES), BF),
            pltpu.VMEM((count, sent), F32),
            pltpu.VMEM((count, sent), F32),
            pltpu.VMEM((count, qkv_cols), BF),
            pltpu.VMEM((sent, count), BF),
            pltpu.VMEM((heads, LANES, count), F32),
            pltpu.VMEM((count, count), F32),
            pltpu.SMEM((groups,), jnp.int32),
            dma((3 + heads,)),
        ],
        heads * 2 * count * count * 512,
        6 * count * sent,
        40 * MIB,
    )(page_table, arrived, segrow, left, right, cols)
    beside, state = lax.optimization_barrier((beside, state))
    beside = exchange(beside, "group")
    state = lax.ppermute(state, "group", [(i, i + 1) for i in range(groups - 1)])

    far, near = len(far_tables(shards)), len(near_tables(shards))
    part = pltpu.HBM((width, count), BF)
    *far_terms, inputs, kept_state = kernel_call(
        functools.partial(finish_kernel, low, heads, shards),
        [part] * far + [pltpu.HBM((inner + low, count), BF), pltpu.HBM((heads, PHI_PAD, LANES), BF)],
        [ANY] * 2 + [VMEM] * 6 + [ANY] * 2,
        [ANY] * (far + 2),
        [
            pltpu.VMEM((heads, FEAT, count), BF),
            pltpu.VMEM((heads, LANES, count), F32),
            pltpu.VMEM((far, inner + low, window), BF),
            pltpu.VMEM((inner + low, count), BF),
            pltpu.VMEM((far, width, count), BF),
            dma((far + 2 * heads + 3,)),
            dma((2 * far,)),
        ],
        20 * count * (inner + low) * model_width,
        40 * count * model_width,
    )(ordered_t, nd, state, segrow, slotrow, left, right, cols, out_weight, adapter_up)
    near_terms = kernel_call(
        functools.partial(near_kernel, shards),
        [part] * near,
        [ANY] * 3,
        [ANY] * near,
        [
            pltpu.VMEM((near, inner + low, window), BF),
            pltpu.VMEM((inner + low, count), BF),
            pltpu.VMEM((near, width, count), BF),
            dma((near + 1,)),
            dma((2 * near,)),
        ],
        1,
        1,
    )(out_weight, adapter_up, inputs)

    [logits] = staged_call(
        functools.partial(logits_kernel, dims, shards, width),
        [shape((shards, scored, count // shards), BF)],
        [page_table],
        [inputs],
        [
            pltpu.VMEM((scored, inner + low + width), BF),
            pltpu.VMEM((inner + low + width, count), BF),
            pltpu.VMEM((count, width), F32),
            pltpu.VMEM((count, width), F32),
            pltpu.SMEM((groups,), jnp.int32),
        ],
        1,
        1,
        given=[beside],
        limit=(40 if scored <= 512 else 56) * MIB,
    )
    [state_norms] = staged_call(
        functools.partial(norms_kernel, low, heads),
        [shape((heads, count), F32)],
        [],
        [ordered, ordered_t, kept_state, segrow, left, right, cols],
        [pltpu.VMEM((count, count), F32)],
        1,
        1,
    )
    (own_term, *others), [state_norms, _] = line_sums(far_terms, near_terms, "mp", [state_norms, logits])
    logits = exchange(logits, "mp")
    best = kernel_call(
        functools.partial(best_kernel, shards),
        shape((1, count // shards), F32),
        [VMEM],
        VMEM,
        [],
        1,
        1,
        32 * MIB,
    )(logits)
    own_term, best = lax.optimization_barrier((own_term, best))
    return joined(own_term, *others).T, state_norms, best.reshape(-1)


def solution(mesh):
    placed = (
        P("group", None),
        P(),
        P(None, "mp"),
        P("mp", None),
        P(None, "mp"),
        P("mp", None),
        P(("group", "mp"), None),
        P("group"),
        P(),
        P(),
        P(),
    )
    return jax.shard_map(
        on_device,
        mesh=mesh,
        in_specs=placed,
        out_specs=(P("group", "mp"), P("mp", "group"), P(("group", "mp"))),
        check_vma=False,
    )
```
